32 devices in a mesh: dp: 4 (over y, x), expert: 8 (over z, core).
Axes of the slice: x: 2, y: 2, z: 4, core: 2. Of those that a mesh axis runs over, the one named last changes fastest.
Arguments:
- layer_input: bfloat16 [32768, 1024], P(('dp', 'expert')), may hold values from -6 to 6
- segments: int32 [32, 1024], P(('dp', 'expert')), may hold values from 0 to 7, never falling along the last dimension, each value on 1 to 256 neighbouring positions
- keep_mask: int32 [32, 1024], P(('dp', 'expert')), may hold values 0 or 1
- att_routes: int32 [32768, 8, 2], P(('dp', 'expert')), may hold values from 0 to 4, all different within a row
- moe_routes: int32 [32768, 16], P(('dp', 'expert')), may hold values from 0 to 47, all different within a row; in each aligned block of 1024 rows (0 to 1023, 1024 to 2047, ...) at most 488 rows name the same one
- expert_counts: int32 [48], P('expert'), may hold values from 0 to 2729
- norm_gain: float32 [1024], replicated, may hold values from 0.5 to 1.5
- w_query: bfloat16 [1024, 512], replicated, may hold values from -0.25 to 0.25
- w_key: bfloat16 [1024, 512], replicated, may hold values from -0.1875 to 0.1875
- w_select: bfloat16 [1024, 40], replicated, may hold values from -0.125 to 0.125
- w_value: bfloat16 [1024, 2560], replicated, may hold values from -0.1875 to 0.1875
- w_output: bfloat16 [2560, 1024], replicated, may hold values from -3 to 3
- w_router: bfloat16 [48, 1024], P('expert'), may hold values from -0.09375 to 0.09375
- w_in: bfloat16 [48, 1024, 128], P('expert'), may hold values from -0.1875 to 0.1875
- w_out: bfloat16 [48, 128, 1024], P('expert'), may hold values from -0.25 to 0.25
- cotangent: bfloat16 [32768, 1024], P(('dp', 'expert')), may hold values from -6 to 6
Outputs:
- layer_output: bfloat16 [32768, 1024], P(('dp', 'expert'))
- grad_input: bfloat16 [32768, 1024], P(('dp', 'expert'))
- grad_gain: float32 [1024], P(('dp', 'expert'))
- grad_query: float32 [1024, 512], P(('dp', 'expert'))
- grad_key: float32 [1024, 512], P(('dp', 'expert'))
- grad_select: float32 [1024, 40], P(('dp', 'expert'))
- grad_value: float32 [1024, 2560], P(('dp', 'expert'))
- grad_output: float32 [2560, 1024], P(None, ('dp', 'expert'))
- grad_router: float32 [48, 1024], P('expert')
- grad_w_in: float32 [48, 1024, 128], P('expert')
- grad_w_out: float32 [48, 128, 1024], P('expert')
- counts_out: int32 [48], P('expert')
The draws below stay inside these ranges and needn't reach their ends.
Inputs may be any that keep to these rules, and one draw needn't show every extreme that they name: `moe_routes`: in each aligned block of 1024 rows (the tokens of one device), no expert is named by more than 488 pairs, a bound that some block reaches; a row names 16 different experts. `att_routes`: each row names two different experts. `segments`: never falling along a sequence; each document holds 1 to 256 tokens.
All inputs are finite; a program needn't handle non-finite values. No bound on the sum of `keep_mask` on one device may be relied on, other than what follows from the above.
Results may differ from the reference program's by a relative error of at most 0.015.
The reference program's roundings to bfloat16 on the way count: a program that leaves them out, or rounds other values in their place, can miss the bound.
Values may be sent and summed in bfloat16 or wider, within the bound.
A program may use at most 576 MiB of HBM per device.

```python
import math
import jax
import jax.numpy as jnp
import numpy as np
from jax import lax

D = 1024
H = 4
DH = 128
VEXP = 5
FF_E = 128
TOP = 16
SEQ = 1024
DOCS = 8
SEQS_DEV = 1
DOC_MOST = 256
TOK_DEV = 1024
TOKENS = 32768
NSEQ = 32
EXPERTS = 48
CAP = 488


def plant(drawn, own_key, smallest, top_value):
    extent = drawn.shape
    spot = [jax.random.randint(jax.random.fold_in(own_key, axis), (), 0, extent[axis]) for axis in range(len(extent))]
    drawn = drawn.at[tuple(spot)].set(smallest)
    longest = extent.index(max(extent))
    spot[longest] = (spot[longest] + 1) % extent[longest]
    return drawn.at[tuple(spot)].set(top_value)


def levels(rng, extent, pieces, least, high):
    gain, own = 1.0, jax.random.fold_in(rng, 6)
    for dim, blocks in pieces:
        draws = jnp.exp(jax.random.uniform(jax.random.fold_in(own, dim), (blocks,), jnp.float32, least / len(pieces), high / len(pieces)))
        gain = gain * jnp.repeat(draws, extent[dim] // blocks).reshape([-1 if axis == dim else 1 for axis in range(len(extent))])
    return gain


def different_ones(stream_key, rows, number_of, top, lift):
    ranking = jax.random.permutation(jax.random.fold_in(stream_key, 1), number_of)
    pull = ranking
    for power in range(3):
        pull = pull * pull // number_of
    pull = pull * lift // number_of
    tickets = jax.random.randint(jax.random.fold_in(stream_key, 2), (rows, number_of), 0, 4096) + pull
    holders = jax.random.permutation(jax.random.fold_in(stream_key, 3), rows)[jnp.arange(number_of) % rows]
    tickets = jnp.where(jnp.arange(rows)[:, None] == holders[None, :], 1 << 14, tickets)
    merit = tickets * number_of + jnp.arange(number_of)
    return lax.top_k(merit.astype(jnp.int32), top)[1].astype(jnp.int32)


def split_up(number_of, total, limit, slope):
    weights = [(1 << 20) // math.isqrt(grade ** slope) + 1 for grade in range(2, number_of + 1)]
    spare, given = total - limit - (number_of - 1), [1] * (number_of - 1)
    while spare > 0:
        free = [i for i in range(number_of - 1) if given[i] < limit]
        mass, left = sum([weights[i] for i in free]), spare
        for i in free:
            addition = min(limit - given[i], max(1, left * weights[i] // mass), spare)
            given[i] = given[i] + addition
            spare = spare - addition
    return np.array([limit] + given)


def uneven(key, count, total, reach, skew):
    if count == 2:
        one = jax.random.randint(key, (), max(1, total - reach), min(reach, total - 1) + 1)
        return jnp.stack([one, total - one])
    tallies = jnp.asarray(split_up(count, total, reach, skew), jnp.int32)
    twos = (count - 1) // 2
    giver, receiver = tallies[1:1 + 2 * twos:2], tallies[2:2 + 2 * twos:2]
    margin = jnp.minimum(giver - 1, reach - receiver)
    moved = jax.random.randint(jax.random.fold_in(key, 1), (twos,), 0, 1 << 20) % (margin + 1)
    tallies = tallies.at[1:1 + 2 * twos:2].set(giver - moved).at[2:2 + 2 * twos:2].set(receiver + moved)
    return tallies[jax.random.permutation(jax.random.fold_in(key, 2), count)]


def shared_out(rng, own, number, rows, count, top, reach, skew):
    order = jax.random.permutation(rng, count)
    heavy_load, ordinary = load_shares(count, rows * top, reach, skew, True), load_shares(count, rows * top, reach, skew, False)
    places = jnp.arange(count)

    def named(tallies, turn):
        used = int((tallies > 0).sum())
        fixed = max(1, used // 4)
        shifted = fixed + (places - fixed + turn * (used - fixed)) % max(1, count - fixed)
        return jnp.zeros((count,), jnp.int32).at[order[jnp.where(places < fixed, places, shifted)]].set(jnp.asarray(tallies, jnp.int32))

    tallies = jnp.where(number % 4 == 0, named(heavy_load, number // 4), named(ordinary, number - number // 4 - 1))
    mixed = jax.random.permutation(jax.random.fold_in(own, 3), count)
    donor, sink = mixed[0:count // 2 * 2:2], mixed[1:count // 2 * 2:2]
    room = jnp.minimum(tallies[donor] - 1, reach - tallies[sink]) // 2
    room = jnp.where((donor == order[0]) | (sink == order[0]) | (tallies[sink] == 0), 0, jnp.maximum(room, 0))
    shifted = jax.random.randint(jax.random.fold_in(own, 4), (count // 2,), 0, 1 << 20) % (room + 1)
    tallies = tallies.at[donor].add(-shifted).at[sink].add(shifted)
    labels = jnp.searchsorted(jnp.cumsum(tallies), jnp.arange(rows * top), side="right").astype(jnp.int32)
    listing = labels.reshape(top, rows).T
    listing = listing[jax.random.permutation(jax.random.fold_in(own, 1), rows)]
    turn = jax.random.randint(jax.random.fold_in(own, 2), (rows, 1), 0, top)
    return jnp.take_along_axis(listing, (jnp.arange(top)[None, :] + turn) % top, axis=1)


def load_shares(number_of, total, reach, lean, full):
    loads = [(1 << 20) // math.isqrt(standing ** lean) + 1 for standing in range(1, number_of + 1)]
    largest = reach if full else min(reach, max(-(-total // number_of), total * loads[0] // sum(loads)))
    least = 1 if total - largest >= number_of - 1 else 0
    holding, spare = [largest] + [least] * (number_of - 1), total - largest - least * (number_of - 1)
    while spare > 0:
        free = [i for i in range(1, number_of) if holding[i] < largest] or [i for i in range(1, number_of) if holding[i] < reach]
        whole, left = sum([loads[i] for i in free]), spare
        for i in free:
            more = min(reach - holding[i], max(1, left * loads[i] // whole), spare)
            holding[i] = holding[i] + more
            spare = spare - more
    return np.array(holding)


def bell_draw(key, extent, scale, limit, cuts=(), kind=jnp.bfloat16):
    values = jax.random.normal(key, extent, jnp.float32) * scale
    if len(cuts) > 0:
        values = levels(key, extent, cuts, -0.22, 0.18) * values
    return jnp.clip(values, min=-limit, max=limit).astype(kind)


def setup_inputs(seed: int = 0) -> dict:
    seeds = jax.random.split(jax.random.key(seed), 17)
    layer_input = bell_draw(seeds[0], (TOKENS, D), 1.0, 6.0, ((0, 32),))
    segments = jax.vmap(lambda own: jnp.searchsorted(jnp.cumsum(uneven(own, DOCS, SEQ, DOC_MOST, 1)), jnp.arange(SEQ), side="right"))(jax.random.split(seeds[1], NSEQ)).reshape((NSEQ, SEQ)).astype(jnp.int32)
    keep_mask = plant((jax.random.randint(seeds[2], (NSEQ, SEQ), 0, 8) < 7).astype(jnp.int32), jax.random.fold_in(seeds[2], 1), 0, 1)
    att_routes = different_ones(seeds[3], TOKENS * (2 * H), VEXP, 2, 0).reshape((TOKENS, 2 * H, 2))
    moe_routes_keys = jax.random.split(jax.random.fold_in(seeds[4], 1), TOKENS // TOK_DEV)
    moe_routes_turns = jax.random.permutation(jax.random.fold_in(seeds[4], 3), TOKENS // TOK_DEV)
    moe_routes = jax.vmap(lambda own, number: shared_out(jax.random.fold_in(seeds[4], 2), own, number, TOK_DEV, EXPERTS, TOP, CAP, 2))(moe_routes_keys, moe_routes_turns).reshape((TOKENS, TOP))
    expert_counts = plant(jax.random.randint(seeds[5], (EXPERTS,), 0, TOKENS * TOP // (4 * EXPERTS)), jax.random.fold_in(seeds[5], 1), 0, (TOKENS * TOP // (4 * EXPERTS)) - 1).astype(jnp.int32)
    norm_gain = jnp.clip(1.0 + 0.1 * jax.random.normal(seeds[6], (D,), jnp.float32), 0.5, 1.5)
    w_query = bell_draw(seeds[7], (D, H * DH), (D // 2) ** -0.5, 0.25)
    w_key = bell_draw(seeds[8], (D, H * DH), D ** -0.5, 0.1875)
    w_select = bell_draw(seeds[9], (D, 2 * H * VEXP), (2 * D) ** -0.5, 0.125)
    w_value = bell_draw(seeds[10], (D, H * VEXP * DH), D ** -0.5, 0.1875)
    w_output = bell_draw(seeds[11], (H * VEXP * DH, D), 4 ** -0.5, 3.0)
    w_router = bell_draw(seeds[12], (EXPERTS, D), (4 * D) ** -0.5, 0.09375, ((0, 8),))
    w_in = bell_draw(seeds[13], (EXPERTS, D, FF_E), D ** -0.5, 0.1875, ((0, 8),))
    w_out = bell_draw(seeds[14], (EXPERTS, FF_E, D), (4 * FF_E) ** -0.5, 0.25, ((0, 8),))
    cotangent = bell_draw(seeds[15], (TOKENS, D), 1.0, 6.0, ((0, 32),))
    return dict(layer_input=layer_input, segments=segments, keep_mask=keep_mask, att_routes=att_routes, moe_routes=moe_routes, expert_counts=expert_counts, norm_gain=norm_gain, w_query=w_query, w_key=w_key, w_select=w_select, w_value=w_value, w_output=w_output, w_router=w_router, w_in=w_in, w_out=w_out, cotangent=cotangent)


@jax.custom_vjp
def low(v):
    return lax.optimization_barrier(v.astype(jnp.bfloat16)).astype(jnp.float32)

@jax.custom_vjp
def low_back(v):
    return v

def low_keep(v):
    return (low(v), None)

def low_pass(kept, grad):
    return (grad,)

def back_keep(v):
    return (v, None)

def back_low(kept, grad):
    return (low(grad),)
low.defvjp(low_keep, low_pass)
low_back.defvjp(back_keep, back_low)
NORM_EPS = 1e-05
ROPE_BASE = 10000.0
MASK_FILL = -1e+30
HIGHEST = lax.Precision.HIGHEST

def layer_norm(values, gain_vec):
    center = values - lax.optimization_barrier(jnp.mean(values, axis=-1, keepdims=True))
    spread = lax.optimization_barrier(jnp.mean(center * center, axis=-1, keepdims=True))
    return center * lax.rsqrt(spread + NORM_EPS) * gain_vec

def rope_tables(position, width_dh):
    half_dh = width_dh // 2
    freq_row = jnp.power(ROPE_BASE, jnp.arange(half_dh, dtype=jnp.float32) * (-2.0 / width_dh))
    angle_tab = position.astype(jnp.float32)[:, None] * freq_row[None, :]
    return (jnp.cos(angle_tab), jnp.sin(angle_tab))

def rotate(values, cos_tab, sin_tab):
    half_dh = values.shape[-1] // 2
    first_half = values[..., :half_dh]
    second_half = values[..., half_dh:]
    cos_b = cos_tab[:, None, :]
    sin_b = sin_tab[:, None, :]
    return jnp.concatenate([first_half * cos_b - second_half * sin_b, second_half * cos_b + first_half * sin_b], axis=-1)

def doc_layout(seg_row, keep_row):
    length_s = seg_row.shape[0]
    column = jnp.arange(length_s, dtype=jnp.int32)
    new_doc = jnp.concatenate([jnp.ones((1,), dtype=jnp.bool_), seg_row[1:] != seg_row[:-1]])
    doc_start = lax.cummax(jnp.where(new_doc, column, jnp.zeros_like(column)), axis=0)
    position = column - doc_start
    same_doc = seg_row[:, None] == seg_row[None, :]
    causal = column[None, :] <= column[:, None]
    visible = (keep_row[None, :] == 1) | (column[None, :] == column[:, None])
    return (position, same_doc & causal & visible)

def slot_table(routes, exp_total, capacity):
    flat_ids = routes.reshape(-1).astype(jnp.int32)
    pair_count = flat_ids.shape[0]
    top_k = routes.shape[1]
    sort_order = jnp.argsort(flat_ids, stable=True).astype(jnp.int32)
    ranked = flat_ids[sort_order]
    first_slot = jnp.searchsorted(ranked, jnp.arange(exp_total, dtype=jnp.int32), side='left').astype(jnp.int32)
    slot_rank = jnp.arange(pair_count, dtype=jnp.int32) - first_slot[ranked]
    slot_dest = ranked * capacity + slot_rank
    owner = jnp.zeros((exp_total * capacity,), jnp.int32).at[slot_dest].set(sort_order // top_k)
    filled = jnp.zeros((exp_total * capacity,), jnp.float32).at[slot_dest].set(1.0)
    return (owner, filled)

def attend_sequence(q_rows, k_rows, v_rows, allowed):
    scores = low_back(jnp.einsum('qhd,khd->hqk', q_rows, k_rows, precision=HIGHEST))
    scores = jnp.where(allowed[None, :, :], scores, MASK_FILL)
    row_max = lax.optimization_barrier(jnp.max(scores, axis=-1, keepdims=True))
    exp_terms = jnp.exp(scores - row_max)
    probs_f = exp_terms / lax.optimization_barrier(jnp.sum(exp_terms, axis=-1, keepdims=True))
    return low_back(jnp.einsum('hqk,khd->qhd', low(probs_f), v_rows, precision=HIGHEST))

def moe_part(hidden, routes_blk, w_router, w_in, w_out):
    exp_total = w_in.shape[0]
    owner, filled = slot_table(routes_blk, exp_total, CAP)
    sent = low(hidden)
    gathered = low_back((sent[owner] * filled[:, None]).reshape(exp_total, CAP, hidden.shape[1]))
    router_logit = lax.optimization_barrier(jnp.sum(gathered * w_router[:, None, :], axis=-1))
    gate_moe = jax.nn.sigmoid(router_logit)
    pre_act = low_back(jnp.einsum('ecd,edf->ecf', gathered, w_in, precision=HIGHEST))
    act_low = low(jax.nn.gelu(pre_act))
    expert_out = low_back(jnp.einsum('ecf,efd->ecd', act_low, w_out, precision=HIGHEST))
    reply = low(gate_moe[..., None] * expert_out).reshape(exp_total * CAP, hidden.shape[1])
    return jnp.zeros_like(hidden).at[owner].add(reply * filled[:, None])

def block_forward(weight_set, block_x, seg_blk, keep_blk, att_blk, moe_blk):
    norm_gain, w_query, w_key, w_select, w_value, w_output, w_router, w_in, w_out = weight_set
    row_count = block_x.shape[0]
    normed = low(layer_norm(block_x, norm_gain))
    query_rows = low_back(jnp.dot(normed, w_query, precision=HIGHEST)).reshape(row_count, H, DH)
    key_rows = low_back(jnp.dot(normed, w_key, precision=HIGHEST)).reshape(row_count, H, DH)
    logits = low_back(jnp.dot(block_x, w_select, precision=HIGHEST))
    named_mask = lax.optimization_barrier(jnp.sum((att_blk[..., None] == jnp.arange(VEXP, dtype=jnp.int32)).astype(jnp.float32), axis=2))
    head_gates = jax.nn.sigmoid(logits).reshape(row_count, 2 * H, VEXP) * named_mask
    value_all = low_back(jnp.dot(block_x, w_value, precision=HIGHEST)).reshape(row_count, H, VEXP, DH)
    value_rows = low(lax.optimization_barrier(jnp.sum(head_gates[:, :H, :, None] * value_all, axis=2)))
    position, allowed = jax.vmap(doc_layout)(seg_blk, keep_blk)
    cos_tab, sin_tab = rope_tables(position.reshape(-1), DH)
    q_rot = low(rotate(query_rows, cos_tab, sin_tab) * DH ** (-0.5))
    k_rot = low(rotate(key_rows, cos_tab, sin_tab))
    seq_shape = (SEQS_DEV, SEQ, H, DH)
    attended = jax.vmap(attend_sequence)(q_rot.reshape(seq_shape), k_rot.reshape(seq_shape), value_rows.reshape(seq_shape), allowed).reshape(row_count, H, DH)
    mixed_low = low(head_gates[:, H:, :, None] * attended[:, :, None, :]).reshape(row_count, H * VEXP * DH)
    hidden = block_x + low_back(jnp.dot(mixed_low, w_output, precision=HIGHEST))
    return hidden + moe_part(hidden, moe_blk, w_router, w_in, w_out)

def reference(layer_input, segments, keep_mask, att_routes, moe_routes, expert_counts, norm_gain, w_query, w_key, w_select, w_value, w_output, w_router, w_in, w_out, cotangent):
    block_count = TOKENS // TOK_DEV
    weight_set = jax.tree.map(lambda arr_in: arr_in.astype(jnp.float32), (norm_gain, w_query, w_key, w_select, w_value, w_output, w_router, w_in, w_out))
    inputs_f = layer_input.astype(jnp.float32).reshape(block_count, TOK_DEV, D)
    seg_blocks = segments.reshape(block_count, SEQS_DEV, SEQ)
    keep_blocks = keep_mask.reshape(block_count, SEQS_DEV, SEQ)
    att_blocks = att_routes.reshape(block_count, TOK_DEV, 2 * H, 2)
    moe_blocks = moe_routes.reshape(block_count, TOK_DEV, TOP)
    block_fn = jax.checkpoint(block_forward)

    def forward(weights_now, inputs_all):

        def one_block(carry, items):
            return (carry, block_fn(weights_now, items[0], items[1], items[2], items[3], items[4]))
        unused, outputs = lax.scan(one_block, jnp.zeros((), jnp.float32), (inputs_all, seg_blocks, keep_blocks, att_blocks, moe_blocks))
        return outputs
    outputs, pullback = jax.vjp(forward, weight_set, inputs_f)
    grad_weights, grad_in = pullback(cotangent.astype(jnp.float32).reshape(block_count, TOK_DEV, D))
    counts_out = expert_counts + jnp.zeros((EXPERTS,), jnp.int32).at[moe_routes.reshape(-1)].add(1)
    return (outputs.reshape(TOKENS, D).astype(jnp.bfloat16), grad_in.reshape(TOKENS, D).astype(jnp.bfloat16), grad_weights[0], grad_weights[1], grad_weights[2], grad_weights[3], grad_weights[4], grad_weights[5], grad_weights[6], grad_weights[7], grad_weights[8], counts_out)
```

```python
import jax
import jax.numpy as jnp
from jax import lax
from jax.sharding import PartitionSpec as P

DH = 128
VEXP = 5


NORM_EPS = 1e-05
ROPE_BASE = 10000.0
MASK_FILL = -1e30
HIGHEST = lax.Precision.HIGHEST


def layer_norm(values, gain_vec):
    center = values - jnp.mean(values, axis=-1, keepdims=True)
    spread = jnp.mean(center * center, axis=-1, keepdims=True)
    return center * lax.rsqrt(spread + NORM_EPS) * gain_vec


def rope_tables(position, width_dh):
    half_dh = width_dh // 2
    freq_row = jnp.power(ROPE_BASE, jnp.arange(half_dh, dtype=jnp.float32) * (-2.0 / width_dh))
    angle_tab = position.astype(jnp.float32)[:, None] * freq_row[None, :]
    return (jnp.cos(angle_tab), jnp.sin(angle_tab))


def rotate(values, cos_tab, sin_tab):
    half_dh = values.shape[-1] // 2
    first_half = values[..., :half_dh]
    second_half = values[..., half_dh:]
    cos_b = cos_tab[:, None, :]
    sin_b = sin_tab[:, None, :]
    return jnp.concatenate(
        [first_half * cos_b - second_half * sin_b, second_half * cos_b + first_half * sin_b],
        axis=-1,
    )


def rotate_back(grad_rot, cos_tab, sin_tab):
    half_dh = grad_rot.shape[-1] // 2
    grad_first = grad_rot[..., :half_dh]
    grad_second = grad_rot[..., half_dh:]
    cos_b = cos_tab[:, None, :]
    sin_b = sin_tab[:, None, :]
    return jnp.concatenate(
        [grad_first * cos_b + grad_second * sin_b, grad_second * cos_b - grad_first * sin_b],
        axis=-1,
    )


def doc_layout(seg_row, keep_row):
    length_s = seg_row.shape[0]
    column = jnp.arange(length_s, dtype=jnp.int32)
    new_doc = jnp.concatenate([jnp.ones((1,), dtype=jnp.bool_), seg_row[1:] != seg_row[:-1]])
    doc_start = lax.cummax(jnp.where(new_doc, column, jnp.zeros_like(column)), axis=0)
    position = column - doc_start
    same_doc = seg_row[:, None] == seg_row[None, :]
    causal = column[None, :] <= column[:, None]
    visible = (keep_row[None, :] == 1) | (column[None, :] == column[:, None])
    return (position, same_doc & causal & visible)


def slot_table(routes, exp_total, capacity):
    flat_ids = routes.reshape(-1)
    pair_count = flat_ids.shape[0]
    top_k = routes.shape[1]
    sort_order = jnp.argsort(flat_ids, stable=True)
    ranked = flat_ids[sort_order]
    first_slot = jnp.searchsorted(ranked, jnp.arange(exp_total, dtype=jnp.int32), side="left")
    slot_rank = jnp.arange(pair_count, dtype=jnp.int32) - first_slot[ranked]
    slot_dest = ranked * capacity + slot_rank
    owner = jnp.zeros((exp_total * capacity,), jnp.int32).at[slot_dest].set(sort_order // top_k)
    filled = jnp.zeros((exp_total * capacity,), jnp.float32).at[slot_dest].set(1.0)
    slot_of = (
        jnp.zeros((pair_count,), jnp.int32).at[sort_order].set(slot_dest).reshape(routes.shape)
    )
    return (owner, filled, slot_of)


def block_scores(q_blk, k_rows, allowed_blk):
    scores = jnp.einsum("qhd,khd->hqk", q_blk, k_rows, preferred_element_type=jnp.float32)
    return jnp.where(allowed_blk[None, :, :], scores, MASK_FILL)


def attend_forward(pieces):
    q_rows, k_rows, v_rows, allowed = pieces
    length_s = q_rows.shape[0]
    block_len = min(512, length_s)
    outs_list = []
    lse_list = []
    for begin_at in range(0, length_s, block_len):
        scores = block_scores(
            q_rows[begin_at : begin_at + block_len],
            k_rows,
            allowed[begin_at : begin_at + block_len],
        )
        row_max = jnp.max(scores, axis=-1, keepdims=True)
        exp_terms = jnp.exp(scores - row_max)
        row_sum = jnp.sum(exp_terms, axis=-1, keepdims=True)
        probs_bf = (exp_terms / row_sum).astype(jnp.bfloat16)
        outs_list.append(
            jnp.einsum("hqk,khd->qhd", probs_bf, v_rows, preferred_element_type=jnp.float32)
        )
        lse_list.append((row_max + jnp.log(row_sum))[..., 0])
    return (jnp.concatenate(outs_list, axis=0), jnp.concatenate(lse_list, axis=1))


def attend_backward(pieces):
    q_rows, k_rows, v_rows, allowed, log_total, grad_rows = pieces
    length_s = q_rows.shape[0]
    block_len = min(512, length_s)
    grad_q_list = []
    grad_k = jnp.zeros(k_rows.shape, jnp.float32)
    grad_v = jnp.zeros(v_rows.shape, jnp.float32)
    for begin_at in range(0, length_s, block_len):
        q_blk = q_rows[begin_at : begin_at + block_len]
        grad_blk = grad_rows[begin_at : begin_at + block_len]
        scores = block_scores(q_blk, k_rows, allowed[begin_at : begin_at + block_len])
        probs_f = jnp.exp(scores - log_total[:, begin_at : begin_at + block_len, None])
        grad_prob = jnp.einsum("qhd,khd->hqk", grad_blk, v_rows, preferred_element_type=jnp.float32)
        grad_score = (
            probs_f * (grad_prob - jnp.sum(probs_f * grad_prob, axis=-1, keepdims=True))
        ).astype(jnp.bfloat16)
        grad_v = grad_v + jnp.einsum(
            "hqk,qhd->khd",
            probs_f.astype(jnp.bfloat16),
            grad_blk,
            preferred_element_type=jnp.float32,
        )
        grad_q_list.append(
            jnp.einsum("hqk,khd->qhd", grad_score, k_rows, preferred_element_type=jnp.float32)
        )
        grad_k = grad_k + jnp.einsum(
            "hqk,qhd->khd", grad_score, q_blk, preferred_element_type=jnp.float32
        )
    return (jnp.concatenate(grad_q_list, axis=0), grad_k, grad_v)


def moe_dispatched(hidden, moe_routes, w_router, w_in, w_out, cotangent, capacity):
    dev_count = lax.axis_size("expert")
    exp_local = w_in.shape[0]
    exp_total = dev_count * exp_local
    tok_rows, model_dim = hidden.shape
    owner, filled, slot_of = slot_table(moe_routes, exp_total, capacity)
    keep_slot = filled[:, None] > 0
    zero_bf = jnp.zeros((), jnp.bfloat16)
    hidden_bf = hidden.astype(jnp.bfloat16)
    send_rows = jnp.where(keep_slot, hidden_bf[owner], zero_bf).reshape(
        dev_count, exp_local * capacity, model_dim
    )
    rows_in = lax.all_to_all(send_rows, "expert", split_axis=0, concat_axis=0, tiled=True)
    histogram = jnp.zeros((exp_total,), jnp.float32).at[moe_routes.reshape(-1)].add(1.0)
    tally = lax.psum_scatter(histogram, "expert", scatter_dimension=0, tiled=True)
    slot_shape = (dev_count, exp_local, capacity, model_dim)
    rows_four = rows_in.reshape(slot_shape)
    pre_act = jnp.einsum("necd,edf->necf", rows_four, w_in, preferred_element_type=jnp.float32)
    gelu_out, gelu_pull = jax.vjp(jax.nn.gelu, pre_act)
    act_bf = gelu_out.astype(jnp.bfloat16)
    router_logit = jnp.einsum(
        "necd,ed->nec", rows_four, w_router, preferred_element_type=jnp.float32
    )
    gate_moe = jax.nn.sigmoid(router_logit)
    expert_out = jnp.einsum("necf,efd->necd", act_bf, w_out, preferred_element_type=jnp.float32)
    reply = (
        (gate_moe[..., None] * expert_out)
        .astype(jnp.bfloat16)
        .reshape(dev_count, exp_local * capacity, model_dim)
    )
    returned = lax.all_to_all(reply, "expert", split_axis=0, concat_axis=0, tiled=True)
    moe_sum = jnp.sum(returned.reshape(-1, model_dim)[slot_of].astype(jnp.float32), axis=1)
    layer_output = (hidden + moe_sum).astype(jnp.bfloat16)
    cot_f = cotangent.astype(jnp.float32)
    send_cot = jnp.where(keep_slot, cotangent[owner], zero_bf).reshape(
        dev_count, exp_local * capacity, model_dim
    )
    cot_in, rows_again = (
        lax.all_to_all(send_cot, "expert", split_axis=0, concat_axis=0, tiled=True),
        lax.all_to_all(send_rows, "expert", split_axis=0, concat_axis=0, tiled=True),
    )
    rows_grad = rows_again.reshape(slot_shape)
    cot_bf = cot_in.reshape(slot_shape)
    raw_back = jnp.einsum("necd,efd->necf", cot_bf, w_out, preferred_element_type=jnp.float32)
    dgate = jnp.sum(act_bf.astype(jnp.float32) * raw_back, axis=-1)
    dlogit = dgate * gate_moe * (1.0 - gate_moe)
    dexpert = (gate_moe[..., None] * cot_bf.astype(jnp.float32)).astype(jnp.bfloat16)
    grad_w_out = jnp.einsum("necf,necd->efd", act_bf, dexpert, preferred_element_type=jnp.float32)
    dact = jnp.einsum("necd,efd->necf", dexpert, w_out, preferred_element_type=jnp.float32)
    dpre_bf = gelu_pull(dact)[0].astype(jnp.bfloat16)
    grad_w_in = jnp.einsum("necd,necf->edf", rows_grad, dpre_bf, preferred_element_type=jnp.float32)
    grad_router = jnp.einsum(
        "nec,necd->ed",
        dlogit,
        rows_grad.astype(jnp.float32),
        preferred_element_type=jnp.float32,
        precision=HIGHEST,
    )
    dsent = jnp.einsum("necf,edf->necd", dpre_bf, w_in, preferred_element_type=jnp.float32)
    dsent = (dsent + dlogit[..., None] * w_router[None, :, None, :].astype(jnp.float32)).astype(
        jnp.bfloat16
    )
    grad_back = lax.all_to_all(
        dsent.reshape(dev_count, exp_local * capacity, model_dim),
        "expert",
        split_axis=0,
        concat_axis=0,
        tiled=True,
    )
    dhidden = cot_f + jnp.sum(grad_back.reshape(-1, model_dim)[slot_of].astype(jnp.float32), axis=1)
    return (layer_output, dhidden, grad_w_in, grad_w_out, grad_router, tally)


def moe_dense(hidden, moe_routes, w_router, w_in, w_out, cotangent, capacity):
    exp_local = w_in.shape[0]
    exp_total = lax.axis_size("expert") * exp_local
    win_all = lax.all_gather(w_in, "expert", axis=0, tiled=True)
    wout_all = lax.all_gather(w_out, "expert", axis=0, tiled=True)
    router_all = lax.all_gather(w_router, "expert", axis=0, tiled=True)
    hidden_bf = hidden.astype(jnp.bfloat16)
    named_exp = jnp.sum(
        (moe_routes[..., None] == jnp.arange(exp_total, dtype=jnp.int32)).astype(jnp.float32), axis=1
    )
    tally = lax.psum_scatter(jnp.sum(named_exp, axis=0), "expert", scatter_dimension=0, tiled=True)
    router_logit = jnp.einsum("td,ed->te", hidden_bf, router_all, preferred_element_type=jnp.float32)
    gate_sig = jax.nn.sigmoid(router_logit)
    gate_moe = gate_sig * named_exp
    pre_act = jnp.einsum("td,edf->tef", hidden_bf, win_all, preferred_element_type=jnp.float32)
    gelu_out, gelu_pull = jax.vjp(jax.nn.gelu, pre_act)
    act_bf = gelu_out.astype(jnp.bfloat16)
    gated_bf = (gate_moe[..., None] * act_bf.astype(jnp.float32)).astype(jnp.bfloat16)
    moe_sum = jnp.einsum("tef,efd->td", gated_bf, wout_all, preferred_element_type=jnp.float32)
    layer_output = (hidden + moe_sum).astype(jnp.bfloat16)
    cot_f = cotangent.astype(jnp.float32)
    raw_back = jnp.einsum("td,efd->tef", cotangent, wout_all, preferred_element_type=jnp.float32)
    dgate = jnp.sum(act_bf.astype(jnp.float32) * raw_back, axis=-1)
    dlogit = dgate * gate_moe * (1.0 - gate_sig)
    dpre_bf = gelu_pull(gate_moe[..., None] * raw_back)[0].astype(jnp.bfloat16)
    grad_w_out = jnp.einsum("tef,td->efd", gated_bf, cotangent, preferred_element_type=jnp.float32)
    grad_w_in = jnp.einsum("td,tef->edf", hidden_bf, dpre_bf, preferred_element_type=jnp.float32)
    grad_router = jnp.einsum(
        "te,td->ed",
        dlogit,
        hidden_bf.astype(jnp.float32),
        preferred_element_type=jnp.float32,
        precision=HIGHEST,
    )
    dsent = jnp.einsum("tef,edf->td", dpre_bf, win_all, preferred_element_type=jnp.float32)
    dsent = dsent + jnp.einsum(
        "te,ed->td",
        dlogit,
        router_all.astype(jnp.float32),
        preferred_element_type=jnp.float32,
        precision=HIGHEST,
    )
    dhidden = cot_f + dsent
    grad_w_in = lax.psum_scatter(grad_w_in.astype(jnp.bfloat16), "expert", scatter_dimension=0, tiled=True)
    grad_w_out = lax.psum_scatter(grad_w_out.astype(jnp.bfloat16), "expert", scatter_dimension=0, tiled=True)
    grad_router = lax.psum_scatter(grad_router, "expert", scatter_dimension=0, tiled=True)
    return (layer_output, dhidden, grad_w_in, grad_w_out, grad_router, tally)


def local(
    layer_input,
    segments,
    keep_mask,
    att_routes,
    moe_routes,
    expert_counts,
    norm_gain,
    w_query,
    w_key,
    w_select,
    w_value,
    w_output,
    w_router,
    w_in,
    w_out,
    cotangent,
):
    tok_rows, model_dim = layer_input.shape
    seq_count, seq_len = segments.shape
    head_count = w_query.shape[1] // DH
    score_scale = DH ** (-0.5)
    inputs_f = layer_input.astype(jnp.float32)
    normed, norm_pull = jax.vjp(layer_norm, inputs_f, norm_gain)
    normed_bf = normed.astype(jnp.bfloat16)
    query_rows = jnp.dot(normed_bf, w_query, preferred_element_type=jnp.float32).reshape(
        tok_rows, head_count, DH
    )
    key_rows = jnp.dot(normed_bf, w_key, preferred_element_type=jnp.float32).reshape(
        tok_rows, head_count, DH
    )
    logits = jnp.dot(layer_input, w_select, preferred_element_type=jnp.float32)
    named_mask = jnp.sum(
        (att_routes[..., None] == jnp.arange(VEXP, dtype=jnp.int32)).astype(jnp.float32), axis=2
    )
    select_sig = jax.nn.sigmoid(logits).reshape(tok_rows, 2 * head_count, VEXP)
    head_gates = select_sig * named_mask
    value_all = jnp.dot(layer_input, w_value, preferred_element_type=jnp.float32).reshape(
        tok_rows, head_count, VEXP, DH
    )
    value_bf = jnp.sum(head_gates[:, :head_count, :, None] * value_all, axis=2).astype(jnp.bfloat16)
    position, allowed = jax.vmap(doc_layout)(segments, keep_mask)
    cos_tab, sin_tab = rope_tables(position.reshape(-1), DH)
    q_rot = (rotate(query_rows, cos_tab, sin_tab) * score_scale).astype(jnp.bfloat16)
    k_rot = rotate(key_rows, cos_tab, sin_tab).astype(jnp.bfloat16)
    seq_shape = (seq_count, seq_len, head_count, DH)
    attended, log_total = lax.map(
        attend_forward,
        (q_rot.reshape(seq_shape), k_rot.reshape(seq_shape), value_bf.reshape(seq_shape), allowed),
    )
    attended = attended.reshape(tok_rows, head_count, DH)
    mixed_bf = (
        (head_gates[:, head_count:, :, None] * attended[:, :, None, :])
        .astype(jnp.bfloat16)
        .reshape(tok_rows, head_count * VEXP * DH)
    )
    hidden = inputs_f + jnp.dot(mixed_bf, w_output, preferred_element_type=jnp.float32)
    top_k = moe_routes.shape[1]
    exp_total = lax.axis_size("expert") * w_in.shape[0]
    capacity = 10 * tok_rows * top_k // (7 * exp_total) + 1
    moe_layer = moe_dense if 4 * capacity > tok_rows else moe_dispatched
    layer_output, dhidden, grad_w_in, grad_w_out, grad_router, tally = moe_layer(
        hidden, moe_routes, w_router, w_in, w_out, cotangent, capacity
    )
    dy_bf = dhidden.astype(jnp.bfloat16)
    grad_output = jnp.einsum("tk,td->kd", mixed_bf, dy_bf, preferred_element_type=jnp.float32)
    dmixed = jnp.einsum("td,kd->tk", dy_bf, w_output, preferred_element_type=jnp.float32).reshape(
        tok_rows, head_count, VEXP, DH
    )
    dgate_out = jnp.sum(dmixed * attended[:, :, None, :], axis=-1)
    dattend = jnp.sum(head_gates[:, head_count:, :, None] * dmixed, axis=2).astype(jnp.bfloat16)
    grad_q, grad_k, grad_v = lax.map(
        attend_backward,
        (
            q_rot.reshape(seq_shape),
            k_rot.reshape(seq_shape),
            value_bf.reshape(seq_shape),
            allowed,
            log_total,
            dattend.reshape(seq_shape),
        ),
    )
    dquery = (
        (rotate_back(grad_q.reshape(tok_rows, head_count, DH), cos_tab, sin_tab) * score_scale)
        .astype(jnp.bfloat16)
        .reshape(tok_rows, head_count * DH)
    )
    dkey = (
        rotate_back(grad_k.reshape(tok_rows, head_count, DH), cos_tab, sin_tab)
        .astype(jnp.bfloat16)
        .reshape(tok_rows, head_count * DH)
    )
    grad_query = jnp.einsum("td,tk->dk", normed_bf, dquery, preferred_element_type=jnp.float32)
    grad_key = jnp.einsum("td,tk->dk", normed_bf, dkey, preferred_element_type=jnp.float32)
    dnormed = jnp.einsum(
        "tk,dk->td", dquery, w_query, preferred_element_type=jnp.float32
    ) + jnp.einsum("tk,dk->td", dkey, w_key, preferred_element_type=jnp.float32)
    dx_norm, grad_gain = norm_pull(dnormed)
    dvalue = grad_v.reshape(tok_rows, head_count, DH)
    dgate_val = jnp.sum(dvalue[:, :, None, :] * value_all, axis=-1)
    dvalue_all = (
        (head_gates[:, :head_count, :, None] * dvalue[:, :, None, :])
        .astype(jnp.bfloat16)
        .reshape(tok_rows, head_count * VEXP * DH)
    )
    grad_value = jnp.einsum(
        "td,tk->dk", layer_input, dvalue_all, preferred_element_type=jnp.float32
    )
    dgates = jnp.concatenate([dgate_val, dgate_out], axis=1)
    dlogits = (
        (dgates * named_mask * select_sig * (1.0 - select_sig))
        .astype(jnp.bfloat16)
        .reshape(tok_rows, 2 * head_count * VEXP)
    )
    grad_select = jnp.einsum("td,tk->dk", layer_input, dlogits, preferred_element_type=jnp.float32)
    grad_input = (
        dhidden
        + dx_norm
        + jnp.einsum("tk,dk->td", dvalue_all, w_value, preferred_element_type=jnp.float32)
    )
    grad_input = (
        grad_input + jnp.einsum("tk,dk->td", dlogits, w_select, preferred_element_type=jnp.float32)
    ).astype(jnp.bfloat16)
    expert_sums = (
        lax.psum(grad_w_in.astype(jnp.bfloat16), "dp").astype(jnp.float32),
        lax.psum(grad_w_out.astype(jnp.bfloat16), "dp").astype(jnp.float32),
        lax.psum(grad_router.astype(jnp.bfloat16), "dp").astype(jnp.float32),
        lax.psum(tally.astype(jnp.bfloat16), "dp").astype(jnp.float32),
    )
    dense_sums = (
        lax.psum_scatter(grad_gain, ("dp", "expert"), scatter_dimension=0, tiled=True),
        lax.psum_scatter(grad_query, ("dp", "expert"), scatter_dimension=0, tiled=True),
        lax.psum_scatter(grad_key, ("dp", "expert"), scatter_dimension=0, tiled=True),
        lax.psum_scatter(grad_select, ("dp", "expert"), scatter_dimension=0, tiled=True),
        lax.psum_scatter(grad_value, ("dp", "expert"), scatter_dimension=0, tiled=True),
        lax.psum_scatter(grad_output, ("dp", "expert"), scatter_dimension=1, tiled=True),
    )
    counts_out = expert_counts + expert_sums[3].astype(jnp.int32)
    return (
        layer_output,
        grad_input,
        dense_sums[0],
        dense_sums[1],
        dense_sums[2],
        dense_sums[3],
        dense_sums[4],
        dense_sums[5],
        expert_sums[2],
        expert_sums[0],
        expert_sums[1],
        counts_out,
    )


def solution(mesh):
    placed = (
        P(("dp", "expert"), None),
        P(("dp", "expert"), None),
        P(("dp", "expert"), None),
        P(("dp", "expert"), None, None),
        P(("dp", "expert"), None),
        P("expert"),
        P(),
        P(),
        P(),
        P(),
        P(),
        P(),
        P("expert", None),
        P("expert", None, None),
        P("expert", None, None),
        P(("dp", "expert"), None),
    )
    return jax.shard_map(
        local,
        mesh=mesh,
        in_specs=placed,
        out_specs=(
            P(("dp", "expert"), None),
            P(("dp", "expert"), None),
            P(("dp", "expert")),
            P(("dp", "expert"), None),
            P(("dp", "expert"), None),
            P(("dp", "expert"), None),
            P(("dp", "expert"), None),
            P(None, ("dp", "expert")),
            P("expert", None),
            P("expert", None, None),
            P("expert", None, None),
            P("expert"),
        ),
        check_vma=False,
    )
```

```python
import jax
import jax.numpy as jnp
from jax import lax
from jax.sharding import PartitionSpec as P

DH = 128
VEXP = 5


NORM_EPS = 1e-05
ROPE_BASE = 10000.0
MASK_FILL = -1e30
HIGHEST = lax.Precision.HIGHEST
ROUTER_ROWS = 64
DIGITS = 5
LANE = 128


def layer_norm(values, gain_vec):
    center = values - jnp.mean(values, axis=-1, keepdims=True)
    spread = jnp.mean(center * center, axis=-1, keepdims=True)
    return center * lax.rsqrt(spread + NORM_EPS) * gain_vec


def rope_tables(position, width_dh):
    half_dh = width_dh // 2
    freq_row = jnp.power(ROPE_BASE, jnp.arange(half_dh, dtype=jnp.float32) * (-2.0 / width_dh))
    angle_tab = position.astype(jnp.float32)[:, None] * freq_row[None, :]
    return (jnp.cos(angle_tab), jnp.sin(angle_tab))


def rotate(values, cos_tab, sin_tab):
    half_dh = values.shape[-1] // 2
    first_half = values[..., :half_dh]
    second_half = values[..., half_dh:]
    cos_b = cos_tab[:, None, :]
    sin_b = sin_tab[:, None, :]
    return jnp.concatenate(
        [first_half * cos_b - second_half * sin_b, second_half * cos_b + first_half * sin_b],
        axis=-1,
    )


def rotate_back(grad_rot, cos_tab, sin_tab):
    half_dh = grad_rot.shape[-1] // 2
    grad_first = grad_rot[..., :half_dh]
    grad_second = grad_rot[..., half_dh:]
    cos_b = cos_tab[:, None, :]
    sin_b = sin_tab[:, None, :]
    return jnp.concatenate(
        [grad_first * cos_b + grad_second * sin_b, grad_second * cos_b - grad_first * sin_b],
        axis=-1,
    )


def doc_layout(seg_row, keep_row):
    length_s = seg_row.shape[0]
    column = jnp.arange(length_s, dtype=jnp.int32)
    new_doc = jnp.concatenate([jnp.ones((1,), dtype=jnp.bool_), seg_row[1:] != seg_row[:-1]])
    doc_start = lax.cummax(jnp.where(new_doc, column, jnp.zeros_like(column)), axis=0)
    position = column - doc_start
    same_doc = seg_row[:, None] == seg_row[None, :]
    causal = column[None, :] <= column[:, None]
    visible = (keep_row[None, :] == 1) | (column[None, :] == column[:, None])
    return (position, same_doc & causal & visible)


def slot_table(routes, exp_total, capacity):
    flat_ids = routes.reshape(-1)
    pair_count = flat_ids.shape[0]
    top_k = routes.shape[1]
    sort_order = jnp.argsort(flat_ids, stable=True)
    ranked = flat_ids[sort_order]
    first_slot = jnp.searchsorted(ranked, jnp.arange(exp_total, dtype=jnp.int32), side="left")
    slot_rank = jnp.arange(pair_count, dtype=jnp.int32) - first_slot[ranked]
    slot_dest = ranked * capacity + slot_rank
    owner = jnp.zeros((exp_total * capacity,), jnp.int32).at[slot_dest].set(sort_order // top_k)
    filled = jnp.zeros((exp_total * capacity,), jnp.float32).at[slot_dest].set(1.0)
    slot_of = (
        jnp.zeros((pair_count,), jnp.int32).at[sort_order].set(slot_dest).reshape(routes.shape)
    )
    return (owner, filled, slot_of)


def block_scores(q_blk, k_rows, allowed_blk):
    scores = jnp.einsum("qhd,khd->hqk", q_blk, k_rows, preferred_element_type=jnp.float32)
    return jnp.where(allowed_blk[None, :, :], scores, MASK_FILL)


def attend_forward(pieces):
    q_rows, k_rows, v_rows, allowed = pieces
    length_s = q_rows.shape[0]
    block_len = min(512, length_s)
    outs_list = []
    lse_list = []
    for begin_at in range(0, length_s, block_len):
        scores = block_scores(
            q_rows[begin_at : begin_at + block_len],
            k_rows,
            allowed[begin_at : begin_at + block_len],
        )
        row_max = jnp.max(scores, axis=-1, keepdims=True)
        exp_terms = jnp.exp(scores - row_max)
        row_sum = jnp.sum(exp_terms, axis=-1, keepdims=True)
        probs_bf = (exp_terms / row_sum).astype(jnp.bfloat16)
        outs_list.append(
            jnp.einsum("hqk,khd->qhd", probs_bf, v_rows, preferred_element_type=jnp.float32)
        )
        lse_list.append((row_max + jnp.log(row_sum))[..., 0])
    return (jnp.concatenate(outs_list, axis=0), jnp.concatenate(lse_list, axis=1))


def attend_backward(pieces):
    q_rows, k_rows, v_rows, allowed, log_total, grad_rows = pieces
    length_s = q_rows.shape[0]
    block_len = min(512, length_s)
    grad_q_list = []
    grad_k = jnp.zeros(k_rows.shape, jnp.float32)
    grad_v = jnp.zeros(v_rows.shape, jnp.float32)
    for begin_at in range(0, length_s, block_len):
        q_blk = q_rows[begin_at : begin_at + block_len]
        grad_blk = grad_rows[begin_at : begin_at + block_len]
        scores = block_scores(q_blk, k_rows, allowed[begin_at : begin_at + block_len])
        probs_f = jnp.exp(scores - log_total[:, begin_at : begin_at + block_len, None])
        grad_prob = jnp.einsum("qhd,khd->hqk", grad_blk, v_rows, preferred_element_type=jnp.float32)
        grad_score = (
            probs_f * (grad_prob - jnp.sum(probs_f * grad_prob, axis=-1, keepdims=True))
        ).astype(jnp.bfloat16)
        grad_v = grad_v + jnp.einsum(
            "hqk,qhd->khd",
            probs_f.astype(jnp.bfloat16),
            grad_blk,
            preferred_element_type=jnp.float32,
        )
        grad_q_list.append(
            jnp.einsum("hqk,khd->qhd", grad_score, k_rows, preferred_element_type=jnp.float32)
        )
        grad_k = grad_k + jnp.einsum(
            "hqk,qhd->khd", grad_score, q_blk, preferred_element_type=jnp.float32
        )
    return (jnp.concatenate(grad_q_list, axis=0), grad_k, grad_v)


def moe_dispatched(hidden, moe_routes, w_router, w_in, w_out, cotangent, capacity):
    dev_count = lax.axis_size("expert")
    exp_local = w_in.shape[0]
    exp_total = dev_count * exp_local
    tok_rows, model_dim = hidden.shape
    owner, filled, slot_of = slot_table(moe_routes, exp_total, capacity)
    keep_slot = filled[:, None] > 0
    zero_bf = jnp.zeros((), jnp.bfloat16)
    hidden_bf = hidden.astype(jnp.bfloat16)
    send_rows = jnp.where(keep_slot, hidden_bf[owner], zero_bf).reshape(
        dev_count, exp_local * capacity, model_dim
    )
    rows_in = lax.all_to_all(send_rows, "expert", split_axis=0, concat_axis=0, tiled=True)
    histogram = jnp.zeros((exp_total,), jnp.float32).at[moe_routes.reshape(-1)].add(1.0)
    tally = lax.psum_scatter(histogram, "expert", scatter_dimension=0, tiled=True)
    slot_shape = (dev_count, exp_local, capacity, model_dim)
    rows_four = rows_in.reshape(slot_shape)
    pre_act = jnp.einsum("necd,edf->necf", rows_four, w_in, preferred_element_type=jnp.float32)
    gelu_out, gelu_pull = jax.vjp(jax.nn.gelu, pre_act)
    act_bf = gelu_out.astype(jnp.bfloat16)
    router_logit = jnp.einsum(
        "necd,ed->nec", rows_four, w_router, preferred_element_type=jnp.float32
    )
    gate_moe = jax.nn.sigmoid(router_logit)
    expert_out = jnp.einsum("necf,efd->necd", act_bf, w_out, preferred_element_type=jnp.float32)
    reply = (
        (gate_moe[..., None] * expert_out)
        .astype(jnp.bfloat16)
        .reshape(dev_count, exp_local * capacity, model_dim)
    )
    returned = lax.all_to_all(reply, "expert", split_axis=0, concat_axis=0, tiled=True)
    moe_sum = jnp.sum(returned.reshape(-1, model_dim)[slot_of].astype(jnp.float32), axis=1)
    layer_output = (hidden + moe_sum).astype(jnp.bfloat16)
    cot_f = cotangent.astype(jnp.float32)
    send_cot = jnp.where(keep_slot, cotangent[owner], zero_bf).reshape(
        dev_count, exp_local * capacity, model_dim
    )
    cot_in, rows_again = (
        lax.all_to_all(send_cot, "expert", split_axis=0, concat_axis=0, tiled=True),
        lax.all_to_all(send_rows, "expert", split_axis=0, concat_axis=0, tiled=True),
    )
    rows_grad = rows_again.reshape(slot_shape)
    cot_bf = cot_in.reshape(slot_shape)
    raw_back = jnp.einsum("necd,efd->necf", cot_bf, w_out, preferred_element_type=jnp.float32)
    dgate = jnp.sum(act_bf.astype(jnp.float32) * raw_back, axis=-1)
    dlogit = dgate * gate_moe * (1.0 - gate_moe)
    dexpert = (gate_moe[..., None] * cot_bf.astype(jnp.float32)).astype(jnp.bfloat16)
    grad_w_out = jnp.einsum("necf,necd->efd", act_bf, dexpert, preferred_element_type=jnp.float32)
    dact = jnp.einsum("necd,efd->necf", dexpert, w_out, preferred_element_type=jnp.float32)
    dpre_bf = gelu_pull(dact)[0].astype(jnp.bfloat16)
    grad_w_in = jnp.einsum("necd,necf->edf", rows_grad, dpre_bf, preferred_element_type=jnp.float32)
    grad_router = jnp.einsum(
        "nec,necd->ed",
        dlogit,
        rows_grad.astype(jnp.float32),
        preferred_element_type=jnp.float32,
        precision=HIGHEST,
    )
    dsent = jnp.einsum("necf,edf->necd", dpre_bf, w_in, preferred_element_type=jnp.float32)
    dsent = (dsent + dlogit[..., None] * w_router[None, :, None, :].astype(jnp.float32)).astype(
        jnp.bfloat16
    )
    grad_back = lax.all_to_all(
        dsent.reshape(dev_count, exp_local * capacity, model_dim),
        "expert",
        split_axis=0,
        concat_axis=0,
        tiled=True,
    )
    dhidden = cot_f + jnp.sum(grad_back.reshape(-1, model_dim)[slot_of].astype(jnp.float32), axis=1)
    expert_sums = (
        lax.psum(grad_w_in.astype(jnp.bfloat16), "dp").astype(jnp.float32),
        lax.psum(grad_w_out.astype(jnp.bfloat16), "dp").astype(jnp.float32),
        lax.psum(grad_router.astype(jnp.bfloat16), "dp").astype(jnp.float32),
        lax.psum(tally, "dp").astype(jnp.int32),
    )
    return (layer_output, dhidden) + expert_sums


def core_swap(arr):
    size = lax.axis_size("expert")
    return lax.ppermute(arr, "expert", [(i, i ^ 1) for i in range(size)])


def chip_shift(arr, hop):
    size = lax.axis_size("expert")
    chips = size // 2
    return lax.ppermute(
        arr, "expert", [(i, (i // 2 + hop) % chips * 2 + i % 2) for i in range(size)]
    )


def dp_swap(arr, flip):
    return lax.ppermute(arr, "dp", [(i, i ^ flip) for i in range(lax.axis_size("dp"))])


def row_part(arr, index, count):
    return lax.dynamic_slice_in_dim(arr, index * (arr.shape[0] // count), arr.shape[0] // count, 0)


def dp_gather(part):
    mine = lax.axis_index("dp")
    rows = part.shape[0]
    whole = jnp.zeros((4 * rows,) + part.shape[1:], part.dtype)
    for flip in range(4):
        piece = part if flip == 0 else dp_swap(part, flip)
        whole = lax.dynamic_update_slice_in_dim(whole, piece, (mine ^ flip) * rows, 0)
    return whole


def dp_scatter(whole):
    mine = lax.axis_index("dp")
    total = row_part(whole, mine, 4).astype(jnp.float32)
    for flip in range(1, 4):
        total = total + dp_swap(row_part(whole, mine ^ flip, 4), flip).astype(jnp.float32)
    return total


def scatter_rows(whole):
    dev_count = lax.axis_size("expert")
    chips = dev_count // 2
    rows, width = whole.shape
    mine = lax.axis_index("expert")
    chip, core = mine // 2, mine % 2
    by_core = whole.reshape(4 * chips, 2, rows // (8 * chips), width)
    kept = lax.dynamic_index_in_dim(by_core, core, 1, keepdims=False)
    given = lax.dynamic_index_in_dim(by_core, 1 - core, 1, keepdims=False)
    pair = (kept.astype(jnp.float32) + core_swap(given).astype(jnp.float32)).astype(jnp.bfloat16)
    quarter = dp_scatter(pair.reshape(rows // 2, width)).astype(jnp.bfloat16)
    total = row_part(quarter, chip, chips).astype(jnp.float32)
    for hop in range(1, chips):
        piece = row_part(quarter, (chip + hop) % chips, chips)
        total = total + chip_shift(piece, hop).astype(jnp.float32)
    return total


def gather_weights(w_router, w_in, w_out):
    exp_local, model_dim, ff_dim = w_in.shape
    chips = lax.axis_size("expert") // 2
    router_rows = jnp.zeros((ROUTER_ROWS, model_dim), jnp.bfloat16).at[:exp_local].set(w_router)
    own = jnp.concatenate(
        [
            jnp.swapaxes(w_in, 1, 2).reshape(exp_local * ff_dim, model_dim),
            router_rows,
            w_out.reshape(exp_local * ff_dim, model_dim),
        ]
    )
    quarter = row_part(own, lax.axis_index("dp"), 4)
    chunks = [own] + [None] * (chips - 1)
    for hop in range(2, chips):
        chunks[hop] = dp_gather(chip_shift(quarter, -hop))
    if chips > 1:
        chunks[1] = chip_shift(own, -1)
    return chunks


def moe_dense(hidden, moe_routes, w_router, w_in, w_out, cotangent, capacity):
    tok_rows, model_dim = hidden.shape
    exp_local, _, ff_dim = w_in.shape
    dev_count = lax.axis_size("expert")
    chips = dev_count // 2
    wide = exp_local * ff_dim
    mine = lax.axis_index("expert")
    chip, core = mine // 2, mine % 2
    chunks = gather_weights(w_router, w_in, w_out)
    named = jnp.sum(
        (moe_routes[..., None] == jnp.arange(dev_count * exp_local, dtype=jnp.int32)).astype(
            jnp.bfloat16
        ),
        axis=1,
    )
    named = jnp.concatenate([named, core_swap(named)])
    cot_two = jnp.concatenate([cotangent, core_swap(cotangent)])
    hidden_bf = hidden.astype(jnp.bfloat16)
    sent_two = jnp.concatenate([hidden_bf, core_swap(hidden_bf)])
    out_two = jnp.zeros((2 * tok_rows, model_dim), jnp.float32)
    grad_two = jnp.zeros((2 * tok_rows, model_dim), jnp.float32)
    grads = [None] * chips
    for hop in [0] + list(range(2, chips)) + [1]:
        w_ext = chunks[hop][: wide + ROUTER_ROWS]
        w_back = chunks[hop][wide + ROUTER_ROWS :]
        first = ((chip + hop) % chips * 2 + core) * exp_local
        mask = lax.dynamic_slice_in_dim(named, first, exp_local, 1).astype(jnp.float32)
        pre_ext = jnp.einsum("td,fd->tf", sent_two, w_ext, preferred_element_type=jnp.float32)
        gate_sig = jax.nn.sigmoid(pre_ext[:, wide : wide + exp_local])
        gate = gate_sig * mask
        gate_wide = jnp.repeat(gate, ff_dim, axis=1)
        gelu_out, gelu_pull = jax.vjp(jax.nn.gelu, pre_ext[:, :wide])
        act_f = gelu_out.astype(jnp.bfloat16).astype(jnp.float32)
        gated_bf = (gate_wide * act_f).astype(jnp.bfloat16)
        raw_back = jnp.einsum("td,fd->tf", cot_two, w_back, preferred_element_type=jnp.float32)
        dgate = jnp.sum((act_f * raw_back).reshape(-1, exp_local, ff_dim), axis=-1)
        dlogit = dgate * gate * (1.0 - gate_sig)
        dpre = gelu_pull(gate_wide * raw_back)[0]
        dpre_ext = jnp.concatenate(
            [dpre, jnp.pad(dlogit, ((0, 0), (0, ROUTER_ROWS - exp_local)))], axis=1
        ).astype(jnp.bfloat16)
        out_two = out_two + jnp.dot(gated_bf, w_back, preferred_element_type=jnp.float32)
        grad_two = grad_two + jnp.dot(dpre_ext, w_ext, preferred_element_type=jnp.float32)
        grad_ext = jnp.einsum("tf,td->fd", dpre_ext, sent_two, preferred_element_type=jnp.float32)
        grad_back = jnp.einsum("tf,td->fd", gated_bf, cot_two, preferred_element_type=jnp.float32)
        chunk_grad = jnp.concatenate([grad_ext, grad_back]).astype(jnp.bfloat16)
        counts = jnp.sum(mask, axis=0).astype(jnp.int32)
        digits = jnp.stack([(counts >> (2 * place)) & 3 for place in range(DIGITS)])
        grads[hop] = chunk_grad.at[
            wide + exp_local : wide + exp_local + DIGITS, :exp_local
        ].set(digits.astype(jnp.bfloat16))
    back = core_swap(grad_two[tok_rows:].astype(jnp.bfloat16))
    dhidden = cotangent.astype(jnp.float32) + grad_two[:tok_rows] + back.astype(jnp.float32)
    back = core_swap(out_two[tok_rows:].astype(jnp.bfloat16))
    layer_output = (hidden + out_two[:tok_rows] + back.astype(jnp.float32)).astype(jnp.bfloat16)
    near = grads[0].astype(jnp.float32)
    if chips > 1:
        near = near + chip_shift(grads[1], 1).astype(jnp.float32)
    total = 0.0
    for hop in range(2, chips):
        part = dp_scatter(grads[hop]).astype(jnp.bfloat16)
        total = total + chip_shift(part, hop).astype(jnp.float32)
    total = total + dp_scatter(near.astype(jnp.bfloat16))
    summed = dp_gather(total.astype(jnp.bfloat16)).astype(jnp.float32)
    grad_w_in = jnp.swapaxes(summed[:wide].reshape(exp_local, ff_dim, model_dim), 1, 2)
    grad_router = summed[wide : wide + exp_local]
    digits = summed[wide + exp_local : wide + exp_local + DIGITS, :exp_local].astype(jnp.int32)
    tally = sum(digits[place] << (2 * place) for place in range(DIGITS))
    grad_w_out = summed[wide + ROUTER_ROWS :].reshape(exp_local, ff_dim, model_dim)
    return (layer_output, dhidden, grad_w_in, grad_w_out, grad_router, tally)


def local(
    layer_input,
    segments,
    keep_mask,
    att_routes,
    moe_routes,
    expert_counts,
    norm_gain,
    w_query,
    w_key,
    w_select,
    w_value,
    w_output,
    w_router,
    w_in,
    w_out,
    cotangent,
):
    tok_rows, model_dim = layer_input.shape
    seq_count, seq_len = segments.shape
    head_count = w_query.shape[1] // DH
    score_scale = DH ** (-0.5)
    inputs_f = layer_input.astype(jnp.float32)
    normed, norm_pull = jax.vjp(layer_norm, inputs_f, norm_gain)
    normed_bf = normed.astype(jnp.bfloat16)
    query_rows = jnp.dot(normed_bf, w_query, preferred_element_type=jnp.float32).reshape(
        tok_rows, head_count, DH
    )
    key_rows = jnp.dot(normed_bf, w_key, preferred_element_type=jnp.float32).reshape(
        tok_rows, head_count, DH
    )
    logits = jnp.dot(layer_input, w_select, preferred_element_type=jnp.float32)
    named_mask = jnp.sum(
        (att_routes[..., None] == jnp.arange(VEXP, dtype=jnp.int32)).astype(jnp.float32), axis=2
    )
    select_sig = jax.nn.sigmoid(logits).reshape(tok_rows, 2 * head_count, VEXP)
    head_gates = select_sig * named_mask
    value_all = jnp.dot(layer_input, w_value, preferred_element_type=jnp.float32).reshape(
        tok_rows, head_count, VEXP, DH
    )
    value_bf = jnp.sum(head_gates[:, :head_count, :, None] * value_all, axis=2).astype(jnp.bfloat16)
    position, allowed = jax.vmap(doc_layout)(segments, keep_mask)
    cos_tab, sin_tab = rope_tables(position.reshape(-1), DH)
    q_rot = (rotate(query_rows, cos_tab, sin_tab) * score_scale).astype(jnp.bfloat16)
    k_rot = rotate(key_rows, cos_tab, sin_tab).astype(jnp.bfloat16)
    seq_shape = (seq_count, seq_len, head_count, DH)
    attended, log_total = lax.map(
        attend_forward,
        (q_rot.reshape(seq_shape), k_rot.reshape(seq_shape), value_bf.reshape(seq_shape), allowed),
    )
    attended = attended.reshape(tok_rows, head_count, DH)
    mixed_bf = (
        (head_gates[:, head_count:, :, None] * attended[:, :, None, :])
        .astype(jnp.bfloat16)
        .reshape(tok_rows, head_count * VEXP * DH)
    )
    hidden = inputs_f + jnp.dot(mixed_bf, w_output, preferred_element_type=jnp.float32)
    top_k = moe_routes.shape[1]
    exp_total = lax.axis_size("expert") * w_in.shape[0]
    capacity = 10 * tok_rows * top_k // (7 * exp_total) + 1
    dense = 4 * capacity > tok_rows
    moe_layer = moe_dense if dense else moe_dispatched
    layer_output, dhidden, grad_w_in, grad_w_out, grad_router, tally = moe_layer(
        hidden, moe_routes, w_router, w_in, w_out, cotangent, capacity
    )
    dy_bf = dhidden.astype(jnp.bfloat16)
    grad_output = jnp.einsum("tk,td->kd", mixed_bf, dy_bf, preferred_element_type=jnp.float32)
    dmixed = jnp.einsum("td,kd->tk", dy_bf, w_output, preferred_element_type=jnp.float32).reshape(
        tok_rows, head_count, VEXP, DH
    )
    dgate_out = jnp.sum(dmixed * attended[:, :, None, :], axis=-1)
    dattend = jnp.sum(head_gates[:, head_count:, :, None] * dmixed, axis=2).astype(jnp.bfloat16)
    grad_q, grad_k, grad_v = lax.map(
        attend_backward,
        (
            q_rot.reshape(seq_shape),
            k_rot.reshape(seq_shape),
            value_bf.reshape(seq_shape),
            allowed,
            log_total,
            dattend.reshape(seq_shape),
        ),
    )
    dquery = (
        (rotate_back(grad_q.reshape(tok_rows, head_count, DH), cos_tab, sin_tab) * score_scale)
        .astype(jnp.bfloat16)
        .reshape(tok_rows, head_count * DH)
    )
    dkey = (
        rotate_back(grad_k.reshape(tok_rows, head_count, DH), cos_tab, sin_tab)
        .astype(jnp.bfloat16)
        .reshape(tok_rows, head_count * DH)
    )
    grad_query = jnp.einsum("td,tk->dk", normed_bf, dquery, preferred_element_type=jnp.float32)
    grad_key = jnp.einsum("td,tk->dk", normed_bf, dkey, preferred_element_type=jnp.float32)
    dnormed = jnp.einsum(
        "tk,dk->td", dquery, w_query, preferred_element_type=jnp.float32
    ) + jnp.einsum("tk,dk->td", dkey, w_key, preferred_element_type=jnp.float32)
    dx_norm, grad_gain = norm_pull(dnormed)
    dvalue = grad_v.reshape(tok_rows, head_count, DH)
    dgate_val = jnp.sum(dvalue[:, :, None, :] * value_all, axis=-1)
    dvalue_all = (
        (head_gates[:, :head_count, :, None] * dvalue[:, :, None, :])
        .astype(jnp.bfloat16)
        .reshape(tok_rows, head_count * VEXP * DH)
    )
    grad_value = jnp.einsum(
        "td,tk->dk", layer_input, dvalue_all, preferred_element_type=jnp.float32
    )
    dgates = jnp.concatenate([dgate_val, dgate_out], axis=1)
    dlogits = (
        (dgates * named_mask * select_sig * (1.0 - select_sig))
        .astype(jnp.bfloat16)
        .reshape(tok_rows, 2 * head_count * VEXP)
    )
    grad_select = jnp.einsum("td,tk->dk", layer_input, dlogits, preferred_element_type=jnp.float32)
    grad_input = (
        dhidden
        + dx_norm
        + jnp.einsum("tk,dk->td", dvalue_all, w_value, preferred_element_type=jnp.float32)
    )
    grad_input = (
        grad_input + jnp.einsum("tk,dk->td", dlogits, w_select, preferred_element_type=jnp.float32)
    ).astype(jnp.bfloat16)
    if dense:
        wide, narrow, few = head_count * VEXP * DH, head_count * DH, 2 * head_count * VEXP
        filler = jnp.zeros((model_dim, -(few + 1) % LANE), jnp.float32)
        joined = jnp.concatenate(
            [grad_value, grad_query, grad_key, grad_select, grad_gain[:, None], filler], axis=1
        ).astype(jnp.bfloat16)
        summed = scatter_rows(joined)
        out_sum = scatter_rows(grad_output.T.astype(jnp.bfloat16)).T
        cuts = [0, wide, wide + narrow, wide + 2 * narrow, wide + 2 * narrow + few]
        value_sum, query_sum, key_sum, select_sum = [
            summed[:, cuts[i] : cuts[i + 1]] for i in range(4)
        ]
        gain_sum = summed[:, cuts[4]]
    else:
        both = ("dp", "expert")
        gain_sum, query_sum, key_sum, select_sum, value_sum = [
            lax.psum_scatter(grad, both, scatter_dimension=0, tiled=True)
            for grad in (grad_gain, grad_query, grad_key, grad_select, grad_value)
        ]
        out_sum = lax.psum_scatter(grad_output, both, scatter_dimension=1, tiled=True)
    counts_out = expert_counts + tally
    return (
        layer_output,
        grad_input,
        gain_sum,
        query_sum,
        key_sum,
        select_sum,
        value_sum,
        out_sum,
        grad_router,
        grad_w_in,
        grad_w_out,
        counts_out,
    )


def solution(mesh):
    placed = (
        P(("dp", "expert"), None),
        P(("dp", "expert"), None),
        P(("dp", "expert"), None),
        P(("dp", "expert"), None, None),
        P(("dp", "expert"), None),
        P("expert"),
        P(),
        P(),
        P(),
        P(),
        P(),
        P(),
        P("expert", None),
        P("expert", None, None),
        P("expert", None, None),
        P(("dp", "expert"), None),
    )
    return jax.shard_map(
        local,
        mesh=mesh,
        in_specs=placed,
        out_specs=(
            P(("dp", "expert"), None),
            P(("dp", "expert"), None),
            P(("dp", "expert")),
            P(("dp", "expert"), None),
            P(("dp", "expert"), None),
            P(("dp", "expert"), None),
            P(("dp", "expert"), None),
            P(None, ("dp", "expert")),
            P("expert", None),
            P("expert", None, None),
            P("expert", None, None),
            P("expert"),
        ),
        check_vma=False,
    )
```

```python
import functools

import jax
import jax.numpy as jnp
from jax import lax
from jax.experimental import pallas as pl
from jax.experimental.pallas import tpu as pltpu
from jax.sharding import PartitionSpec as P

DH = 128
VEXP = 5


NORM_EPS = 1e-05
ROPE_BASE = 10000.0
MASK_FILL = -1e30
HIGHEST = lax.Precision.HIGHEST
ROUTER_ROWS = 64
DIGITS = 5
LANE = 128
GAIN_ROWS = 16
TILE = 256
VMEM_BYTES = 60 << 20
GELU_A = 0.7978845608028654
GELU_B = 0.044715


def layer_norm(values, gain_vec):
    center = values - jnp.mean(values, axis=-1, keepdims=True)
    spread = jnp.mean(center * center, axis=-1, keepdims=True)
    return center * lax.rsqrt(spread + NORM_EPS) * gain_vec


def rope_tables(position, width_dh):
    half_dh = width_dh // 2
    freq_row = jnp.power(ROPE_BASE, jnp.arange(half_dh, dtype=jnp.float32) * (-2.0 / width_dh))
    angle_tab = position.astype(jnp.float32)[:, None] * freq_row[None, :]
    return (jnp.cos(angle_tab), jnp.sin(angle_tab))


def rotate(values, cos_tab, sin_tab):
    half_dh = values.shape[-1] // 2
    first_half = values[..., :half_dh]
    second_half = values[..., half_dh:]
    cos_b = cos_tab[:, None, :]
    sin_b = sin_tab[:, None, :]
    return jnp.concatenate(
        [first_half * cos_b - second_half * sin_b, second_half * cos_b + first_half * sin_b],
        axis=-1,
    )


def rotate_back(grad_rot, cos_tab, sin_tab):
    half_dh = grad_rot.shape[-1] // 2
    grad_first = grad_rot[..., :half_dh]
    grad_second = grad_rot[..., half_dh:]
    cos_b = cos_tab[:, None, :]
    sin_b = sin_tab[:, None, :]
    return jnp.concatenate(
        [grad_first * cos_b + grad_second * sin_b, grad_second * cos_b - grad_first * sin_b],
        axis=-1,
    )


def doc_layout(seg_row, keep_row):
    length_s = seg_row.shape[0]
    column = jnp.arange(length_s, dtype=jnp.int32)
    new_doc = jnp.concatenate([jnp.ones((1,), dtype=jnp.bool_), seg_row[1:] != seg_row[:-1]])
    doc_start = lax.cummax(jnp.where(new_doc, column, jnp.zeros_like(column)), axis=0)
    position = column - doc_start
    same_doc = seg_row[:, None] == seg_row[None, :]
    causal = column[None, :] <= column[:, None]
    visible = (keep_row[None, :] == 1) | (column[None, :] == column[:, None])
    return (position, same_doc & causal & visible)


def slot_table(routes, exp_total, capacity):
    flat_ids = routes.reshape(-1)
    pair_count = flat_ids.shape[0]
    top_k = routes.shape[1]
    sort_order = jnp.argsort(flat_ids, stable=True)
    ranked = flat_ids[sort_order]
    first_slot = jnp.searchsorted(ranked, jnp.arange(exp_total, dtype=jnp.int32), side="left")
    slot_rank = jnp.arange(pair_count, dtype=jnp.int32) - first_slot[ranked]
    slot_dest = ranked * capacity + slot_rank
    owner = jnp.zeros((exp_total * capacity,), jnp.int32).at[slot_dest].set(sort_order // top_k)
    filled = jnp.zeros((exp_total * capacity,), jnp.float32).at[slot_dest].set(1.0)
    slot_of = (
        jnp.zeros((pair_count,), jnp.int32).at[sort_order].set(slot_dest).reshape(routes.shape)
    )
    return (owner, filled, slot_of)


def block_scores(q_blk, k_rows, allowed_blk):
    scores = jnp.einsum("qhd,khd->hqk", q_blk, k_rows, preferred_element_type=jnp.float32)
    return jnp.where(allowed_blk[None, :, :], scores, MASK_FILL)


def attend_forward(pieces):
    q_rows, k_rows, v_rows, allowed = pieces
    length_s = q_rows.shape[0]
    block_len = min(512, length_s)
    outs_list = []
    lse_list = []
    for begin_at in range(0, length_s, block_len):
        scores = block_scores(
            q_rows[begin_at : begin_at + block_len],
            k_rows,
            allowed[begin_at : begin_at + block_len],
        )
        row_max = jnp.max(scores, axis=-1, keepdims=True)
        exp_terms = jnp.exp(scores - row_max)
        row_sum = jnp.sum(exp_terms, axis=-1, keepdims=True)
        probs_bf = (exp_terms / row_sum).astype(jnp.bfloat16)
        outs_list.append(
            jnp.einsum("hqk,khd->qhd", probs_bf, v_rows, preferred_element_type=jnp.float32)
        )
        lse_list.append((row_max + jnp.log(row_sum))[..., 0])
    return (jnp.concatenate(outs_list, axis=0), jnp.concatenate(lse_list, axis=1))


def attend_backward(pieces):
    q_rows, k_rows, v_rows, allowed, log_total, grad_rows = pieces
    length_s = q_rows.shape[0]
    block_len = min(512, length_s)
    grad_q_list = []
    grad_k = jnp.zeros(k_rows.shape, jnp.float32)
    grad_v = jnp.zeros(v_rows.shape, jnp.float32)
    for begin_at in range(0, length_s, block_len):
        q_blk = q_rows[begin_at : begin_at + block_len]
        grad_blk = grad_rows[begin_at : begin_at + block_len]
        scores = block_scores(q_blk, k_rows, allowed[begin_at : begin_at + block_len])
        probs_f = jnp.exp(scores - log_total[:, begin_at : begin_at + block_len, None])
        grad_prob = jnp.einsum("qhd,khd->hqk", grad_blk, v_rows, preferred_element_type=jnp.float32)
        grad_score = (
            probs_f * (grad_prob - jnp.sum(probs_f * grad_prob, axis=-1, keepdims=True))
        ).astype(jnp.bfloat16)
        grad_v = grad_v + jnp.einsum(
            "hqk,qhd->khd",
            probs_f.astype(jnp.bfloat16),
            grad_blk,
            preferred_element_type=jnp.float32,
        )
        grad_q_list.append(
            jnp.einsum("hqk,khd->qhd", grad_score, k_rows, preferred_element_type=jnp.float32)
        )
        grad_k = grad_k + jnp.einsum(
            "hqk,qhd->khd", grad_score, q_blk, preferred_element_type=jnp.float32
        )
    return (jnp.concatenate(grad_q_list, axis=0), grad_k, grad_v)


def dot_nt(left, right):
    return lax.dot_general(left, right, (((1,), (1,)), ((), ())), preferred_element_type=jnp.float32)


def dot_nn(left, right):
    return lax.dot_general(left, right, (((1,), (0,)), ((), ())), preferred_element_type=jnp.float32)


def dot_tn(left, right):
    return lax.dot_general(left, right, (((0,), (0,)), ((), ())), preferred_element_type=jnp.float32)


def spin(values, cos_two, sin_two):
    return values * cos_two + pltpu.roll(values, DH // 2, 1) * sin_two


def spin_back(values, cos_two, sin_two):
    return values * cos_two - pltpu.roll(values, DH // 2, 1) * sin_two


def window_mask(step, tile, start_col, keep_before, keep_now):
    row = step * tile + lax.broadcasted_iota(jnp.int32, (tile, 2 * tile), 0)
    col = (step - 1) * tile + lax.broadcasted_iota(jnp.int32, (tile, 2 * tile), 1)
    keep_row = jnp.concatenate([keep_before, keep_now], axis=1)
    return (col >= start_col) & (col <= row) & ((keep_row == 1) | (col == row))


def neighbour(kind, amount):
    mine, place = lax.axis_index("dp"), lax.axis_index("expert")
    chips = lax.axis_size("expert") // 2
    chip, core = place // 2, lax.rem(place, 2)
    if kind == "dp":
        flipped = [mine, mine + 1 - 2 * lax.rem(mine, 2), lax.rem(mine + 2, 4), 3 - mine]
        return (flipped[amount], place)
    if kind == "core":
        return (mine, place + 1 - 2 * core)
    return (mine, 2 * lax.rem(chip + amount + chips, chips) + core)


def own_part(rows):
    return lambda mine, flipped: mine * rows


def far_part(rows):
    return lambda mine, flipped: flipped * rows


def fixed(start):
    return lambda mine, flipped: start


def shift_move(src, dst, hop, src_at, dst_at, count):
    return [(src, dst, "chip", hop, src_at, dst_at, count)]


def gather_moves(buf_in, buf_out, rows):
    return [(buf_in, buf_out, "dp", flip, own_part(rows), own_part(rows), rows) for flip in (1, 2, 3)]


def scatter_moves(src, dst, rows):
    return [
        (src, dst, "dp", flip, far_part(rows), fixed((flip - 1) * rows), rows) for flip in (1, 2, 3)
    ]


def greet(peers):
    barrier = pltpu.get_barrier_semaphore()
    for peer in peers:
        pl.semaphore_signal(barrier, inc=1, device_id=peer, device_id_type=pl.DeviceIdType.MESH)
    pl.semaphore_wait(barrier, len(peers))


def peers_of(moves):
    peers = []
    for _, _, kind, amount, _, _, _ in moves:
        peers.append(neighbour(kind, amount))
        if kind == "chip":
            peers.append(neighbour(kind, -amount))
    return peers


def copies_of(moves, ins, outs, send_sem, recv_sem):
    mine = lax.axis_index("dp")
    copies = []
    for i, (src, dst, kind, amount, src_at, dst_at, count) in enumerate(moves):
        peer = neighbour(kind, amount)
        copies.append(
            pltpu.make_async_remote_copy(
                src_ref=ins[src].at[pl.ds(pl.multiple_of(src_at(mine, peer[0]), 16), count)],
                dst_ref=outs[dst].at[pl.ds(pl.multiple_of(dst_at(mine, peer[0]), 16), count)],
                send_sem=send_sem.at[i],
                recv_sem=recv_sem.at[i],
                device_id=peer,
                device_id_type=pl.DeviceIdType.MESH,
            )
        )
    return copies


ANYWHERE = pl.BlockSpec(memory_space=pl.ANY)


def tile_rows(index, tile):
    return pl.ds(pl.multiple_of(index * tile, tile), tile)


def forward_body(heads, tile, steps, *refs):
    (
        own_any,
        cot_any,
        x_ref,
        start_ref,
        keep_ref,
        cos_ref,
        sin_ref,
        mask_ref,
        gain_ref,
        wqk_ref,
        wsel_ref,
        wval_ref,
        wout_ref,
        chunk_any,
        cot_far_any,
        sent_far_any,
        hid_ref,
        norm_ref,
        q_ref,
        k_ref,
        v_ref,
        val_ref,
        att_ref,
        sig_ref,
        lse_ref,
        mix_ref,
        sent_all,
        send_sem,
        recv_sem,
        tile_send,
        tile_recv,
    ) = refs
    step = pl.program_id(0)
    rows = steps * tile
    quarter = own_any.shape[0] // 4
    moves = shift_move(0, 0, -2, own_part(quarter), own_part(quarter), quarter)
    moves = moves + [(1, 1, "core", 1, fixed(0), fixed(0), rows)]
    partner = neighbour("core", 1)
    copies = copies_of(moves, [own_any, cot_any], [chunk_any, cot_far_any], send_sem, recv_sem)

    def tile_copy(index):
        return pltpu.make_async_remote_copy(
            src_ref=sent_all.at[pl.ds(index * tile, tile)],
            dst_ref=sent_far_any.at[pl.ds(index * tile, tile)],
            send_sem=tile_send.at[index],
            recv_sem=tile_recv.at[index],
            device_id=partner,
            device_id_type=pl.DeviceIdType.MESH,
        )


    @pl.when(step == 0)
    def _():
        greet(peers_of(moves))
        for copy in copies:
            copy.start()

    now = tile_rows(step, tile)
    before = tile_rows(jnp.maximum(step - 1, 0), tile)
    x = x_ref[...]
    x_f = x.astype(jnp.float32)
    center = x_f - jnp.mean(x_f, axis=1, keepdims=True)
    spread = jnp.mean(center * center, axis=1, keepdims=True)
    normed = (center * lax.rsqrt(spread + NORM_EPS) * gain_ref[...]).astype(jnp.bfloat16)
    norm_ref[...] = normed
    sig = 1.0 / (1.0 + jnp.exp(-dot_nn(x, wsel_ref[...])))
    sig_ref[...] = sig
    gates = sig * mask_ref[...].astype(jnp.float32)
    cos_two, sin_two = cos_ref[...], sin_ref[...]
    allowed = window_mask(step, tile, start_ref[...], keep_ref[:, before], keep_ref[:, now])
    scale = DH ** (-0.5)
    lanes = lax.broadcasted_iota(jnp.int32, (tile, LANE), 1)
    lse = jnp.zeros((tile, LANE), jnp.float32)
    for head in range(heads):
        cols = slice(head * DH, (head + 1) * DH)
        value = dot_nn(x, wval_ref[:, head * VEXP * DH : (head + 1) * VEXP * DH])
        val_ref[:, head * VEXP * DH : (head + 1) * VEXP * DH] = value.astype(jnp.bfloat16)
        total = jnp.zeros((tile, DH), jnp.float32)
        for e in range(VEXP):
            at = head * VEXP + e
            total = total + gates[:, at : at + 1] * value[:, e * DH : (e + 1) * DH]
        v_ref[now, cols] = total.astype(jnp.bfloat16)
    qk = dot_nn(normed, wqk_ref[...])
    for head in range(heads):
        cols = slice(head * DH, (head + 1) * DH)
        q_head = (spin(qk[:, cols], cos_two, sin_two) * scale).astype(jnp.bfloat16)
        k_head = spin(
            qk[:, (heads + head) * DH : (heads + head + 1) * DH], cos_two, sin_two
        ).astype(jnp.bfloat16)
        q_ref[:, cols] = q_head
        k_ref[now, cols] = k_head
        scores = jnp.concatenate(
            [dot_nt(q_head, k_ref[before, cols]), dot_nt(q_head, k_head)], axis=1
        )
        scores = jnp.where(allowed, scores, MASK_FILL)
        row_max = jnp.max(scores, axis=1, keepdims=True)
        terms = jnp.exp(scores - row_max)
        row_sum = jnp.sum(terms, axis=1, keepdims=True)
        probs = (terms * (1.0 / row_sum)).astype(jnp.bfloat16)
        attended = dot_nn(probs[:, :tile], v_ref[before, cols]) + dot_nn(
            probs[:, tile:], v_ref[now, cols]
        )
        att_ref[:, cols] = attended
        lse = jnp.where(lanes == head, row_max + jnp.log(row_sum), lse)
        for e in range(VEXP):
            at = head * VEXP + e
            gate = gates[:, heads * VEXP + at : heads * VEXP + at + 1]
            mix_ref[:, at * DH : (at + 1) * DH] = (gate * attended).astype(jnp.bfloat16)
    lse_ref[...] = lse
    hidden = x_f + dot_nn(mix_ref[...], wout_ref[...])
    hid_ref[...] = hidden
    sent_all[now, :] = hidden.astype(jnp.bfloat16)
    for index in range(steps):

        @pl.when(step == index)
        def _(index=index):
            tile_copy(index).start()

    @pl.when(step == steps - 1)
    def _():
        for copy in copies:
            copy.wait()
        for index in range(steps):
            tile_copy(index).wait()


def whole_block(shape):
    return pl.BlockSpec(shape, lambda step: (0,) * len(shape), pipeline_mode=pl.Buffered(1))


def attention_forward(own, cot, x, start, keep, cos_two, sin_two, mask, gain, wqk, wsel, wval, wout, tile):
    rows, model = x.shape
    heads = wqk.shape[1] // (2 * DH)
    per_tile = lambda width: pl.BlockSpec((tile, width), lambda step: (step, 0))
    full = lambda arr: whole_block(arr.shape)
    narrow, wide = heads * DH, heads * VEXP * DH
    shapes = [
        (model, jnp.float32, False),
        (model, jnp.bfloat16, False),
        (narrow, jnp.bfloat16, False),
        (narrow, jnp.bfloat16, True),
        (narrow, jnp.bfloat16, True),
        (wide, jnp.bfloat16, False),
        (narrow, jnp.float32, False),
        (LANE, jnp.float32, False),
        (LANE, jnp.float32, False),
        (wide, jnp.bfloat16, False),
        (model, jnp.bfloat16, True),
    ]
    return pl.pallas_call(
        functools.partial(forward_body, heads, tile, rows // tile),
        grid=(rows // tile,),
        in_specs=[
            ANYWHERE,
            ANYWHERE,
            per_tile(model),
            per_tile(1),
            full(keep),
            per_tile(LANE),
            per_tile(LANE),
            per_tile(LANE),
            full(gain),
            full(wqk),
            full(wsel),
            full(wval),
            full(wout),
        ],
        out_specs=[ANYWHERE] * 3
        + [whole_block((rows, width)) if whole else per_tile(width) for width, _, whole in shapes],
        out_shape=[
            jax.ShapeDtypeStruct(own.shape, jnp.bfloat16),
            jax.ShapeDtypeStruct((rows, model), jnp.bfloat16),
            jax.ShapeDtypeStruct((rows, model), jnp.bfloat16),
        ]
        + [jax.ShapeDtypeStruct((rows, width), kind) for width, kind, _ in shapes],
        scratch_shapes=[
            pltpu.SemaphoreType.DMA((2,)),
            pltpu.SemaphoreType.DMA((2,)),
            pltpu.SemaphoreType.DMA((rows // tile,)),
            pltpu.SemaphoreType.DMA((rows // tile,)),
        ],
        compiler_params=pltpu.CompilerParams(
            vmem_limit_bytes=VMEM_BYTES, collective_id=1, has_side_effects=True
        ),
        cost_estimate=pl.CostEstimate(
            flops=2 * rows * model * (2 * narrow + 2 * wide), bytes_accessed=40 << 20, transcendentals=0
        ),
    )(own, cot, x, start, keep, cos_two, sin_two, mask, gain, wqk, wsel, wval, wout)


def backward_body(heads, tile, steps, moves, n_in, n_out, *refs):
    ins, refs = refs[:n_in], refs[n_in:]
    (
        dy_ref,
        q_ref,
        k_ref,
        v_ref,
        att_ref,
        lse_ref,
        start_ref,
        keep_ref,
        sig_now_ref,
        mask_now_ref,
        cos_now_ref,
        sin_now_ref,
        sig_old_ref,
        mask_old_ref,
        cos_old_ref,
        sin_old_ref,
        x_ref,
        val_ref,
        dhid_ref,
        gain_ref,
        wqk_ref,
        wsel_ref,
        wval_ref,
        wout_ref,
        *outs_and_rest,
    ) = refs
    outs, rest = outs_and_rest[:n_out], outs_and_rest[n_out:]
    (
        gin_ref,
        dqk_ref,
        dval_ref,
        dlog_ref,
        ggain_ref,
        dk_acc,
        dv_acc,
        dq_keep,
        dgate_keep,
        gain_acc,
        send_sem,
        recv_sem,
    ) = rest
    step = pl.program_id(0)
    copies = copies_of(moves, ins, outs, send_sem, recv_sem)

    @pl.when(step == 0)
    def _():
        greet(peers_of(moves))
        for copy in copies:
            copy.start()

    slot = lax.rem(step, 2)
    old = 1 - slot
    lanes = lax.broadcasted_iota(jnp.int32, (tile, LANE), 1)
    scale = DH ** (-0.5)
    narrow = heads * DH

    @pl.when(step == 0)
    def _():
        gain_acc[...] = jnp.zeros_like(gain_acc)
        dk_acc[...] = jnp.zeros_like(dk_acc)
        dv_acc[...] = jnp.zeros_like(dv_acc)

    @pl.when(step < steps)
    def _():
        now = tile_rows(jnp.minimum(step, steps - 1), tile)
        before = tile_rows(jnp.maximum(step - 1, 0), tile)
        allowed = window_mask(step, tile, start_ref[...], keep_ref[:, before], keep_ref[:, now])
        gates = sig_now_ref[...] * mask_now_ref[...].astype(jnp.float32)
        dy = dy_ref[...]
        dgate = jnp.zeros((tile, LANE), jnp.float32)
        for head in range(heads):
            cols = slice(head * DH, (head + 1) * DH)
            dmixed = dot_nt(dy, wout_ref[head * VEXP * DH : (head + 1) * VEXP * DH, :])
            attended = att_ref[:, cols]
            dattend = jnp.zeros((tile, DH), jnp.float32)
            for e in range(VEXP):
                at = (heads + head) * VEXP + e
                part = dmixed[:, e * DH : (e + 1) * DH]
                dattend = dattend + gates[:, at : at + 1] * part
                dgate = jnp.where(
                    lanes == at, jnp.sum(part * attended, axis=1, keepdims=True), dgate
                )
            dattend = dattend.astype(jnp.bfloat16)
            q_head = q_ref[:, cols]
            k_old, k_now = k_ref[before, cols], k_ref[now, cols]
            v_old, v_now = v_ref[before, cols], v_ref[now, cols]
            scores = jnp.concatenate([dot_nt(q_head, k_old), dot_nt(q_head, k_now)], axis=1)
            scores = jnp.where(allowed, scores, MASK_FILL)
            probs = jnp.exp(scores - lse_ref[:, head : head + 1])
            dprob = jnp.concatenate([dot_nt(dattend, v_old), dot_nt(dattend, v_now)], axis=1)
            delta = jnp.sum(probs * dprob, axis=1, keepdims=True)
            dscore = (probs * (dprob - delta)).astype(jnp.bfloat16)
            probs = probs.astype(jnp.bfloat16)
            dv_acc[old, :, cols] += dot_tn(probs[:, :tile], dattend)
            dv_acc[slot, :, cols] = dot_tn(probs[:, tile:], dattend)
            dk_acc[old, :, cols] += dot_tn(dscore[:, :tile], q_head)
            dk_acc[slot, :, cols] = dot_tn(dscore[:, tile:], q_head)
            dq = dot_nn(dscore[:, :tile], k_old) + dot_nn(dscore[:, tile:], k_now)
            dq_keep[slot, :, cols] = (
                spin_back(dq, cos_now_ref[...], sin_now_ref[...]) * scale
            ).astype(jnp.bfloat16)
        dgate_keep[slot] = dgate

    @pl.when(step > 0)
    def _():
        sig = sig_old_ref[...]
        mask = mask_old_ref[...].astype(jnp.float32)
        gates = sig * mask
        dgate = dgate_keep[old]
        for head in range(heads):
            cols = slice(head * DH, (head + 1) * DH)
            dqk_ref[:, cols] = dq_keep[old, :, cols]
            dqk_ref[:, narrow + head * DH : narrow + (head + 1) * DH] = spin_back(
                dk_acc[old, :, cols], cos_old_ref[...], sin_old_ref[...]
            ).astype(jnp.bfloat16)
            dvalue = dv_acc[old, :, cols]
            for e in range(VEXP):
                at = head * VEXP + e
                wide = slice(at * DH, (at + 1) * DH)
                val = val_ref[:, wide].astype(jnp.float32)
                dgate = jnp.where(lanes == at, jnp.sum(dvalue * val, axis=1, keepdims=True), dgate)
                dval_ref[:, wide] = (gates[:, at : at + 1] * dvalue).astype(jnp.bfloat16)
        dlog = (dgate * gates * (1.0 - sig)).astype(jnp.bfloat16)
        dlog_ref[...] = dlog
        dnormed = dot_nt(dqk_ref[...], wqk_ref[...])
        x_f = x_ref[...].astype(jnp.float32)
        center = x_f - jnp.mean(x_f, axis=1, keepdims=True)
        inv = lax.rsqrt(jnp.mean(center * center, axis=1, keepdims=True) + NORM_EPS)
        x_hat = center * inv
        gain_acc[...] += jnp.sum(dnormed * x_hat, axis=0, keepdims=True)
        grad = dnormed * gain_ref[...]
        dx = inv * (
            grad
            - jnp.mean(grad, axis=1, keepdims=True)
            - x_hat * jnp.mean(grad * x_hat, axis=1, keepdims=True)
        )
        dx = dx + dhid_ref[...] + dot_nt(dval_ref[...], wval_ref[...]) + dot_nt(dlog, wsel_ref[...])
        gin_ref[...] = dx.astype(jnp.bfloat16)

    @pl.when(step == steps)
    def _():
        gain = gain_acc[...]
        high = gain.astype(jnp.bfloat16).astype(jnp.float32)
        row = lax.broadcasted_iota(jnp.int32, (GAIN_ROWS, gain.shape[1]), 0)
        split = jnp.where(row == 0, high, jnp.where(row == 1, gain - high, 0.0))
        ggain_ref[...] = split.astype(jnp.bfloat16)
        for copy in copies:
            copy.wait()


def attention_backward(
    sources, results, moves, dy, q, k, v, att, lse, start, keep, sig, mask, cos_two, sin_two, x, val, dhid, gain, wqk, wsel, wval, wout, tile
):
    rows, model = x.shape
    heads = wqk.shape[1] // (2 * DH)
    steps = rows // tile
    narrow, wide = heads * DH, heads * VEXP * DH
    at_now = lambda width: pl.BlockSpec((tile, width), lambda step: (jnp.minimum(step, steps - 1), 0))
    at_old = lambda width: pl.BlockSpec((tile, width), lambda step: (jnp.maximum(step - 1, 0), 0))
    full = lambda arr: whole_block(arr.shape)
    return pl.pallas_call(
        functools.partial(backward_body, heads, tile, steps, moves, len(sources), len(results)),
        grid=(steps + 1,),
        in_specs=[ANYWHERE] * len(sources)
        + [
            at_now(model),
            at_now(narrow),
            full(k),
            full(v),
            at_now(narrow),
            at_now(LANE),
            at_now(1),
            full(keep),
            at_now(LANE),
            at_now(LANE),
            at_now(LANE),
            at_now(LANE),
            at_old(LANE),
            at_old(LANE),
            at_old(LANE),
            at_old(LANE),
            at_old(model),
            at_old(wide),
            at_old(model),
            full(gain),
            full(wqk),
            full(wsel),
            full(wval),
            full(wout),
        ],
        out_specs=[ANYWHERE] * len(results)
        + [
            at_old(model),
            at_old(2 * narrow),
            at_old(wide),
            at_old(LANE),
            whole_block((GAIN_ROWS, model)),
        ],
        out_shape=[jax.ShapeDtypeStruct(shape, jnp.bfloat16) for shape in results]
        + [
            jax.ShapeDtypeStruct((rows, model), jnp.bfloat16),
            jax.ShapeDtypeStruct((rows, 2 * narrow), jnp.bfloat16),
            jax.ShapeDtypeStruct((rows, wide), jnp.bfloat16),
            jax.ShapeDtypeStruct((rows, LANE), jnp.bfloat16),
            jax.ShapeDtypeStruct((GAIN_ROWS, model), jnp.bfloat16),
        ],
        scratch_shapes=[
            pltpu.VMEM((2, tile, narrow), jnp.float32),
            pltpu.VMEM((2, tile, narrow), jnp.float32),
            pltpu.VMEM((2, tile, narrow), jnp.bfloat16),
            pltpu.VMEM((2, tile, LANE), jnp.float32),
            pltpu.VMEM((1, model), jnp.float32),
            pltpu.SemaphoreType.DMA((len(moves),)),
            pltpu.SemaphoreType.DMA((len(moves),)),
        ],
        compiler_params=pltpu.CompilerParams(
            vmem_limit_bytes=VMEM_BYTES, collective_id=6, has_side_effects=True
        ),
        cost_estimate=pl.CostEstimate(
            flops=2 * rows * model * (2 * narrow + 2 * wide), bytes_accessed=50 << 20, transcendentals=0
        ),
    )(
        *sources, dy, q, k, v, att, lse, start, keep, sig, mask, cos_two, sin_two, sig, mask, cos_two, sin_two,
        x, val, dhid, gain, wqk, wsel, wval, wout,
    )


def outer_body(groups, *refs):
    out_ref = refs[-1]
    at = 0
    for pairs in groups:
        total = sum(dot_tn(refs[left][...], refs[right][...]) for left, right in pairs)
        out_ref[:, at : at + total.shape[1]] = total.astype(jnp.bfloat16)
        at += total.shape[1]


def outer_products(arrays, groups, lefts, block):
    rows, model = arrays[0].shape
    width = sum(arrays[pairs[0][1]].shape[1] for pairs in groups)
    return pl.pallas_call(
        functools.partial(outer_body, groups),
        grid=(model // block,),
        in_specs=[
            pl.BlockSpec((arr.shape[0], block), lambda step: (0, step))
            if i < lefts
            else whole_block(arr.shape)
            for i, arr in enumerate(arrays)
        ],
        out_specs=pl.BlockSpec((block, width), lambda step: (step, 0)),
        out_shape=jax.ShapeDtypeStruct((model, width), jnp.bfloat16),
        compiler_params=pltpu.CompilerParams(vmem_limit_bytes=VMEM_BYTES),
        cost_estimate=pl.CostEstimate(
            flops=2 * rows * model * width, bytes_accessed=20 << 20, transcendentals=0
        ),
    )(*arrays)


def expert_body(first, last, exp_local, ff_dim, tile, steps, moves, n_in, n_out, *refs):
    ins, refs = refs[:n_in], refs[n_in:]
    x_own, x_far, c_own, c_far, w_ref, mask_ref, digit_ref = refs[:7]
    at = 7
    if not first:
        out_in, grad_in = refs[at : at + 2]
        at += 2
    if last:
        hid_ref = refs[at]
        at += 1
    outs = refs[at : at + n_out]
    at += n_out
    results = refs[at : at + 3]
    g_ref = refs[at + 3 if last else at + 2]
    at += 4 if last else 3
    act_all, dpre_all, x_ref, c_ref, load_sem, send_sem, recv_sem = refs[at : at + 7]
    wide = exp_local * ff_dim
    back = wide + ROUTER_ROWS
    half = steps // 2
    step = pl.program_id(0)
    copies = copies_of(moves, ins, outs, send_sem, recv_sem)
    peers = peers_of(moves)
    if last:
        given, taken, tile_send, tile_recv = refs[at + 7 :]
        partner = neighbour("core", 1)
        peers.append(partner)

        def tile_copy(index, kind):
            return pltpu.make_async_remote_copy(
                src_ref=given.at[kind, pl.ds(index * tile, tile)],
                dst_ref=taken.at[kind, pl.ds(index * tile, tile)],
                send_sem=tile_send.at[kind, index],
                recv_sem=tile_recv.at[kind, index],
                device_id=partner,
                device_id_type=pl.DeviceIdType.MESH,
            )

    def load(index, kind):
        near, far, whole = ((x_own, x_far, x_ref), (c_own, c_far, c_ref))[kind]
        source = near if index < half else far
        return pltpu.make_async_copy(
            source.at[pl.ds(index % half * tile, tile)],
            whole.at[pl.ds(index * tile, tile)],
            load_sem.at[kind, index],
        )

    @pl.when(step == 0)
    def _():
        for turn in range(steps):
            for kind in range(2):
                load((turn + half) % steps if last else turn, kind).start()
        greet(peers)
        for copy in copies:
            copy.start()

    for turn in range(steps):

        @pl.when(step == turn)
        def _(turn=turn):
            for kind in range(2):
                load((turn + half) % steps if last else turn, kind).wait()

    rows = tile_rows(lax.rem(step + half, steps) if last else step, tile)
    x, c = x_ref[rows, :], c_ref[rows, :]
    sig = 1.0 / (1.0 + jnp.exp(-dot_nt(x, w_ref[wide:back, :])))
    gate = sig * mask_ref[:, :ROUTER_ROWS].astype(jnp.float32)
    lanes = lax.broadcasted_iota(jnp.int32, (tile, ROUTER_ROWS), 1)
    dgate = jnp.zeros((tile, ROUTER_ROWS), jnp.float32)
    for pair in range(exp_local // 2):
        lo, hi = 2 * pair * ff_dim, 2 * (pair + 1) * ff_dim
        pre_two = dot_nt(x, w_ref[lo:hi, :])
        raw_two = dot_nt(c, w_ref[back + lo : back + hi, :])
        for side in range(2):
            e = 2 * pair + side
            pre = pre_two[:, side * ff_dim : (side + 1) * ff_dim]
            raw = raw_two[:, side * ff_dim : (side + 1) * ff_dim]
            square = pre * pre
            bend = jnp.tanh(pre * (GELU_A + GELU_A * GELU_B * square))
            upper = 0.5 * bend + 0.5
            act = (pre * upper).astype(jnp.bfloat16).astype(jnp.float32)
            slope = upper + (0.5 * pre) * (1.0 - bend * bend) * (GELU_A + 3 * GELU_A * GELU_B * square)
            gate_col = gate[:, e : e + 1]
            act_all[rows, e * ff_dim : (e + 1) * ff_dim] = (gate_col * act).astype(jnp.bfloat16)
            dpre_all[rows, e * ff_dim : (e + 1) * ff_dim] = (gate_col * raw * slope).astype(
                jnp.bfloat16
            )
            dgate = jnp.where(lanes == e, jnp.sum(act * raw, axis=1, keepdims=True), dgate)
    dpre_all[rows, wide:back] = (dgate * gate * (1.0 - sig)).astype(jnp.bfloat16)
    out_new = dot_nn(act_all[rows, :], w_ref[back:, :])
    grad_new = dot_nn(dpre_all[rows, :], w_ref[:back, :])
    if not first:
        out_new = out_new + out_in[...]
        grad_new = grad_new + grad_in[...]
    if last:

        @pl.when(step < half)
        def _():
            mine = tile_rows(jnp.minimum(step, half - 1), tile)
            given[0, mine, :] = out_new.astype(jnp.bfloat16)
            given[1, mine, :] = grad_new.astype(jnp.bfloat16)

        for index in range(half):

            @pl.when(step == index)
            def _(index=index):
                tile_copy(index, 0).start()
                tile_copy(index, 1).start()

            @pl.when(step == index + half)
            def _(index=index):
                tile_copy(index, 0).wait_recv()
                tile_copy(index, 1).wait_recv()

        @pl.when(step >= half)
        def _():
            mine = tile_rows(jnp.maximum(step - half, 0), tile)
            total = hid_ref[...] + out_new + taken[0, mine, :].astype(jnp.float32)
            results[0][...] = total.astype(jnp.bfloat16)
            dhidden = c.astype(jnp.float32) + grad_new + taken[1, mine, :].astype(jnp.float32)
            results[1][...] = dhidden
            results[2][...] = dhidden.astype(jnp.bfloat16)

    else:
        results[0][...] = out_new
        results[1][...] = grad_new

    @pl.when(step == steps - 1)
    def _():
        for lo in range(0, wide, 2 * ff_dim):
            g_ref[lo : lo + 2 * ff_dim, :] = dot_tn(
                dpre_all[:, lo : lo + 2 * ff_dim], x_ref[...]
            ).astype(jnp.bfloat16)
            g_ref[back + lo : back + lo + 2 * ff_dim, :] = dot_tn(
                act_all[:, lo : lo + 2 * ff_dim], c_ref[...]
            ).astype(jnp.bfloat16)
        extra = dot_tn(dpre_all[:, wide:back], x_ref[...])
        g_ref[wide:back, :LANE] = (extra[:, :LANE] + digit_ref[...]).astype(jnp.bfloat16)
        g_ref[wide:back, LANE:] = extra[:, LANE:].astype(jnp.bfloat16)
        for copy in copies:
            copy.wait()
        if last:
            for index in range(half):
                tile_copy(index, 0).wait_send()
                tile_copy(index, 1).wait_send()


def expert_chunk(
    sources, results, aliases, moves, tokens, weights, masks, digits, hop, sums, hidden, exp_local, ff_dim, tile
):
    rows, model = 2 * tokens[0].shape[0], tokens[0].shape[1]
    steps = rows // tile
    half = steps // 2
    first, last = sums is None, hidden is not None
    turn = (lambda step: lax.rem(step + half, steps)) if last else (lambda step: step)
    per_tile = lambda: pl.BlockSpec((tile, model), lambda step: (turn(step), 0))
    late = lambda: pl.BlockSpec((tile, model), lambda step: (jnp.maximum(step - half, 0), 0))
    in_specs = [ANYWHERE] * (len(sources) + 4) + [
        whole_block(weights.shape),
        pl.BlockSpec((tile, LANE), lambda step: (turn(step), hop)),
        pl.BlockSpec((ROUTER_ROWS, LANE), lambda step: (0, hop)),
    ]
    args = list(sources) + list(tokens) + [weights, masks, digits]
    if not first:
        in_specs += [per_tile(), per_tile()]
        args += list(sums)
    wide = exp_local * ff_dim
    scratch = [
        pltpu.VMEM((rows, wide), jnp.bfloat16),
        pltpu.VMEM((rows, wide + ROUTER_ROWS), jnp.bfloat16),
        pltpu.VMEM((rows, model), jnp.bfloat16),
        pltpu.VMEM((rows, model), jnp.bfloat16),
        pltpu.SemaphoreType.DMA((2, steps)),
        pltpu.SemaphoreType.DMA((len(moves),)),
        pltpu.SemaphoreType.DMA((len(moves),)),
    ]
    if last:
        in_specs.append(late())
        args.append(hidden)
        out_specs = [late(), late(), late()]
        out_shape = [
            jax.ShapeDtypeStruct((rows // 2, model), kind)
            for kind in (jnp.bfloat16, jnp.float32, jnp.bfloat16)
        ]
        scratch += [
            pltpu.VMEM((2, rows // 2, model), jnp.bfloat16),
            pltpu.VMEM((2, rows // 2, model), jnp.bfloat16),
            pltpu.SemaphoreType.DMA((2, half)),
            pltpu.SemaphoreType.DMA((2, half)),
        ]
    else:
        out_specs = [per_tile(), per_tile()]
        out_shape = [jax.ShapeDtypeStruct((rows, model), jnp.float32)] * 2
    outs = pl.pallas_call(
        functools.partial(
            expert_body, first, last, exp_local, ff_dim, tile, steps, moves, len(sources), len(results)
        ),
        grid=(steps,),
        in_specs=in_specs,
        out_specs=[ANYWHERE] * len(results) + out_specs + [whole_block(weights.shape)],
        out_shape=[jax.ShapeDtypeStruct(shape, jnp.bfloat16) for shape in results]
        + out_shape
        + [jax.ShapeDtypeStruct(weights.shape, jnp.bfloat16)],
        input_output_aliases=aliases,
        scratch_shapes=scratch,
        compiler_params=pltpu.CompilerParams(
            vmem_limit_bytes=VMEM_BYTES, collective_id=2 + hop, has_side_effects=True
        ),
        cost_estimate=pl.CostEstimate(
            flops=12 * rows * model * wide, bytes_accessed=40 << 20, transcendentals=rows * wide
        ),
    )(*args)
    return outs[: len(results)], outs[len(results) : -1], outs[-1]


def core_swap(arr):
    size = lax.axis_size("expert")
    return lax.ppermute(arr, "expert", [(i, i ^ 1) for i in range(size)])


def chip_shift(arr, hop):
    size = lax.axis_size("expert")
    chips = size // 2
    return lax.ppermute(
        arr, "expert", [(i, (i // 2 + hop) % chips * 2 + i % 2) for i in range(size)]
    )


def dp_swap(arr, flip):
    return lax.ppermute(arr, "dp", [(i, i ^ flip) for i in range(lax.axis_size("dp"))])


def row_part(arr, index, count):
    return lax.dynamic_slice_in_dim(arr, index * (arr.shape[0] // count), arr.shape[0] // count, 0)


def dp_gather(part):
    mine = lax.axis_index("dp")
    rows = part.shape[0]
    whole = jnp.zeros((4 * rows,) + part.shape[1:], part.dtype)
    for flip in range(4):
        piece = part if flip == 0 else dp_swap(part, flip)
        whole = lax.dynamic_update_slice_in_dim(whole, piece, (mine ^ flip) * rows, 0)
    return whole


def dp_scatter(whole):
    mine = lax.axis_index("dp")
    total = row_part(whole, mine, 4).astype(jnp.float32)
    for flip in range(1, 4):
        total = total + dp_swap(row_part(whole, mine ^ flip, 4), flip).astype(jnp.float32)
    return total


def scatter_rows(whole):
    dev_count = lax.axis_size("expert")
    chips = dev_count // 2
    rows, width = whole.shape
    mine = lax.axis_index("expert")
    chip, core = mine // 2, mine % 2
    by_core = whole.reshape(4 * chips, 2, rows // (8 * chips), width)
    kept = lax.dynamic_index_in_dim(by_core, core, 1, keepdims=False)
    given = lax.dynamic_index_in_dim(by_core, 1 - core, 1, keepdims=False)
    pair = (kept.astype(jnp.float32) + core_swap(given).astype(jnp.float32)).astype(jnp.bfloat16)
    quarter = dp_scatter(pair.reshape(rows // 2, width)).astype(jnp.bfloat16)
    total = row_part(quarter, chip, chips).astype(jnp.float32)
    for hop in range(1, chips):
        piece = row_part(quarter, (chip + hop) % chips, chips)
        total = total + chip_shift(piece, hop).astype(jnp.float32)
    return total


def own_weights(w_router, w_in, w_out):
    exp_local, model_dim, ff_dim = w_in.shape
    router_rows = jnp.zeros((ROUTER_ROWS, model_dim), jnp.bfloat16).at[:exp_local].set(w_router)
    return jnp.concatenate(
        [
            jnp.swapaxes(w_in, 1, 2).reshape(exp_local * ff_dim, model_dim),
            router_rows,
            w_out.reshape(exp_local * ff_dim, model_dim),
        ]
    )


def block_dense(
    layer_input,
    segments,
    keep_mask,
    att_routes,
    moe_routes,
    expert_counts,
    norm_gain,
    w_query,
    w_key,
    w_select,
    w_value,
    w_output,
    w_router,
    w_in,
    w_out,
    cotangent,
):
    rows, model = layer_input.shape
    seqs, seq_len = segments.shape
    exp_local, _, ff_dim = w_in.shape
    heads = w_query.shape[1] // DH
    chips = lax.axis_size("expert") // 2
    wide, narrow, gates = heads * VEXP * DH, heads * DH, 2 * heads * VEXP
    moe_wide = exp_local * ff_dim
    mine = lax.axis_index("expert")
    chip, core = mine // 2, mine % 2

    own = own_weights(w_router, w_in, w_out)
    exp_total = 2 * chips * exp_local
    named = jnp.sum(
        (moe_routes[..., None] == jnp.arange(exp_total, dtype=jnp.int32)).astype(jnp.bfloat16), axis=1
    )
    named = jnp.concatenate([named, core_swap(named)])

    column = jnp.arange(seq_len, dtype=jnp.int32)
    changed = jnp.concatenate(
        [jnp.ones((seqs, 1), jnp.bool_), segments[:, 1:] != segments[:, :-1]], axis=1
    )
    start = lax.cummax(jnp.where(changed, column, 0), axis=1)
    cos_tab, sin_tab = rope_tables((column - start).reshape(-1), DH)
    cos_two = jnp.concatenate([cos_tab, cos_tab], axis=1)
    sin_two = jnp.concatenate([-sin_tab, sin_tab], axis=1)
    start = (start + seq_len * jnp.arange(seqs, dtype=jnp.int32)[:, None]).reshape(rows, 1)
    keep = keep_mask.reshape(1, rows)
    att_mask = jnp.sum(
        (att_routes[..., None] == jnp.arange(VEXP, dtype=jnp.int32)).astype(jnp.bfloat16), axis=2
    ).reshape(rows, gates)
    att_mask = jnp.pad(att_mask, ((0, 0), (0, LANE - gates)))
    gain_row = norm_gain.reshape(1, model)
    wqk = jnp.concatenate([w_query, w_key], axis=1)
    wsel = jnp.pad(w_select, ((0, 0), (0, LANE - gates)))

    second, cot_far, sent_far, hidden, normed, q_rot, k_rot, value_bf, value_all, attended, sig, lse, mixed, sent = (
        attention_forward(
            own, cotangent, layer_input, start, keep, cos_two, sin_two, att_mask, gain_row, wqk, wsel, w_value, w_output, TILE
        )
    )

    lane = jnp.arange(chips * LANE, dtype=jnp.int32)
    owner = ((chip + lane // LANE) % chips * 2 + core) * exp_local + lane % LANE
    pick = (lane % LANE < exp_local) & (jnp.arange(exp_total, dtype=jnp.int32)[:, None] == owner)
    masks = jnp.dot(named, pick.astype(jnp.bfloat16), preferred_element_type=jnp.float32)
    counts = jnp.sum(masks, axis=0).astype(jnp.int32)
    masks = masks.astype(jnp.bfloat16)
    place = jnp.arange(ROUTER_ROWS, dtype=jnp.int32)[:, None] - exp_local
    digits = jnp.where(
        (place >= 0) & (place < DIGITS), (counts >> (2 * jnp.clip(place, 0, DIGITS))) & 3, 0
    ).astype(jnp.float32)

    part = own.shape[0] // 4
    shape, three = own.shape, (3 * part, model)

    def run(hop, sources, results, aliases, moves, weights, sums, last_hidden):
        return expert_chunk(
            sources, results, aliases, moves, (sent, sent_far, cotangent, cot_far), weights, masks, digits, hop, sums,
            last_hidden, exp_local, ff_dim, TILE,
        )

    def sum_parts(whole, three_parts):
        total = row_part(whole, lax.axis_index("dp"), 4).astype(jnp.float32)
        for flip in range(3):
            total = total + three_parts[flip * part : (flip + 1) * part].astype(jnp.float32)
        return total

    (second, third, first), sums, grad_0 = run(
        0,
        [second, own],
        [shape, shape, shape],
        {0: 0},
        gather_moves(0, 0, part)
        + shift_move(1, 1, -3, own_part(part), own_part(part), part)
        + shift_move(1, 2, -1, fixed(0), fixed(0), part),
        own,
        None,
        None,
    )
    (third, first), sums, grad_2 = run(
        2,
        [third, first, own],
        [shape, shape],
        {0: 0, 1: 1},
        gather_moves(0, 0, part) + shift_move(2, 1, -1, fixed(part), fixed(part), 2 * part),
        second,
        sums,
        None,
    )
    (first, from_2), sums, grad_3 = run(
        3,
        [first, own, grad_2],
        [shape, three],
        {0: 0},
        shift_move(1, 0, -1, fixed(3 * part), fixed(3 * part), part) + scatter_moves(2, 1, part),
        third,
        sums,
        None,
    )
    part_2 = sum_parts(grad_2, from_2).astype(jnp.bfloat16)
    (from_3, got_2), (layer_output, dhidden, dy), grad_1 = run(
        1,
        [grad_3, part_2],
        [three, (part, model)],
        {},
        scatter_moves(0, 0, part) + shift_move(1, 1, 2, fixed(0), fixed(0), part),
        first,
        sums,
        hidden,
    )
    part_3 = sum_parts(grad_3, from_3).astype(jnp.bfloat16)
    out_joined = outer_products([dy, mixed], [[(0, 1)]], 1, TILE)
    from_0, got_3, grad_input, dqk, dval, dlog, gain_rows = attention_backward(
        [grad_0, part_3],
        [three, (part, model)],
        scatter_moves(0, 0, part) + shift_move(1, 1, 3, fixed(0), fixed(0), part),
        dy, q_rot, k_rot, value_bf, attended, lse, start, keep, sig, att_mask, cos_two, sin_two,
        layer_input, value_all, dhidden, gain_row, wqk, wsel, w_value, w_output, TILE,
    )
    out_sum = scatter_rows(out_joined).T
    part_1 = dp_scatter(grad_1).astype(jnp.bfloat16)
    total = sum_parts(grad_0, from_0) + got_2.astype(jnp.float32) + got_3.astype(jnp.float32)
    total = total + chip_shift(part_1, 1).astype(jnp.float32)
    summed = dp_gather(total.astype(jnp.bfloat16)).astype(jnp.float32)
    grad_w_in = jnp.swapaxes(summed[:moe_wide].reshape(exp_local, ff_dim, model), 1, 2)
    extra = summed[moe_wide : moe_wide + ROUTER_ROWS]
    grad_router = extra[:exp_local]
    parts = extra[exp_local : exp_local + DIGITS, :exp_local].astype(jnp.int32)
    tally = sum(parts[i] << (2 * i) for i in range(DIGITS))
    grad_w_out = summed[moe_wide + ROUTER_ROWS :].reshape(exp_local, ff_dim, model)

    unit = (
        (jnp.arange(GAIN_ROWS)[:, None] < 2) & (jnp.arange(LANE)[None, :] == gates)
    ).astype(jnp.bfloat16)
    joined = outer_products(
        [layer_input, normed, gain_rows, dval, dlog, dqk, unit],
        [[(0, 3)], [(0, 4), (2, 6)], [(1, 5)]],
        3,
        TILE,
    )
    summed = scatter_rows(joined)
    at_qk = wide + LANE
    return (
        layer_output,
        grad_input,
        summed[:, wide + gates],
        summed[:, at_qk : at_qk + narrow],
        summed[:, at_qk + narrow : at_qk + 2 * narrow],
        summed[:, wide : wide + gates],
        summed[:, :wide],
        out_sum,
        grad_router,
        grad_w_in,
        grad_w_out,
        expert_counts + tally,
    )


def block_dispatched(
    layer_input,
    segments,
    keep_mask,
    att_routes,
    moe_routes,
    expert_counts,
    norm_gain,
    w_query,
    w_key,
    w_select,
    w_value,
    w_output,
    w_router,
    w_in,
    w_out,
    cotangent,
):
    tok_rows, model_dim = layer_input.shape
    seq_count, seq_len = segments.shape
    head_count = w_query.shape[1] // DH
    score_scale = DH ** (-0.5)
    inputs_f = layer_input.astype(jnp.float32)
    normed, norm_pull = jax.vjp(layer_norm, inputs_f, norm_gain)
    normed_bf = normed.astype(jnp.bfloat16)
    query_rows = jnp.dot(normed_bf, w_query, preferred_element_type=jnp.float32).reshape(
        tok_rows, head_count, DH
    )
    key_rows = jnp.dot(normed_bf, w_key, preferred_element_type=jnp.float32).reshape(
        tok_rows, head_count, DH
    )
    logits = jnp.dot(layer_input, w_select, preferred_element_type=jnp.float32)
    named_mask = jnp.sum(
        (att_routes[..., None] == jnp.arange(VEXP, dtype=jnp.int32)).astype(jnp.float32), axis=2
    )
    select_sig = jax.nn.sigmoid(logits).reshape(tok_rows, 2 * head_count, VEXP)
    head_gates = select_sig * named_mask
    value_all = jnp.dot(layer_input, w_value, preferred_element_type=jnp.float32).reshape(
        tok_rows, head_count, VEXP, DH
    )
    value_bf = jnp.sum(head_gates[:, :head_count, :, None] * value_all, axis=2).astype(jnp.bfloat16)
    position, allowed = jax.vmap(doc_layout)(segments, keep_mask)
    cos_tab, sin_tab = rope_tables(position.reshape(-1), DH)
    q_rot = (rotate(query_rows, cos_tab, sin_tab) * score_scale).astype(jnp.bfloat16)
    k_rot = rotate(key_rows, cos_tab, sin_tab).astype(jnp.bfloat16)
    seq_shape = (seq_count, seq_len, head_count, DH)
    attended, log_total = lax.map(
        attend_forward,
        (q_rot.reshape(seq_shape), k_rot.reshape(seq_shape), value_bf.reshape(seq_shape), allowed),
    )
    attended = attended.reshape(tok_rows, head_count, DH)
    mixed_bf = (
        (head_gates[:, head_count:, :, None] * attended[:, :, None, :])
        .astype(jnp.bfloat16)
        .reshape(tok_rows, head_count * VEXP * DH)
    )
    hidden = inputs_f + jnp.dot(mixed_bf, w_output, preferred_element_type=jnp.float32)
    dev_count = lax.axis_size("expert")
    exp_local = w_in.shape[0]
    exp_total = dev_count * exp_local
    top_k = moe_routes.shape[1]
    capacity = 10 * tok_rows * top_k // (7 * exp_total) + 1
    owner, filled, slot_of = slot_table(moe_routes, exp_total, capacity)
    keep_slot = filled[:, None] > 0
    zero_bf = jnp.zeros((), jnp.bfloat16)
    hidden_bf = hidden.astype(jnp.bfloat16)
    send_rows = jnp.where(keep_slot, hidden_bf[owner], zero_bf).reshape(
        dev_count, exp_local * capacity, model_dim
    )
    rows_in = lax.all_to_all(send_rows, "expert", split_axis=0, concat_axis=0, tiled=True)
    histogram = jnp.zeros((exp_total,), jnp.float32).at[moe_routes.reshape(-1)].add(1.0)
    tally = lax.psum_scatter(histogram, "expert", scatter_dimension=0, tiled=True)
    slot_shape = (dev_count, exp_local, capacity, model_dim)
    rows_four = rows_in.reshape(slot_shape)
    pre_act = jnp.einsum("necd,edf->necf", rows_four, w_in, preferred_element_type=jnp.float32)
    gelu_out, gelu_pull = jax.vjp(jax.nn.gelu, pre_act)
    act_bf = gelu_out.astype(jnp.bfloat16)
    router_logit = jnp.einsum(
        "necd,ed->nec", rows_four, w_router, preferred_element_type=jnp.float32
    )
    gate_moe = jax.nn.sigmoid(router_logit)
    expert_out = jnp.einsum("necf,efd->necd", act_bf, w_out, preferred_element_type=jnp.float32)
    reply = (
        (gate_moe[..., None] * expert_out)
        .astype(jnp.bfloat16)
        .reshape(dev_count, exp_local * capacity, model_dim)
    )
    returned = lax.all_to_all(reply, "expert", split_axis=0, concat_axis=0, tiled=True)
    moe_sum = jnp.sum(returned.reshape(-1, model_dim)[slot_of].astype(jnp.float32), axis=1)
    layer_output = (hidden + moe_sum).astype(jnp.bfloat16)
    cot_f = cotangent.astype(jnp.float32)
    send_cot = jnp.where(keep_slot, cotangent[owner], zero_bf).reshape(
        dev_count, exp_local * capacity, model_dim
    )
    cot_in, rows_again = (
        lax.all_to_all(send_cot, "expert", split_axis=0, concat_axis=0, tiled=True),
        lax.all_to_all(send_rows, "expert", split_axis=0, concat_axis=0, tiled=True),
    )
    rows_grad = rows_again.reshape(slot_shape)
    cot_bf = cot_in.reshape(slot_shape)
    raw_back = jnp.einsum("necd,efd->necf", cot_bf, w_out, preferred_element_type=jnp.float32)
    dgate = jnp.sum(act_bf.astype(jnp.float32) * raw_back, axis=-1)
    dlogit = dgate * gate_moe * (1.0 - gate_moe)
    dexpert = (gate_moe[..., None] * cot_bf.astype(jnp.float32)).astype(jnp.bfloat16)
    grad_w_out = jnp.einsum("necf,necd->efd", act_bf, dexpert, preferred_element_type=jnp.float32)
    dact = jnp.einsum("necd,efd->necf", dexpert, w_out, preferred_element_type=jnp.float32)
    dpre_bf = gelu_pull(dact)[0].astype(jnp.bfloat16)
    grad_w_in = jnp.einsum("necd,necf->edf", rows_grad, dpre_bf, preferred_element_type=jnp.float32)
    grad_router = jnp.einsum(
        "nec,necd->ed",
        dlogit,
        rows_grad.astype(jnp.float32),
        preferred_element_type=jnp.float32,
        precision=HIGHEST,
    )
    dsent = jnp.einsum("necf,edf->necd", dpre_bf, w_in, preferred_element_type=jnp.float32)
    dsent = (dsent + dlogit[..., None] * w_router[None, :, None, :].astype(jnp.float32)).astype(
        jnp.bfloat16
    )
    grad_back = lax.all_to_all(
        dsent.reshape(dev_count, exp_local * capacity, model_dim),
        "expert",
        split_axis=0,
        concat_axis=0,
        tiled=True,
    )
    dhidden = cot_f + jnp.sum(grad_back.reshape(-1, model_dim)[slot_of].astype(jnp.float32), axis=1)
    dy_bf = dhidden.astype(jnp.bfloat16)
    grad_output = jnp.einsum("tk,td->kd", mixed_bf, dy_bf, preferred_element_type=jnp.float32)
    dmixed = jnp.einsum("td,kd->tk", dy_bf, w_output, preferred_element_type=jnp.float32).reshape(
        tok_rows, head_count, VEXP, DH
    )
    dgate_out = jnp.sum(dmixed * attended[:, :, None, :], axis=-1)
    dattend = jnp.sum(head_gates[:, head_count:, :, None] * dmixed, axis=2).astype(jnp.bfloat16)
    grad_q, grad_k, grad_v = lax.map(
        attend_backward,
        (
            q_rot.reshape(seq_shape),
            k_rot.reshape(seq_shape),
            value_bf.reshape(seq_shape),
            allowed,
            log_total,
            dattend.reshape(seq_shape),
        ),
    )
    dquery = (
        (rotate_back(grad_q.reshape(tok_rows, head_count, DH), cos_tab, sin_tab) * score_scale)
        .astype(jnp.bfloat16)
        .reshape(tok_rows, head_count * DH)
    )
    dkey = (
        rotate_back(grad_k.reshape(tok_rows, head_count, DH), cos_tab, sin_tab)
        .astype(jnp.bfloat16)
        .reshape(tok_rows, head_count * DH)
    )
    grad_query = jnp.einsum("td,tk->dk", normed_bf, dquery, preferred_element_type=jnp.float32)
    grad_key = jnp.einsum("td,tk->dk", normed_bf, dkey, preferred_element_type=jnp.float32)
    dnormed = jnp.einsum(
        "tk,dk->td", dquery, w_query, preferred_element_type=jnp.float32
    ) + jnp.einsum("tk,dk->td", dkey, w_key, preferred_element_type=jnp.float32)
    dx_norm, grad_gain = norm_pull(dnormed)
    dvalue = grad_v.reshape(tok_rows, head_count, DH)
    dgate_val = jnp.sum(dvalue[:, :, None, :] * value_all, axis=-1)
    dvalue_all = (
        (head_gates[:, :head_count, :, None] * dvalue[:, :, None, :])
        .astype(jnp.bfloat16)
        .reshape(tok_rows, head_count * VEXP * DH)
    )
    grad_value = jnp.einsum(
        "td,tk->dk", layer_input, dvalue_all, preferred_element_type=jnp.float32
    )
    dgates = jnp.concatenate([dgate_val, dgate_out], axis=1)
    dlogits = (
        (dgates * named_mask * select_sig * (1.0 - select_sig))
        .astype(jnp.bfloat16)
        .reshape(tok_rows, 2 * head_count * VEXP)
    )
    grad_select = jnp.einsum("td,tk->dk", layer_input, dlogits, preferred_element_type=jnp.float32)
    grad_input = (
        dhidden
        + dx_norm
        + jnp.einsum("tk,dk->td", dvalue_all, w_value, preferred_element_type=jnp.float32)
    )
    grad_input = (
        grad_input + jnp.einsum("tk,dk->td", dlogits, w_select, preferred_element_type=jnp.float32)
    ).astype(jnp.bfloat16)
    expert_sums = (
        lax.psum(grad_w_in.astype(jnp.bfloat16), "dp").astype(jnp.float32),
        lax.psum(grad_w_out.astype(jnp.bfloat16), "dp").astype(jnp.float32),
        lax.psum(grad_router.astype(jnp.bfloat16), "dp").astype(jnp.float32),
        lax.psum(tally.astype(jnp.bfloat16), "dp").astype(jnp.float32),
    )
    dense_sums = (
        lax.psum_scatter(grad_gain, ("dp", "expert"), scatter_dimension=0, tiled=True),
        lax.psum_scatter(grad_query, ("dp", "expert"), scatter_dimension=0, tiled=True),
        lax.psum_scatter(grad_key, ("dp", "expert"), scatter_dimension=0, tiled=True),
        lax.psum_scatter(grad_select, ("dp", "expert"), scatter_dimension=0, tiled=True),
        lax.psum_scatter(grad_value, ("dp", "expert"), scatter_dimension=0, tiled=True),
        lax.psum_scatter(grad_output, ("dp", "expert"), scatter_dimension=1, tiled=True),
    )
    counts_out = expert_counts + expert_sums[3].astype(jnp.int32)
    return (
        layer_output,
        grad_input,
        dense_sums[0],
        dense_sums[1],
        dense_sums[2],
        dense_sums[3],
        dense_sums[4],
        dense_sums[5],
        expert_sums[2],
        expert_sums[0],
        expert_sums[1],
        counts_out,
    )


def local(*args):
    rows, top_k = args[4].shape
    experts, _, ff_dim = args[13].shape
    exp_total = lax.axis_size("expert") * experts
    capacity = 10 * rows * top_k // (7 * exp_total) + 1
    regular = lax.axis_size("dp") == 4 and lax.axis_size("expert") == 8 and experts % 2 == 0 and ff_dim == LANE
    return (block_dense if regular and 4 * capacity > rows else block_dispatched)(*args)


def solution(mesh):
    placed = (
        P(("dp", "expert"), None),
        P(("dp", "expert"), None),
        P(("dp", "expert"), None),
        P(("dp", "expert"), None, None),
        P(("dp", "expert"), None),
        P("expert"),
        P(),
        P(),
        P(),
        P(),
        P(),
        P(),
        P("expert", None),
        P("expert", None, None),
        P("expert", None, None),
        P(("dp", "expert"), None),
    )
    return jax.shard_map(
        local,
        mesh=mesh,
        in_specs=placed,
        out_specs=(
            P(("dp", "expert"), None),
            P(("dp", "expert"), None),
            P(("dp", "expert")),
            P(("dp", "expert"), None),
            P(("dp", "expert"), None),
            P(("dp", "expert"), None),
            P(("dp", "expert"), None),
            P(None, ("dp", "expert")),
            P("expert", None),
            P("expert", None, None),
            P("expert", None, None),
            P("expert"),
        ),
        check_vma=False,
    )
```

```python
import functools

import jax
import jax.numpy as jnp
from jax import lax
from jax.experimental import pallas as pl
from jax.experimental.pallas import tpu as pltpu
from jax.sharding import PartitionSpec as P

DH = 128
VEXP = 5


NORM_EPS = 1e-05
ROPE_BASE = 10000.0
MASK_FILL = -1e30
HIGHEST = lax.Precision.HIGHEST
ROUTER_ROWS = 64
DIGITS = 5
LANE = 128
GAIN_ROWS = 16
TILE = 256
VMEM_BYTES = 60 << 20
GELU_A = 0.7978845608028654
GELU_B = 0.044715


def layer_norm(values, gain_vec):
    center = values - jnp.mean(values, axis=-1, keepdims=True)
    spread = jnp.mean(center * center, axis=-1, keepdims=True)
    return center * lax.rsqrt(spread + NORM_EPS) * gain_vec


def rope_tables(position, width_dh):
    half_dh = width_dh // 2
    freq_row = jnp.power(ROPE_BASE, jnp.arange(half_dh, dtype=jnp.float32) * (-2.0 / width_dh))
    angle_tab = position.astype(jnp.float32)[:, None] * freq_row[None, :]
    return (jnp.cos(angle_tab), jnp.sin(angle_tab))


def rotate(values, cos_tab, sin_tab):
    half_dh = values.shape[-1] // 2
    first_half = values[..., :half_dh]
    second_half = values[..., half_dh:]
    cos_b = cos_tab[:, None, :]
    sin_b = sin_tab[:, None, :]
    return jnp.concatenate(
        [first_half * cos_b - second_half * sin_b, second_half * cos_b + first_half * sin_b],
        axis=-1,
    )


def rotate_back(grad_rot, cos_tab, sin_tab):
    half_dh = grad_rot.shape[-1] // 2
    grad_first = grad_rot[..., :half_dh]
    grad_second = grad_rot[..., half_dh:]
    cos_b = cos_tab[:, None, :]
    sin_b = sin_tab[:, None, :]
    return jnp.concatenate(
        [grad_first * cos_b + grad_second * sin_b, grad_second * cos_b - grad_first * sin_b],
        axis=-1,
    )


def doc_layout(seg_row, keep_row):
    length_s = seg_row.shape[0]
    column = jnp.arange(length_s, dtype=jnp.int32)
    new_doc = jnp.concatenate([jnp.ones((1,), dtype=jnp.bool_), seg_row[1:] != seg_row[:-1]])
    doc_start = lax.cummax(jnp.where(new_doc, column, jnp.zeros_like(column)), axis=0)
    position = column - doc_start
    same_doc = seg_row[:, None] == seg_row[None, :]
    causal = column[None, :] <= column[:, None]
    visible = (keep_row[None, :] == 1) | (column[None, :] == column[:, None])
    return (position, same_doc & causal & visible)


def slot_table(routes, exp_total, capacity):
    flat_ids = routes.reshape(-1)
    pair_count = flat_ids.shape[0]
    top_k = routes.shape[1]
    sort_order = jnp.argsort(flat_ids, stable=True)
    ranked = flat_ids[sort_order]
    first_slot = jnp.searchsorted(ranked, jnp.arange(exp_total, dtype=jnp.int32), side="left")
    slot_rank = jnp.arange(pair_count, dtype=jnp.int32) - first_slot[ranked]
    slot_dest = ranked * capacity + slot_rank
    owner = jnp.zeros((exp_total * capacity,), jnp.int32).at[slot_dest].set(sort_order // top_k)
    filled = jnp.zeros((exp_total * capacity,), jnp.float32).at[slot_dest].set(1.0)
    slot_of = (
        jnp.zeros((pair_count,), jnp.int32).at[sort_order].set(slot_dest).reshape(routes.shape)
    )
    return (owner, filled, slot_of)


def block_scores(q_blk, k_rows, allowed_blk):
    scores = jnp.einsum("qhd,khd->hqk", q_blk, k_rows, preferred_element_type=jnp.float32)
    return jnp.where(allowed_blk[None, :, :], scores, MASK_FILL)


def attend_forward(pieces):
    q_rows, k_rows, v_rows, allowed = pieces
    length_s = q_rows.shape[0]
    block_len = min(512, length_s)
    outs_list = []
    lse_list = []
    for begin_at in range(0, length_s, block_len):
        scores = block_scores(
            q_rows[begin_at : begin_at + block_len],
            k_rows,
            allowed[begin_at : begin_at + block_len],
        )
        row_max = jnp.max(scores, axis=-1, keepdims=True)
        exp_terms = jnp.exp(scores - row_max)
        row_sum = jnp.sum(exp_terms, axis=-1, keepdims=True)
        probs_bf = (exp_terms / row_sum).astype(jnp.bfloat16)
        outs_list.append(
            jnp.einsum("hqk,khd->qhd", probs_bf, v_rows, preferred_element_type=jnp.float32)
        )
        lse_list.append((row_max + jnp.log(row_sum))[..., 0])
    return (jnp.concatenate(outs_list, axis=0), jnp.concatenate(lse_list, axis=1))


def attend_backward(pieces):
    q_rows, k_rows, v_rows, allowed, log_total, grad_rows = pieces
    length_s = q_rows.shape[0]
    block_len = min(512, length_s)
    grad_q_list = []
    grad_k = jnp.zeros(k_rows.shape, jnp.float32)
    grad_v = jnp.zeros(v_rows.shape, jnp.float32)
    for begin_at in range(0, length_s, block_len):
        q_blk = q_rows[begin_at : begin_at + block_len]
        grad_blk = grad_rows[begin_at : begin_at + block_len]
        scores = block_scores(q_blk, k_rows, allowed[begin_at : begin_at + block_len])
        probs_f = jnp.exp(scores - log_total[:, begin_at : begin_at + block_len, None])
        grad_prob = jnp.einsum("qhd,khd->hqk", grad_blk, v_rows, preferred_element_type=jnp.float32)
        grad_score = (
            probs_f * (grad_prob - jnp.sum(probs_f * grad_prob, axis=-1, keepdims=True))
        ).astype(jnp.bfloat16)
        grad_v = grad_v + jnp.einsum(
            "hqk,qhd->khd",
            probs_f.astype(jnp.bfloat16),
            grad_blk,
            preferred_element_type=jnp.float32,
        )
        grad_q_list.append(
            jnp.einsum("hqk,khd->qhd", grad_score, k_rows, preferred_element_type=jnp.float32)
        )
        grad_k = grad_k + jnp.einsum(
            "hqk,qhd->khd", grad_score, q_blk, preferred_element_type=jnp.float32
        )
    return (jnp.concatenate(grad_q_list, axis=0), grad_k, grad_v)


def dot_nt(left, right):
    return lax.dot_general(left, right, (((1,), (1,)), ((), ())), preferred_element_type=jnp.float32)


def dot_nn(left, right):
    return lax.dot_general(left, right, (((1,), (0,)), ((), ())), preferred_element_type=jnp.float32)


def dot_tn(left, right):
    return lax.dot_general(left, right, (((0,), (0,)), ((), ())), preferred_element_type=jnp.float32)


def spin(values, cos_two, sin_two):
    return values * cos_two + pltpu.roll(values, DH // 2, 1) * sin_two


def spin_back(values, cos_two, sin_two):
    return values * cos_two - pltpu.roll(values, DH // 2, 1) * sin_two


def window_mask(step, tile, start_col, keep_before, keep_now):
    row = step * tile + lax.broadcasted_iota(jnp.int32, (tile, 2 * tile), 0)
    col = (step - 1) * tile + lax.broadcasted_iota(jnp.int32, (tile, 2 * tile), 1)
    keep_row = jnp.concatenate([keep_before, keep_now], axis=1)
    return (col >= start_col) & (col <= row) & ((keep_row == 1) | (col == row))


def neighbour(kind, amount):
    mine, place = lax.axis_index("dp"), lax.axis_index("expert")
    chips = lax.axis_size("expert") // 2
    chip, core = place // 2, lax.rem(place, 2)
    if kind == "dp":
        flipped = [mine, mine + 1 - 2 * lax.rem(mine, 2), lax.rem(mine + 2, 4), 3 - mine]
        return (flipped[amount], place)
    if kind == "core":
        return (mine, place + 1 - 2 * core)
    return (mine, 2 * lax.rem(chip + amount + chips, chips) + core)


def own_part(rows):
    return lambda mine, flipped: mine * rows


def fixed(start):
    return lambda mine, flipped: start


def shift_move(src, dst, hop, src_at, dst_at, count):
    return [(src, dst, "chip", hop, src_at, dst_at, count)]


def greet(peers):
    barrier = pltpu.get_barrier_semaphore()
    for peer in peers:
        pl.semaphore_signal(barrier, inc=1, device_id=peer, device_id_type=pl.DeviceIdType.MESH)
    pl.semaphore_wait(barrier, len(peers))


def peers_of(moves):
    peers = []
    for _, _, kind, amount, _, _, _ in moves:
        peers.append(neighbour(kind, amount))
        if kind == "chip":
            peers.append(neighbour(kind, -amount))
    return peers


def copies_of(moves, ins, outs, send_sem, recv_sem):
    mine = lax.axis_index("dp")
    copies = []
    for i, (src, dst, kind, amount, src_at, dst_at, count) in enumerate(moves):
        peer = neighbour(kind, amount)
        copies.append(
            pltpu.make_async_remote_copy(
                src_ref=ins[src].at[pl.ds(pl.multiple_of(src_at(mine, peer[0]), 16), count)],
                dst_ref=outs[dst].at[pl.ds(pl.multiple_of(dst_at(mine, peer[0]), 16), count)],
                send_sem=send_sem.at[i],
                recv_sem=recv_sem.at[i],
                device_id=peer,
                device_id_type=pl.DeviceIdType.MESH,
            )
        )
    return copies


ANYWHERE = pl.BlockSpec(memory_space=pl.ANY)


def tile_rows(index, tile):
    return pl.ds(pl.multiple_of(index * tile, tile), tile)


def flips():
    mine = lax.axis_index("dp")
    return [mine, mine + 1 - 2 * lax.rem(mine, 2), lax.rem(mine + 2, 4), 3 - mine]


def remote(src, dst, sems, index, peer):
    return pltpu.make_async_remote_copy(
        src_ref=src,
        dst_ref=dst,
        send_sem=sems.at[0, index],
        recv_sem=sems.at[1, index],
        device_id=peer,
        device_id_type=pl.DeviceIdType.MESH,
    )


def span(start, count):
    return pl.ds(pl.multiple_of(start, 16), count)


def halving_first(source, near, far, part, cut, sems, at):
    dp = flips()
    low = part - cut
    copies = []
    for slot, owner in enumerate((1, 3)):
        copies.append(
            remote(
                source.at[span(dp[owner] * part, cut)],
                near.at[pl.ds(slot * cut, cut)],
                sems,
                at + slot,
                neighbour("dp", 1),
            )
        )
    for slot, owner in enumerate((2, 3)):
        copies.append(
            remote(
                source.at[span(dp[owner] * part + cut, low)],
                far.at[pl.ds(slot * low, low)],
                sems,
                at + 2 + slot,
                neighbour("dp", 2),
            )
        )
    return copies


def halving_second(send, land, part, cut, sems, at):
    low = part - cut
    return [
        remote(send.at[pl.ds(0, cut)], land.at[pl.ds(0, cut)], sems, at, neighbour("dp", 2)),
        remote(send.at[pl.ds(cut, low)], land.at[pl.ds(cut, low)], sems, at + 1, neighbour("dp", 1)),
    ]


def as_f32(ref, start, count):
    return ref[pl.ds(start, count), :].astype(jnp.float32)


def spread_first(source, target, part, cut, sems, at):
    mine = lax.axis_index("dp")
    return [
        remote(
            source.at[pl.ds(0, cut)],
            target.at[span(mine * part, cut)],
            sems,
            at,
            neighbour("dp", 1),
        ),
        remote(
            source.at[pl.ds(cut, part - cut)],
            target.at[span(mine * part + cut, part - cut)],
            sems,
            at + 1,
            neighbour("dp", 2),
        ),
    ]


def spread_second(source, target, part, cut, sems, at):
    dp = flips()
    low = part - cut
    mine_up, mine_down = span(dp[0] * part, cut), span(dp[0] * part + cut, low)
    got_up, got_down = span(dp[1] * part, cut), span(dp[2] * part + cut, low)
    return [
        remote(source.at[pl.ds(0, cut)], target.at[mine_up], sems, at, neighbour("dp", 2)),
        remote(target.at[got_up], target.at[got_up], sems, at + 1, neighbour("dp", 2)),
        remote(source.at[pl.ds(cut, low)], target.at[mine_down], sems, at + 2, neighbour("dp", 1)),
        remote(target.at[got_down], target.at[got_down], sems, at + 3, neighbour("dp", 1)),
    ]


def load_own(source, own, part, cut, sems):
    dp = flips()
    low = part - cut
    return [
        pltpu.make_async_copy(
            source.at[span(dp[owner] * part + start, count)], own.at[pl.ds(at, count)], sems.at[i]
        )
        for i, (owner, start, count, at) in enumerate(
            [(0, 0, cut, 0), (2, 0, cut, cut), (0, cut, low, 2 * cut), (1, cut, low, 2 * cut + low)]
        )
    ]


class Halving:
    def __init__(self, source, total, buffers, part, cut):
        own, near, far, send, land, load_sems, sems = buffers
        self.source, self.total, self.part, self.cut = source, total, part, cut
        self.own, self.near, self.far, self.send, self.land = own, near, far, send, land
        self.loads = load_own(source, own, part, cut, load_sems)
        self.first = halving_first(source, near, far, part, cut, sems, 0)
        self.second = halving_second(send, land, part, cut, sems, 4)

    def start(self):
        for copy in self.first + self.loads:
            copy.start()

    def turn(self):
        part, cut = self.part, self.cut
        low = part - cut
        for copy in self.first + self.loads:
            copy.wait()
        up = as_f32(self.own, cut, cut) + as_f32(self.near, cut, cut)
        down = as_f32(self.own, 2 * cut + low, low) + as_f32(self.far, low, low)
        self.send[:cut, :] = up.astype(jnp.bfloat16)
        self.send[cut:, :] = down.astype(jnp.bfloat16)
        for copy in self.second:
            copy.start()

    def finish(self):
        part, cut = self.part, self.cut
        low = part - cut
        for copy in self.second:
            copy.wait()
        up = as_f32(self.own, 0, cut) + as_f32(self.near, 0, cut) + as_f32(self.land, 0, cut)
        down = as_f32(self.own, 2 * cut, low) + as_f32(self.far, 0, low) + as_f32(self.land, cut, low)
        self.total[:cut, :] = up.astype(jnp.bfloat16)
        self.total[cut:, :] = down.astype(jnp.bfloat16)


def halving_buffers(part, cut, model):
    bf16 = lambda rows: pltpu.VMEM((rows, model), jnp.bfloat16)
    return [
        bf16(2 * part),
        bf16(2 * cut),
        bf16(2 * (part - cut)),
        bf16(part),
        bf16(part),
        pltpu.SemaphoreType.DMA((4,)),
        pltpu.SemaphoreType.DMA((2, 6)),
    ]


class Spreading:
    def __init__(self, target, part, cut, sems):
        mine = target.at[span(lax.axis_index("dp") * part, part)]
        self.first = spread_first(mine, target, part, cut, sems, 0)
        self.second = spread_second(mine, target, part, cut, sems, 2)

    def start(self):
        for copy in self.first:
            copy.start()

    def turn(self):
        for copy in self.first:
            copy.wait()
        for copy in self.second:
            copy.start()

    def finish(self):
        for copy in self.second:
            copy.wait()


def forward_body(heads, tile, steps, ahead, *refs):
    (
        own_any,
        cot_any,
        x_ref,
        start_ref,
        keep_ref,
        cos_ref,
        sin_ref,
        mask_ref,
        gain_ref,
        wqk_ref,
        wsel_ref,
        wval_ref,
        wout_ref,
        chunk_any,
        near_any,
        cot_far_any,
        sent_far_any,
        hid_ref,
        norm_ref,
        q_ref,
        k_ref,
        v_ref,
        val_ref,
        att_ref,
        sig_ref,
        lse_ref,
        mix_ref,
        sent_all,
        send_sem,
        recv_sem,
        tile_send,
        tile_recv,
    ) = refs
    step = pl.program_id(0)
    rows = steps * tile
    quarter = own_any.shape[0] // 4
    moves = shift_move(0, 0, -3, own_part(quarter), own_part(quarter), quarter)
    moves = moves + shift_move(0, 1, -1, fixed(0), fixed(0), ahead)
    moves = moves + [(1, 2, "core", 1, fixed(0), fixed(0), rows)]
    partner = neighbour("core", 1)
    copies = copies_of(moves, [own_any, cot_any], [chunk_any, near_any, cot_far_any], send_sem, recv_sem)

    def tile_copy(index):
        return pltpu.make_async_remote_copy(
            src_ref=sent_all.at[pl.ds(index * tile, tile)],
            dst_ref=sent_far_any.at[pl.ds(index * tile, tile)],
            send_sem=tile_send.at[index],
            recv_sem=tile_recv.at[index],
            device_id=partner,
            device_id_type=pl.DeviceIdType.MESH,
        )


    @pl.when(step == 0)
    def _():
        greet(peers_of(moves))
        for copy in copies:
            copy.start()

    now = tile_rows(step, tile)
    before = tile_rows(jnp.maximum(step - 1, 0), tile)
    x = x_ref[...]
    x_f = x.astype(jnp.float32)
    center = x_f - jnp.mean(x_f, axis=1, keepdims=True)
    spread = jnp.mean(center * center, axis=1, keepdims=True)
    normed = (center * lax.rsqrt(spread + NORM_EPS) * gain_ref[...]).astype(jnp.bfloat16)
    norm_ref[...] = normed
    sig = 1.0 / (1.0 + jnp.exp(-dot_nn(x, wsel_ref[...])))
    sig_ref[...] = sig
    gates = sig * mask_ref[...].astype(jnp.float32)
    cos_two, sin_two = cos_ref[...], sin_ref[...]
    allowed = window_mask(step, tile, start_ref[...], keep_ref[:, before], keep_ref[:, now])
    scale = DH ** (-0.5)
    lanes = lax.broadcasted_iota(jnp.int32, (tile, LANE), 1)
    lse = jnp.zeros((tile, LANE), jnp.float32)
    for head in range(heads):
        cols = slice(head * DH, (head + 1) * DH)
        value = dot_nn(x, wval_ref[:, head * VEXP * DH : (head + 1) * VEXP * DH])
        val_ref[:, head * VEXP * DH : (head + 1) * VEXP * DH] = value.astype(jnp.bfloat16)
        total = jnp.zeros((tile, DH), jnp.float32)
        for e in range(VEXP):
            at = head * VEXP + e
            total = total + gates[:, at : at + 1] * value[:, e * DH : (e + 1) * DH]
        v_ref[now, cols] = total.astype(jnp.bfloat16)
    qk = dot_nn(normed, wqk_ref[...])
    for head in range(heads):
        cols = slice(head * DH, (head + 1) * DH)
        q_head = (spin(qk[:, cols], cos_two, sin_two) * scale).astype(jnp.bfloat16)
        k_head = spin(
            qk[:, (heads + head) * DH : (heads + head + 1) * DH], cos_two, sin_two
        ).astype(jnp.bfloat16)
        q_ref[:, cols] = q_head
        k_ref[now, cols] = k_head
        scores = jnp.concatenate(
            [dot_nt(q_head, k_ref[before, cols]), dot_nt(q_head, k_head)], axis=1
        )
        scores = jnp.where(allowed, scores, MASK_FILL)
        row_max = jnp.max(scores, axis=1, keepdims=True)
        terms = jnp.exp(scores - row_max)
        row_sum = jnp.sum(terms, axis=1, keepdims=True)
        probs = (terms * (1.0 / row_sum)).astype(jnp.bfloat16)
        attended = dot_nn(probs[:, :tile], v_ref[before, cols]) + dot_nn(
            probs[:, tile:], v_ref[now, cols]
        )
        att_ref[:, cols] = attended
        lse = jnp.where(lanes == head, row_max + jnp.log(row_sum), lse)
        for e in range(VEXP):
            at = head * VEXP + e
            gate = gates[:, heads * VEXP + at : heads * VEXP + at + 1]
            mix_ref[:, at * DH : (at + 1) * DH] = (gate * attended).astype(jnp.bfloat16)
    lse_ref[...] = lse
    hidden = x_f + dot_nn(mix_ref[...], wout_ref[...])
    hid_ref[...] = hidden
    sent_all[now, :] = hidden.astype(jnp.bfloat16)
    for index in range(steps):

        @pl.when(step == index)
        def _(index=index):
            tile_copy(index).start()

    @pl.when(step == steps - 1)
    def _():
        for copy in copies:
            copy.wait()
        for index in range(steps):
            tile_copy(index).wait()


def whole_block(shape):
    return pl.BlockSpec(shape, lambda step: (0,) * len(shape), pipeline_mode=pl.Buffered(1))


def attention_forward(ahead, own, cot, x, start, keep, cos_two, sin_two, mask, gain, wqk, wsel, wval, wout, tile):
    rows, model = x.shape
    heads = wqk.shape[1] // (2 * DH)
    per_tile = lambda width: pl.BlockSpec((tile, width), lambda step: (step, 0))
    full = lambda arr: whole_block(arr.shape)
    narrow, wide = heads * DH, heads * VEXP * DH
    shapes = [
        (model, jnp.float32, False),
        (model, jnp.bfloat16, False),
        (narrow, jnp.bfloat16, False),
        (narrow, jnp.bfloat16, True),
        (narrow, jnp.bfloat16, True),
        (wide, jnp.bfloat16, False),
        (narrow, jnp.float32, False),
        (LANE, jnp.float32, False),
        (LANE, jnp.float32, False),
        (wide, jnp.bfloat16, False),
        (model, jnp.bfloat16, True),
    ]
    return pl.pallas_call(
        functools.partial(forward_body, heads, tile, rows // tile, ahead),
        grid=(rows // tile,),
        in_specs=[
            ANYWHERE,
            ANYWHERE,
            per_tile(model),
            per_tile(1),
            full(keep),
            per_tile(LANE),
            per_tile(LANE),
            per_tile(LANE),
            full(gain),
            full(wqk),
            full(wsel),
            full(wval),
            full(wout),
        ],
        out_specs=[ANYWHERE] * 4
        + [whole_block((rows, width)) if whole else per_tile(width) for width, _, whole in shapes],
        out_shape=[
            jax.ShapeDtypeStruct(own.shape, jnp.bfloat16),
            jax.ShapeDtypeStruct(own.shape, jnp.bfloat16),
            jax.ShapeDtypeStruct((rows, model), jnp.bfloat16),
            jax.ShapeDtypeStruct((rows, model), jnp.bfloat16),
        ]
        + [jax.ShapeDtypeStruct((rows, width), kind) for width, kind, _ in shapes],
        scratch_shapes=[
            pltpu.SemaphoreType.DMA((3,)),
            pltpu.SemaphoreType.DMA((3,)),
            pltpu.SemaphoreType.DMA((rows // tile,)),
            pltpu.SemaphoreType.DMA((rows // tile,)),
        ],
        compiler_params=pltpu.CompilerParams(
            vmem_limit_bytes=VMEM_BYTES, collective_id=1, has_side_effects=True
        ),
        cost_estimate=pl.CostEstimate(
            flops=2 * rows * model * (2 * narrow + 2 * wide), bytes_accessed=40 << 20, transcendentals=0
        ),
    )(own, cot, x, start, keep, cos_two, sin_two, mask, gain, wqk, wsel, wval, wout)


def backward_body(heads, tile, steps, moves, halve, part, n_in, n_out, *refs):
    ins, refs = refs[:n_in], refs[n_in:]
    (
        dy_ref,
        q_ref,
        k_ref,
        v_ref,
        att_ref,
        lse_ref,
        start_ref,
        keep_ref,
        sig_now_ref,
        mask_now_ref,
        cos_now_ref,
        sin_now_ref,
        sig_old_ref,
        mask_old_ref,
        cos_old_ref,
        sin_old_ref,
        x_ref,
        val_ref,
        dhid_ref,
        gain_ref,
        wqk_ref,
        wsel_ref,
        wval_ref,
        wout_ref,
        *outs_and_rest,
    ) = refs
    outs, rest = outs_and_rest[:n_out], outs_and_rest[n_out:]
    (
        gin_ref,
        dqk_ref,
        dval_ref,
        dlog_ref,
        ggain_ref,
        *totals_and_rest,
    ) = rest
    totals, rest = totals_and_rest[: len(halve)], totals_and_rest[len(halve) :]
    (
        dk_acc,
        dv_acc,
        dq_keep,
        dgate_keep,
        gain_acc,
        send_sem,
        recv_sem,
        *buffers,
    ) = rest
    step = pl.program_id(0)
    copies = copies_of(moves, ins, outs, send_sem, recv_sem)
    riders = [
        Halving(ins[source], totals[i], buffers[7 * i : 7 * i + 7], part, part // 32 * 16)
        for i, source in enumerate(halve)
    ]

    @pl.when(step == 0)
    def _():
        greet(peers_of(moves) + [neighbour("dp", 1), neighbour("dp", 2)])
        for copy in copies:
            copy.start()
        for rider in riders:
            rider.start()

    @pl.when(step == steps - 1)
    def _():
        riders[0].turn()

    slot = lax.rem(step, 2)
    old = 1 - slot
    lanes = lax.broadcasted_iota(jnp.int32, (tile, LANE), 1)
    scale = DH ** (-0.5)
    narrow = heads * DH

    @pl.when(step == 0)
    def _():
        gain_acc[...] = jnp.zeros_like(gain_acc)
        dk_acc[...] = jnp.zeros_like(dk_acc)
        dv_acc[...] = jnp.zeros_like(dv_acc)

    @pl.when(step < steps)
    def _():
        now = tile_rows(jnp.minimum(step, steps - 1), tile)
        before = tile_rows(jnp.maximum(step - 1, 0), tile)
        allowed = window_mask(step, tile, start_ref[...], keep_ref[:, before], keep_ref[:, now])
        gates = sig_now_ref[...] * mask_now_ref[...].astype(jnp.float32)
        dy = dy_ref[...]
        dgate = jnp.zeros((tile, LANE), jnp.float32)
        for head in range(heads):
            cols = slice(head * DH, (head + 1) * DH)
            dmixed = dot_nt(dy, wout_ref[head * VEXP * DH : (head + 1) * VEXP * DH, :])
            attended = att_ref[:, cols]
            dattend = jnp.zeros((tile, DH), jnp.float32)
            for e in range(VEXP):
                at = (heads + head) * VEXP + e
                part = dmixed[:, e * DH : (e + 1) * DH]
                dattend = dattend + gates[:, at : at + 1] * part
                dgate = jnp.where(
                    lanes == at, jnp.sum(part * attended, axis=1, keepdims=True), dgate
                )
            dattend = dattend.astype(jnp.bfloat16)
            q_head = q_ref[:, cols]
            k_old, k_now = k_ref[before, cols], k_ref[now, cols]
            v_old, v_now = v_ref[before, cols], v_ref[now, cols]
            scores = jnp.concatenate([dot_nt(q_head, k_old), dot_nt(q_head, k_now)], axis=1)
            scores = jnp.where(allowed, scores, MASK_FILL)
            probs = jnp.exp(scores - lse_ref[:, head : head + 1])
            dprob = jnp.concatenate([dot_nt(dattend, v_old), dot_nt(dattend, v_now)], axis=1)
            delta = jnp.sum(probs * dprob, axis=1, keepdims=True)
            dscore = (probs * (dprob - delta)).astype(jnp.bfloat16)
            probs = probs.astype(jnp.bfloat16)
            dv_acc[old, :, cols] += dot_tn(probs[:, :tile], dattend)
            dv_acc[slot, :, cols] = dot_tn(probs[:, tile:], dattend)
            dk_acc[old, :, cols] += dot_tn(dscore[:, :tile], q_head)
            dk_acc[slot, :, cols] = dot_tn(dscore[:, tile:], q_head)
            dq = dot_nn(dscore[:, :tile], k_old) + dot_nn(dscore[:, tile:], k_now)
            dq_keep[slot, :, cols] = (
                spin_back(dq, cos_now_ref[...], sin_now_ref[...]) * scale
            ).astype(jnp.bfloat16)
        dgate_keep[slot] = dgate

    @pl.when(step > 0)
    def _():
        sig = sig_old_ref[...]
        mask = mask_old_ref[...].astype(jnp.float32)
        gates = sig * mask
        dgate = dgate_keep[old]
        for head in range(heads):
            cols = slice(head * DH, (head + 1) * DH)
            dqk_ref[:, cols] = dq_keep[old, :, cols]
            dqk_ref[:, narrow + head * DH : narrow + (head + 1) * DH] = spin_back(
                dk_acc[old, :, cols], cos_old_ref[...], sin_old_ref[...]
            ).astype(jnp.bfloat16)
            dvalue = dv_acc[old, :, cols]
            for e in range(VEXP):
                at = head * VEXP + e
                wide = slice(at * DH, (at + 1) * DH)
                val = val_ref[:, wide].astype(jnp.float32)
                dgate = jnp.where(lanes == at, jnp.sum(dvalue * val, axis=1, keepdims=True), dgate)
                dval_ref[:, wide] = (gates[:, at : at + 1] * dvalue).astype(jnp.bfloat16)
        dlog = (dgate * gates * (1.0 - sig)).astype(jnp.bfloat16)
        dlog_ref[...] = dlog
        dnormed = dot_nt(dqk_ref[...], wqk_ref[...])
        x_f = x_ref[...].astype(jnp.float32)
        center = x_f - jnp.mean(x_f, axis=1, keepdims=True)
        inv = lax.rsqrt(jnp.mean(center * center, axis=1, keepdims=True) + NORM_EPS)
        x_hat = center * inv
        gain_acc[...] += jnp.sum(dnormed * x_hat, axis=0, keepdims=True)
        grad = dnormed * gain_ref[...]
        dx = inv * (
            grad
            - jnp.mean(grad, axis=1, keepdims=True)
            - x_hat * jnp.mean(grad * x_hat, axis=1, keepdims=True)
        )
        dx = dx + dhid_ref[...] + dot_nt(dval_ref[...], wval_ref[...]) + dot_nt(dlog, wsel_ref[...])
        gin_ref[...] = dx.astype(jnp.bfloat16)

    @pl.when(step == steps)
    def _():
        gain = gain_acc[...]
        high = gain.astype(jnp.bfloat16).astype(jnp.float32)
        row = lax.broadcasted_iota(jnp.int32, (GAIN_ROWS, gain.shape[1]), 0)
        split = jnp.where(row == 0, high, jnp.where(row == 1, gain - high, 0.0))
        ggain_ref[...] = split.astype(jnp.bfloat16)
        for rider in riders[1:]:
            rider.turn()
        for rider in riders:
            rider.finish()
        for copy in copies:
            copy.wait()


def attention_backward(
    sources, results, moves, halve, part, dy, q, k, v, att, lse, start, keep, sig, mask, cos_two, sin_two, x, val, dhid, gain, wqk, wsel, wval, wout, tile
):
    rows, model = x.shape
    heads = wqk.shape[1] // (2 * DH)
    steps = rows // tile
    narrow, wide = heads * DH, heads * VEXP * DH
    at_now = lambda width: pl.BlockSpec((tile, width), lambda step: (jnp.minimum(step, steps - 1), 0))
    at_old = lambda width: pl.BlockSpec((tile, width), lambda step: (jnp.maximum(step - 1, 0), 0))
    full = lambda arr: whole_block(arr.shape)
    return pl.pallas_call(
        functools.partial(
            backward_body, heads, tile, steps, moves, halve, part, len(sources), len(results)
        ),
        grid=(steps + 1,),
        in_specs=[ANYWHERE] * len(sources)
        + [
            at_now(model),
            at_now(narrow),
            full(k),
            full(v),
            at_now(narrow),
            at_now(LANE),
            at_now(1),
            full(keep),
            at_now(LANE),
            at_now(LANE),
            at_now(LANE),
            at_now(LANE),
            at_old(LANE),
            at_old(LANE),
            at_old(LANE),
            at_old(LANE),
            at_old(model),
            at_old(wide),
            at_old(model),
            full(gain),
            full(wqk),
            full(wsel),
            full(wval),
            full(wout),
        ],
        out_specs=[ANYWHERE] * len(results)
        + [
            at_old(model),
            at_old(2 * narrow),
            at_old(wide),
            at_old(LANE),
            whole_block((GAIN_ROWS, model)),
        ]
        + [whole_block((part, model))] * len(halve),
        out_shape=[jax.ShapeDtypeStruct(shape, jnp.bfloat16) for shape in results]
        + [
            jax.ShapeDtypeStruct((rows, model), jnp.bfloat16),
            jax.ShapeDtypeStruct((rows, 2 * narrow), jnp.bfloat16),
            jax.ShapeDtypeStruct((rows, wide), jnp.bfloat16),
            jax.ShapeDtypeStruct((rows, LANE), jnp.bfloat16),
            jax.ShapeDtypeStruct((GAIN_ROWS, model), jnp.bfloat16),
        ]
        + [jax.ShapeDtypeStruct((part, model), jnp.bfloat16)] * len(halve),
        scratch_shapes=[
            pltpu.VMEM((2, tile, narrow), jnp.float32),
            pltpu.VMEM((2, tile, narrow), jnp.float32),
            pltpu.VMEM((2, tile, narrow), jnp.bfloat16),
            pltpu.VMEM((2, tile, LANE), jnp.float32),
            pltpu.VMEM((1, model), jnp.float32),
            pltpu.SemaphoreType.DMA((len(moves),)),
            pltpu.SemaphoreType.DMA((len(moves),)),
        ]
        + halving_buffers(part, part // 32 * 16, model) * len(halve),
        compiler_params=pltpu.CompilerParams(
            vmem_limit_bytes=VMEM_BYTES, collective_id=6, has_side_effects=True
        ),
        cost_estimate=pl.CostEstimate(
            flops=2 * rows * model * (2 * narrow + 2 * wide), bytes_accessed=50 << 20, transcendentals=0
        ),
    )(
        *sources, dy, q, k, v, att, lse, start, keep, sig, mask, cos_two, sin_two, sig, mask, cos_two, sin_two,
        x, val, dhid, gain, wqk, wsel, wval, wout,
    )


def tail_body(blocks, chips, part, cut, *refs):
    (
        part_1,
        part_0,
        got_2,
        got_3,
        dy_ref,
        x_ref,
        norm_ref,
        gain_ref,
        mix_ref,
        dval_ref,
        dlog_ref,
        dqk_ref,
        unit_ref,
        dense_ref,
        whole_any,
        came,
        quarter,
        product,
        pair,
        near,
        far,
        send,
        land,
        sums,
        last,
        link,
        core_sems,
        xy_sems,
        z_sems,
        local_sem,
    ) = refs
    place = lax.axis_index("expert")
    chip, core = place // 2, lax.rem(place, 2)
    model = x_ref.shape[1]
    piece = model // 4 // chips // 2
    quart = chips * piece
    halfway = quart // 2
    rights = {"out": mix_ref, "val": dval_ref, "log": dlog_ref, "qk": dqk_ref}
    lefts = {"out": dy_ref, "val": x_ref, "log": x_ref, "qk": norm_ref}

    peers = [neighbour("core", 1)] + [neighbour("dp", flip) for flip in (1, 2)]
    for hop in range(1, chips):
        peers.append(neighbour("chip", hop))
    greet(peers)
    first = remote(part_1, came, link, 0, neighbour("chip", 1))
    first.start()

    def width_of(b):
        return sum(hi - lo for _, lo, hi in blocks[b])

    def core_copy(b):
        width = width_of(b)
        return remote(
            product.at[b % 2, :, span((1 - core) * piece, piece), pl.ds(0, width)],
            pair.at[b, :, :, pl.ds(0, width)],
            core_sems,
            b,
            neighbour("core", 1),
        )

    def compute(b):
        if b >= 2:
            core_copy(b - 2).wait_send()
        at = 0
        for name, lo, hi in blocks[b]:
            total = dot_tn(lefts[name][...], rights[name][:, lo:hi])
            if name == "log":
                total = total + dot_tn(gain_ref[...], unit_ref[...])
            product[b % 2, :, :, at : at + hi - lo] = total.astype(jnp.bfloat16).reshape(
                4 * chips, 2 * piece, hi - lo
            )
            at += hi - lo
        core_copy(b).start()

    def pair_rows(b):
        return pair.at[b].reshape(4 * quart, pair.shape[3])

    def first_copies(b):
        return halving_first(pair_rows(b), near.at[b], far.at[b], quart, halfway, xy_sems.at[b], 0)

    def second_copies(b):
        return halving_second(send.at[b], land.at[b], quart, halfway, xy_sems.at[b], 4)

    def chip_copies(b):
        copies = []
        for hop in range(1, chips):
            target = lax.rem(chip + hop, chips)
            copies.append(
                remote(
                    sums.at[b, span(target * piece, piece)],
                    last.at[b, hop - 1],
                    z_sems.at[b],
                    hop - 1,
                    neighbour("chip", hop),
                )
            )
        return copies

    def stage_1(b):
        core_copy(b).wait_recv()
        kept = product[b % 2, :, span(core * piece, piece), :].astype(jnp.float32)
        pair[b] = (kept + pair[b].astype(jnp.float32)).astype(jnp.bfloat16)
        for copy in first_copies(b):
            copy.start()

    def own_rows(b, owner, start):
        return as_f32(pair_rows(b), pl.multiple_of(flips()[owner] * quart + start, 16), halfway)

    def stage_2(b):
        for copy in first_copies(b):
            copy.wait()
        send[b, :halfway, :] = (own_rows(b, 2, 0) + as_f32(near.at[b], halfway, halfway)).astype(
            jnp.bfloat16
        )
        send[b, halfway:, :] = (own_rows(b, 1, halfway) + as_f32(far.at[b], halfway, halfway)).astype(
            jnp.bfloat16
        )
        for copy in second_copies(b):
            copy.start()

    def stage_3(b):
        for copy in second_copies(b):
            copy.wait()
        up = own_rows(b, 0, 0) + as_f32(near.at[b], 0, halfway) + as_f32(land.at[b], 0, halfway)
        down = own_rows(b, 0, halfway) + as_f32(far.at[b], 0, halfway)
        down = down + as_f32(land.at[b], halfway, halfway)
        sums[b, :halfway, :] = up.astype(jnp.bfloat16)
        sums[b, halfway:, :] = down.astype(jnp.bfloat16)
        for copy in chip_copies(b):
            copy.start()

    def stage_4(b):
        for copy in chip_copies(b):
            copy.wait()
        total = sums[b, span(chip * piece, piece), :].astype(jnp.float32)
        for hop in range(chips - 1):
            total = total + last[b, hop].astype(jnp.float32)
        start = sum(width_of(i) for i in range(b))
        dense_ref[:, start : start + width_of(b)] = total[:, : width_of(b)]

    def spread_1():
        return spread_first(quarter, whole_any, part, cut, link, 1)

    def spread_2():
        return spread_second(quarter, whole_any, part, cut, link, 3)

    mine = lax.axis_index("dp")
    keep = pltpu.make_async_copy(quarter, whole_any.at[span(mine * part, part)], local_sem)
    count = len(blocks)
    compute(0)
    compute(1)
    for b in range(count):
        stage_1(b)
        if b + 2 < count:
            compute(b + 2)
    first.wait()
    quarter[...] = sum(
        ref[...].astype(jnp.float32) for ref in (part_0, got_2, got_3, came)
    ).astype(jnp.bfloat16)
    keep.start()
    for copy in spread_1():
        copy.start()
    for b in range(count):
        stage_2(b)
    for copy in spread_1():
        copy.wait()
    for copy in spread_2():
        copy.start()
    for b in range(count):
        stage_3(b)
    for b in range(count):
        stage_4(b)
    for copy in spread_2():
        copy.wait()
    keep.wait()
    for b in range(max(0, count - 2), count):
        core_copy(b).wait_send()


def tail(part_1, part_0, got_2, got_3, dy, x, normed, gain_rows, mixed, dval, dlog, dqk, unit, shape, chips):
    rows, model = x.shape
    part = shape[0] // 4
    cut = part // 32 * 16
    wide, narrow = mixed.shape[1], dqk.shape[1]
    half = wide // 2
    blocks = [
        [("out", 0, half)],
        [("out", half, wide)],
        [("val", 0, half)],
        [("val", half, wide)],
        [("log", 0, LANE), ("qk", 0, narrow)],
    ]
    width = max(half, LANE + narrow)
    total = 2 * wide + LANE + narrow
    count = len(blocks)
    piece = model // 4 // chips // 2
    quart = chips * piece
    bf16 = lambda *shape: pltpu.VMEM(shape, jnp.bfloat16)
    dma = lambda *shape: pltpu.SemaphoreType.DMA(shape)
    vmem = pl.BlockSpec(memory_space=pltpu.VMEM)
    return pl.pallas_call(
        functools.partial(tail_body, blocks, chips, part, cut),
        in_specs=[vmem] * 13,
        out_specs=[vmem, ANYWHERE],
        out_shape=[
            jax.ShapeDtypeStruct((piece, total), jnp.float32),
            jax.ShapeDtypeStruct(shape, jnp.bfloat16),
        ],
        scratch_shapes=[
            bf16(part, model),
            bf16(part, model),
            bf16(2, 4 * chips, 2 * piece, width),
            bf16(count, 4 * chips, piece, width),
            bf16(count, quart, width),
            bf16(count, quart, width),
            bf16(count, quart, width),
            bf16(count, quart, width),
            bf16(count, quart, width),
            bf16(count, chips - 1, piece, width),
            dma(2, 7),
            dma(2, count),
            dma(count, 2, 6),
            dma(count, 2, chips - 1),
            dma(),
        ],
        compiler_params=pltpu.CompilerParams(
            vmem_limit_bytes=VMEM_BYTES, collective_id=7, has_side_effects=True
        ),
        cost_estimate=pl.CostEstimate(
            flops=2 * rows * model * total, bytes_accessed=20 << 20, transcendentals=0
        ),
    )(part_1, part_0, got_2, got_3, dy, x, normed, gain_rows, mixed, dval, dlog, dqk, unit)


def expert_body(first, last, exp_local, ff_dim, tile, steps, moves, spread, halve, n_in, n_out, *refs):
    ins, refs = refs[:n_in], refs[n_in:]
    x_own, x_far, c_own, c_far, w_ref, mask_ref, digit_ref = refs[:7]
    at = 7
    if not first:
        out_in, grad_in = refs[at : at + 2]
        at += 2
    if last:
        hid_ref = refs[at]
        at += 1
    outs = refs[at : at + n_out]
    at += n_out
    results = refs[at : at + 3]
    at += 3 if last else 2
    if halve is not None:
        total = refs[at]
        at += 1
    g_ref = refs[at]
    at += 1
    act_all, dpre_all, x_ref, c_ref, load_sem, send_sem, recv_sem = refs[at : at + 7]
    wide = exp_local * ff_dim
    back = wide + ROUTER_ROWS
    half = steps // 2
    step = pl.program_id(0)
    copies = copies_of(moves, ins, outs, send_sem, recv_sem)
    peers = peers_of(moves)
    at += 7
    part = w_ref.shape[0] // 4
    cut = part // 32 * 16
    riders = []
    if spread is not None:
        riders.append((Spreading(outs[spread], part, cut, refs[at]), steps // 2 - 1))
        at += 1
    if halve is not None:
        riders.append((Halving(ins[halve], total, refs[at : at + 7], part, cut), steps - 2))
        at += 7
    if riders:
        peers += [neighbour("dp", 1), neighbour("dp", 2)]
    if last:
        given, taken, tile_send, tile_recv = refs[at:]
        partner = neighbour("core", 1)
        peers.append(partner)

        def tile_copy(index, kind):
            return pltpu.make_async_remote_copy(
                src_ref=given.at[kind, pl.ds(index * tile, tile)],
                dst_ref=taken.at[kind, pl.ds(index * tile, tile)],
                send_sem=tile_send.at[kind, index],
                recv_sem=tile_recv.at[kind, index],
                device_id=partner,
                device_id_type=pl.DeviceIdType.MESH,
            )

    def load(index, kind):
        near, far, whole = ((x_own, x_far, x_ref), (c_own, c_far, c_ref))[kind]
        source = near if index < half else far
        return pltpu.make_async_copy(
            source.at[pl.ds(index % half * tile, tile)],
            whole.at[pl.ds(index * tile, tile)],
            load_sem.at[kind, index],
        )

    @pl.when(step == 0)
    def _():
        for turn in range(steps):
            for kind in range(2):
                load((turn + half) % steps if last else turn, kind).start()
        greet(peers)
        for copy in copies:
            copy.start()
        for rider, _ in riders:
            rider.start()

    for turn in range(steps):

        @pl.when(step == turn)
        def _(turn=turn):
            for rider, at_step in riders:
                if at_step == turn:
                    rider.turn()
            for kind in range(2):
                load((turn + half) % steps if last else turn, kind).wait()

    rows = tile_rows(lax.rem(step + half, steps) if last else step, tile)
    x, c = x_ref[rows, :], c_ref[rows, :]
    sig = 1.0 / (1.0 + jnp.exp(-dot_nt(x, w_ref[wide:back, :])))
    gate = sig * mask_ref[:, :ROUTER_ROWS].astype(jnp.float32)
    lanes = lax.broadcasted_iota(jnp.int32, (tile, ROUTER_ROWS), 1)
    dgate = jnp.zeros((tile, ROUTER_ROWS), jnp.float32)
    for pair in range(exp_local // 2):
        lo, hi = 2 * pair * ff_dim, 2 * (pair + 1) * ff_dim
        pre_two = dot_nt(x, w_ref[lo:hi, :])
        raw_two = dot_nt(c, w_ref[back + lo : back + hi, :])
        for side in range(2):
            e = 2 * pair + side
            pre = pre_two[:, side * ff_dim : (side + 1) * ff_dim]
            raw = raw_two[:, side * ff_dim : (side + 1) * ff_dim]
            square = pre * pre
            bend = jnp.tanh(pre * (GELU_A + GELU_A * GELU_B * square))
            upper = 0.5 * bend + 0.5
            act = (pre * upper).astype(jnp.bfloat16).astype(jnp.float32)
            slope = upper + (0.5 * pre) * (1.0 - bend * bend) * (GELU_A + 3 * GELU_A * GELU_B * square)
            gate_col = gate[:, e : e + 1]
            act_all[rows, e * ff_dim : (e + 1) * ff_dim] = (gate_col * act).astype(jnp.bfloat16)
            dpre_all[rows, e * ff_dim : (e + 1) * ff_dim] = (gate_col * raw * slope).astype(
                jnp.bfloat16
            )
            dgate = jnp.where(lanes == e, jnp.sum(act * raw, axis=1, keepdims=True), dgate)
    dpre_all[rows, wide:back] = (dgate * gate * (1.0 - sig)).astype(jnp.bfloat16)
    out_new = dot_nn(act_all[rows, :], w_ref[back:, :])
    grad_new = dot_nn(dpre_all[rows, :], w_ref[:back, :])
    if not first:
        out_new = out_new + out_in[...]
        grad_new = grad_new + grad_in[...]
    if last:

        @pl.when(step < half)
        def _():
            mine = tile_rows(jnp.minimum(step, half - 1), tile)
            given[0, mine, :] = out_new.astype(jnp.bfloat16)
            given[1, mine, :] = grad_new.astype(jnp.bfloat16)

        for index in range(half):

            @pl.when(step == index)
            def _(index=index):
                tile_copy(index, 0).start()
                tile_copy(index, 1).start()

            @pl.when(step == index + half)
            def _(index=index):
                tile_copy(index, 0).wait_recv()
                tile_copy(index, 1).wait_recv()

        @pl.when(step >= half)
        def _():
            mine = tile_rows(jnp.maximum(step - half, 0), tile)
            total = hid_ref[...] + out_new + taken[0, mine, :].astype(jnp.float32)
            results[0][...] = total.astype(jnp.bfloat16)
            dhidden = c.astype(jnp.float32) + grad_new + taken[1, mine, :].astype(jnp.float32)
            results[1][...] = dhidden
            results[2][...] = dhidden.astype(jnp.bfloat16)

    else:
        results[0][...] = out_new
        results[1][...] = grad_new

    @pl.when(step == steps - 1)
    def _():
        for lo in range(0, wide, 2 * ff_dim):
            g_ref[lo : lo + 2 * ff_dim, :] = dot_tn(
                dpre_all[:, lo : lo + 2 * ff_dim], x_ref[...]
            ).astype(jnp.bfloat16)
            g_ref[back + lo : back + lo + 2 * ff_dim, :] = dot_tn(
                act_all[:, lo : lo + 2 * ff_dim], c_ref[...]
            ).astype(jnp.bfloat16)
        extra = dot_tn(dpre_all[:, wide:back], x_ref[...])
        g_ref[wide:back, :LANE] = (extra[:, :LANE] + digit_ref[...]).astype(jnp.bfloat16)
        g_ref[wide:back, LANE:] = extra[:, LANE:].astype(jnp.bfloat16)
        for rider, _ in riders:
            rider.finish()
        for copy in copies:
            copy.wait()
        if last:
            for index in range(half):
                tile_copy(index, 0).wait_send()
                tile_copy(index, 1).wait_send()


def expert_chunk(
    sources, results, aliases, moves, spread, halve, tokens, weights, masks, digits, hop, sums, hidden, exp_local, ff_dim, tile
):
    rows, model = 2 * tokens[0].shape[0], tokens[0].shape[1]
    steps = rows // tile
    half = steps // 2
    first, last = sums is None, hidden is not None
    turn = (lambda step: lax.rem(step + half, steps)) if last else (lambda step: step)
    per_tile = lambda: pl.BlockSpec((tile, model), lambda step: (turn(step), 0))
    late = lambda: pl.BlockSpec((tile, model), lambda step: (jnp.maximum(step - half, 0), 0))
    in_specs = [ANYWHERE] * (len(sources) + 4) + [
        whole_block(weights.shape),
        pl.BlockSpec((tile, LANE), lambda step: (turn(step), hop)),
        pl.BlockSpec((ROUTER_ROWS, LANE), lambda step: (0, hop)),
    ]
    args = list(sources) + list(tokens) + [weights, masks, digits]
    if not first:
        in_specs += [per_tile(), per_tile()]
        args += list(sums)
    wide = exp_local * ff_dim
    part = weights.shape[0] // 4
    cut = part // 32 * 16
    scratch = [
        pltpu.VMEM((rows, wide), jnp.bfloat16),
        pltpu.VMEM((rows, wide + ROUTER_ROWS), jnp.bfloat16),
        pltpu.VMEM((rows, model), jnp.bfloat16),
        pltpu.VMEM((rows, model), jnp.bfloat16),
        pltpu.SemaphoreType.DMA((2, steps)),
        pltpu.SemaphoreType.DMA((max(1, len(moves)),)),
        pltpu.SemaphoreType.DMA((max(1, len(moves)),)),
    ]
    if spread is not None:
        scratch.append(pltpu.SemaphoreType.DMA((2, 6)))
    if halve is not None:
        scratch += halving_buffers(part, cut, model)
    if last:
        in_specs.append(late())
        args.append(hidden)
        out_specs = [late(), late(), late()]
        out_shape = [
            jax.ShapeDtypeStruct((rows // 2, model), kind)
            for kind in (jnp.bfloat16, jnp.float32, jnp.bfloat16)
        ]
        scratch += [
            pltpu.VMEM((2, rows // 2, model), jnp.bfloat16),
            pltpu.VMEM((2, rows // 2, model), jnp.bfloat16),
            pltpu.SemaphoreType.DMA((2, half)),
            pltpu.SemaphoreType.DMA((2, half)),
        ]
    else:
        out_specs = [per_tile(), per_tile()]
        out_shape = [jax.ShapeDtypeStruct((rows, model), jnp.float32)] * 2
    if halve is not None:
        out_specs.append(whole_block((part, model)))
        out_shape.append(jax.ShapeDtypeStruct((part, model), jnp.bfloat16))
    outs = pl.pallas_call(
        functools.partial(
            expert_body, first, last, exp_local, ff_dim, tile, steps, moves, spread, halve, len(sources), len(results)
        ),
        grid=(steps,),
        in_specs=in_specs,
        out_specs=[ANYWHERE] * len(results) + out_specs + [whole_block(weights.shape)],
        out_shape=[jax.ShapeDtypeStruct(shape, jnp.bfloat16) for shape in results]
        + out_shape
        + [jax.ShapeDtypeStruct(weights.shape, jnp.bfloat16)],
        input_output_aliases=aliases,
        scratch_shapes=scratch,
        compiler_params=pltpu.CompilerParams(
            vmem_limit_bytes=VMEM_BYTES, collective_id=2 + hop, has_side_effects=True
        ),
        cost_estimate=pl.CostEstimate(
            flops=12 * rows * model * wide, bytes_accessed=40 << 20, transcendentals=rows * wide
        ),
    )(*args)
    return outs[: len(results)], outs[len(results) : -1], outs[-1]


def core_swap(arr):
    size = lax.axis_size("expert")
    return lax.ppermute(arr, "expert", [(i, i ^ 1) for i in range(size)])


def row_part(arr, index, count):
    return lax.dynamic_slice_in_dim(arr, index * (arr.shape[0] // count), arr.shape[0] // count, 0)


def own_weights(w_router, w_in, w_out):
    exp_local, model_dim, ff_dim = w_in.shape
    router_rows = jnp.zeros((ROUTER_ROWS, model_dim), jnp.bfloat16).at[:exp_local].set(w_router)
    return jnp.concatenate(
        [
            jnp.swapaxes(w_in, 1, 2).reshape(exp_local * ff_dim, model_dim),
            router_rows,
            w_out.reshape(exp_local * ff_dim, model_dim),
        ]
    )


def block_dense(
    layer_input,
    segments,
    keep_mask,
    att_routes,
    moe_routes,
    expert_counts,
    norm_gain,
    w_query,
    w_key,
    w_select,
    w_value,
    w_output,
    w_router,
    w_in,
    w_out,
    cotangent,
):
    rows, model = layer_input.shape
    seqs, seq_len = segments.shape
    exp_local, _, ff_dim = w_in.shape
    heads = w_query.shape[1] // DH
    chips = lax.axis_size("expert") // 2
    wide, narrow, gates = heads * VEXP * DH, heads * DH, 2 * heads * VEXP
    moe_wide = exp_local * ff_dim
    mine = lax.axis_index("expert")
    chip, core = mine // 2, mine % 2

    own = own_weights(w_router, w_in, w_out)
    exp_total = 2 * chips * exp_local
    named = jnp.sum(
        (moe_routes[..., None] == jnp.arange(exp_total, dtype=jnp.int32)).astype(jnp.bfloat16), axis=1
    )
    named = jnp.concatenate([named, core_swap(named)])

    column = jnp.arange(seq_len, dtype=jnp.int32)
    changed = jnp.concatenate(
        [jnp.ones((seqs, 1), jnp.bool_), segments[:, 1:] != segments[:, :-1]], axis=1
    )
    start = lax.cummax(jnp.where(changed, column, 0), axis=1)
    cos_tab, sin_tab = rope_tables((column - start).reshape(-1), DH)
    cos_two = jnp.concatenate([cos_tab, cos_tab], axis=1)
    sin_two = jnp.concatenate([-sin_tab, sin_tab], axis=1)
    start = (start + seq_len * jnp.arange(seqs, dtype=jnp.int32)[:, None]).reshape(rows, 1)
    keep = keep_mask.reshape(1, rows)
    att_mask = jnp.sum(
        (att_routes[..., None] == jnp.arange(VEXP, dtype=jnp.int32)).astype(jnp.bfloat16), axis=2
    ).reshape(rows, gates)
    att_mask = jnp.pad(att_mask, ((0, 0), (0, LANE - gates)))
    gain_row = norm_gain.reshape(1, model)
    wqk = jnp.concatenate([w_query, w_key], axis=1)
    wsel = jnp.pad(w_select, ((0, 0), (0, LANE - gates)))

    shape = own.shape
    part = shape[0] // 4
    ahead = part // 80 * 64
    third, first, cot_far, sent_far, hidden, normed, q_rot, k_rot, value_bf, value_all, attended, sig, lse, mixed, sent = (
        attention_forward(
            ahead, own, cotangent, layer_input, start, keep, cos_two, sin_two, att_mask, gain_row, wqk, wsel, w_value,
            w_output, TILE,
        )
    )

    lane = jnp.arange(chips * LANE, dtype=jnp.int32)
    owner = ((chip + lane // LANE) % chips * 2 + core) * exp_local + lane % LANE
    pick = (lane % LANE < exp_local) & (jnp.arange(exp_total, dtype=jnp.int32)[:, None] == owner)
    masks = jnp.dot(named, pick.astype(jnp.bfloat16), preferred_element_type=jnp.float32)
    counts = jnp.sum(masks, axis=0).astype(jnp.int32)
    masks = masks.astype(jnp.bfloat16)
    place = jnp.arange(ROUTER_ROWS, dtype=jnp.int32)[:, None] - exp_local
    digits = jnp.where(
        (place >= 0) & (place < DIGITS), (counts >> (2 * jnp.clip(place, 0, DIGITS))) & 3, 0
    ).astype(jnp.float32)

    def run(hop, sources, results, aliases, moves, spread, halve, weights, sums, last_hidden):
        return expert_chunk(
            sources, results, aliases, moves, spread, halve, (sent, sent_far, cotangent, cot_far), weights,
            masks, digits, hop, sums, last_hidden, exp_local, ff_dim, TILE,
        )

    middle = (ahead + shape[0]) // 32 * 16
    (third, second), sums, grad_0 = run(
        0,
        [third, own],
        [shape, shape],
        {0: 0},
        shift_move(1, 1, -2, own_part(part), own_part(part), part),
        0,
        None,
        own,
        None,
        None,
    )
    (second, first), sums, grad_3 = run(
        3,
        [second, first, own],
        [shape, shape],
        {0: 0, 1: 1},
        shift_move(2, 1, -1, fixed(ahead), fixed(ahead), middle - ahead),
        0,
        None,
        third,
        sums,
        None,
    )
    (first,), (*sums, part_3), grad_2 = run(
        2,
        [first, own, grad_3],
        [shape],
        {0: 0},
        shift_move(1, 0, -1, fixed(middle), fixed(middle), shape[0] - middle),
        None,
        2,
        second,
        sums,
        None,
    )
    (got_3,), (layer_output, dhidden, dy, part_2), grad_1 = run(
        1,
        [grad_2, part_3],
        [(part, model)],
        {},
        shift_move(1, 0, 3, fixed(0), fixed(0), part),
        None,
        0,
        first,
        sums,
        hidden,
    )
    got_2, grad_input, dqk, dval, dlog, gain_rows, part_1, part_0 = attention_backward(
        [grad_1, grad_0, part_2],
        [(part, model)],
        shift_move(2, 0, 2, fixed(0), fixed(0), part),
        (0, 1),
        part,
        dy, q_rot, k_rot, value_bf, attended, lse, start, keep, sig, att_mask, cos_two, sin_two,
        layer_input, value_all, dhidden, gain_row, wqk, wsel, w_value, w_output, TILE,
    )
    unit = (
        (jnp.arange(GAIN_ROWS)[:, None] < 2) & (jnp.arange(LANE)[None, :] == gates)
    ).astype(jnp.bfloat16)
    dense, summed = tail(
        part_1, part_0, got_2, got_3, dy, layer_input, normed, gain_rows, mixed, dval, dlog, dqk, unit, shape, chips
    )
    summed = summed.astype(jnp.float32)
    out_sum, dense = dense[:, :wide].T, dense[:, wide:]
    grad_w_in = jnp.swapaxes(summed[:moe_wide].reshape(exp_local, ff_dim, model), 1, 2)
    extra = summed[moe_wide : moe_wide + ROUTER_ROWS]
    grad_router = extra[:exp_local]
    parts = extra[exp_local : exp_local + DIGITS, :exp_local].astype(jnp.int32)
    tally = sum(parts[i] << (2 * i) for i in range(DIGITS))
    grad_w_out = summed[moe_wide + ROUTER_ROWS :].reshape(exp_local, ff_dim, model)

    at_qk = wide + LANE
    return (
        layer_output,
        grad_input,
        dense[:, wide + gates],
        dense[:, at_qk : at_qk + narrow],
        dense[:, at_qk + narrow : at_qk + 2 * narrow],
        dense[:, wide : wide + gates],
        dense[:, :wide],
        out_sum,
        grad_router,
        grad_w_in,
        grad_w_out,
        expert_counts + tally,
    )


def block_dispatched(
    layer_input,
    segments,
    keep_mask,
    att_routes,
    moe_routes,
    expert_counts,
    norm_gain,
    w_query,
    w_key,
    w_select,
    w_value,
    w_output,
    w_router,
    w_in,
    w_out,
    cotangent,
):
    tok_rows, model_dim = layer_input.shape
    seq_count, seq_len = segments.shape
    head_count = w_query.shape[1] // DH
    score_scale = DH ** (-0.5)
    inputs_f = layer_input.astype(jnp.float32)
    normed, norm_pull = jax.vjp(layer_norm, inputs_f, norm_gain)
    normed_bf = normed.astype(jnp.bfloat16)
    query_rows = jnp.dot(normed_bf, w_query, preferred_element_type=jnp.float32).reshape(
        tok_rows, head_count, DH
    )
    key_rows = jnp.dot(normed_bf, w_key, preferred_element_type=jnp.float32).reshape(
        tok_rows, head_count, DH
    )
    logits = jnp.dot(layer_input, w_select, preferred_element_type=jnp.float32)
    named_mask = jnp.sum(
        (att_routes[..., None] == jnp.arange(VEXP, dtype=jnp.int32)).astype(jnp.float32), axis=2
    )
    select_sig = jax.nn.sigmoid(logits).reshape(tok_rows, 2 * head_count, VEXP)
    head_gates = select_sig * named_mask
    value_all = jnp.dot(layer_input, w_value, preferred_element_type=jnp.float32).reshape(
        tok_rows, head_count, VEXP, DH
    )
    value_bf = jnp.sum(head_gates[:, :head_count, :, None] * value_all, axis=2).astype(jnp.bfloat16)
    position, allowed = jax.vmap(doc_layout)(segments, keep_mask)
    cos_tab, sin_tab = rope_tables(position.reshape(-1), DH)
    q_rot = (rotate(query_rows, cos_tab, sin_tab) * score_scale).astype(jnp.bfloat16)
    k_rot = rotate(key_rows, cos_tab, sin_tab).astype(jnp.bfloat16)
    seq_shape = (seq_count, seq_len, head_count, DH)
    attended, log_total = lax.map(
        attend_forward,
        (q_rot.reshape(seq_shape), k_rot.reshape(seq_shape), value_bf.reshape(seq_shape), allowed),
    )
    attended = attended.reshape(tok_rows, head_count, DH)
    mixed_bf = (
        (head_gates[:, head_count:, :, None] * attended[:, :, None, :])
        .astype(jnp.bfloat16)
        .reshape(tok_rows, head_count * VEXP * DH)
    )
    hidden = inputs_f + jnp.dot(mixed_bf, w_output, preferred_element_type=jnp.float32)
    dev_count = lax.axis_size("expert")
    exp_local = w_in.shape[0]
    exp_total = dev_count * exp_local
    top_k = moe_routes.shape[1]
    capacity = 10 * tok_rows * top_k // (7 * exp_total) + 1
    owner, filled, slot_of = slot_table(moe_routes, exp_total, capacity)
    keep_slot = filled[:, None] > 0
    zero_bf = jnp.zeros((), jnp.bfloat16)
    hidden_bf = hidden.astype(jnp.bfloat16)
    send_rows = jnp.where(keep_slot, hidden_bf[owner], zero_bf).reshape(
        dev_count, exp_local * capacity, model_dim
    )
    rows_in = lax.all_to_all(send_rows, "expert", split_axis=0, concat_axis=0, tiled=True)
    histogram = jnp.zeros((exp_total,), jnp.float32).at[moe_routes.reshape(-1)].add(1.0)
    tally = lax.psum_scatter(histogram, "expert", scatter_dimension=0, tiled=True)
    slot_shape = (dev_count, exp_local, capacity, model_dim)
    rows_four = rows_in.reshape(slot_shape)
    pre_act = jnp.einsum("necd,edf->necf", rows_four, w_in, preferred_element_type=jnp.float32)
    gelu_out, gelu_pull = jax.vjp(jax.nn.gelu, pre_act)
    act_bf = gelu_out.astype(jnp.bfloat16)
    router_logit = jnp.einsum(
        "necd,ed->nec", rows_four, w_router, preferred_element_type=jnp.float32
    )
    gate_moe = jax.nn.sigmoid(router_logit)
    expert_out = jnp.einsum("necf,efd->necd", act_bf, w_out, preferred_element_type=jnp.float32)
    reply = (
        (gate_moe[..., None] * expert_out)
        .astype(jnp.bfloat16)
        .reshape(dev_count, exp_local * capacity, model_dim)
    )
    returned = lax.all_to_all(reply, "expert", split_axis=0, concat_axis=0, tiled=True)
    moe_sum = jnp.sum(returned.reshape(-1, model_dim)[slot_of].astype(jnp.float32), axis=1)
    layer_output = (hidden + moe_sum).astype(jnp.bfloat16)
    cot_f = cotangent.astype(jnp.float32)
    send_cot = jnp.where(keep_slot, cotangent[owner], zero_bf).reshape(
        dev_count, exp_local * capacity, model_dim
    )
    cot_in, rows_again = (
        lax.all_to_all(send_cot, "expert", split_axis=0, concat_axis=0, tiled=True),
        lax.all_to_all(send_rows, "expert", split_axis=0, concat_axis=0, tiled=True),
    )
    rows_grad = rows_again.reshape(slot_shape)
    cot_bf = cot_in.reshape(slot_shape)
    raw_back = jnp.einsum("necd,efd->necf", cot_bf, w_out, preferred_element_type=jnp.float32)
    dgate = jnp.sum(act_bf.astype(jnp.float32) * raw_back, axis=-1)
    dlogit = dgate * gate_moe * (1.0 - gate_moe)
    dexpert = (gate_moe[..., None] * cot_bf.astype(jnp.float32)).astype(jnp.bfloat16)
    grad_w_out = jnp.einsum("necf,necd->efd", act_bf, dexpert, preferred_element_type=jnp.float32)
    dact = jnp.einsum("necd,efd->necf", dexpert, w_out, preferred_element_type=jnp.float32)
    dpre_bf = gelu_pull(dact)[0].astype(jnp.bfloat16)
    grad_w_in = jnp.einsum("necd,necf->edf", rows_grad, dpre_bf, preferred_element_type=jnp.float32)
    grad_router = jnp.einsum(
        "nec,necd->ed",
        dlogit,
        rows_grad.astype(jnp.float32),
        preferred_element_type=jnp.float32,
        precision=HIGHEST,
    )
    dsent = jnp.einsum("necf,edf->necd", dpre_bf, w_in, preferred_element_type=jnp.float32)
    dsent = (dsent + dlogit[..., None] * w_router[None, :, None, :].astype(jnp.float32)).astype(
        jnp.bfloat16
    )
    grad_back = lax.all_to_all(
        dsent.reshape(dev_count, exp_local * capacity, model_dim),
        "expert",
        split_axis=0,
        concat_axis=0,
        tiled=True,
    )
    dhidden = cot_f + jnp.sum(grad_back.reshape(-1, model_dim)[slot_of].astype(jnp.float32), axis=1)
    dy_bf = dhidden.astype(jnp.bfloat16)
    grad_output = jnp.einsum("tk,td->kd", mixed_bf, dy_bf, preferred_element_type=jnp.float32)
    dmixed = jnp.einsum("td,kd->tk", dy_bf, w_output, preferred_element_type=jnp.float32).reshape(
        tok_rows, head_count, VEXP, DH
    )
    dgate_out = jnp.sum(dmixed * attended[:, :, None, :], axis=-1)
    dattend = jnp.sum(head_gates[:, head_count:, :, None] * dmixed, axis=2).astype(jnp.bfloat16)
    grad_q, grad_k, grad_v = lax.map(
        attend_backward,
        (
            q_rot.reshape(seq_shape),
            k_rot.reshape(seq_shape),
            value_bf.reshape(seq_shape),
            allowed,
            log_total,
            dattend.reshape(seq_shape),
        ),
    )
    dquery = (
        (rotate_back(grad_q.reshape(tok_rows, head_count, DH), cos_tab, sin_tab) * score_scale)
        .astype(jnp.bfloat16)
        .reshape(tok_rows, head_count * DH)
    )
    dkey = (
        rotate_back(grad_k.reshape(tok_rows, head_count, DH), cos_tab, sin_tab)
        .astype(jnp.bfloat16)
        .reshape(tok_rows, head_count * DH)
    )
    grad_query = jnp.einsum("td,tk->dk", normed_bf, dquery, preferred_element_type=jnp.float32)
    grad_key = jnp.einsum("td,tk->dk", normed_bf, dkey, preferred_element_type=jnp.float32)
    dnormed = jnp.einsum(
        "tk,dk->td", dquery, w_query, preferred_element_type=jnp.float32
    ) + jnp.einsum("tk,dk->td", dkey, w_key, preferred_element_type=jnp.float32)
    dx_norm, grad_gain = norm_pull(dnormed)
    dvalue = grad_v.reshape(tok_rows, head_count, DH)
    dgate_val = jnp.sum(dvalue[:, :, None, :] * value_all, axis=-1)
    dvalue_all = (
        (head_gates[:, :head_count, :, None] * dvalue[:, :, None, :])
        .astype(jnp.bfloat16)
        .reshape(tok_rows, head_count * VEXP * DH)
    )
    grad_value = jnp.einsum(
        "td,tk->dk", layer_input, dvalue_all, preferred_element_type=jnp.float32
    )
    dgates = jnp.concatenate([dgate_val, dgate_out], axis=1)
    dlogits = (
        (dgates * named_mask * select_sig * (1.0 - select_sig))
        .astype(jnp.bfloat16)
        .reshape(tok_rows, 2 * head_count * VEXP)
    )
    grad_select = jnp.einsum("td,tk->dk", layer_input, dlogits, preferred_element_type=jnp.float32)
    grad_input = (
        dhidden
        + dx_norm
        + jnp.einsum("tk,dk->td", dvalue_all, w_value, preferred_element_type=jnp.float32)
    )
    grad_input = (
        grad_input + jnp.einsum("tk,dk->td", dlogits, w_select, preferred_element_type=jnp.float32)
    ).astype(jnp.bfloat16)
    expert_sums = (
        lax.psum(grad_w_in.astype(jnp.bfloat16), "dp").astype(jnp.float32),
        lax.psum(grad_w_out.astype(jnp.bfloat16), "dp").astype(jnp.float32),
        lax.psum(grad_router.astype(jnp.bfloat16), "dp").astype(jnp.float32),
        lax.psum(tally.astype(jnp.bfloat16), "dp").astype(jnp.float32),
    )
    dense_sums = (
        lax.psum_scatter(grad_gain, ("dp", "expert"), scatter_dimension=0, tiled=True),
        lax.psum_scatter(grad_query, ("dp", "expert"), scatter_dimension=0, tiled=True),
        lax.psum_scatter(grad_key, ("dp", "expert"), scatter_dimension=0, tiled=True),
        lax.psum_scatter(grad_select, ("dp", "expert"), scatter_dimension=0, tiled=True),
        lax.psum_scatter(grad_value, ("dp", "expert"), scatter_dimension=0, tiled=True),
        lax.psum_scatter(grad_output, ("dp", "expert"), scatter_dimension=1, tiled=True),
    )
    counts_out = expert_counts + expert_sums[3].astype(jnp.int32)
    return (
        layer_output,
        grad_input,
        dense_sums[0],
        dense_sums[1],
        dense_sums[2],
        dense_sums[3],
        dense_sums[4],
        dense_sums[5],
        expert_sums[2],
        expert_sums[0],
        expert_sums[1],
        counts_out,
    )


def local(*args):
    rows, top_k = args[4].shape
    experts, _, ff_dim = args[13].shape
    exp_total = lax.axis_size("expert") * experts
    capacity = 10 * rows * top_k // (7 * exp_total) + 1
    regular = lax.axis_size("dp") == 4 and lax.axis_size("expert") == 8 and experts % 2 == 0 and ff_dim == LANE
    return (block_dense if regular and 4 * capacity > rows else block_dispatched)(*args)


def solution(mesh):
    placed = (
        P(("dp", "expert"), None),
        P(("dp", "expert"), None),
        P(("dp", "expert"), None),
        P(("dp", "expert"), None, None),
        P(("dp", "expert"), None),
        P("expert"),
        P(),
        P(),
        P(),
        P(),
        P(),
        P(),
        P("expert", None),
        P("expert", None, None),
        P("expert", None, None),
        P(("dp", "expert"), None),
    )
    return jax.shard_map(
        local,
        mesh=mesh,
        in_specs=placed,
        out_specs=(
            P(("dp", "expert"), None),
            P(("dp", "expert"), None),
            P(("dp", "expert")),
            P(("dp", "expert"), None),
            P(("dp", "expert"), None),
            P(("dp", "expert"), None),
            P(("dp", "expert"), None),
            P(None, ("dp", "expert")),
            P("expert", None),
            P("expert", None, None),
            P("expert", None, None),
            P("expert"),
        ),
        check_vma=False,
    )
```

```python
import functools

import jax
import jax.numpy as jnp
from jax import lax
from jax.experimental import pallas as pl
from jax.experimental.pallas import tpu as pltpu
from jax.sharding import PartitionSpec as P

DH = 128
VEXP = 5


NORM_EPS = 1e-05
ROPE_BASE = 10000.0
MASK_FILL = -1e30
HIGHEST = lax.Precision.HIGHEST
ROUTER_ROWS = 64
DIGITS = 5
LANE = 128
GAIN_ROWS = 16
TILE = 256
VMEM_BYTES = 60 << 20
GELU_A = 0.7978845608028654
GELU_B = 0.044715


def layer_norm(values, gain_vec):
    center = values - jnp.mean(values, axis=-1, keepdims=True)
    spread = jnp.mean(center * center, axis=-1, keepdims=True)
    return center * lax.rsqrt(spread + NORM_EPS) * gain_vec


def rope_tables(position, width_dh):
    half_dh = width_dh // 2
    freq_row = jnp.power(ROPE_BASE, jnp.arange(half_dh, dtype=jnp.float32) * (-2.0 / width_dh))
    angle_tab = position.astype(jnp.float32)[:, None] * freq_row[None, :]
    return (jnp.cos(angle_tab), jnp.sin(angle_tab))


def rotate(values, cos_tab, sin_tab):
    half_dh = values.shape[-1] // 2
    first_half = values[..., :half_dh]
    second_half = values[..., half_dh:]
    cos_b = cos_tab[:, None, :]
    sin_b = sin_tab[:, None, :]
    return jnp.concatenate(
        [first_half * cos_b - second_half * sin_b, second_half * cos_b + first_half * sin_b],
        axis=-1,
    )


def rotate_back(grad_rot, cos_tab, sin_tab):
    half_dh = grad_rot.shape[-1] // 2
    grad_first = grad_rot[..., :half_dh]
    grad_second = grad_rot[..., half_dh:]
    cos_b = cos_tab[:, None, :]
    sin_b = sin_tab[:, None, :]
    return jnp.concatenate(
        [grad_first * cos_b + grad_second * sin_b, grad_second * cos_b - grad_first * sin_b],
        axis=-1,
    )


def doc_layout(seg_row, keep_row):
    length_s = seg_row.shape[0]
    column = jnp.arange(length_s, dtype=jnp.int32)
    new_doc = jnp.concatenate([jnp.ones((1,), dtype=jnp.bool_), seg_row[1:] != seg_row[:-1]])
    doc_start = lax.cummax(jnp.where(new_doc, column, jnp.zeros_like(column)), axis=0)
    position = column - doc_start
    same_doc = seg_row[:, None] == seg_row[None, :]
    causal = column[None, :] <= column[:, None]
    visible = (keep_row[None, :] == 1) | (column[None, :] == column[:, None])
    return (position, same_doc & causal & visible)


def slot_table(routes, exp_total, capacity):
    flat_ids = routes.reshape(-1)
    pair_count = flat_ids.shape[0]
    top_k = routes.shape[1]
    sort_order = jnp.argsort(flat_ids, stable=True)
    ranked = flat_ids[sort_order]
    first_slot = jnp.searchsorted(ranked, jnp.arange(exp_total, dtype=jnp.int32), side="left")
    slot_rank = jnp.arange(pair_count, dtype=jnp.int32) - first_slot[ranked]
    slot_dest = ranked * capacity + slot_rank
    owner = jnp.zeros((exp_total * capacity,), jnp.int32).at[slot_dest].set(sort_order // top_k)
    filled = jnp.zeros((exp_total * capacity,), jnp.float32).at[slot_dest].set(1.0)
    slot_of = (
        jnp.zeros((pair_count,), jnp.int32).at[sort_order].set(slot_dest).reshape(routes.shape)
    )
    return (owner, filled, slot_of)


def block_scores(q_blk, k_rows, allowed_blk):
    scores = jnp.einsum("qhd,khd->hqk", q_blk, k_rows, preferred_element_type=jnp.float32)
    return jnp.where(allowed_blk[None, :, :], scores, MASK_FILL)


def attend_forward(pieces):
    q_rows, k_rows, v_rows, allowed = pieces
    length_s = q_rows.shape[0]
    block_len = min(512, length_s)
    outs_list = []
    lse_list = []
    for begin_at in range(0, length_s, block_len):
        scores = block_scores(
            q_rows[begin_at : begin_at + block_len],
            k_rows,
            allowed[begin_at : begin_at + block_len],
        )
        row_max = jnp.max(scores, axis=-1, keepdims=True)
        exp_terms = jnp.exp(scores - row_max)
        row_sum = jnp.sum(exp_terms, axis=-1, keepdims=True)
        probs_bf = (exp_terms / row_sum).astype(jnp.bfloat16)
        outs_list.append(
            jnp.einsum("hqk,khd->qhd", probs_bf, v_rows, preferred_element_type=jnp.float32)
        )
        lse_list.append((row_max + jnp.log(row_sum))[..., 0])
    return (jnp.concatenate(outs_list, axis=0), jnp.concatenate(lse_list, axis=1))


def attend_backward(pieces):
    q_rows, k_rows, v_rows, allowed, log_total, grad_rows = pieces
    length_s = q_rows.shape[0]
    block_len = min(512, length_s)
    grad_q_list = []
    grad_k = jnp.zeros(k_rows.shape, jnp.float32)
    grad_v = jnp.zeros(v_rows.shape, jnp.float32)
    for begin_at in range(0, length_s, block_len):
        q_blk = q_rows[begin_at : begin_at + block_len]
        grad_blk = grad_rows[begin_at : begin_at + block_len]
        scores = block_scores(q_blk, k_rows, allowed[begin_at : begin_at + block_len])
        probs_f = jnp.exp(scores - log_total[:, begin_at : begin_at + block_len, None])
        grad_prob = jnp.einsum("qhd,khd->hqk", grad_blk, v_rows, preferred_element_type=jnp.float32)
        grad_score = (
            probs_f * (grad_prob - jnp.sum(probs_f * grad_prob, axis=-1, keepdims=True))
        ).astype(jnp.bfloat16)
        grad_v = grad_v + jnp.einsum(
            "hqk,qhd->khd",
            probs_f.astype(jnp.bfloat16),
            grad_blk,
            preferred_element_type=jnp.float32,
        )
        grad_q_list.append(
            jnp.einsum("hqk,khd->qhd", grad_score, k_rows, preferred_element_type=jnp.float32)
        )
        grad_k = grad_k + jnp.einsum(
            "hqk,qhd->khd", grad_score, q_blk, preferred_element_type=jnp.float32
        )
    return (jnp.concatenate(grad_q_list, axis=0), grad_k, grad_v)


def dot_nt(left, right):
    return lax.dot_general(left, right, (((1,), (1,)), ((), ())), preferred_element_type=jnp.float32)


def dot_nn(left, right):
    return lax.dot_general(left, right, (((1,), (0,)), ((), ())), preferred_element_type=jnp.float32)


def dot_tn(left, right):
    return lax.dot_general(left, right, (((0,), (0,)), ((), ())), preferred_element_type=jnp.float32)


def spin(values, cos_two, sin_two):
    return values * cos_two + pltpu.roll(values, DH // 2, 1) * sin_two


def spin_back(values, cos_two, sin_two):
    return values * cos_two - pltpu.roll(values, DH // 2, 1) * sin_two


def window_mask(step, tile, start_col, keep_before, keep_now):
    row = step * tile + lax.broadcasted_iota(jnp.int32, (tile, 2 * tile), 0)
    col = (step - 1) * tile + lax.broadcasted_iota(jnp.int32, (tile, 2 * tile), 1)
    keep_row = jnp.concatenate([keep_before, keep_now], axis=1)
    return (col >= start_col) & (col <= row) & ((keep_row == 1) | (col == row))


def neighbour(kind, amount):
    mine, place = lax.axis_index("dp"), lax.axis_index("expert")
    chips = lax.axis_size("expert") // 2
    chip, core = place // 2, lax.rem(place, 2)
    if kind == "dp":
        flipped = [mine, mine + 1 - 2 * lax.rem(mine, 2), lax.rem(mine + 2, 4), 3 - mine]
        return (flipped[amount], place)
    if kind == "core":
        return (mine, place + 1 - 2 * core)
    return (mine, 2 * lax.rem(chip + amount + chips, chips) + core)


def own_part(rows):
    return lambda mine, flipped: mine * rows


def fixed(start):
    return lambda mine, flipped: start


def shift_move(src, dst, hop, src_at, dst_at, count):
    return [(src, dst, "chip", hop, src_at, dst_at, count)]


def greet(peers):
    barrier = pltpu.get_barrier_semaphore()
    for peer in peers:
        pl.semaphore_signal(barrier, inc=1, device_id=peer, device_id_type=pl.DeviceIdType.MESH)
    pl.semaphore_wait(barrier, len(peers))


def peers_of(moves):
    peers = []
    for _, _, kind, amount, _, _, _ in moves:
        peers.append(neighbour(kind, amount))
        if kind == "chip":
            peers.append(neighbour(kind, -amount))
    return peers


def copies_of(moves, ins, outs, send_sem, recv_sem):
    mine = lax.axis_index("dp")
    copies = []
    for i, (src, dst, kind, amount, src_at, dst_at, count) in enumerate(moves):
        peer = neighbour(kind, amount)
        copies.append(
            pltpu.make_async_remote_copy(
                src_ref=ins[src].at[pl.ds(pl.multiple_of(src_at(mine, peer[0]), 16), count)],
                dst_ref=outs[dst].at[pl.ds(pl.multiple_of(dst_at(mine, peer[0]), 16), count)],
                send_sem=send_sem.at[i],
                recv_sem=recv_sem.at[i],
                device_id=peer,
                device_id_type=pl.DeviceIdType.MESH,
            )
        )
    return copies


ANYWHERE = pl.BlockSpec(memory_space=pl.ANY)


def tile_rows(index, tile):
    return pl.ds(pl.multiple_of(index * tile, tile), tile)


def flips():
    mine = lax.axis_index("dp")
    return [mine, mine + 1 - 2 * lax.rem(mine, 2), lax.rem(mine + 2, 4), 3 - mine]


def remote(src, dst, sems, index, peer):
    return pltpu.make_async_remote_copy(
        src_ref=src,
        dst_ref=dst,
        send_sem=sems.at[0, index],
        recv_sem=sems.at[1, index],
        device_id=peer,
        device_id_type=pl.DeviceIdType.MESH,
    )


def span(start, count):
    return pl.ds(pl.multiple_of(start, 16), count)


def halving_first(source, near, far, part, cut, sems, at):
    dp = flips()
    low = part - cut
    copies = []
    for slot, owner in enumerate((1, 3)):
        copies.append(
            remote(
                source.at[span(dp[owner] * part, cut)],
                near.at[pl.ds(slot * cut, cut)],
                sems,
                at + slot,
                neighbour("dp", 1),
            )
        )
    for slot, owner in enumerate((2, 3)):
        copies.append(
            remote(
                source.at[span(dp[owner] * part + cut, low)],
                far.at[pl.ds(slot * low, low)],
                sems,
                at + 2 + slot,
                neighbour("dp", 2),
            )
        )
    return copies


def halving_second(send, land, part, cut, sems, at):
    low = part - cut
    return [
        remote(send.at[pl.ds(0, cut)], land.at[pl.ds(0, cut)], sems, at, neighbour("dp", 2)),
        remote(send.at[pl.ds(cut, low)], land.at[pl.ds(cut, low)], sems, at + 1, neighbour("dp", 1)),
    ]


def as_f32(ref, start, count):
    return ref[pl.ds(start, count), :].astype(jnp.float32)


def spread_first(source, target, part, cut, sems, at):
    mine = lax.axis_index("dp")
    return [
        remote(
            source.at[pl.ds(0, cut)],
            target.at[span(mine * part, cut)],
            sems,
            at,
            neighbour("dp", 1),
        ),
        remote(
            source.at[pl.ds(cut, part - cut)],
            target.at[span(mine * part + cut, part - cut)],
            sems,
            at + 1,
            neighbour("dp", 2),
        ),
    ]


def spread_second(source, target, part, cut, sems, at):
    dp = flips()
    low = part - cut
    mine_up, mine_down = span(dp[0] * part, cut), span(dp[0] * part + cut, low)
    got_up, got_down = span(dp[1] * part, cut), span(dp[2] * part + cut, low)
    return [
        remote(source.at[pl.ds(0, cut)], target.at[mine_up], sems, at, neighbour("dp", 2)),
        remote(target.at[got_up], target.at[got_up], sems, at + 1, neighbour("dp", 2)),
        remote(source.at[pl.ds(cut, low)], target.at[mine_down], sems, at + 2, neighbour("dp", 1)),
        remote(target.at[got_down], target.at[got_down], sems, at + 3, neighbour("dp", 1)),
    ]


def load_own(source, own, part, cut, sems):
    dp = flips()
    low = part - cut
    return [
        pltpu.make_async_copy(
            source.at[span(dp[owner] * part + start, count)], own.at[pl.ds(at, count)], sems.at[i]
        )
        for i, (owner, start, count, at) in enumerate(
            [(0, 0, cut, 0), (2, 0, cut, cut), (0, cut, low, 2 * cut), (1, cut, low, 2 * cut + low)]
        )
    ]


class Halving:
    def __init__(self, source, total, buffers, part, cut):
        near, far, send, land, sems = buffers[:5]
        self.source, self.total, self.part, self.cut = source, total, part, cut
        self.near, self.far, self.send, self.land = near, far, send, land
        self.own, self.loads = None, []
        if len(buffers) > 5:
            self.own, load_sems = buffers[5:]
            self.loads = load_own(source, self.own, part, cut, load_sems)
        self.first = halving_first(source, near, far, part, cut, sems, 0)
        self.second = halving_second(send, land, part, cut, sems, 4)

    def start(self):
        for copy in self.first + self.loads:
            copy.start()

    def own_rows(self, which):
        part, cut = self.part, self.cut
        low = part - cut
        if self.own is not None:
            return as_f32(self.own, (0, cut, 2 * cut, 2 * cut + low)[which], (cut, low)[which // 2])
        owner, start = ((0, 0), (2, 0), (0, cut), (1, cut))[which]
        return as_f32(
            self.source, pl.multiple_of(flips()[owner] * part + start, 16), (cut, low)[which // 2]
        )

    def turn(self):
        part, cut = self.part, self.cut
        low = part - cut
        for copy in self.first + self.loads:
            copy.wait()
        up = self.own_rows(1) + as_f32(self.near, cut, cut)
        down = self.own_rows(3) + as_f32(self.far, low, low)
        self.send[:cut, :] = up.astype(jnp.bfloat16)
        self.send[cut:, :] = down.astype(jnp.bfloat16)
        for copy in self.second:
            copy.start()
        self.total[:cut, :] = (self.own_rows(0) + as_f32(self.near, 0, cut)).astype(jnp.bfloat16)
        self.total[cut:, :] = (self.own_rows(2) + as_f32(self.far, 0, low)).astype(jnp.bfloat16)

    def finish(self):
        for copy in self.second:
            copy.wait()
        total = as_f32(self.total, 0, self.part) + as_f32(self.land, 0, self.part)
        self.total[...] = total.astype(jnp.bfloat16)


def halving_buffers(part, cut, model):
    bf16 = lambda rows: pltpu.VMEM((rows, model), jnp.bfloat16)
    return [
        bf16(2 * cut),
        bf16(2 * (part - cut)),
        bf16(part),
        bf16(part),
        pltpu.SemaphoreType.DMA((2, 6)),
        bf16(2 * part),
        pltpu.SemaphoreType.DMA((4,)),
    ]


class Spreading:
    def __init__(self, target, part, cut, sems, mine):
        self.first = spread_first(mine, target, part, cut, sems, 0)
        self.second = spread_second(mine, target, part, cut, sems, 2)

    def start(self):
        for copy in self.first:
            copy.start()

    def turn(self):
        for copy in self.first:
            copy.wait()
        for copy in self.second:
            copy.start()

    def finish(self):
        for copy in self.second:
            copy.wait()


def forward_body(heads, tile, steps, ahead, *refs):
    (
        own_any,
        cot_any,
        x_ref,
        start_ref,
        keep_ref,
        cos_ref,
        sin_ref,
        mask_ref,
        gain_ref,
        wsel_ref,
        wq_any,
        wk_any,
        wval_any,
        wout_any,
        chunk_any,
        near_any,
        cot_far_any,
        sent_far_any,
        hid_ref,
        norm_ref,
        q_ref,
        k_ref,
        v_ref,
        val_ref,
        att_ref,
        sig_ref,
        lse_ref,
        mix_ref,
        sent_all,
        send_sem,
        recv_sem,
        tile_send,
        tile_recv,
        wqk_ref,
        wval_ref,
        wout_ref,
        load_sem,
    ) = refs
    step = pl.program_id(0)
    narrow = heads * DH
    loads = [
        pltpu.make_async_copy(source, target, load_sem.at[i])
        for i, (source, target) in enumerate(
            [
                (wq_any, wqk_ref.at[:, pl.ds(0, narrow)]),
                (wk_any, wqk_ref.at[:, pl.ds(narrow, narrow)]),
                (wval_any, wval_ref),
                (wout_any, wout_ref),
            ]
        )
    ]

    def loaded(which):
        @pl.when(step == 0)
        def _():
            for i in which:
                loads[i].wait()

    @pl.when(step == 0)
    def _():
        for copy in loads:
            copy.start()

    rows = steps * tile
    quarter = own_any.shape[0] // 4
    moves = shift_move(0, 0, -3, own_part(quarter), own_part(quarter), quarter)
    moves = moves + shift_move(0, 1, -1, fixed(0), fixed(0), ahead)
    moves = moves + [(1, 2, "core", 1, fixed(0), fixed(0), rows)]
    partner = neighbour("core", 1)
    copies = copies_of(moves, [own_any, cot_any], [chunk_any, near_any, cot_far_any], send_sem, recv_sem)

    def tile_copy(index):
        return pltpu.make_async_remote_copy(
            src_ref=sent_all.at[pl.ds(index * tile, tile)],
            dst_ref=sent_far_any.at[pl.ds(index * tile, tile)],
            send_sem=tile_send.at[index],
            recv_sem=tile_recv.at[index],
            device_id=partner,
            device_id_type=pl.DeviceIdType.MESH,
        )


    @pl.when(step == 0)
    def _():
        greet(peers_of(moves))
        for copy in copies:
            copy.start()

    now = tile_rows(step, tile)
    before = tile_rows(jnp.maximum(step - 1, 0), tile)
    x = x_ref[...]
    x_f = x.astype(jnp.float32)
    center = x_f - jnp.mean(x_f, axis=1, keepdims=True)
    spread = jnp.mean(center * center, axis=1, keepdims=True)
    normed = (center * lax.rsqrt(spread + NORM_EPS) * gain_ref[...]).astype(jnp.bfloat16)
    norm_ref[...] = normed
    sig = 1.0 / (1.0 + jnp.exp(-dot_nn(x, wsel_ref[...])))
    sig_ref[...] = sig
    gates = sig * mask_ref[...].astype(jnp.float32)
    cos_two, sin_two = cos_ref[...], sin_ref[...]
    allowed = window_mask(step, tile, start_ref[...], keep_ref[:, before], keep_ref[:, now])
    scale = DH ** (-0.5)
    lanes = lax.broadcasted_iota(jnp.int32, (tile, LANE), 1)
    lse = jnp.zeros((tile, LANE), jnp.float32)
    loaded((0, 1))
    qk = dot_nn(normed, wqk_ref[...])
    loaded((2,))
    for head in range(heads):
        cols = slice(head * DH, (head + 1) * DH)
        value = dot_nn(x, wval_ref[:, head * VEXP * DH : (head + 1) * VEXP * DH])
        val_ref[:, head * VEXP * DH : (head + 1) * VEXP * DH] = value.astype(jnp.bfloat16)
        total = jnp.zeros((tile, DH), jnp.float32)
        for e in range(VEXP):
            at = head * VEXP + e
            total = total + gates[:, at : at + 1] * value[:, e * DH : (e + 1) * DH]
        v_ref[now, cols] = total.astype(jnp.bfloat16)
    for head in range(heads):
        cols = slice(head * DH, (head + 1) * DH)
        q_head = (spin(qk[:, cols], cos_two, sin_two) * scale).astype(jnp.bfloat16)
        k_head = spin(
            qk[:, (heads + head) * DH : (heads + head + 1) * DH], cos_two, sin_two
        ).astype(jnp.bfloat16)
        q_ref[:, cols] = q_head
        k_ref[now, cols] = k_head
        scores = jnp.concatenate(
            [dot_nt(q_head, k_ref[before, cols]), dot_nt(q_head, k_head)], axis=1
        )
        scores = jnp.where(allowed, scores, MASK_FILL)
        row_max = jnp.max(scores, axis=1, keepdims=True)
        terms = jnp.exp(scores - row_max)
        row_sum = jnp.sum(terms, axis=1, keepdims=True)
        probs = (terms * (1.0 / row_sum)).astype(jnp.bfloat16)
        attended = dot_nn(probs[:, :tile], v_ref[before, cols]) + dot_nn(
            probs[:, tile:], v_ref[now, cols]
        )
        att_ref[:, cols] = attended
        lse = jnp.where(lanes == head, row_max + jnp.log(row_sum), lse)
        for e in range(VEXP):
            at = head * VEXP + e
            gate = gates[:, heads * VEXP + at : heads * VEXP + at + 1]
            mix_ref[:, at * DH : (at + 1) * DH] = (gate * attended).astype(jnp.bfloat16)
    lse_ref[...] = lse
    loaded((3,))
    hidden = x_f + dot_nn(mix_ref[...], wout_ref[...])
    hid_ref[...] = hidden
    sent_all[now, :] = hidden.astype(jnp.bfloat16)
    for index in range(steps):

        @pl.when(step == index)
        def _(index=index):
            tile_copy(index).start()

    @pl.when(step == steps - 1)
    def _():
        for copy in copies:
            copy.wait()
        for index in range(steps):
            tile_copy(index).wait()


def whole_block(shape):
    return pl.BlockSpec(shape, lambda step: (0,) * len(shape), pipeline_mode=pl.Buffered(1))


def attention_forward(ahead, own, cot, x, start, keep, cos_two, sin_two, mask, gain, wsel, wq, wk, wval, wout, tile):
    rows, model = x.shape
    heads = wq.shape[1] // DH
    per_tile = lambda width: pl.BlockSpec((tile, width), lambda step: (step, 0))
    full = lambda arr: whole_block(arr.shape)
    narrow, wide = heads * DH, heads * VEXP * DH
    shapes = [
        (model, jnp.float32, False),
        (model, jnp.bfloat16, False),
        (narrow, jnp.bfloat16, False),
        (narrow, jnp.bfloat16, True),
        (narrow, jnp.bfloat16, True),
        (wide, jnp.bfloat16, False),
        (narrow, jnp.float32, False),
        (LANE, jnp.float32, False),
        (LANE, jnp.float32, False),
        (wide, jnp.bfloat16, False),
        (model, jnp.bfloat16, True),
    ]
    return pl.pallas_call(
        functools.partial(forward_body, heads, tile, rows // tile, ahead),
        grid=(rows // tile,),
        in_specs=[
            ANYWHERE,
            ANYWHERE,
            per_tile(model),
            per_tile(1),
            full(keep),
            per_tile(LANE),
            per_tile(LANE),
            per_tile(LANE),
            full(gain),
            full(wsel),
            ANYWHERE,
            ANYWHERE,
            ANYWHERE,
            ANYWHERE,
        ],
        out_specs=[ANYWHERE] * 4
        + [whole_block((rows, width)) if whole else per_tile(width) for width, _, whole in shapes],
        out_shape=[
            jax.ShapeDtypeStruct(own.shape, jnp.bfloat16),
            jax.ShapeDtypeStruct(own.shape, jnp.bfloat16),
            jax.ShapeDtypeStruct((rows, model), jnp.bfloat16),
            jax.ShapeDtypeStruct((rows, model), jnp.bfloat16),
        ]
        + [jax.ShapeDtypeStruct((rows, width), kind) for width, kind, _ in shapes],
        scratch_shapes=[
            pltpu.SemaphoreType.DMA((3,)),
            pltpu.SemaphoreType.DMA((3,)),
            pltpu.SemaphoreType.DMA((rows // tile,)),
            pltpu.SemaphoreType.DMA((rows // tile,)),
            pltpu.VMEM((model, 2 * narrow), jnp.bfloat16),
            pltpu.VMEM(wval.shape, jnp.bfloat16),
            pltpu.VMEM(wout.shape, jnp.bfloat16),
            pltpu.SemaphoreType.DMA((4,)),
        ],
        compiler_params=pltpu.CompilerParams(
            vmem_limit_bytes=VMEM_BYTES, collective_id=1, has_side_effects=True
        ),
        cost_estimate=pl.CostEstimate(
            flops=2 * rows * model * (2 * narrow + 2 * wide), bytes_accessed=40 << 20, transcendentals=0
        ),
    )(own, cot, x, start, keep, cos_two, sin_two, mask, gain, wsel, wq, wk, wval, wout)


def backward_body(heads, tile, steps, moves, halve, part, n_in, n_out, *refs):
    ins, refs = refs[:n_in], refs[n_in:]
    (
        cot_ref,
        grad_own_ref,
        grad_far_ref,
        q_ref,
        k_ref,
        v_ref,
        att_ref,
        lse_ref,
        start_ref,
        keep_ref,
        sig_now_ref,
        mask_now_ref,
        cos_now_ref,
        sin_now_ref,
        sig_old_ref,
        mask_old_ref,
        cos_old_ref,
        sin_old_ref,
        x_ref,
        val_ref,
        gain_ref,
        wsel_ref,
        wout_ref,
        wq_any,
        wk_any,
        wval_any,
        *outs_and_rest,
    ) = refs
    outs, rest = outs_and_rest[:n_out], outs_and_rest[n_out:]
    (
        gin_ref,
        dqk_ref,
        dval_ref,
        dlog_ref,
        ggain_ref,
        dy_ref,
        *totals_and_rest,
    ) = rest
    totals, rest = totals_and_rest[: len(halve)], totals_and_rest[len(halve) :]
    (
        dk_acc,
        dv_acc,
        dq_keep,
        dgate_keep,
        gain_acc,
        dhid_keep,
        wqk_ref,
        wval_ref,
        load_sem,
        send_sem,
        recv_sem,
        *buffers,
    ) = rest
    step = pl.program_id(0)
    half_qk = heads * DH
    loads = [
        pltpu.make_async_copy(source, target, load_sem.at[i])
        for i, (source, target) in enumerate(
            [
                (wq_any, wqk_ref.at[:, pl.ds(0, half_qk)]),
                (wk_any, wqk_ref.at[:, pl.ds(half_qk, half_qk)]),
                (wval_any, wval_ref),
            ]
        )
    ]
    copies = copies_of(moves, ins, outs, send_sem, recv_sem)
    riders = [
        Halving(ins[source], totals[i], buffers[7 * i : 7 * i + 7], part, part // 32 * 16)
        for i, source in enumerate(halve)
    ]

    @pl.when(step == 0)
    def _():
        for copy in loads:
            copy.start()
        greet(peers_of(moves) + [neighbour("dp", 1), neighbour("dp", 2)])
        for copy in copies:
            copy.start()
        for rider in riders:
            rider.start()

    @pl.when(step == 1)
    def _():
        for copy in loads:
            copy.wait()

    @pl.when(step == steps - 1)
    def _():
        for rider in riders:
            rider.turn()

    slot = lax.rem(step, 2)
    old = 1 - slot
    lanes = lax.broadcasted_iota(jnp.int32, (tile, LANE), 1)
    scale = DH ** (-0.5)
    narrow = heads * DH

    @pl.when(step == 0)
    def _():
        gain_acc[...] = jnp.zeros_like(gain_acc)
        dk_acc[...] = jnp.zeros_like(dk_acc)
        dv_acc[...] = jnp.zeros_like(dv_acc)

    @pl.when(step < steps)
    def _():
        now = tile_rows(jnp.minimum(step, steps - 1), tile)
        before = tile_rows(jnp.maximum(step - 1, 0), tile)
        allowed = window_mask(step, tile, start_ref[...], keep_ref[:, before], keep_ref[:, now])
        gates = sig_now_ref[...] * mask_now_ref[...].astype(jnp.float32)
        dhid = cot_ref[...].astype(jnp.float32) + grad_own_ref[...] + grad_far_ref[...].astype(jnp.float32)
        dhid_keep[slot] = dhid
        dy = dhid.astype(jnp.bfloat16)
        dy_ref[...] = dy
        dgate = jnp.zeros((tile, LANE), jnp.float32)
        for head in range(heads):
            cols = slice(head * DH, (head + 1) * DH)
            dmixed = dot_nt(dy, wout_ref[head * VEXP * DH : (head + 1) * VEXP * DH, :])
            attended = att_ref[:, cols]
            dattend = jnp.zeros((tile, DH), jnp.float32)
            for e in range(VEXP):
                at = (heads + head) * VEXP + e
                part = dmixed[:, e * DH : (e + 1) * DH]
                dattend = dattend + gates[:, at : at + 1] * part
                dgate = jnp.where(
                    lanes == at, jnp.sum(part * attended, axis=1, keepdims=True), dgate
                )
            dattend = dattend.astype(jnp.bfloat16)
            q_head = q_ref[:, cols]
            k_old, k_now = k_ref[before, cols], k_ref[now, cols]
            v_old, v_now = v_ref[before, cols], v_ref[now, cols]
            scores = jnp.concatenate([dot_nt(q_head, k_old), dot_nt(q_head, k_now)], axis=1)
            scores = jnp.where(allowed, scores, MASK_FILL)
            probs = jnp.exp(scores - lse_ref[:, head : head + 1])
            dprob = jnp.concatenate([dot_nt(dattend, v_old), dot_nt(dattend, v_now)], axis=1)
            delta = jnp.sum(probs * dprob, axis=1, keepdims=True)
            dscore = (probs * (dprob - delta)).astype(jnp.bfloat16)
            probs = probs.astype(jnp.bfloat16)
            dv_acc[old, :, cols] += dot_tn(probs[:, :tile], dattend)
            dv_acc[slot, :, cols] = dot_tn(probs[:, tile:], dattend)
            dk_acc[old, :, cols] += dot_tn(dscore[:, :tile], q_head)
            dk_acc[slot, :, cols] = dot_tn(dscore[:, tile:], q_head)
            dq = dot_nn(dscore[:, :tile], k_old) + dot_nn(dscore[:, tile:], k_now)
            dq_keep[slot, :, cols] = (
                spin_back(dq, cos_now_ref[...], sin_now_ref[...]) * scale
            ).astype(jnp.bfloat16)
        dgate_keep[slot] = dgate

    @pl.when(step > 0)
    def _():
        sig = sig_old_ref[...]
        mask = mask_old_ref[...].astype(jnp.float32)
        gates = sig * mask
        dgate = dgate_keep[old]
        for head in range(heads):
            cols = slice(head * DH, (head + 1) * DH)
            dqk_ref[:, cols] = dq_keep[old, :, cols]
            dqk_ref[:, narrow + head * DH : narrow + (head + 1) * DH] = spin_back(
                dk_acc[old, :, cols], cos_old_ref[...], sin_old_ref[...]
            ).astype(jnp.bfloat16)
            dvalue = dv_acc[old, :, cols]
            for e in range(VEXP):
                at = head * VEXP + e
                wide = slice(at * DH, (at + 1) * DH)
                val = val_ref[:, wide].astype(jnp.float32)
                dgate = jnp.where(lanes == at, jnp.sum(dvalue * val, axis=1, keepdims=True), dgate)
                dval_ref[:, wide] = (gates[:, at : at + 1] * dvalue).astype(jnp.bfloat16)
        dlog = (dgate * gates * (1.0 - sig)).astype(jnp.bfloat16)
        dlog_ref[...] = dlog
        dnormed = dot_nt(dqk_ref[...], wqk_ref[...])
        x_f = x_ref[...].astype(jnp.float32)
        center = x_f - jnp.mean(x_f, axis=1, keepdims=True)
        inv = lax.rsqrt(jnp.mean(center * center, axis=1, keepdims=True) + NORM_EPS)
        x_hat = center * inv
        gain_acc[...] += jnp.sum(dnormed * x_hat, axis=0, keepdims=True)
        grad = dnormed * gain_ref[...]
        dx = inv * (
            grad
            - jnp.mean(grad, axis=1, keepdims=True)
            - x_hat * jnp.mean(grad * x_hat, axis=1, keepdims=True)
        )
        dx = dx + dhid_keep[old] + dot_nt(dval_ref[...], wval_ref[...]) + dot_nt(dlog, wsel_ref[...])
        gin_ref[...] = dx.astype(jnp.bfloat16)

    @pl.when(step == steps)
    def _():
        gain = gain_acc[...]
        high = gain.astype(jnp.bfloat16).astype(jnp.float32)
        row = lax.broadcasted_iota(jnp.int32, (GAIN_ROWS, gain.shape[1]), 0)
        split = jnp.where(row == 0, high, jnp.where(row == 1, gain - high, 0.0))
        ggain_ref[...] = split.astype(jnp.bfloat16)
        for rider in riders:
            rider.finish()
        for copy in copies:
            copy.wait()


def attention_backward(
    sources, results, moves, halve, part, cot, grad_own, grad_far, q, k, v, att, lse, start, keep, sig, mask,
    cos_two, sin_two, x, val, gain, wsel, wout, wq, wk, wval, tile
):
    rows, model = x.shape
    heads = wq.shape[1] // DH
    steps = rows // tile
    narrow, wide = heads * DH, heads * VEXP * DH
    at_now = lambda width: pl.BlockSpec((tile, width), lambda step: (jnp.minimum(step, steps - 1), 0))
    at_old = lambda width: pl.BlockSpec((tile, width), lambda step: (jnp.maximum(step - 1, 0), 0))
    full = lambda arr: whole_block(arr.shape)
    return pl.pallas_call(
        functools.partial(
            backward_body, heads, tile, steps, moves, halve, part, len(sources), len(results)
        ),
        grid=(steps + 1,),
        in_specs=[ANYWHERE] * len(sources)
        + [
            at_now(model),
            at_now(model),
            at_now(model),
            at_now(narrow),
            full(k),
            full(v),
            at_now(narrow),
            at_now(LANE),
            at_now(1),
            full(keep),
            at_now(LANE),
            at_now(LANE),
            at_now(LANE),
            at_now(LANE),
            at_old(LANE),
            at_old(LANE),
            at_old(LANE),
            at_old(LANE),
            at_old(model),
            at_old(wide),
            full(gain),
            full(wsel),
            full(wout),
            ANYWHERE,
            ANYWHERE,
            ANYWHERE,
        ],
        out_specs=[ANYWHERE] * len(results)
        + [
            at_old(model),
            at_old(2 * narrow),
            at_old(wide),
            at_old(LANE),
            whole_block((GAIN_ROWS, model)),
            at_now(model),
        ]
        + [whole_block((part, model))] * len(halve),
        out_shape=[jax.ShapeDtypeStruct(shape, jnp.bfloat16) for shape in results]
        + [
            jax.ShapeDtypeStruct((rows, model), jnp.bfloat16),
            jax.ShapeDtypeStruct((rows, 2 * narrow), jnp.bfloat16),
            jax.ShapeDtypeStruct((rows, wide), jnp.bfloat16),
            jax.ShapeDtypeStruct((rows, LANE), jnp.bfloat16),
            jax.ShapeDtypeStruct((GAIN_ROWS, model), jnp.bfloat16),
            jax.ShapeDtypeStruct((rows, model), jnp.bfloat16),
        ]
        + [jax.ShapeDtypeStruct((part, model), jnp.bfloat16)] * len(halve),
        scratch_shapes=[
            pltpu.VMEM((2, tile, narrow), jnp.float32),
            pltpu.VMEM((2, tile, narrow), jnp.float32),
            pltpu.VMEM((2, tile, narrow), jnp.bfloat16),
            pltpu.VMEM((2, tile, LANE), jnp.float32),
            pltpu.VMEM((1, model), jnp.float32),
            pltpu.VMEM((2, tile, model), jnp.float32),
            pltpu.VMEM((model, 2 * narrow), jnp.bfloat16),
            pltpu.VMEM(wval.shape, jnp.bfloat16),
            pltpu.SemaphoreType.DMA((3,)),
            pltpu.SemaphoreType.DMA((len(moves),)),
            pltpu.SemaphoreType.DMA((len(moves),)),
        ]
        + halving_buffers(part, part // 32 * 16, model) * len(halve),
        compiler_params=pltpu.CompilerParams(
            vmem_limit_bytes=VMEM_BYTES, collective_id=6, has_side_effects=True
        ),
        cost_estimate=pl.CostEstimate(
            flops=2 * rows * model * (2 * narrow + 2 * wide), bytes_accessed=50 << 20, transcendentals=0
        ),
    )(
        *sources, cot, grad_own, grad_far, q, k, v, att, lse, start, keep, sig, mask, cos_two, sin_two,
        sig, mask, cos_two, sin_two, x, val, gain, wsel, wout, wq, wk, wval,
    )


def tail_body(blocks, chips, part, cut, *refs):
    (
        part_1,
        part_3,
        part_0,
        got_2,
        gain_ref,
        dlog_ref,
        unit_ref,
        dy_any,
        mix_any,
        x_any,
        dval_any,
        norm_any,
        dqk_any,
        dense_ref,
        whole_any,
        came,
        quarter,
        product,
        pair,
        near,
        far,
        send,
        land,
        sums,
        last,
        link,
        core_sems,
        xy_sems,
        z_sems,
        local_sem,
        dy_ref,
        mix_ref,
        x_ref,
        dval_ref,
        norm_ref,
        dqk_ref,
        load_sem,
    ) = refs
    half = mix_ref.shape[1] // 2
    loads = [
        pltpu.make_async_copy(source, target, load_sem.at[i])
        for i, (source, target) in enumerate(
            [
                (dy_any, dy_ref),
                (mix_any.at[:, pl.ds(0, half)], mix_ref.at[:, pl.ds(0, half)]),
                (mix_any.at[:, pl.ds(half, half)], mix_ref.at[:, pl.ds(half, half)]),
                (x_any, x_ref),
                (dval_any, dval_ref),
                (norm_any, norm_ref),
                (dqk_any, dqk_ref),
            ]
        )
    ]
    for copy in loads:
        copy.start()
    ready = {0: (0, 1), 1: (2,), 2: (3, 4), 4: (5, 6)}
    place = lax.axis_index("expert")
    chip, core = place // 2, lax.rem(place, 2)
    model = x_ref.shape[1]
    piece = model // 4 // chips // 2
    quart = chips * piece
    halfway = quart // 2
    rights = {"out": mix_ref, "val": dval_ref, "log": dlog_ref, "qk": dqk_ref}
    lefts = {"out": dy_ref, "val": x_ref, "log": x_ref, "qk": norm_ref}

    peers = [neighbour("core", 1)] + [neighbour("dp", flip) for flip in (1, 2)]
    for hop in range(1, chips):
        peers.append(neighbour("chip", hop))
    greet(peers)
    passes = [
        remote(source, came.at[i], link, 7 + i, neighbour("chip", hop))
        for i, (source, hop) in enumerate(((part_1, 1), (part_3, 3)))
    ]
    for copy in passes:
        copy.start()

    def width_of(b):
        return sum(hi - lo for _, lo, hi in blocks[b])

    def core_copy(b):
        width = width_of(b)
        return remote(
            product.at[b % 2, :, span((1 - core) * piece, piece), pl.ds(0, width)],
            pair.at[b, :, :, pl.ds(0, width)],
            core_sems,
            b,
            neighbour("core", 1),
        )

    def compute(b):
        if b >= 2:
            core_copy(b - 2).wait_send()
        for i in ready.get(b, ()):
            loads[i].wait()
        at = 0
        for name, lo, hi in blocks[b]:
            total = dot_tn(lefts[name][...], rights[name][:, lo:hi])
            if name == "log":
                total = total + dot_tn(gain_ref[...], unit_ref[...])
            product[b % 2, :, :, at : at + hi - lo] = total.astype(jnp.bfloat16).reshape(
                4 * chips, 2 * piece, hi - lo
            )
            at += hi - lo
        core_copy(b).start()

    def pair_rows(b):
        return pair.at[b].reshape(4 * quart, pair.shape[3])

    def first_copies(b):
        return halving_first(pair_rows(b), near.at[b], far.at[b], quart, halfway, xy_sems.at[b], 0)

    def second_copies(b):
        return halving_second(send.at[b], land.at[b], quart, halfway, xy_sems.at[b], 4)

    def chip_copies(b):
        copies = []
        for hop in range(1, chips):
            target = lax.rem(chip + hop, chips)
            copies.append(
                remote(
                    sums.at[b, span(target * piece, piece)],
                    last.at[b, hop - 1],
                    z_sems.at[b],
                    hop - 1,
                    neighbour("chip", hop),
                )
            )
        return copies

    def stage_1(b):
        core_copy(b).wait_recv()
        kept = product[b % 2, :, span(core * piece, piece), :].astype(jnp.float32)
        pair[b] = (kept + pair[b].astype(jnp.float32)).astype(jnp.bfloat16)
        for copy in first_copies(b):
            copy.start()

    def own_rows(b, owner, start):
        return as_f32(pair_rows(b), pl.multiple_of(flips()[owner] * quart + start, 16), halfway)

    def stage_2(b):
        for copy in first_copies(b):
            copy.wait()
        send[b, :halfway, :] = (own_rows(b, 2, 0) + as_f32(near.at[b], halfway, halfway)).astype(
            jnp.bfloat16
        )
        send[b, halfway:, :] = (own_rows(b, 1, halfway) + as_f32(far.at[b], halfway, halfway)).astype(
            jnp.bfloat16
        )
        for copy in second_copies(b):
            copy.start()

    def stage_3(b):
        for copy in second_copies(b):
            copy.wait()
        up = own_rows(b, 0, 0) + as_f32(near.at[b], 0, halfway) + as_f32(land.at[b], 0, halfway)
        down = own_rows(b, 0, halfway) + as_f32(far.at[b], 0, halfway)
        down = down + as_f32(land.at[b], halfway, halfway)
        sums[b, :halfway, :] = up.astype(jnp.bfloat16)
        sums[b, halfway:, :] = down.astype(jnp.bfloat16)
        for copy in chip_copies(b):
            copy.start()

    def stage_4(b):
        for copy in chip_copies(b):
            copy.wait()
        total = sums[b, span(chip * piece, piece), :].astype(jnp.float32)
        for hop in range(chips - 1):
            total = total + last[b, hop].astype(jnp.float32)
        start = sum(width_of(i) for i in range(b))
        dense_ref[:, start : start + width_of(b)] = total[:, : width_of(b)]

    def spread_1():
        return spread_first(quarter, whole_any, part, cut, link, 1)

    def spread_2():
        return spread_second(quarter, whole_any, part, cut, link, 3)

    mine = lax.axis_index("dp")
    keep = pltpu.make_async_copy(quarter, whole_any.at[span(mine * part, part)], local_sem)
    count = len(blocks)
    compute(0)
    compute(1)
    for b in range(count):
        stage_1(b)
        if b + 2 < count:
            compute(b + 2)
    for copy in passes:
        copy.wait()
    quarter[...] = sum(
        ref[...].astype(jnp.float32) for ref in (part_0, got_2, came.at[0], came.at[1])
    ).astype(jnp.bfloat16)
    keep.start()
    for copy in spread_1():
        copy.start()
    for b in range(count):
        stage_2(b)
    for copy in spread_1():
        copy.wait()
    for copy in spread_2():
        copy.start()
    for b in range(count):
        stage_3(b)
    for b in range(count):
        stage_4(b)
    for copy in spread_2():
        copy.wait()
    keep.wait()
    for b in range(max(0, count - 2), count):
        core_copy(b).wait_send()


def tail(part_1, part_3, part_0, got_2, dy, x, normed, gain_rows, mixed, dval, dlog, dqk, unit, shape, chips):
    rows, model = x.shape
    part = shape[0] // 4
    cut = part // 32 * 16
    wide, narrow = mixed.shape[1], dqk.shape[1]
    narrow_one = narrow // 2
    half = wide // 2
    blocks = [
        [("out", 0, half)],
        [("out", half, wide)],
        [("val", 0, half)],
        [("val", half, wide)],
        [("log", 0, LANE), ("qk", 0, narrow)],
    ]
    width = max(half, LANE + narrow)
    total = 2 * wide + LANE + narrow
    count = len(blocks)
    piece = model // 4 // chips // 2
    quart = chips * piece
    bf16 = lambda *shape: pltpu.VMEM(shape, jnp.bfloat16)
    dma = lambda *shape: pltpu.SemaphoreType.DMA(shape)
    vmem = pl.BlockSpec(memory_space=pltpu.VMEM)
    return pl.pallas_call(
        functools.partial(tail_body, blocks, chips, part, cut),
        in_specs=[ANYWHERE] * 2 + [vmem] * 5 + [ANYWHERE] * 6,
        out_specs=[vmem, ANYWHERE],
        out_shape=[
            jax.ShapeDtypeStruct((piece, total), jnp.float32),
            jax.ShapeDtypeStruct(shape, jnp.bfloat16),
        ],
        scratch_shapes=[
            bf16(2, part, model),
            bf16(part, model),
            bf16(2, 4 * chips, 2 * piece, width),
            bf16(count, 4 * chips, piece, width),
            bf16(count, quart, width),
            bf16(count, quart, width),
            bf16(count, quart, width),
            bf16(count, quart, width),
            bf16(count, quart, width),
            bf16(count, chips - 1, piece, width),
            dma(2, 9),
            dma(2, count),
            dma(count, 2, 6),
            dma(count, 2, chips - 1),
            dma(),
            bf16(rows, model),
            bf16(rows, wide),
            bf16(rows, model),
            bf16(rows, wide),
            bf16(rows, model),
            bf16(rows, 2 * narrow_one),
            dma(7),
        ],
        compiler_params=pltpu.CompilerParams(
            vmem_limit_bytes=VMEM_BYTES, collective_id=7, has_side_effects=True
        ),
        cost_estimate=pl.CostEstimate(
            flops=2 * rows * model * total, bytes_accessed=20 << 20, transcendentals=0
        ),
    )(part_1, part_3, part_0, got_2, gain_rows, dlog, unit, dy, mixed, x, dval, normed, dqk)


def experts_body(exp_local, ff_dim, tile, steps, chips, ahead, *refs):
    (
        own_any,
        third_any,
        first_any,
        x_own,
        x_far,
        c_own,
        c_far,
        mask_ref,
        digit_ref,
        grad_own,
        out_own,
        grad_far,
        out_far,
        grad_1,
        part_0,
        part_3,
        part_2,
        w_all,
        x_ref,
        c_ref,
        grad_acc,
        out_acc,
        act_all,
        dpre_all,
        g_ref,
        given,
        near,
        far,
        send,
        land,
        load_sem,
        local_sem,
        chip_sems,
        spread_sems,
        halve_sems,
        tile_sems,
    ) = refs
    wide = exp_local * ff_dim
    back = wide + ROUTER_ROWS
    half = steps // 2
    part = g_ref.shape[0] // 4
    cut = part // 32 * 16
    step = pl.program_id(0)
    turn_of, index = lax.div(step, steps), lax.rem(step, steps)
    mine = span(lax.axis_index("dp") * part, part)
    partner = neighbour("core", 1)

    quarter_2 = remote(
        own_any.at[mine], w_all.at[2, mine], chip_sems, 0, neighbour("chip", -2)
    )
    near_rows = remote(
        own_any.at[pl.ds(ahead, 4 * part - ahead)],
        w_all.at[3, pl.ds(ahead, 4 * part - ahead)],
        chip_sems,
        1,
        neighbour("chip", -1),
    )
    load_own = pltpu.make_async_copy(own_any, w_all.at[0], local_sem.at[0])
    load_third = pltpu.make_async_copy(third_any.at[mine], w_all.at[1, mine], local_sem.at[1])
    load_first = pltpu.make_async_copy(
        first_any.at[pl.ds(0, ahead)], w_all.at[3, pl.ds(0, ahead)], local_sem.at[2]
    )
    spread_3 = Spreading(w_all.at[1], part, cut, spread_sems.at[0], third_any.at[mine])
    spread_2 = Spreading(w_all.at[2], part, cut, spread_sems.at[1], w_all.at[2, mine])
    halvings = [
        Halving(
            g_ref,
            total,
            (near.at[i % 2], far.at[i % 2], send.at[i % 2], land.at[i % 2], halve_sems.at[i]),
            part,
            cut,
        )
        for i, total in enumerate((part_0, part_3, part_2))
    ]

    def load(at, kind):
        source = ((x_own, x_far), (c_own, c_far))[kind][at // half]
        return pltpu.make_async_copy(
            source.at[pl.ds(at % half * tile, tile)],
            (x_ref, c_ref)[kind].at[pl.ds(at * tile, tile)],
            load_sem.at[kind, at],
        )

    def tile_copy(at, kind):
        rows = pl.ds(at * tile, tile)
        source = (given.at[rows], out_acc.at[pl.ds((half + at) * tile, tile)])[kind]
        return remote(source, (grad_far, out_far)[kind].at[rows], tile_sems.at[kind], at, partner)

    def store(kind):
        rows = pl.ds(0, half * tile)
        source = (grad_acc, out_acc)[kind].at[rows]
        return pltpu.make_async_copy(source, (grad_own, out_own)[kind], local_sem.at[3 + kind])

    store_grad = pltpu.make_async_copy(g_ref, grad_1, local_sem.at[5])

    def when(at):
        return pl.when(step == at)

    @when(0)
    def _():
        load_own.start()
        for at in range(steps):
            for kind in range(2):
                load(at, kind).start()
        load_third.start()
        load_first.start()
        peers = [partner, neighbour("dp", 1), neighbour("dp", 2)]
        greet(peers + [neighbour("chip", hop) for hop in range(1, chips)])
        spread_3.start()
        quarter_2.start()
        load_own.wait()

    @when(half)
    def _():
        spread_3.turn()

    @when(steps)
    def _():
        load_third.wait()
        spread_3.finish()

    @when(steps + half - 1)
    def _():
        quarter_2.wait()
        spread_2.start()
        near_rows.start()

    @when(2 * steps - 2)
    def _():
        spread_2.turn()

    @when(2 * steps - 1)
    def _():
        halvings[0].turn()

    @when(2 * steps)
    def _():
        spread_2.finish()

    @when(2 * steps + half - 1)
    def _():
        halvings[0].finish()

    @when(3 * steps - 1)
    def _():
        halvings[1].turn()

    @when(3 * steps)
    def _():
        load_first.wait()
        near_rows.wait()

    @when(3 * steps + half - 1)
    def _():
        halvings[1].finish()

    @when(4 * steps - 2)
    def _():
        halvings[2].turn()

    for at in range(steps):

        @when(at)
        def _(at=at):
            for kind in range(2):
                load(at, kind).wait()

    final = lax.div(turn_of, chips - 1)
    place = lax.rem(index + half * final, steps)
    rows = tile_rows(place, tile)
    x, c = x_ref[rows, :], c_ref[rows, :]
    sig = 1.0 / (1.0 + jnp.exp(-dot_nt(x, w_all[turn_of, wide:back, :])))
    gate = sig * mask_ref[:, :ROUTER_ROWS].astype(jnp.float32)
    lanes = lax.broadcasted_iota(jnp.int32, (tile, ROUTER_ROWS), 1)
    dgate = jnp.zeros((tile, ROUTER_ROWS), jnp.float32)
    for pair in range(exp_local // 2):
        lo, hi = 2 * pair * ff_dim, 2 * (pair + 1) * ff_dim
        pre_two = dot_nt(x, w_all[turn_of, lo:hi, :])
        raw_two = dot_nt(c, w_all[turn_of, back + lo : back + hi, :])
        for side in range(2):
            e = 2 * pair + side
            pre = pre_two[:, side * ff_dim : (side + 1) * ff_dim]
            raw = raw_two[:, side * ff_dim : (side + 1) * ff_dim]
            square = pre * pre
            bend = jnp.tanh(pre * (GELU_A + GELU_A * GELU_B * square))
            upper = 0.5 * bend + 0.5
            act = (pre * upper).astype(jnp.bfloat16).astype(jnp.float32)
            slope = upper + (0.5 * pre) * (1.0 - bend * bend) * (GELU_A + 3 * GELU_A * GELU_B * square)
            gate_col = gate[:, e : e + 1]
            act_all[rows, e * ff_dim : (e + 1) * ff_dim] = (gate_col * act).astype(jnp.bfloat16)
            dpre_all[rows, e * ff_dim : (e + 1) * ff_dim] = (gate_col * raw * slope).astype(
                jnp.bfloat16
            )
            dgate = jnp.where(lanes == e, jnp.sum(act * raw, axis=1, keepdims=True), dgate)
    dpre_all[rows, wide:back] = (dgate * gate * (1.0 - sig)).astype(jnp.bfloat16)
    out_new = dot_nn(act_all[rows, :], w_all[turn_of, back:, :])
    grad_new = dot_nn(dpre_all[rows, :], w_all[turn_of, :back, :])

    @pl.when(turn_of == 0)
    def _():
        out_acc[rows, :] = out_new.astype(jnp.bfloat16)
        grad_acc[rows, :] = grad_new

    @pl.when(turn_of > 0)
    def _():
        out_acc[rows, :] = (out_acc[rows, :].astype(jnp.float32) + out_new).astype(jnp.bfloat16)
        grad_acc[rows, :] += grad_new

    for at in range(half):

        @when((chips - 1) * steps + at)
        def _(at=at):
            given[at * tile : (at + 1) * tile, :] = grad_acc[
                (half + at) * tile : (half + at + 1) * tile, :
            ].astype(jnp.bfloat16)
            tile_copy(at, 0).start()
            tile_copy(at, 1).start()

    @pl.when(index == steps - 1)
    def _():
        for lo in range(0, wide, 2 * ff_dim):
            g_ref[lo : lo + 2 * ff_dim, :] = dot_tn(
                dpre_all[:, lo : lo + 2 * ff_dim], x_ref[...]
            ).astype(jnp.bfloat16)
            g_ref[back + lo : back + lo + 2 * ff_dim, :] = dot_tn(
                act_all[:, lo : lo + 2 * ff_dim], c_ref[...]
            ).astype(jnp.bfloat16)
        extra = dot_tn(dpre_all[:, wide:back], x_ref[...])
        g_ref[wide:back, :LANE] = (extra[:, :LANE] + digit_ref[...]).astype(jnp.bfloat16)
        g_ref[wide:back, LANE:] = extra[:, LANE:].astype(jnp.bfloat16)

    for i in range(chips - 1):

        @when((i + 1) * steps - 1)
        def _(i=i):
            halvings[i].start()

    @when(chips * steps - 1)
    def _():
        store_grad.start()
        store(0).start()
        store(1).start()
        halvings[2].finish()
        for at in range(half):
            tile_copy(at, 0).wait()
            tile_copy(at, 1).wait()
        store_grad.wait()
        store(0).wait()
        store(1).wait()


def experts(own, third, first, tokens, masks, digits, exp_local, ff_dim, ahead, chips, tile):
    rows, model = 2 * tokens[0].shape[0], tokens[0].shape[1]
    steps = rows // tile
    half = steps // 2
    wide = exp_local * ff_dim
    part = own.shape[0] // 4
    cut = part // 32 * 16

    def mask_block(step):
        turn_of, index = lax.div(step, steps), lax.rem(step, steps)
        place = lax.rem(index + half * lax.div(turn_of, chips - 1), steps)
        return (place, lax.rem(chips - turn_of, chips))

    def digit_block(step):
        return (0, lax.rem(chips - lax.div(step, steps), chips))

    bf16 = lambda *shape: pltpu.VMEM(shape, jnp.bfloat16)
    dma = lambda *shape: pltpu.SemaphoreType.DMA(shape)
    full = lambda count, kind: jax.ShapeDtypeStruct((count, model), kind)
    return pl.pallas_call(
        functools.partial(experts_body, exp_local, ff_dim, tile, steps, chips, ahead),
        grid=(chips * steps,),
        in_specs=[ANYWHERE] * 7
        + [pl.BlockSpec((tile, LANE), mask_block), pl.BlockSpec((ROUTER_ROWS, LANE), digit_block)],
        out_specs=[ANYWHERE] * 5 + [whole_block((part, model))] * 3,
        out_shape=[
            full(rows // 2, jnp.float32),
            full(rows // 2, jnp.bfloat16),
            full(rows // 2, jnp.bfloat16),
            full(rows // 2, jnp.bfloat16),
            full(4 * part, jnp.bfloat16),
            full(part, jnp.bfloat16),
            full(part, jnp.bfloat16),
            full(part, jnp.bfloat16),
        ],
        scratch_shapes=[
            bf16(chips, 4 * part, model),
            bf16(rows, model),
            bf16(rows, model),
            pltpu.VMEM((rows, model), jnp.float32),
            bf16(rows, model),
            bf16(rows, wide),
            bf16(rows, wide + ROUTER_ROWS),
            bf16(4 * part, model),
            bf16(rows // 2, model),
            bf16(2, 2 * cut, model),
            bf16(2, 2 * (part - cut), model),
            bf16(2, part, model),
            bf16(2, part, model),
            dma(2, steps),
            dma(6),
            dma(2, 2),
            dma(2, 2, 6),
            dma(chips - 1, 2, 6),
            dma(2, 2, half),
        ],
        compiler_params=pltpu.CompilerParams(
            vmem_limit_bytes=VMEM_BYTES, collective_id=2, has_side_effects=True
        ),
        cost_estimate=pl.CostEstimate(
            flops=12 * chips * rows * model * wide, bytes_accessed=40 << 20, transcendentals=rows * wide
        ),
    )(own, third, first, *tokens, masks, digits)


def core_swap(arr):
    size = lax.axis_size("expert")
    return lax.ppermute(arr, "expert", [(i, i ^ 1) for i in range(size)])


def row_part(arr, index, count):
    return lax.dynamic_slice_in_dim(arr, index * (arr.shape[0] // count), arr.shape[0] // count, 0)


def own_weights(w_router, w_in, w_out):
    exp_local, model_dim, ff_dim = w_in.shape
    router_rows = jnp.zeros((ROUTER_ROWS, model_dim), jnp.bfloat16).at[:exp_local].set(w_router)
    return jnp.concatenate(
        [
            jnp.swapaxes(w_in, 1, 2).reshape(exp_local * ff_dim, model_dim),
            router_rows,
            w_out.reshape(exp_local * ff_dim, model_dim),
        ]
    )


def block_dense(
    layer_input,
    segments,
    keep_mask,
    att_routes,
    moe_routes,
    expert_counts,
    norm_gain,
    w_query,
    w_key,
    w_select,
    w_value,
    w_output,
    w_router,
    w_in,
    w_out,
    cotangent,
):
    rows, model = layer_input.shape
    seqs, seq_len = segments.shape
    exp_local, _, ff_dim = w_in.shape
    heads = w_query.shape[1] // DH
    chips = lax.axis_size("expert") // 2
    wide, narrow, gates = heads * VEXP * DH, heads * DH, 2 * heads * VEXP
    moe_wide = exp_local * ff_dim
    mine = lax.axis_index("expert")
    chip, core = mine // 2, mine % 2

    own = own_weights(w_router, w_in, w_out)
    exp_total = 2 * chips * exp_local
    named = jnp.sum(
        (moe_routes[..., None] == jnp.arange(exp_total, dtype=jnp.int32)).astype(jnp.bfloat16), axis=1
    )
    named = jnp.concatenate([named, core_swap(named)])

    column = jnp.arange(seq_len, dtype=jnp.int32)
    changed = jnp.concatenate(
        [jnp.ones((seqs, 1), jnp.bool_), segments[:, 1:] != segments[:, :-1]], axis=1
    )
    start = lax.cummax(jnp.where(changed, column, 0), axis=1)
    cos_tab, sin_tab = rope_tables((column - start).reshape(-1), DH)
    cos_two = jnp.concatenate([cos_tab, cos_tab], axis=1)
    sin_two = jnp.concatenate([-sin_tab, sin_tab], axis=1)
    start = (start + seq_len * jnp.arange(seqs, dtype=jnp.int32)[:, None]).reshape(rows, 1)
    keep = keep_mask.reshape(1, rows)
    att_mask = jnp.sum(
        (att_routes[..., None] == jnp.arange(VEXP, dtype=jnp.int32)).astype(jnp.bfloat16), axis=2
    ).reshape(rows, gates)
    att_mask = jnp.pad(att_mask, ((0, 0), (0, LANE - gates)))
    gain_row = norm_gain.reshape(1, model)
    wsel = jnp.pad(w_select, ((0, 0), (0, LANE - gates)))

    shape = own.shape
    part = shape[0] // 4
    ahead = part // 80 * 64
    third, first, cot_far, sent_far, hidden, normed, q_rot, k_rot, value_bf, value_all, attended, sig, lse, mixed, sent = (
        attention_forward(
            ahead, own, cotangent, layer_input, start, keep, cos_two, sin_two, att_mask, gain_row, wsel, w_query, w_key,
            w_value, w_output, TILE,
        )
    )

    lane = jnp.arange(chips * LANE, dtype=jnp.int32)
    owner = ((chip + lane // LANE) % chips * 2 + core) * exp_local + lane % LANE
    pick = (lane % LANE < exp_local) & (jnp.arange(exp_total, dtype=jnp.int32)[:, None] == owner)
    masks = jnp.dot(named, pick.astype(jnp.bfloat16), preferred_element_type=jnp.float32)
    counts = jnp.sum(masks, axis=0).astype(jnp.int32)
    masks = masks.astype(jnp.bfloat16)
    place = jnp.arange(ROUTER_ROWS, dtype=jnp.int32)[:, None] - exp_local
    digits = jnp.where(
        (place >= 0) & (place < DIGITS), (counts >> (2 * jnp.clip(place, 0, DIGITS))) & 3, 0
    ).astype(jnp.float32)

    grad_own, out_own, grad_far, out_far, grad_1, part_0, part_3, part_2 = experts(
        own, third, first, (sent, sent_far, cotangent, cot_far), masks, digits, exp_local, ff_dim, ahead, chips, TILE
    )
    layer_output = hidden + out_own.astype(jnp.float32) + out_far.astype(jnp.float32)
    layer_output = layer_output.astype(jnp.bfloat16)
    got_2, grad_input, dqk, dval, dlog, gain_rows, dy, part_1 = attention_backward(
        [grad_1, part_2],
        [(part, model)],
        shift_move(1, 0, 2, fixed(0), fixed(0), part),
        (0,),
        part,
        cotangent, grad_own, grad_far, q_rot, k_rot, value_bf, attended, lse, start, keep, sig, att_mask, cos_two,
        sin_two, layer_input, value_all, gain_row, wsel, w_output, w_query, w_key, w_value, TILE,
    )
    unit = (
        (jnp.arange(GAIN_ROWS)[:, None] < 2) & (jnp.arange(LANE)[None, :] == gates)
    ).astype(jnp.bfloat16)
    dense, summed = tail(
        part_1, part_3, part_0, got_2, dy, layer_input, normed, gain_rows, mixed, dval, dlog, dqk, unit, shape, chips
    )
    out_sum, dense = dense[:, :wide].T, dense[:, wide:]
    grad_w_in = jnp.swapaxes(
        summed[:moe_wide].astype(jnp.float32).reshape(exp_local, ff_dim, model), 1, 2
    )
    extra = summed[moe_wide : moe_wide + ROUTER_ROWS].astype(jnp.float32)
    grad_router = extra[:exp_local]
    parts = extra[exp_local : exp_local + DIGITS, :exp_local].astype(jnp.int32)
    tally = sum(parts[i] << (2 * i) for i in range(DIGITS))
    grad_w_out = (
        summed[moe_wide + ROUTER_ROWS :].astype(jnp.float32).reshape(exp_local, ff_dim, model)
    )
    at_qk = wide + LANE
    return (
        layer_output,
        grad_input,
        dense[:, wide + gates],
        dense[:, at_qk : at_qk + narrow],
        dense[:, at_qk + narrow : at_qk + 2 * narrow],
        dense[:, wide : wide + gates],
        dense[:, :wide],
        out_sum,
        grad_router,
        grad_w_in,
        grad_w_out,
        expert_counts + tally,
    )


def block_dispatched(
    layer_input,
    segments,
    keep_mask,
    att_routes,
    moe_routes,
    expert_counts,
    norm_gain,
    w_query,
    w_key,
    w_select,
    w_value,
    w_output,
    w_router,
    w_in,
    w_out,
    cotangent,
):
    tok_rows, model_dim = layer_input.shape
    seq_count, seq_len = segments.shape
    head_count = w_query.shape[1] // DH
    score_scale = DH ** (-0.5)
    inputs_f = layer_input.astype(jnp.float32)
    normed, norm_pull = jax.vjp(layer_norm, inputs_f, norm_gain)
    normed_bf = normed.astype(jnp.bfloat16)
    query_rows = jnp.dot(normed_bf, w_query, preferred_element_type=jnp.float32).reshape(
        tok_rows, head_count, DH
    )
    key_rows = jnp.dot(normed_bf, w_key, preferred_element_type=jnp.float32).reshape(
        tok_rows, head_count, DH
    )
    logits = jnp.dot(layer_input, w_select, preferred_element_type=jnp.float32)
    named_mask = jnp.sum(
        (att_routes[..., None] == jnp.arange(VEXP, dtype=jnp.int32)).astype(jnp.float32), axis=2
    )
    select_sig = jax.nn.sigmoid(logits).reshape(tok_rows, 2 * head_count, VEXP)
    head_gates = select_sig * named_mask
    value_all = jnp.dot(layer_input, w_value, preferred_element_type=jnp.float32).reshape(
        tok_rows, head_count, VEXP, DH
    )
    value_bf = jnp.sum(head_gates[:, :head_count, :, None] * value_all, axis=2).astype(jnp.bfloat16)
    position, allowed = jax.vmap(doc_layout)(segments, keep_mask)
    cos_tab, sin_tab = rope_tables(position.reshape(-1), DH)
    q_rot = (rotate(query_rows, cos_tab, sin_tab) * score_scale).astype(jnp.bfloat16)
    k_rot = rotate(key_rows, cos_tab, sin_tab).astype(jnp.bfloat16)
    seq_shape = (seq_count, seq_len, head_count, DH)
    attended, log_total = lax.map(
        attend_forward,
        (q_rot.reshape(seq_shape), k_rot.reshape(seq_shape), value_bf.reshape(seq_shape), allowed),
    )
    attended = attended.reshape(tok_rows, head_count, DH)
    mixed_bf = (
        (head_gates[:, head_count:, :, None] * attended[:, :, None, :])
        .astype(jnp.bfloat16)
        .reshape(tok_rows, head_count * VEXP * DH)
    )
    hidden = inputs_f + jnp.dot(mixed_bf, w_output, preferred_element_type=jnp.float32)
    dev_count = lax.axis_size("expert")
    exp_local = w_in.shape[0]
    exp_total = dev_count * exp_local
    top_k = moe_routes.shape[1]
    capacity = 10 * tok_rows * top_k // (7 * exp_total) + 1
    owner, filled, slot_of = slot_table(moe_routes, exp_total, capacity)
    keep_slot = filled[:, None] > 0
    zero_bf = jnp.zeros((), jnp.bfloat16)
    hidden_bf = hidden.astype(jnp.bfloat16)
    send_rows = jnp.where(keep_slot, hidden_bf[owner], zero_bf).reshape(
        dev_count, exp_local * capacity, model_dim
    )
    rows_in = lax.all_to_all(send_rows, "expert", split_axis=0, concat_axis=0, tiled=True)
    histogram = jnp.zeros((exp_total,), jnp.float32).at[moe_routes.reshape(-1)].add(1.0)
    tally = lax.psum_scatter(histogram, "expert", scatter_dimension=0, tiled=True)
    slot_shape = (dev_count, exp_local, capacity, model_dim)
    rows_four = rows_in.reshape(slot_shape)
    pre_act = jnp.einsum("necd,edf->necf", rows_four, w_in, preferred_element_type=jnp.float32)
    gelu_out, gelu_pull = jax.vjp(jax.nn.gelu, pre_act)
    act_bf = gelu_out.astype(jnp.bfloat16)
    router_logit = jnp.einsum(
        "necd,ed->nec", rows_four, w_router, preferred_element_type=jnp.float32
    )
    gate_moe = jax.nn.sigmoid(router_logit)
    expert_out = jnp.einsum("necf,efd->necd", act_bf, w_out, preferred_element_type=jnp.float32)
    reply = (
        (gate_moe[..., None] * expert_out)
        .astype(jnp.bfloat16)
        .reshape(dev_count, exp_local * capacity, model_dim)
    )
    returned = lax.all_to_all(reply, "expert", split_axis=0, concat_axis=0, tiled=True)
    moe_sum = jnp.sum(returned.reshape(-1, model_dim)[slot_of].astype(jnp.float32), axis=1)
    layer_output = (hidden + moe_sum).astype(jnp.bfloat16)
    cot_f = cotangent.astype(jnp.float32)
    send_cot = jnp.where(keep_slot, cotangent[owner], zero_bf).reshape(
        dev_count, exp_local * capacity, model_dim
    )
    cot_in, rows_again = (
        lax.all_to_all(send_cot, "expert", split_axis=0, concat_axis=0, tiled=True),
        lax.all_to_all(send_rows, "expert", split_axis=0, concat_axis=0, tiled=True),
    )
    rows_grad = rows_again.reshape(slot_shape)
    cot_bf = cot_in.reshape(slot_shape)
    raw_back = jnp.einsum("necd,efd->necf", cot_bf, w_out, preferred_element_type=jnp.float32)
    dgate = jnp.sum(act_bf.astype(jnp.float32) * raw_back, axis=-1)
    dlogit = dgate * gate_moe * (1.0 - gate_moe)
    dexpert = (gate_moe[..., None] * cot_bf.astype(jnp.float32)).astype(jnp.bfloat16)
    grad_w_out = jnp.einsum("necf,necd->efd", act_bf, dexpert, preferred_element_type=jnp.float32)
    dact = jnp.einsum("necd,efd->necf", dexpert, w_out, preferred_element_type=jnp.float32)
    dpre_bf = gelu_pull(dact)[0].astype(jnp.bfloat16)
    grad_w_in = jnp.einsum("necd,necf->edf", rows_grad, dpre_bf, preferred_element_type=jnp.float32)
    grad_router = jnp.einsum(
        "nec,necd->ed",
        dlogit,
        rows_grad.astype(jnp.float32),
        preferred_element_type=jnp.float32,
        precision=HIGHEST,
    )
    dsent = jnp.einsum("necf,edf->necd", dpre_bf, w_in, preferred_element_type=jnp.float32)
    dsent = (dsent + dlogit[..., None] * w_router[None, :, None, :].astype(jnp.float32)).astype(
        jnp.bfloat16
    )
    grad_back = lax.all_to_all(
        dsent.reshape(dev_count, exp_local * capacity, model_dim),
        "expert",
        split_axis=0,
        concat_axis=0,
        tiled=True,
    )
    dhidden = cot_f + jnp.sum(grad_back.reshape(-1, model_dim)[slot_of].astype(jnp.float32), axis=1)
    dy_bf = dhidden.astype(jnp.bfloat16)
    grad_output = jnp.einsum("tk,td->kd", mixed_bf, dy_bf, preferred_element_type=jnp.float32)
    dmixed = jnp.einsum("td,kd->tk", dy_bf, w_output, preferred_element_type=jnp.float32).reshape(
        tok_rows, head_count, VEXP, DH
    )
    dgate_out = jnp.sum(dmixed * attended[:, :, None, :], axis=-1)
    dattend = jnp.sum(head_gates[:, head_count:, :, None] * dmixed, axis=2).astype(jnp.bfloat16)
    grad_q, grad_k, grad_v = lax.map(
        attend_backward,
        (
            q_rot.reshape(seq_shape),
            k_rot.reshape(seq_shape),
            value_bf.reshape(seq_shape),
            allowed,
            log_total,
            dattend.reshape(seq_shape),
        ),
    )
    dquery = (
        (rotate_back(grad_q.reshape(tok_rows, head_count, DH), cos_tab, sin_tab) * score_scale)
        .astype(jnp.bfloat16)
        .reshape(tok_rows, head_count * DH)
    )
    dkey = (
        rotate_back(grad_k.reshape(tok_rows, head_count, DH), cos_tab, sin_tab)
        .astype(jnp.bfloat16)
        .reshape(tok_rows, head_count * DH)
    )
    grad_query = jnp.einsum("td,tk->dk", normed_bf, dquery, preferred_element_type=jnp.float32)
    grad_key = jnp.einsum("td,tk->dk", normed_bf, dkey, preferred_element_type=jnp.float32)
    dnormed = jnp.einsum(
        "tk,dk->td", dquery, w_query, preferred_element_type=jnp.float32
    ) + jnp.einsum("tk,dk->td", dkey, w_key, preferred_element_type=jnp.float32)
    dx_norm, grad_gain = norm_pull(dnormed)
    dvalue = grad_v.reshape(tok_rows, head_count, DH)
    dgate_val = jnp.sum(dvalue[:, :, None, :] * value_all, axis=-1)
    dvalue_all = (
        (head_gates[:, :head_count, :, None] * dvalue[:, :, None, :])
        .astype(jnp.bfloat16)
        .reshape(tok_rows, head_count * VEXP * DH)
    )
    grad_value = jnp.einsum(
        "td,tk->dk", layer_input, dvalue_all, preferred_element_type=jnp.float32
    )
    dgates = jnp.concatenate([dgate_val, dgate_out], axis=1)
    dlogits = (
        (dgates * named_mask * select_sig * (1.0 - select_sig))
        .astype(jnp.bfloat16)
        .reshape(tok_rows, 2 * head_count * VEXP)
    )
    grad_select = jnp.einsum("td,tk->dk", layer_input, dlogits, preferred_element_type=jnp.float32)
    grad_input = (
        dhidden
        + dx_norm
        + jnp.einsum("tk,dk->td", dvalue_all, w_value, preferred_element_type=jnp.float32)
    )
    grad_input = (
        grad_input + jnp.einsum("tk,dk->td", dlogits, w_select, preferred_element_type=jnp.float32)
    ).astype(jnp.bfloat16)
    expert_sums = (
        lax.psum(grad_w_in.astype(jnp.bfloat16), "dp").astype(jnp.float32),
        lax.psum(grad_w_out.astype(jnp.bfloat16), "dp").astype(jnp.float32),
        lax.psum(grad_router.astype(jnp.bfloat16), "dp").astype(jnp.float32),
        lax.psum(tally.astype(jnp.bfloat16), "dp").astype(jnp.float32),
    )
    dense_sums = (
        lax.psum_scatter(grad_gain, ("dp", "expert"), scatter_dimension=0, tiled=True),
        lax.psum_scatter(grad_query, ("dp", "expert"), scatter_dimension=0, tiled=True),
        lax.psum_scatter(grad_key, ("dp", "expert"), scatter_dimension=0, tiled=True),
        lax.psum_scatter(grad_select, ("dp", "expert"), scatter_dimension=0, tiled=True),
        lax.psum_scatter(grad_value, ("dp", "expert"), scatter_dimension=0, tiled=True),
        lax.psum_scatter(grad_output, ("dp", "expert"), scatter_dimension=1, tiled=True),
    )
    counts_out = expert_counts + expert_sums[3].astype(jnp.int32)
    return (
        layer_output,
        grad_input,
        dense_sums[0],
        dense_sums[1],
        dense_sums[2],
        dense_sums[3],
        dense_sums[4],
        dense_sums[5],
        expert_sums[2],
        expert_sums[0],
        expert_sums[1],
        counts_out,
    )


def local(*args):
    rows, top_k = args[4].shape
    experts, _, ff_dim = args[13].shape
    exp_total = lax.axis_size("expert") * experts
    capacity = 10 * rows * top_k // (7 * exp_total) + 1
    regular = lax.axis_size("dp") == 4 and lax.axis_size("expert") == 8 and experts % 2 == 0 and ff_dim == LANE
    return (block_dense if regular and 4 * capacity > rows else block_dispatched)(*args)


def solution(mesh):
    placed = (
        P(("dp", "expert"), None),
        P(("dp", "expert"), None),
        P(("dp", "expert"), None),
        P(("dp", "expert"), None, None),
        P(("dp", "expert"), None),
        P("expert"),
        P(),
        P(),
        P(),
        P(),
        P(),
        P(),
        P("expert", None),
        P("expert", None, None),
        P("expert", None, None),
        P(("dp", "expert"), None),
    )
    return jax.shard_map(
        local,
        mesh=mesh,
        in_specs=placed,
        out_specs=(
            P(("dp", "expert"), None),
            P(("dp", "expert"), None),
            P(("dp", "expert")),
            P(("dp", "expert"), None),
            P(("dp", "expert"), None),
            P(("dp", "expert"), None),
            P(("dp", "expert"), None),
            P(None, ("dp", "expert")),
            P("expert", None),
            P("expert", None, None),
            P("expert", None, None),
            P("expert"),
        ),
        check_vma=False,
    )
```

```python
import functools

import jax
import jax.numpy as jnp
from jax import lax
from jax.experimental import pallas as pl
from jax.experimental.pallas import tpu as pltpu
from jax.sharding import PartitionSpec as P

DH = 128
VEXP = 5


NORM_EPS = 1e-05
ROPE_BASE = 10000.0
MASK_FILL = -1e30
HIGHEST = lax.Precision.HIGHEST
ROUTER_ROWS = 64
DIGITS = 5
LANE = 128
GAIN_ROWS = 16
TILE = 256
VMEM_BYTES = 60 << 20
GELU_A = 0.7978845608028654
GELU_B = 0.044715


def layer_norm(values, gain_vec):
    center = values - jnp.mean(values, axis=-1, keepdims=True)
    spread = jnp.mean(center * center, axis=-1, keepdims=True)
    return center * lax.rsqrt(spread + NORM_EPS) * gain_vec


def rope_tables(position, width_dh):
    half_dh = width_dh // 2
    freq_row = jnp.power(ROPE_BASE, jnp.arange(half_dh, dtype=jnp.float32) * (-2.0 / width_dh))
    angle_tab = position.astype(jnp.float32)[:, None] * freq_row[None, :]
    return (jnp.cos(angle_tab), jnp.sin(angle_tab))


def rotate(values, cos_tab, sin_tab):
    half_dh = values.shape[-1] // 2
    first_half = values[..., :half_dh]
    second_half = values[..., half_dh:]
    cos_b = cos_tab[:, None, :]
    sin_b = sin_tab[:, None, :]
    return jnp.concatenate(
        [first_half * cos_b - second_half * sin_b, second_half * cos_b + first_half * sin_b],
        axis=-1,
    )


def rotate_back(grad_rot, cos_tab, sin_tab):
    half_dh = grad_rot.shape[-1] // 2
    grad_first = grad_rot[..., :half_dh]
    grad_second = grad_rot[..., half_dh:]
    cos_b = cos_tab[:, None, :]
    sin_b = sin_tab[:, None, :]
    return jnp.concatenate(
        [grad_first * cos_b + grad_second * sin_b, grad_second * cos_b - grad_first * sin_b],
        axis=-1,
    )


def doc_layout(seg_row, keep_row):
    length_s = seg_row.shape[0]
    column = jnp.arange(length_s, dtype=jnp.int32)
    new_doc = jnp.concatenate([jnp.ones((1,), dtype=jnp.bool_), seg_row[1:] != seg_row[:-1]])
    doc_start = lax.cummax(jnp.where(new_doc, column, jnp.zeros_like(column)), axis=0)
    position = column - doc_start
    same_doc = seg_row[:, None] == seg_row[None, :]
    causal = column[None, :] <= column[:, None]
    visible = (keep_row[None, :] == 1) | (column[None, :] == column[:, None])
    return (position, same_doc & causal & visible)


def slot_table(routes, exp_total, capacity):
    flat_ids = routes.reshape(-1)
    pair_count = flat_ids.shape[0]
    top_k = routes.shape[1]
    sort_order = jnp.argsort(flat_ids, stable=True)
    ranked = flat_ids[sort_order]
    first_slot = jnp.searchsorted(ranked, jnp.arange(exp_total, dtype=jnp.int32), side="left")
    slot_rank = jnp.arange(pair_count, dtype=jnp.int32) - first_slot[ranked]
    slot_dest = ranked * capacity + slot_rank
    owner = jnp.zeros((exp_total * capacity,), jnp.int32).at[slot_dest].set(sort_order // top_k)
    filled = jnp.zeros((exp_total * capacity,), jnp.float32).at[slot_dest].set(1.0)
    slot_of = (
        jnp.zeros((pair_count,), jnp.int32).at[sort_order].set(slot_dest).reshape(routes.shape)
    )
    return (owner, filled, slot_of)


def block_scores(q_blk, k_rows, allowed_blk):
    scores = jnp.einsum("qhd,khd->hqk", q_blk, k_rows, preferred_element_type=jnp.float32)
    return jnp.where(allowed_blk[None, :, :], scores, MASK_FILL)


def attend_forward(pieces):
    q_rows, k_rows, v_rows, allowed = pieces
    length_s = q_rows.shape[0]
    block_len = min(512, length_s)
    outs_list = []
    lse_list = []
    for begin_at in range(0, length_s, block_len):
        scores = block_scores(
            q_rows[begin_at : begin_at + block_len],
            k_rows,
            allowed[begin_at : begin_at + block_len],
        )
        row_max = jnp.max(scores, axis=-1, keepdims=True)
        exp_terms = jnp.exp(scores - row_max)
        row_sum = jnp.sum(exp_terms, axis=-1, keepdims=True)
        probs_bf = (exp_terms / row_sum).astype(jnp.bfloat16)
        outs_list.append(
            jnp.einsum("hqk,khd->qhd", probs_bf, v_rows, preferred_element_type=jnp.float32)
        )
        lse_list.append((row_max + jnp.log(row_sum))[..., 0])
    return (jnp.concatenate(outs_list, axis=0), jnp.concatenate(lse_list, axis=1))


def attend_backward(pieces):
    q_rows, k_rows, v_rows, allowed, log_total, grad_rows = pieces
    length_s = q_rows.shape[0]
    block_len = min(512, length_s)
    grad_q_list = []
    grad_k = jnp.zeros(k_rows.shape, jnp.float32)
    grad_v = jnp.zeros(v_rows.shape, jnp.float32)
    for begin_at in range(0, length_s, block_len):
        q_blk = q_rows[begin_at : begin_at + block_len]
        grad_blk = grad_rows[begin_at : begin_at + block_len]
        scores = block_scores(q_blk, k_rows, allowed[begin_at : begin_at + block_len])
        probs_f = jnp.exp(scores - log_total[:, begin_at : begin_at + block_len, None])
        grad_prob = jnp.einsum("qhd,khd->hqk", grad_blk, v_rows, preferred_element_type=jnp.float32)
        grad_score = (
            probs_f * (grad_prob - jnp.sum(probs_f * grad_prob, axis=-1, keepdims=True))
        ).astype(jnp.bfloat16)
        grad_v = grad_v + jnp.einsum(
            "hqk,qhd->khd",
            probs_f.astype(jnp.bfloat16),
            grad_blk,
            preferred_element_type=jnp.float32,
        )
        grad_q_list.append(
            jnp.einsum("hqk,khd->qhd", grad_score, k_rows, preferred_element_type=jnp.float32)
        )
        grad_k = grad_k + jnp.einsum(
            "hqk,qhd->khd", grad_score, q_blk, preferred_element_type=jnp.float32
        )
    return (jnp.concatenate(grad_q_list, axis=0), grad_k, grad_v)


def dot_nt(left, right):
    return lax.dot_general(left, right, (((1,), (1,)), ((), ())), preferred_element_type=jnp.float32)


def dot_nn(left, right):
    return lax.dot_general(left, right, (((1,), (0,)), ((), ())), preferred_element_type=jnp.float32)


def dot_tn(left, right):
    return lax.dot_general(left, right, (((0,), (0,)), ((), ())), preferred_element_type=jnp.float32)


def spin(values, cos_two, sin_two):
    return values * cos_two + pltpu.roll(values, DH // 2, 1) * sin_two


def spin_back(values, cos_two, sin_two):
    return values * cos_two - pltpu.roll(values, DH // 2, 1) * sin_two


def window_mask(step, tile, start_col, keep_before, keep_now):
    row = step * tile + lax.broadcasted_iota(jnp.int32, (tile, 2 * tile), 0)
    col = (step - 1) * tile + lax.broadcasted_iota(jnp.int32, (tile, 2 * tile), 1)
    keep_row = jnp.concatenate([keep_before, keep_now], axis=1)
    return (col >= start_col) & (col <= row) & ((keep_row == 1) | (col == row))


def neighbour(kind, amount):
    mine, place = lax.axis_index("dp"), lax.axis_index("expert")
    chips = lax.axis_size("expert") // 2
    chip, core = place // 2, lax.rem(place, 2)
    if kind == "dp":
        flipped = [mine, mine + 1 - 2 * lax.rem(mine, 2), lax.rem(mine + 2, 4), 3 - mine]
        return (flipped[amount], place)
    if kind == "core":
        return (mine, place + 1 - 2 * core)
    return (mine, 2 * lax.rem(chip + amount + chips, chips) + core)


def own_part(rows):
    return lambda mine, flipped: mine * rows


def fixed(start):
    return lambda mine, flipped: start


def shift_move(src, dst, hop, src_at, dst_at, count):
    return [(src, dst, "chip", hop, src_at, dst_at, count)]


def greet(peers):
    barrier = pltpu.get_barrier_semaphore()
    for peer in peers:
        pl.semaphore_signal(barrier, inc=1, device_id=peer, device_id_type=pl.DeviceIdType.MESH)
    pl.semaphore_wait(barrier, len(peers))


def peers_of(moves):
    peers = []
    for _, _, kind, amount, _, _, _ in moves:
        peers.append(neighbour(kind, amount))
        if kind == "chip":
            peers.append(neighbour(kind, -amount))
    return peers


def copies_of(moves, ins, outs, send_sem, recv_sem):
    mine = lax.axis_index("dp")
    copies = []
    for i, (src, dst, kind, amount, src_at, dst_at, count) in enumerate(moves):
        peer = neighbour(kind, amount)
        copies.append(
            pltpu.make_async_remote_copy(
                src_ref=ins[src].at[pl.ds(pl.multiple_of(src_at(mine, peer[0]), 16), count)],
                dst_ref=outs[dst].at[pl.ds(pl.multiple_of(dst_at(mine, peer[0]), 16), count)],
                send_sem=send_sem.at[i],
                recv_sem=recv_sem.at[i],
                device_id=peer,
                device_id_type=pl.DeviceIdType.MESH,
            )
        )
    return copies


ANYWHERE = pl.BlockSpec(memory_space=pl.ANY)


def tile_rows(index, tile):
    return pl.ds(pl.multiple_of(index * tile, tile), tile)


def flips():
    mine = lax.axis_index("dp")
    return [mine, mine + 1 - 2 * lax.rem(mine, 2), lax.rem(mine + 2, 4), 3 - mine]


def remote(src, dst, sems, index, peer):
    return pltpu.make_async_remote_copy(
        src_ref=src,
        dst_ref=dst,
        send_sem=sems.at[0, index],
        recv_sem=sems.at[1, index],
        device_id=peer,
        device_id_type=pl.DeviceIdType.MESH,
    )


def span(start, count):
    return pl.ds(pl.multiple_of(start, 16), count)


def halving_first(source, near, far, part, cut, sems, at):
    dp = flips()
    low = part - cut
    copies = []
    for slot, owner in enumerate((1, 3)):
        copies.append(
            remote(
                source.at[span(dp[owner] * part, cut)],
                near.at[pl.ds(slot * cut, cut)],
                sems,
                at + slot,
                neighbour("dp", 1),
            )
        )
    for slot, owner in enumerate((2, 3)):
        copies.append(
            remote(
                source.at[span(dp[owner] * part + cut, low)],
                far.at[pl.ds(slot * low, low)],
                sems,
                at + 2 + slot,
                neighbour("dp", 2),
            )
        )
    return copies


def halving_second(send, land, part, cut, sems, at):
    low = part - cut
    return [
        remote(send.at[pl.ds(0, cut)], land.at[pl.ds(0, cut)], sems, at, neighbour("dp", 2)),
        remote(send.at[pl.ds(cut, low)], land.at[pl.ds(cut, low)], sems, at + 1, neighbour("dp", 1)),
    ]


def as_f32(ref, start, count):
    return ref[pl.ds(start, count), :].astype(jnp.float32)


def spread_first(source, target, part, cut, sems, at):
    mine = lax.axis_index("dp")
    return [
        remote(
            source.at[pl.ds(0, cut)],
            target.at[span(mine * part, cut)],
            sems,
            at,
            neighbour("dp", 1),
        ),
        remote(
            source.at[pl.ds(cut, part - cut)],
            target.at[span(mine * part + cut, part - cut)],
            sems,
            at + 1,
            neighbour("dp", 2),
        ),
    ]


def spread_second(source, target, part, cut, sems, at):
    dp = flips()
    low = part - cut
    mine_up, mine_down = span(dp[0] * part, cut), span(dp[0] * part + cut, low)
    got_up, got_down = span(dp[1] * part, cut), span(dp[2] * part + cut, low)
    return [
        remote(source.at[pl.ds(0, cut)], target.at[mine_up], sems, at, neighbour("dp", 2)),
        remote(target.at[got_up], target.at[got_up], sems, at + 1, neighbour("dp", 2)),
        remote(source.at[pl.ds(cut, low)], target.at[mine_down], sems, at + 2, neighbour("dp", 1)),
        remote(target.at[got_down], target.at[got_down], sems, at + 3, neighbour("dp", 1)),
    ]


def load_own(source, own, part, cut, sems):
    dp = flips()
    low = part - cut
    return [
        pltpu.make_async_copy(
            source.at[span(dp[owner] * part + start, count)], own.at[pl.ds(at, count)], sems.at[i]
        )
        for i, (owner, start, count, at) in enumerate(
            [(0, 0, cut, 0), (2, 0, cut, cut), (0, cut, low, 2 * cut), (1, cut, low, 2 * cut + low)]
        )
    ]


class Halving:
    def __init__(self, source, total, buffers, part, cut):
        near, far, send, land, sems = buffers[:5]
        self.source, self.total, self.part, self.cut = source, total, part, cut
        self.near, self.far, self.send, self.land = near, far, send, land
        self.own, self.loads = None, []
        if len(buffers) > 5:
            self.own, load_sems = buffers[5:]
            self.loads = load_own(source, self.own, part, cut, load_sems)
        self.first = halving_first(source, near, far, part, cut, sems, 0)
        self.second = halving_second(send, land, part, cut, sems, 4)

    def start(self):
        for copy in self.first + self.loads:
            copy.start()

    def own_rows(self, which):
        part, cut = self.part, self.cut
        low = part - cut
        if self.own is not None:
            return as_f32(self.own, (0, cut, 2 * cut, 2 * cut + low)[which], (cut, low)[which // 2])
        owner, start = ((0, 0), (2, 0), (0, cut), (1, cut))[which]
        return as_f32(
            self.source, pl.multiple_of(flips()[owner] * part + start, 16), (cut, low)[which // 2]
        )

    def turn(self):
        part, cut = self.part, self.cut
        low = part - cut
        for copy in self.first + self.loads:
            copy.wait()
        up = self.own_rows(1) + as_f32(self.near, cut, cut)
        down = self.own_rows(3) + as_f32(self.far, low, low)
        self.send[:cut, :] = up.astype(jnp.bfloat16)
        self.send[cut:, :] = down.astype(jnp.bfloat16)
        for copy in self.second:
            copy.start()
        self.total[:cut, :] = (self.own_rows(0) + as_f32(self.near, 0, cut)).astype(jnp.bfloat16)
        self.total[cut:, :] = (self.own_rows(2) + as_f32(self.far, 0, low)).astype(jnp.bfloat16)

    def finish(self):
        for copy in self.second:
            copy.wait()
        total = as_f32(self.total, 0, self.part) + as_f32(self.land, 0, self.part)
        self.total[...] = total.astype(jnp.bfloat16)


def halving_buffers(part, cut, model):
    bf16 = lambda rows: pltpu.VMEM((rows, model), jnp.bfloat16)
    return [
        bf16(2 * cut),
        bf16(2 * (part - cut)),
        bf16(part),
        bf16(part),
        pltpu.SemaphoreType.DMA((2, 6)),
        bf16(2 * part),
        pltpu.SemaphoreType.DMA((4,)),
    ]


class Spreading:
    def __init__(self, target, part, cut, sems, mine):
        self.first = spread_first(mine, target, part, cut, sems, 0)
        self.second = spread_second(mine, target, part, cut, sems, 2)

    def start(self):
        for copy in self.first:
            copy.start()

    def turn(self):
        for copy in self.first:
            copy.wait()
        for copy in self.second:
            copy.start()

    def finish(self):
        for copy in self.second:
            copy.wait()


def forward_body(heads, tile, steps, ahead, *refs):
    (
        own_any,
        cot_any,
        x_ref,
        start_ref,
        keep_ref,
        cos_ref,
        sin_ref,
        mask_ref,
        gain_ref,
        wsel_ref,
        wq_any,
        wk_any,
        wval_any,
        wout_any,
        chunk_any,
        near_any,
        cot_far_any,
        sent_far_any,
        hid_ref,
        norm_ref,
        q_ref,
        k_ref,
        v_ref,
        val_ref,
        att_ref,
        sig_ref,
        lse_ref,
        mix_ref,
        sent_all,
        send_sem,
        recv_sem,
        tile_send,
        tile_recv,
        wqk_ref,
        wval_ref,
        wout_ref,
        load_sem,
    ) = refs
    step = pl.program_id(0)
    narrow = heads * DH
    loads = [
        pltpu.make_async_copy(source, target, load_sem.at[i])
        for i, (source, target) in enumerate(
            [
                (wq_any, wqk_ref.at[:, pl.ds(0, narrow)]),
                (wk_any, wqk_ref.at[:, pl.ds(narrow, narrow)]),
                (wval_any, wval_ref),
                (wout_any, wout_ref),
            ]
        )
    ]

    def loaded(which):
        @pl.when(step == 0)
        def _():
            for i in which:
                loads[i].wait()

    @pl.when(step == 0)
    def _():
        for copy in loads:
            copy.start()

    rows = steps * tile
    quarter = own_any.shape[0] // 4
    moves = shift_move(0, 0, -3, own_part(quarter), own_part(quarter), quarter)
    moves = moves + shift_move(0, 1, -2, own_part(quarter), own_part(quarter), ahead)
    moves = moves + [(1, 2, "core", 1, fixed(0), fixed(0), rows)]
    partner = neighbour("core", 1)
    copies = copies_of(moves, [own_any, cot_any], [chunk_any, near_any, cot_far_any], send_sem, recv_sem)

    def tile_copy(index):
        return pltpu.make_async_remote_copy(
            src_ref=sent_all.at[pl.ds(index * tile, tile)],
            dst_ref=sent_far_any.at[pl.ds(index * tile, tile)],
            send_sem=tile_send.at[index],
            recv_sem=tile_recv.at[index],
            device_id=partner,
            device_id_type=pl.DeviceIdType.MESH,
        )


    @pl.when(step == 0)
    def _():
        greet(peers_of(moves))
        for copy in copies:
            copy.start()

    now = tile_rows(step, tile)
    before = tile_rows(jnp.maximum(step - 1, 0), tile)
    x = x_ref[...]
    x_f = x.astype(jnp.float32)
    center = x_f - jnp.mean(x_f, axis=1, keepdims=True)
    spread = jnp.mean(center * center, axis=1, keepdims=True)
    normed = (center * lax.rsqrt(spread + NORM_EPS) * gain_ref[...]).astype(jnp.bfloat16)
    norm_ref[...] = normed
    sig = 1.0 / (1.0 + jnp.exp(-dot_nn(x, wsel_ref[...])))
    sig_ref[...] = sig
    gates = sig * mask_ref[...].astype(jnp.float32)
    cos_two, sin_two = cos_ref[...], sin_ref[...]
    allowed = window_mask(step, tile, start_ref[...], keep_ref[:, before], keep_ref[:, now])
    scale = DH ** (-0.5)
    lanes = lax.broadcasted_iota(jnp.int32, (tile, LANE), 1)
    lse = jnp.zeros((tile, LANE), jnp.float32)
    loaded((0, 1))
    qk = dot_nn(normed, wqk_ref[...])
    loaded((2,))
    for head in range(heads):
        cols = slice(head * DH, (head + 1) * DH)
        value = dot_nn(x, wval_ref[:, head * VEXP * DH : (head + 1) * VEXP * DH])
        val_ref[:, head * VEXP * DH : (head + 1) * VEXP * DH] = value.astype(jnp.bfloat16)
        total = jnp.zeros((tile, DH), jnp.float32)
        for e in range(VEXP):
            at = head * VEXP + e
            total = total + gates[:, at : at + 1] * value[:, e * DH : (e + 1) * DH]
        v_ref[now, cols] = total.astype(jnp.bfloat16)
    for head in range(heads):
        cols = slice(head * DH, (head + 1) * DH)
        q_head = (spin(qk[:, cols], cos_two, sin_two) * scale).astype(jnp.bfloat16)
        k_head = spin(
            qk[:, (heads + head) * DH : (heads + head + 1) * DH], cos_two, sin_two
        ).astype(jnp.bfloat16)
        q_ref[:, cols] = q_head
        k_ref[now, cols] = k_head
        scores = jnp.concatenate(
            [dot_nt(q_head, k_ref[before, cols]), dot_nt(q_head, k_head)], axis=1
        )
        scores = jnp.where(allowed, scores, MASK_FILL)
        row_max = jnp.max(scores, axis=1, keepdims=True)
        terms = jnp.exp(scores - row_max)
        row_sum = jnp.sum(terms, axis=1, keepdims=True)
        probs = (terms * (1.0 / row_sum)).astype(jnp.bfloat16)
        attended = dot_nn(probs[:, :tile], v_ref[before, cols]) + dot_nn(
            probs[:, tile:], v_ref[now, cols]
        )
        att_ref[:, cols] = attended
        lse = jnp.where(lanes == head, row_max + jnp.log(row_sum), lse)
        for e in range(VEXP):
            at = head * VEXP + e
            gate = gates[:, heads * VEXP + at : heads * VEXP + at + 1]
            mix_ref[:, at * DH : (at + 1) * DH] = (gate * attended).astype(jnp.bfloat16)
    lse_ref[...] = lse
    loaded((3,))
    hidden = x_f + dot_nn(mix_ref[...], wout_ref[...])
    hid_ref[...] = hidden
    sent_all[now, :] = hidden.astype(jnp.bfloat16)
    for index in range(steps):

        @pl.when(step == index)
        def _(index=index):
            tile_copy(index).start()

    @pl.when(step == steps - 1)
    def _():
        for copy in copies:
            copy.wait()
        for index in range(steps):
            tile_copy(index).wait()


def whole_block(shape):
    return pl.BlockSpec(shape, lambda step: (0,) * len(shape), pipeline_mode=pl.Buffered(1))


def attention_forward(ahead, own, cot, x, start, keep, cos_two, sin_two, mask, gain, wsel, wq, wk, wval, wout, tile):
    rows, model = x.shape
    heads = wq.shape[1] // DH
    per_tile = lambda width: pl.BlockSpec((tile, width), lambda step: (step, 0))
    full = lambda arr: whole_block(arr.shape)
    narrow, wide = heads * DH, heads * VEXP * DH
    shapes = [
        (model, jnp.float32, False),
        (model, jnp.bfloat16, False),
        (narrow, jnp.bfloat16, False),
        (narrow, jnp.bfloat16, True),
        (narrow, jnp.bfloat16, True),
        (wide, jnp.bfloat16, False),
        (narrow, jnp.float32, False),
        (LANE, jnp.float32, False),
        (LANE, jnp.float32, False),
        (wide, jnp.bfloat16, False),
        (model, jnp.bfloat16, True),
    ]
    return pl.pallas_call(
        functools.partial(forward_body, heads, tile, rows // tile, ahead),
        grid=(rows // tile,),
        in_specs=[
            ANYWHERE,
            ANYWHERE,
            per_tile(model),
            per_tile(1),
            full(keep),
            per_tile(LANE),
            per_tile(LANE),
            per_tile(LANE),
            full(gain),
            full(wsel),
            ANYWHERE,
            ANYWHERE,
            ANYWHERE,
            ANYWHERE,
        ],
        out_specs=[ANYWHERE] * 4
        + [whole_block((rows, width)) if whole else per_tile(width) for width, _, whole in shapes],
        out_shape=[
            jax.ShapeDtypeStruct(own.shape, jnp.bfloat16),
            jax.ShapeDtypeStruct(own.shape, jnp.bfloat16),
            jax.ShapeDtypeStruct((rows, model), jnp.bfloat16),
            jax.ShapeDtypeStruct((rows, model), jnp.bfloat16),
        ]
        + [jax.ShapeDtypeStruct((rows, width), kind) for width, kind, _ in shapes],
        scratch_shapes=[
            pltpu.SemaphoreType.DMA((3,)),
            pltpu.SemaphoreType.DMA((3,)),
            pltpu.SemaphoreType.DMA((rows // tile,)),
            pltpu.SemaphoreType.DMA((rows // tile,)),
            pltpu.VMEM((model, 2 * narrow), jnp.bfloat16),
            pltpu.VMEM(wval.shape, jnp.bfloat16),
            pltpu.VMEM(wout.shape, jnp.bfloat16),
            pltpu.SemaphoreType.DMA((4,)),
        ],
        compiler_params=pltpu.CompilerParams(
            vmem_limit_bytes=VMEM_BYTES, collective_id=1, has_side_effects=True
        ),
        cost_estimate=pl.CostEstimate(
            flops=2 * rows * model * (2 * narrow + 2 * wide), bytes_accessed=40 << 20, transcendentals=0
        ),
    )(own, cot, x, start, keep, cos_two, sin_two, mask, gain, wsel, wq, wk, wval, wout)


def backward_body(heads, tile, steps, moves, halve, part, n_in, n_out, *refs):
    ins, refs = refs[:n_in], refs[n_in:]
    (
        cot_ref,
        grad_own_ref,
        grad_far_ref,
        q_ref,
        k_ref,
        v_ref,
        att_ref,
        lse_ref,
        start_ref,
        keep_ref,
        sig_now_ref,
        mask_now_ref,
        cos_now_ref,
        sin_now_ref,
        sig_old_ref,
        mask_old_ref,
        cos_old_ref,
        sin_old_ref,
        x_ref,
        val_ref,
        gain_ref,
        wsel_ref,
        wout_ref,
        wq_any,
        wk_any,
        wval_any,
        *outs_and_rest,
    ) = refs
    outs, rest = outs_and_rest[:n_out], outs_and_rest[n_out:]
    (
        gin_ref,
        dqk_ref,
        dval_ref,
        dlog_ref,
        ggain_ref,
        dy_ref,
        *totals_and_rest,
    ) = rest
    totals, rest = totals_and_rest[: len(halve)], totals_and_rest[len(halve) :]
    (
        dk_acc,
        dv_acc,
        dq_keep,
        dgate_keep,
        gain_acc,
        dhid_keep,
        wqk_ref,
        wval_ref,
        load_sem,
        send_sem,
        recv_sem,
        *buffers,
    ) = rest
    step = pl.program_id(0)
    half_qk = heads * DH
    loads = [
        pltpu.make_async_copy(source, target, load_sem.at[i])
        for i, (source, target) in enumerate(
            [
                (wq_any, wqk_ref.at[:, pl.ds(0, half_qk)]),
                (wk_any, wqk_ref.at[:, pl.ds(half_qk, half_qk)]),
                (wval_any, wval_ref),
            ]
        )
    ]
    copies = copies_of(moves, ins, outs, send_sem, recv_sem)
    riders = [
        Halving(ins[source], totals[i], buffers[7 * i : 7 * i + 7], part, part // 32 * 16)
        for i, source in enumerate(halve)
    ]

    @pl.when(step == 0)
    def _():
        for copy in loads:
            copy.start()
        greet(peers_of(moves) + [neighbour("dp", 1), neighbour("dp", 2)])
        for copy in copies:
            copy.start()
        for rider in riders:
            rider.start()

    @pl.when(step == 1)
    def _():
        for copy in loads:
            copy.wait()

    @pl.when(step == steps - 1)
    def _():
        for rider in riders:
            rider.turn()

    slot = lax.rem(step, 2)
    old = 1 - slot
    lanes = lax.broadcasted_iota(jnp.int32, (tile, LANE), 1)
    scale = DH ** (-0.5)
    narrow = heads * DH

    @pl.when(step == 0)
    def _():
        gain_acc[...] = jnp.zeros_like(gain_acc)
        dk_acc[...] = jnp.zeros_like(dk_acc)
        dv_acc[...] = jnp.zeros_like(dv_acc)

    @pl.when(step < steps)
    def _():
        now = tile_rows(jnp.minimum(step, steps - 1), tile)
        before = tile_rows(jnp.maximum(step - 1, 0), tile)
        allowed = window_mask(step, tile, start_ref[...], keep_ref[:, before], keep_ref[:, now])
        gates = sig_now_ref[...] * mask_now_ref[...].astype(jnp.float32)
        dhid = cot_ref[...].astype(jnp.float32) + grad_own_ref[...] + grad_far_ref[...].astype(jnp.float32)
        dhid_keep[slot] = dhid
        dy = dhid.astype(jnp.bfloat16)
        dy_ref[...] = dy
        dgate = jnp.zeros((tile, LANE), jnp.float32)
        for head in range(heads):
            cols = slice(head * DH, (head + 1) * DH)
            dmixed = dot_nt(dy, wout_ref[head * VEXP * DH : (head + 1) * VEXP * DH, :])
            attended = att_ref[:, cols]
            dattend = jnp.zeros((tile, DH), jnp.float32)
            for e in range(VEXP):
                at = (heads + head) * VEXP + e
                part = dmixed[:, e * DH : (e + 1) * DH]
                dattend = dattend + gates[:, at : at + 1] * part
                dgate = jnp.where(
                    lanes == at, jnp.sum(part * attended, axis=1, keepdims=True), dgate
                )
            dattend = dattend.astype(jnp.bfloat16)
            q_head = q_ref[:, cols]
            k_old, k_now = k_ref[before, cols], k_ref[now, cols]
            v_old, v_now = v_ref[before, cols], v_ref[now, cols]
            scores = jnp.concatenate([dot_nt(q_head, k_old), dot_nt(q_head, k_now)], axis=1)
            scores = jnp.where(allowed, scores, MASK_FILL)
            probs = jnp.exp(scores - lse_ref[:, head : head + 1])
            dprob = jnp.concatenate([dot_nt(dattend, v_old), dot_nt(dattend, v_now)], axis=1)
            delta = jnp.sum(probs * dprob, axis=1, keepdims=True)
            dscore = (probs * (dprob - delta)).astype(jnp.bfloat16)
            probs = probs.astype(jnp.bfloat16)
            dv_acc[old, :, cols] += dot_tn(probs[:, :tile], dattend)
            dv_acc[slot, :, cols] = dot_tn(probs[:, tile:], dattend)
            dk_acc[old, :, cols] += dot_tn(dscore[:, :tile], q_head)
            dk_acc[slot, :, cols] = dot_tn(dscore[:, tile:], q_head)
            dq = dot_nn(dscore[:, :tile], k_old) + dot_nn(dscore[:, tile:], k_now)
            dq_keep[slot, :, cols] = (
                spin_back(dq, cos_now_ref[...], sin_now_ref[...]) * scale
            ).astype(jnp.bfloat16)
        dgate_keep[slot] = dgate

    @pl.when(step > 0)
    def _():
        sig = sig_old_ref[...]
        mask = mask_old_ref[...].astype(jnp.float32)
        gates = sig * mask
        dgate = dgate_keep[old]
        for head in range(heads):
            cols = slice(head * DH, (head + 1) * DH)
            dqk_ref[:, cols] = dq_keep[old, :, cols]
            dqk_ref[:, narrow + head * DH : narrow + (head + 1) * DH] = spin_back(
                dk_acc[old, :, cols], cos_old_ref[...], sin_old_ref[...]
            ).astype(jnp.bfloat16)
            dvalue = dv_acc[old, :, cols]
            for e in range(VEXP):
                at = head * VEXP + e
                wide = slice(at * DH, (at + 1) * DH)
                val = val_ref[:, wide].astype(jnp.float32)
                dgate = jnp.where(lanes == at, jnp.sum(dvalue * val, axis=1, keepdims=True), dgate)
                dval_ref[:, wide] = (gates[:, at : at + 1] * dvalue).astype(jnp.bfloat16)
        dlog = (dgate * gates * (1.0 - sig)).astype(jnp.bfloat16)
        dlog_ref[...] = dlog
        dnormed = dot_nt(dqk_ref[...], wqk_ref[...])
        x_f = x_ref[...].astype(jnp.float32)
        center = x_f - jnp.mean(x_f, axis=1, keepdims=True)
        inv = lax.rsqrt(jnp.mean(center * center, axis=1, keepdims=True) + NORM_EPS)
        x_hat = center * inv
        gain_acc[...] += jnp.sum(dnormed * x_hat, axis=0, keepdims=True)
        grad = dnormed * gain_ref[...]
        dx = inv * (
            grad
            - jnp.mean(grad, axis=1, keepdims=True)
            - x_hat * jnp.mean(grad * x_hat, axis=1, keepdims=True)
        )
        dx = dx + dhid_keep[old] + dot_nt(dval_ref[...], wval_ref[...]) + dot_nt(dlog, wsel_ref[...])
        gin_ref[...] = dx.astype(jnp.bfloat16)

    @pl.when(step == steps)
    def _():
        gain = gain_acc[...]
        high = gain.astype(jnp.bfloat16).astype(jnp.float32)
        row = lax.broadcasted_iota(jnp.int32, (GAIN_ROWS, gain.shape[1]), 0)
        split = jnp.where(row == 0, high, jnp.where(row == 1, gain - high, 0.0))
        ggain_ref[...] = split.astype(jnp.bfloat16)
        for rider in riders:
            rider.finish()
        for copy in copies:
            copy.wait()


def attention_backward(
    sources, results, moves, halve, part, cot, grad_own, grad_far, q, k, v, att, lse, start, keep, sig, mask,
    cos_two, sin_two, x, val, gain, wsel, wout, wq, wk, wval, tile
):
    rows, model = x.shape
    heads = wq.shape[1] // DH
    steps = rows // tile
    narrow, wide = heads * DH, heads * VEXP * DH
    at_now = lambda width: pl.BlockSpec((tile, width), lambda step: (jnp.minimum(step, steps - 1), 0))
    at_old = lambda width: pl.BlockSpec((tile, width), lambda step: (jnp.maximum(step - 1, 0), 0))
    full = lambda arr: whole_block(arr.shape)
    return pl.pallas_call(
        functools.partial(
            backward_body, heads, tile, steps, moves, halve, part, len(sources), len(results)
        ),
        grid=(steps + 1,),
        in_specs=[ANYWHERE] * len(sources)
        + [
            at_now(model),
            at_now(model),
            at_now(model),
            at_now(narrow),
            full(k),
            full(v),
            at_now(narrow),
            at_now(LANE),
            at_now(1),
            full(keep),
            at_now(LANE),
            at_now(LANE),
            at_now(LANE),
            at_now(LANE),
            at_old(LANE),
            at_old(LANE),
            at_old(LANE),
            at_old(LANE),
            at_old(model),
            at_old(wide),
            full(gain),
            full(wsel),
            full(wout),
            ANYWHERE,
            ANYWHERE,
            ANYWHERE,
        ],
        out_specs=[ANYWHERE] * len(results)
        + [
            at_old(model),
            at_old(2 * narrow),
            at_old(wide),
            at_old(LANE),
            whole_block((GAIN_ROWS, model)),
            at_now(model),
        ]
        + [whole_block((part, model))] * len(halve),
        out_shape=[jax.ShapeDtypeStruct(shape, jnp.bfloat16) for shape in results]
        + [
            jax.ShapeDtypeStruct((rows, model), jnp.bfloat16),
            jax.ShapeDtypeStruct((rows, 2 * narrow), jnp.bfloat16),
            jax.ShapeDtypeStruct((rows, wide), jnp.bfloat16),
            jax.ShapeDtypeStruct((rows, LANE), jnp.bfloat16),
            jax.ShapeDtypeStruct((GAIN_ROWS, model), jnp.bfloat16),
            jax.ShapeDtypeStruct((rows, model), jnp.bfloat16),
        ]
        + [jax.ShapeDtypeStruct((part, model), jnp.bfloat16)] * len(halve),
        scratch_shapes=[
            pltpu.VMEM((2, tile, narrow), jnp.float32),
            pltpu.VMEM((2, tile, narrow), jnp.float32),
            pltpu.VMEM((2, tile, narrow), jnp.bfloat16),
            pltpu.VMEM((2, tile, LANE), jnp.float32),
            pltpu.VMEM((1, model), jnp.float32),
            pltpu.VMEM((2, tile, model), jnp.float32),
            pltpu.VMEM((model, 2 * narrow), jnp.bfloat16),
            pltpu.VMEM(wval.shape, jnp.bfloat16),
            pltpu.SemaphoreType.DMA((3,)),
            pltpu.SemaphoreType.DMA((len(moves),)),
            pltpu.SemaphoreType.DMA((len(moves),)),
        ]
        + halving_buffers(part, part // 32 * 16, model) * len(halve),
        compiler_params=pltpu.CompilerParams(
            vmem_limit_bytes=VMEM_BYTES, collective_id=6, has_side_effects=True
        ),
        cost_estimate=pl.CostEstimate(
            flops=2 * rows * model * (2 * narrow + 2 * wide), bytes_accessed=50 << 20, transcendentals=0
        ),
    )(
        *sources, cot, grad_own, grad_far, q, k, v, att, lse, start, keep, sig, mask, cos_two, sin_two,
        sig, mask, cos_two, sin_two, x, val, gain, wsel, wout, wq, wk, wval,
    )


def tail_body(blocks, chips, part, cut, *refs):
    (
        part_1,
        part_3,
        part_0,
        got_2,
        gain_ref,
        dlog_ref,
        unit_ref,
        dy_any,
        mix_any,
        x_any,
        dval_any,
        norm_any,
        dqk_any,
        hid_any,
        out_own_any,
        out_far_any,
        dense_ref,
        layer_ref,
        whole_any,
        came,
        quarter,
        product,
        pair,
        near,
        far,
        send,
        land,
        sums,
        last,
        link,
        core_sems,
        xy_sems,
        z_sems,
        local_sem,
        dy_ref,
        mix_ref,
        x_ref,
        dval_ref,
        norm_ref,
        dqk_ref,
        hid_ref,
        out_own,
        out_far,
        load_sem,
    ) = refs
    half = mix_ref.shape[1] // 2
    loads = [
        pltpu.make_async_copy(source, target, load_sem.at[i])
        for i, (source, target) in enumerate(
            [
                (dy_any, dy_ref),
                (mix_any.at[:, pl.ds(0, half)], mix_ref.at[:, pl.ds(0, half)]),
                (mix_any.at[:, pl.ds(half, half)], mix_ref.at[:, pl.ds(half, half)]),
                (x_any, x_ref),
                (dval_any, dval_ref),
                (norm_any, norm_ref),
                (dqk_any, dqk_ref),
                (hid_any, hid_ref),
                (out_own_any, out_own),
                (out_far_any, out_far),
            ]
        )
    ]
    for copy in loads:
        copy.start()
    ready = {0: (0, 1), 1: (2,), 2: (3, 4), 4: (5, 6)}
    place = lax.axis_index("expert")
    chip, core = place // 2, lax.rem(place, 2)
    model = x_ref.shape[1]
    piece = model // 4 // chips // 2
    quart = chips * piece
    halfway = quart // 2
    rights = {"out": mix_ref, "val": dval_ref, "log": dlog_ref, "qk": dqk_ref}
    lefts = {"out": dy_ref, "val": x_ref, "log": x_ref, "qk": norm_ref}

    peers = [neighbour("core", 1)] + [neighbour("dp", flip) for flip in (1, 2)]
    for hop in range(1, chips):
        peers.append(neighbour("chip", hop))
    greet(peers)
    passes = [
        remote(source, came.at[i], link, 7 + i, neighbour("chip", hop))
        for i, (source, hop) in enumerate(((part_1, 1), (part_3, 3)))
    ]
    for copy in passes:
        copy.start()

    def width_of(b):
        return sum(hi - lo for _, lo, hi in blocks[b])

    def core_copy(b):
        width = width_of(b)
        return remote(
            product.at[b % 2, :, span((1 - core) * piece, piece), pl.ds(0, width)],
            pair.at[b, :, :, pl.ds(0, width)],
            core_sems,
            b,
            neighbour("core", 1),
        )

    def compute(b):
        if b >= 2:
            core_copy(b - 2).wait_send()
        for i in ready.get(b, ()):
            loads[i].wait()
        at = 0
        for name, lo, hi in blocks[b]:
            total = dot_tn(lefts[name][...], rights[name][:, lo:hi])
            if name == "log":
                total = total + dot_tn(gain_ref[...], unit_ref[...])
            product[b % 2, :, :, at : at + hi - lo] = total.astype(jnp.bfloat16).reshape(
                4 * chips, 2 * piece, hi - lo
            )
            at += hi - lo
        core_copy(b).start()

    def pair_rows(b):
        return pair.at[b].reshape(4 * quart, pair.shape[3])

    def first_copies(b):
        return halving_first(pair_rows(b), near.at[b], far.at[b], quart, halfway, xy_sems.at[b], 0)

    def second_copies(b):
        return halving_second(send.at[b], land.at[b], quart, halfway, xy_sems.at[b], 4)

    def chip_copies(b):
        copies = []
        for hop in range(1, chips):
            target = lax.rem(chip + hop, chips)
            copies.append(
                remote(
                    sums.at[b, span(target * piece, piece)],
                    last.at[b, hop - 1],
                    z_sems.at[b],
                    hop - 1,
                    neighbour("chip", hop),
                )
            )
        return copies

    def stage_1(b):
        core_copy(b).wait_recv()
        kept = product[b % 2, :, span(core * piece, piece), :].astype(jnp.float32)
        pair[b] = (kept + pair[b].astype(jnp.float32)).astype(jnp.bfloat16)
        for copy in first_copies(b):
            copy.start()

    def own_rows(b, owner, start):
        return as_f32(pair_rows(b), pl.multiple_of(flips()[owner] * quart + start, 16), halfway)

    def stage_2(b):
        for copy in first_copies(b):
            copy.wait()
        send[b, :halfway, :] = (own_rows(b, 2, 0) + as_f32(near.at[b], halfway, halfway)).astype(
            jnp.bfloat16
        )
        send[b, halfway:, :] = (own_rows(b, 1, halfway) + as_f32(far.at[b], halfway, halfway)).astype(
            jnp.bfloat16
        )
        for copy in second_copies(b):
            copy.start()

    def stage_3(b):
        for copy in second_copies(b):
            copy.wait()
        up = own_rows(b, 0, 0) + as_f32(near.at[b], 0, halfway) + as_f32(land.at[b], 0, halfway)
        down = own_rows(b, 0, halfway) + as_f32(far.at[b], 0, halfway)
        down = down + as_f32(land.at[b], halfway, halfway)
        sums[b, :halfway, :] = up.astype(jnp.bfloat16)
        sums[b, halfway:, :] = down.astype(jnp.bfloat16)
        for copy in chip_copies(b):
            copy.start()

    def stage_4(b):
        for copy in chip_copies(b):
            copy.wait()
        total = sums[b, span(chip * piece, piece), :].astype(jnp.float32)
        for hop in range(chips - 1):
            total = total + last[b, hop].astype(jnp.float32)
        start = sum(width_of(i) for i in range(b))
        dense_ref[:, start : start + width_of(b)] = total[:, : width_of(b)]

    def spread_1():
        return spread_first(quarter, whole_any, part, cut, link, 1)

    def spread_2():
        return spread_second(quarter, whole_any, part, cut, link, 3)

    mine = lax.axis_index("dp")
    keep = pltpu.make_async_copy(quarter, whole_any.at[span(mine * part, part)], local_sem)
    count = len(blocks)
    compute(0)
    compute(1)
    for b in range(count):
        stage_1(b)
        if b + 2 < count:
            compute(b + 2)
    for copy in passes:
        copy.wait()
    quarter[...] = sum(
        ref[...].astype(jnp.float32) for ref in (part_0, got_2, came.at[0], came.at[1])
    ).astype(jnp.bfloat16)
    keep.start()
    for copy in spread_1():
        copy.start()
    for copy in loads[7:]:
        copy.wait()
    rows = 4 * quart
    for start in range(0, x_ref.shape[0], rows):
        total = hid_ref[start : start + rows, :] + as_f32(out_own, start, rows)
        layer_ref[start : start + rows, :] = (total + as_f32(out_far, start, rows)).astype(jnp.bfloat16)
    for b in range(count):
        stage_2(b)
    for copy in spread_1():
        copy.wait()
    for copy in spread_2():
        copy.start()
    for b in range(count):
        stage_3(b)
    for b in range(count):
        stage_4(b)
    for copy in spread_2():
        copy.wait()
    keep.wait()
    for b in range(max(0, count - 2), count):
        core_copy(b).wait_send()


def tail(hidden, out_own, out_far, part_1, part_3, part_0, got_2, dy, x, normed, gain_rows, mixed, dval, dlog, dqk, unit, shape, chips):
    rows, model = x.shape
    part = shape[0] // 4
    cut = part // 32 * 16
    wide, narrow = mixed.shape[1], dqk.shape[1]
    narrow_one = narrow // 2
    half = wide // 2
    blocks = [
        [("out", 0, half)],
        [("out", half, wide)],
        [("val", 0, half)],
        [("val", half, wide)],
        [("log", 0, LANE), ("qk", 0, narrow)],
    ]
    width = max(half, LANE + narrow)
    total = 2 * wide + LANE + narrow
    count = len(blocks)
    piece = model // 4 // chips // 2
    quart = chips * piece
    bf16 = lambda *shape: pltpu.VMEM(shape, jnp.bfloat16)
    dma = lambda *shape: pltpu.SemaphoreType.DMA(shape)
    vmem = pl.BlockSpec(memory_space=pltpu.VMEM)
    return pl.pallas_call(
        functools.partial(tail_body, blocks, chips, part, cut),
        in_specs=[ANYWHERE] * 2 + [vmem] * 5 + [ANYWHERE] * 9,
        out_specs=[vmem, vmem, ANYWHERE],
        out_shape=[
            jax.ShapeDtypeStruct((piece, total), jnp.float32),
            jax.ShapeDtypeStruct((rows, model), jnp.bfloat16),
            jax.ShapeDtypeStruct(shape, jnp.bfloat16),
        ],
        scratch_shapes=[
            bf16(2, part, model),
            bf16(part, model),
            bf16(2, 4 * chips, 2 * piece, width),
            bf16(count, 4 * chips, piece, width),
            bf16(count, quart, width),
            bf16(count, quart, width),
            bf16(count, quart, width),
            bf16(count, quart, width),
            bf16(count, quart, width),
            bf16(count, chips - 1, piece, width),
            dma(2, 9),
            dma(2, count),
            dma(count, 2, 6),
            dma(count, 2, chips - 1),
            dma(),
            bf16(rows, model),
            bf16(rows, wide),
            bf16(rows, model),
            bf16(rows, wide),
            bf16(rows, model),
            bf16(rows, 2 * narrow_one),
            pltpu.VMEM((rows, model), jnp.float32),
            bf16(rows, model),
            bf16(rows, model),
            dma(10),
        ],
        compiler_params=pltpu.CompilerParams(
            vmem_limit_bytes=VMEM_BYTES, collective_id=7, has_side_effects=True
        ),
        cost_estimate=pl.CostEstimate(
            flops=2 * rows * model * total, bytes_accessed=20 << 20, transcendentals=0
        ),
    )(part_1, part_3, part_0, got_2, gain_rows, dlog, unit, dy, mixed, x, dval, normed, dqk, hidden, out_own, out_far)


def experts_body(exp_local, ff_dim, tile, steps, chips, ahead, *refs):
    (
        own_any,
        third_any,
        second_any,
        x_own,
        x_far,
        c_own,
        c_far,
        mask_ref,
        digit_ref,
        grad_own,
        out_own,
        grad_far,
        out_far,
        grad_1,
        part_0,
        part_3,
        part_2,
        w_all,
        x_ref,
        c_ref,
        grad_acc,
        out_acc,
        act_all,
        dpre_all,
        g_two,
        given,
        near,
        far,
        send,
        land,
        load_sem,
        local_sem,
        chip_sems,
        spread_sems,
        halve_sems,
        tile_sems,
    ) = refs
    wide = exp_local * ff_dim
    back = wide + ROUTER_ROWS
    half = steps // 2
    part = w_all.shape[1] // 4
    cut = part // 32 * 16
    step = pl.program_id(0)
    turn_of, index = lax.div(step, steps), lax.rem(step, steps)
    mine = span(lax.axis_index("dp") * part, part)
    partner = neighbour("core", 1)

    start = lax.axis_index("dp") * part
    rest = span(start + ahead, part - ahead)
    quarter_2 = remote(
        own_any.at[rest], w_all.at[2, rest], chip_sems, 0, neighbour("chip", -2)
    )
    near_rows = remote(own_any, w_all.at[3], chip_sems, 1, neighbour("chip", -1))
    load_own = pltpu.make_async_copy(own_any, w_all.at[0], local_sem.at[0])
    load_third = pltpu.make_async_copy(third_any.at[mine], w_all.at[1, mine], local_sem.at[1])
    load_second = pltpu.make_async_copy(
        second_any.at[span(start, ahead)], w_all.at[2, span(start, ahead)], local_sem.at[2]
    )
    spread_3 = Spreading(w_all.at[1], part, cut, spread_sems.at[0], third_any.at[mine])
    spread_2 = Spreading(w_all.at[2], part, cut, spread_sems.at[1], w_all.at[2, mine])
    halvings = [
        Halving(
            g_two.at[i % 2],
            total,
            (near.at[i % 2], far.at[i % 2], send.at[i % 2], land.at[i % 2], halve_sems.at[i]),
            part,
            cut,
        )
        for i, total in enumerate((part_0, part_3, part_2))
    ]

    def load(at, kind):
        source = ((x_own, x_far), (c_own, c_far))[kind][at // half]
        return pltpu.make_async_copy(
            source.at[pl.ds(at % half * tile, tile)],
            (x_ref, c_ref)[kind].at[pl.ds(at * tile, tile)],
            load_sem.at[kind, at],
        )

    def tile_copy(at, kind):
        rows = pl.ds(at * tile, tile)
        source = (given.at[rows], out_acc.at[pl.ds((half + at) * tile, tile)])[kind]
        return remote(source, (grad_far, out_far)[kind].at[rows], tile_sems.at[kind], at, partner)

    def store(kind):
        rows = pl.ds(0, half * tile)
        source = (grad_acc, out_acc)[kind].at[rows]
        return pltpu.make_async_copy(source, (grad_own, out_own)[kind], local_sem.at[3 + kind])

    store_grad = pltpu.make_async_copy(g_two.at[(chips - 1) % 2], grad_1, local_sem.at[5])

    def when(at):
        return pl.when(step == at)

    @when(0)
    def _():
        load_own.start()
        for at in range(steps):
            for kind in range(2):
                load(at, kind).start()
        load_third.start()
        load_second.start()
        peers = [partner, neighbour("dp", 1), neighbour("dp", 2)]
        greet(peers + [neighbour("chip", hop) for hop in range(1, chips)])
        spread_3.start()
        quarter_2.start()
        load_own.wait()

    @when(steps - 4)
    def _():
        spread_3.turn()

    @when(steps)
    def _():
        load_second.wait()
        quarter_2.wait()
        spread_2.start()
        near_rows.start()
        load_third.wait()
        spread_3.finish()
        halvings[0].start()

    @when(steps + 3)
    def _():
        spread_2.turn()

    @when(steps + 7)
    def _():
        halvings[0].turn()

    @when(2 * steps)
    def _():
        halvings[1].start()
        spread_2.finish()

    @when(2 * steps + 3)
    def _():
        halvings[0].finish()

    @when(2 * steps + 7)
    def _():
        halvings[1].turn()

    @when(3 * steps)
    def _():
        near_rows.wait()
        halvings[2].start()

    @when(3 * steps + 3)
    def _():
        halvings[1].finish()

    @when(3 * steps + 6)
    def _():
        halvings[2].turn()

    for at in range(steps):

        @when(at)
        def _(at=at):
            for kind in range(2):
                load(at, kind).wait()

    final = lax.div(turn_of, chips - 1)
    place = lax.rem(index + half * final, steps)
    rows = tile_rows(place, tile)
    x, c = x_ref[rows, :], c_ref[rows, :]
    sig = 1.0 / (1.0 + jnp.exp(-dot_nt(x, w_all[turn_of, wide:back, :])))
    gate = sig * mask_ref[:, :ROUTER_ROWS].astype(jnp.float32)
    lanes = lax.broadcasted_iota(jnp.int32, (tile, ROUTER_ROWS), 1)
    dgate = jnp.zeros((tile, ROUTER_ROWS), jnp.float32)
    for pair in range(exp_local // 2):
        lo, hi = 2 * pair * ff_dim, 2 * (pair + 1) * ff_dim
        pre_two = dot_nt(x, w_all[turn_of, lo:hi, :])
        raw_two = dot_nt(c, w_all[turn_of, back + lo : back + hi, :])
        for side in range(2):
            e = 2 * pair + side
            pre = pre_two[:, side * ff_dim : (side + 1) * ff_dim]
            raw = raw_two[:, side * ff_dim : (side + 1) * ff_dim]
            square = pre * pre
            bend = jnp.tanh(pre * (GELU_A + GELU_A * GELU_B * square))
            upper = 0.5 * bend + 0.5
            act = (pre * upper).astype(jnp.bfloat16).astype(jnp.float32)
            slope = upper + (0.5 * pre) * (1.0 - bend * bend) * (GELU_A + 3 * GELU_A * GELU_B * square)
            gate_col = gate[:, e : e + 1]
            act_all[rows, e * ff_dim : (e + 1) * ff_dim] = (gate_col * act).astype(jnp.bfloat16)
            dpre_all[rows, e * ff_dim : (e + 1) * ff_dim] = (gate_col * raw * slope).astype(
                jnp.bfloat16
            )
            dgate = jnp.where(lanes == e, jnp.sum(act * raw, axis=1, keepdims=True), dgate)
    dpre_all[rows, wide:back] = (dgate * gate * (1.0 - sig)).astype(jnp.bfloat16)
    out_new = dot_nn(act_all[rows, :], w_all[turn_of, back:, :])
    grad_new = dot_nn(dpre_all[rows, :], w_all[turn_of, :back, :])

    @pl.when(turn_of == 0)
    def _():
        out_acc[rows, :] = out_new.astype(jnp.bfloat16)
        grad_acc[rows, :] = grad_new

    @pl.when(turn_of > 0)
    def _():
        out_acc[rows, :] = (out_acc[rows, :].astype(jnp.float32) + out_new).astype(jnp.bfloat16)
        grad_acc[rows, :] += grad_new

    for at in range(half):

        @when((chips - 1) * steps + at)
        def _(at=at):
            given[at * tile : (at + 1) * tile, :] = grad_acc[
                (half + at) * tile : (half + at + 1) * tile, :
            ].astype(jnp.bfloat16)
            tile_copy(at, 0).start()
            tile_copy(at, 1).start()

    @pl.when(index == steps - 1)
    def _():
        slot = lax.rem(turn_of, 2)
        for lo in range(0, wide, 2 * ff_dim):
            g_two[slot, lo : lo + 2 * ff_dim, :] = dot_tn(
                dpre_all[:, lo : lo + 2 * ff_dim], x_ref[...]
            ).astype(jnp.bfloat16)
            g_two[slot, back + lo : back + lo + 2 * ff_dim, :] = dot_tn(
                act_all[:, lo : lo + 2 * ff_dim], c_ref[...]
            ).astype(jnp.bfloat16)
        extra = dot_tn(dpre_all[:, wide:back], x_ref[...])
        g_two[slot, wide:back, :LANE] = (extra[:, :LANE] + digit_ref[...]).astype(jnp.bfloat16)
        g_two[slot, wide:back, LANE:] = extra[:, LANE:].astype(jnp.bfloat16)

    @when(chips * steps - 1)
    def _():
        store_grad.start()
        store(0).start()
        store(1).start()
        halvings[2].finish()
        for at in range(half):
            tile_copy(at, 0).wait()
            tile_copy(at, 1).wait()
        store_grad.wait()
        store(0).wait()
        store(1).wait()


def experts(own, third, second, tokens, masks, digits, exp_local, ff_dim, ahead, chips, tile):
    rows, model = 2 * tokens[0].shape[0], tokens[0].shape[1]
    steps = rows // tile
    half = steps // 2
    wide = exp_local * ff_dim
    part = own.shape[0] // 4
    cut = part // 32 * 16

    def mask_block(step):
        turn_of, index = lax.div(step, steps), lax.rem(step, steps)
        place = lax.rem(index + half * lax.div(turn_of, chips - 1), steps)
        return (place, lax.rem(chips - turn_of, chips))

    def digit_block(step):
        return (0, lax.rem(chips - lax.div(step, steps), chips))

    bf16 = lambda *shape: pltpu.VMEM(shape, jnp.bfloat16)
    dma = lambda *shape: pltpu.SemaphoreType.DMA(shape)
    full = lambda count, kind: jax.ShapeDtypeStruct((count, model), kind)
    return pl.pallas_call(
        functools.partial(experts_body, exp_local, ff_dim, tile, steps, chips, ahead),
        grid=(chips * steps,),
        in_specs=[ANYWHERE] * 7
        + [pl.BlockSpec((tile, LANE), mask_block), pl.BlockSpec((ROUTER_ROWS, LANE), digit_block)],
        out_specs=[ANYWHERE] * 5 + [whole_block((part, model))] * 3,
        out_shape=[
            full(rows // 2, jnp.float32),
            full(rows // 2, jnp.bfloat16),
            full(rows // 2, jnp.bfloat16),
            full(rows // 2, jnp.bfloat16),
            full(4 * part, jnp.bfloat16),
            full(part, jnp.bfloat16),
            full(part, jnp.bfloat16),
            full(part, jnp.bfloat16),
        ],
        scratch_shapes=[
            bf16(chips, 4 * part, model),
            bf16(rows, model),
            bf16(rows, model),
            pltpu.VMEM((rows, model), jnp.float32),
            bf16(rows, model),
            bf16(rows, wide),
            bf16(rows, wide + ROUTER_ROWS),
            bf16(2, 4 * part, model),
            bf16(rows // 2, model),
            bf16(2, 2 * cut, model),
            bf16(2, 2 * (part - cut), model),
            bf16(2, part, model),
            bf16(2, part, model),
            dma(2, steps),
            dma(6),
            dma(2, 2),
            dma(2, 2, 6),
            dma(chips - 1, 2, 6),
            dma(2, 2, half),
        ],
        compiler_params=pltpu.CompilerParams(
            vmem_limit_bytes=VMEM_BYTES, collective_id=2, has_side_effects=True
        ),
        cost_estimate=pl.CostEstimate(
            flops=12 * chips * rows * model * wide, bytes_accessed=40 << 20, transcendentals=rows * wide
        ),
    )(own, third, second, *tokens, masks, digits)


def core_swap(arr):
    size = lax.axis_size("expert")
    return lax.ppermute(arr, "expert", [(i, i ^ 1) for i in range(size)])


def row_part(arr, index, count):
    return lax.dynamic_slice_in_dim(arr, index * (arr.shape[0] // count), arr.shape[0] // count, 0)


def own_weights(w_router, w_in, w_out):
    exp_local, model_dim, ff_dim = w_in.shape
    router_rows = jnp.zeros((ROUTER_ROWS, model_dim), jnp.bfloat16).at[:exp_local].set(w_router)
    return jnp.concatenate(
        [
            jnp.swapaxes(w_in, 1, 2).reshape(exp_local * ff_dim, model_dim),
            router_rows,
            w_out.reshape(exp_local * ff_dim, model_dim),
        ]
    )


def block_dense(
    layer_input,
    segments,
    keep_mask,
    att_routes,
    moe_routes,
    expert_counts,
    norm_gain,
    w_query,
    w_key,
    w_select,
    w_value,
    w_output,
    w_router,
    w_in,
    w_out,
    cotangent,
):
    rows, model = layer_input.shape
    seqs, seq_len = segments.shape
    exp_local, _, ff_dim = w_in.shape
    heads = w_query.shape[1] // DH
    chips = lax.axis_size("expert") // 2
    wide, narrow, gates = heads * VEXP * DH, heads * DH, 2 * heads * VEXP
    moe_wide = exp_local * ff_dim
    mine = lax.axis_index("expert")
    chip, core = mine // 2, mine % 2

    own = own_weights(w_router, w_in, w_out)
    exp_total = 2 * chips * exp_local
    named = jnp.sum(
        (moe_routes[..., None] == jnp.arange(exp_total, dtype=jnp.int32)).astype(jnp.bfloat16), axis=1
    )
    named = jnp.concatenate([named, core_swap(named)])

    column = jnp.arange(seq_len, dtype=jnp.int32)
    changed = jnp.concatenate(
        [jnp.ones((seqs, 1), jnp.bool_), segments[:, 1:] != segments[:, :-1]], axis=1
    )
    start = lax.cummax(jnp.where(changed, column, 0), axis=1)
    cos_tab, sin_tab = rope_tables((column - start).reshape(-1), DH)
    cos_two = jnp.concatenate([cos_tab, cos_tab], axis=1)
    sin_two = jnp.concatenate([-sin_tab, sin_tab], axis=1)
    start = (start + seq_len * jnp.arange(seqs, dtype=jnp.int32)[:, None]).reshape(rows, 1)
    keep = keep_mask.reshape(1, rows)
    att_mask = jnp.sum(
        (att_routes[..., None] == jnp.arange(VEXP, dtype=jnp.int32)).astype(jnp.bfloat16), axis=2
    ).reshape(rows, gates)
    att_mask = jnp.pad(att_mask, ((0, 0), (0, LANE - gates)))
    gain_row = norm_gain.reshape(1, model)
    wsel = jnp.pad(w_select, ((0, 0), (0, LANE - gates)))

    shape = own.shape
    part = shape[0] // 4
    ahead = 16
    third, second, cot_far, sent_far, hidden, normed, q_rot, k_rot, value_bf, value_all, attended, sig, lse, mixed, sent = (
        attention_forward(
            ahead, own, cotangent, layer_input, start, keep, cos_two, sin_two, att_mask, gain_row, wsel, w_query, w_key,
            w_value, w_output, TILE,
        )
    )

    lane = jnp.arange(chips * LANE, dtype=jnp.int32)
    owner = ((chip + lane // LANE) % chips * 2 + core) * exp_local + lane % LANE
    pick = (lane % LANE < exp_local) & (jnp.arange(exp_total, dtype=jnp.int32)[:, None] == owner)
    masks = jnp.dot(named, pick.astype(jnp.bfloat16), preferred_element_type=jnp.float32)
    counts = jnp.sum(masks, axis=0).astype(jnp.int32)
    masks = masks.astype(jnp.bfloat16)
    place = jnp.arange(ROUTER_ROWS, dtype=jnp.int32)[:, None] - exp_local
    digits = jnp.where(
        (place >= 0) & (place < DIGITS), (counts >> (2 * jnp.clip(place, 0, DIGITS))) & 3, 0
    ).astype(jnp.float32)

    grad_own, out_own, grad_far, out_far, grad_1, part_0, part_3, part_2 = experts(
        own, third, second, (sent, sent_far, cotangent, cot_far), masks, digits, exp_local, ff_dim, ahead, chips, TILE
    )
    got_2, grad_input, dqk, dval, dlog, gain_rows, dy, part_1 = attention_backward(
        [grad_1, part_2],
        [(part, model)],
        shift_move(1, 0, 2, fixed(0), fixed(0), part),
        (0,),
        part,
        cotangent, grad_own, grad_far, q_rot, k_rot, value_bf, attended, lse, start, keep, sig, att_mask, cos_two,
        sin_two, layer_input, value_all, gain_row, wsel, w_output, w_query, w_key, w_value, TILE,
    )
    unit = (
        (jnp.arange(GAIN_ROWS)[:, None] < 2) & (jnp.arange(LANE)[None, :] == gates)
    ).astype(jnp.bfloat16)
    dense, layer_output, summed = tail(
        hidden, out_own, out_far, part_1, part_3, part_0, got_2, dy, layer_input, normed, gain_rows, mixed, dval, dlog, dqk, unit, shape, chips
    )
    out_sum, dense = dense[:, :wide].T, dense[:, wide:]
    grad_w_in = jnp.swapaxes(
        summed[:moe_wide].astype(jnp.float32).reshape(exp_local, ff_dim, model), 1, 2
    )
    extra = summed[moe_wide : moe_wide + ROUTER_ROWS].astype(jnp.float32)
    grad_router = extra[:exp_local]
    parts = extra[exp_local : exp_local + DIGITS, :exp_local].astype(jnp.int32)
    tally = sum(parts[i] << (2 * i) for i in range(DIGITS))
    grad_w_out = (
        summed[moe_wide + ROUTER_ROWS :].astype(jnp.float32).reshape(exp_local, ff_dim, model)
    )
    at_qk = wide + LANE
    return (
        layer_output,
        grad_input,
        dense[:, wide + gates],
        dense[:, at_qk : at_qk + narrow],
        dense[:, at_qk + narrow : at_qk + 2 * narrow],
        dense[:, wide : wide + gates],
        dense[:, :wide],
        out_sum,
        grad_router,
        grad_w_in,
        grad_w_out,
        expert_counts + tally,
    )


def block_dispatched(
    layer_input,
    segments,
    keep_mask,
    att_routes,
    moe_routes,
    expert_counts,
    norm_gain,
    w_query,
    w_key,
    w_select,
    w_value,
    w_output,
    w_router,
    w_in,
    w_out,
    cotangent,
):
    tok_rows, model_dim = layer_input.shape
    seq_count, seq_len = segments.shape
    head_count = w_query.shape[1] // DH
    score_scale = DH ** (-0.5)
    inputs_f = layer_input.astype(jnp.float32)
    normed, norm_pull = jax.vjp(layer_norm, inputs_f, norm_gain)
    normed_bf = normed.astype(jnp.bfloat16)
    query_rows = jnp.dot(normed_bf, w_query, preferred_element_type=jnp.float32).reshape(
        tok_rows, head_count, DH
    )
    key_rows = jnp.dot(normed_bf, w_key, preferred_element_type=jnp.float32).reshape(
        tok_rows, head_count, DH
    )
    logits = jnp.dot(layer_input, w_select, preferred_element_type=jnp.float32)
    named_mask = jnp.sum(
        (att_routes[..., None] == jnp.arange(VEXP, dtype=jnp.int32)).astype(jnp.float32), axis=2
    )
    select_sig = jax.nn.sigmoid(logits).reshape(tok_rows, 2 * head_count, VEXP)
    head_gates = select_sig * named_mask
    value_all = jnp.dot(layer_input, w_value, preferred_element_type=jnp.float32).reshape(
        tok_rows, head_count, VEXP, DH
    )
    value_bf = jnp.sum(head_gates[:, :head_count, :, None] * value_all, axis=2).astype(jnp.bfloat16)
    position, allowed = jax.vmap(doc_layout)(segments, keep_mask)
    cos_tab, sin_tab = rope_tables(position.reshape(-1), DH)
    q_rot = (rotate(query_rows, cos_tab, sin_tab) * score_scale).astype(jnp.bfloat16)
    k_rot = rotate(key_rows, cos_tab, sin_tab).astype(jnp.bfloat16)
    seq_shape = (seq_count, seq_len, head_count, DH)
    attended, log_total = lax.map(
        attend_forward,
        (q_rot.reshape(seq_shape), k_rot.reshape(seq_shape), value_bf.reshape(seq_shape), allowed),
    )
    attended = attended.reshape(tok_rows, head_count, DH)
    mixed_bf = (
        (head_gates[:, head_count:, :, None] * attended[:, :, None, :])
        .astype(jnp.bfloat16)
        .reshape(tok_rows, head_count * VEXP * DH)
    )
    hidden = inputs_f + jnp.dot(mixed_bf, w_output, preferred_element_type=jnp.float32)
    dev_count = lax.axis_size("expert")
    exp_local = w_in.shape[0]
    exp_total = dev_count * exp_local
    top_k = moe_routes.shape[1]
    capacity = 10 * tok_rows * top_k // (7 * exp_total) + 1
    owner, filled, slot_of = slot_table(moe_routes, exp_total, capacity)
    keep_slot = filled[:, None] > 0
    zero_bf = jnp.zeros((), jnp.bfloat16)
    hidden_bf = hidden.astype(jnp.bfloat16)
    send_rows = jnp.where(keep_slot, hidden_bf[owner], zero_bf).reshape(
        dev_count, exp_local * capacity, model_dim
    )
    rows_in = lax.all_to_all(send_rows, "expert", split_axis=0, concat_axis=0, tiled=True)
    histogram = jnp.zeros((exp_total,), jnp.float32).at[moe_routes.reshape(-1)].add(1.0)
    tally = lax.psum_scatter(histogram, "expert", scatter_dimension=0, tiled=True)
    slot_shape = (dev_count, exp_local, capacity, model_dim)
    rows_four = rows_in.reshape(slot_shape)
    pre_act = jnp.einsum("necd,edf->necf", rows_four, w_in, preferred_element_type=jnp.float32)
    gelu_out, gelu_pull = jax.vjp(jax.nn.gelu, pre_act)
    act_bf = gelu_out.astype(jnp.bfloat16)
    router_logit = jnp.einsum(
        "necd,ed->nec", rows_four, w_router, preferred_element_type=jnp.float32
    )
    gate_moe = jax.nn.sigmoid(router_logit)
    expert_out = jnp.einsum("necf,efd->necd", act_bf, w_out, preferred_element_type=jnp.float32)
    reply = (
        (gate_moe[..., None] * expert_out)
        .astype(jnp.bfloat16)
        .reshape(dev_count, exp_local * capacity, model_dim)
    )
    returned = lax.all_to_all(reply, "expert", split_axis=0, concat_axis=0, tiled=True)
    moe_sum = jnp.sum(returned.reshape(-1, model_dim)[slot_of].astype(jnp.float32), axis=1)
    layer_output = (hidden + moe_sum).astype(jnp.bfloat16)
    cot_f = cotangent.astype(jnp.float32)
    send_cot = jnp.where(keep_slot, cotangent[owner], zero_bf).reshape(
        dev_count, exp_local * capacity, model_dim
    )
    cot_in, rows_again = (
        lax.all_to_all(send_cot, "expert", split_axis=0, concat_axis=0, tiled=True),
        lax.all_to_all(send_rows, "expert", split_axis=0, concat_axis=0, tiled=True),
    )
    rows_grad = rows_again.reshape(slot_shape)
    cot_bf = cot_in.reshape(slot_shape)
    raw_back = jnp.einsum("necd,efd->necf", cot_bf, w_out, preferred_element_type=jnp.float32)
    dgate = jnp.sum(act_bf.astype(jnp.float32) * raw_back, axis=-1)
    dlogit = dgate * gate_moe * (1.0 - gate_moe)
    dexpert = (gate_moe[..., None] * cot_bf.astype(jnp.float32)).astype(jnp.bfloat16)
    grad_w_out = jnp.einsum("necf,necd->efd", act_bf, dexpert, preferred_element_type=jnp.float32)
    dact = jnp.einsum("necd,efd->necf", dexpert, w_out, preferred_element_type=jnp.float32)
    dpre_bf = gelu_pull(dact)[0].astype(jnp.bfloat16)
    grad_w_in = jnp.einsum("necd,necf->edf", rows_grad, dpre_bf, preferred_element_type=jnp.float32)
    grad_router = jnp.einsum(
        "nec,necd->ed",
        dlogit,
        rows_grad.astype(jnp.float32),
        preferred_element_type=jnp.float32,
        precision=HIGHEST,
    )
    dsent = jnp.einsum("necf,edf->necd", dpre_bf, w_in, preferred_element_type=jnp.float32)
    dsent = (dsent + dlogit[..., None] * w_router[None, :, None, :].astype(jnp.float32)).astype(
        jnp.bfloat16
    )
    grad_back = lax.all_to_all(
        dsent.reshape(dev_count, exp_local * capacity, model_dim),
        "expert",
        split_axis=0,
        concat_axis=0,
        tiled=True,
    )
    dhidden = cot_f + jnp.sum(grad_back.reshape(-1, model_dim)[slot_of].astype(jnp.float32), axis=1)
    dy_bf = dhidden.astype(jnp.bfloat16)
    grad_output = jnp.einsum("tk,td->kd", mixed_bf, dy_bf, preferred_element_type=jnp.float32)
    dmixed = jnp.einsum("td,kd->tk", dy_bf, w_output, preferred_element_type=jnp.float32).reshape(
        tok_rows, head_count, VEXP, DH
    )
    dgate_out = jnp.sum(dmixed * attended[:, :, None, :], axis=-1)
    dattend = jnp.sum(head_gates[:, head_count:, :, None] * dmixed, axis=2).astype(jnp.bfloat16)
    grad_q, grad_k, grad_v = lax.map(
        attend_backward,
        (
            q_rot.reshape(seq_shape),
            k_rot.reshape(seq_shape),
            value_bf.reshape(seq_shape),
            allowed,
            log_total,
            dattend.reshape(seq_shape),
        ),
    )
    dquery = (
        (rotate_back(grad_q.reshape(tok_rows, head_count, DH), cos_tab, sin_tab) * score_scale)
        .astype(jnp.bfloat16)
        .reshape(tok_rows, head_count * DH)
    )
    dkey = (
        rotate_back(grad_k.reshape(tok_rows, head_count, DH), cos_tab, sin_tab)
        .astype(jnp.bfloat16)
        .reshape(tok_rows, head_count * DH)
    )
    grad_query = jnp.einsum("td,tk->dk", normed_bf, dquery, preferred_element_type=jnp.float32)
    grad_key = jnp.einsum("td,tk->dk", normed_bf, dkey, preferred_element_type=jnp.float32)
    dnormed = jnp.einsum(
        "tk,dk->td", dquery, w_query, preferred_element_type=jnp.float32
    ) + jnp.einsum("tk,dk->td", dkey, w_key, preferred_element_type=jnp.float32)
    dx_norm, grad_gain = norm_pull(dnormed)
    dvalue = grad_v.reshape(tok_rows, head_count, DH)
    dgate_val = jnp.sum(dvalue[:, :, None, :] * value_all, axis=-1)
    dvalue_all = (
        (head_gates[:, :head_count, :, None] * dvalue[:, :, None, :])
        .astype(jnp.bfloat16)
        .reshape(tok_rows, head_count * VEXP * DH)
    )
    grad_value = jnp.einsum(
        "td,tk->dk", layer_input, dvalue_all, preferred_element_type=jnp.float32
    )
    dgates = jnp.concatenate([dgate_val, dgate_out], axis=1)
    dlogits = (
        (dgates * named_mask * select_sig * (1.0 - select_sig))
        .astype(jnp.bfloat16)
        .reshape(tok_rows, 2 * head_count * VEXP)
    )
    grad_select = jnp.einsum("td,tk->dk", layer_input, dlogits, preferred_element_type=jnp.float32)
    grad_input = (
        dhidden
        + dx_norm
        + jnp.einsum("tk,dk->td", dvalue_all, w_value, preferred_element_type=jnp.float32)
    )
    grad_input = (
        grad_input + jnp.einsum("tk,dk->td", dlogits, w_select, preferred_element_type=jnp.float32)
    ).astype(jnp.bfloat16)
    expert_sums = (
        lax.psum(grad_w_in.astype(jnp.bfloat16), "dp").astype(jnp.float32),
        lax.psum(grad_w_out.astype(jnp.bfloat16), "dp").astype(jnp.float32),
        lax.psum(grad_router.astype(jnp.bfloat16), "dp").astype(jnp.float32),
        lax.psum(tally.astype(jnp.bfloat16), "dp").astype(jnp.float32),
    )
    dense_sums = (
        lax.psum_scatter(grad_gain, ("dp", "expert"), scatter_dimension=0, tiled=True),
        lax.psum_scatter(grad_query, ("dp", "expert"), scatter_dimension=0, tiled=True),
        lax.psum_scatter(grad_key, ("dp", "expert"), scatter_dimension=0, tiled=True),
        lax.psum_scatter(grad_select, ("dp", "expert"), scatter_dimension=0, tiled=True),
        lax.psum_scatter(grad_value, ("dp", "expert"), scatter_dimension=0, tiled=True),
        lax.psum_scatter(grad_output, ("dp", "expert"), scatter_dimension=1, tiled=True),
    )
    counts_out = expert_counts + expert_sums[3].astype(jnp.int32)
    return (
        layer_output,
        grad_input,
        dense_sums[0],
        dense_sums[1],
        dense_sums[2],
        dense_sums[3],
        dense_sums[4],
        dense_sums[5],
        expert_sums[2],
        expert_sums[0],
        expert_sums[1],
        counts_out,
    )


def local(*args):
    rows, top_k = args[4].shape
    experts, _, ff_dim = args[13].shape
    exp_total = lax.axis_size("expert") * experts
    capacity = 10 * rows * top_k // (7 * exp_total) + 1
    regular = lax.axis_size("dp") == 4 and lax.axis_size("expert") == 8 and experts % 2 == 0 and ff_dim == LANE
    return (block_dense if regular and 4 * capacity > rows else block_dispatched)(*args)


def solution(mesh):
    placed = (
        P(("dp", "expert"), None),
        P(("dp", "expert"), None),
        P(("dp", "expert"), None),
        P(("dp", "expert"), None, None),
        P(("dp", "expert"), None),
        P("expert"),
        P(),
        P(),
        P(),
        P(),
        P(),
        P(),
        P("expert", None),
        P("expert", None, None),
        P("expert", None, None),
        P(("dp", "expert"), None),
    )
    return jax.shard_map(
        local,
        mesh=mesh,
        in_specs=placed,
        out_specs=(
            P(("dp", "expert"), None),
            P(("dp", "expert"), None),
            P(("dp", "expert")),
            P(("dp", "expert"), None),
            P(("dp", "expert"), None),
            P(("dp", "expert"), None),
            P(("dp", "expert"), None),
            P(None, ("dp", "expert")),
            P("expert", None),
            P("expert", None, None),
            P("expert", None, None),
            P("expert"),
        ),
        check_vma=False,
    )
```

```python
import functools

import jax
import jax.numpy as jnp
from jax import lax
from jax.experimental import pallas as pl
from jax.experimental.pallas import tpu as pltpu
from jax.sharding import PartitionSpec as P

DH = 128
VEXP = 5


NORM_EPS = 1e-05
ROPE_BASE = 10000.0
MASK_FILL = -1e30
HIGHEST = lax.Precision.HIGHEST
ROUTER_ROWS = 64
DIGITS = 5
LANE = 128
GAIN_ROWS = 16
TILE = 256
VMEM_BYTES = 60 << 20
GELU_A = 0.7978845608028654
GELU_B = 0.044715


def layer_norm(values, gain_vec):
    center = values - jnp.mean(values, axis=-1, keepdims=True)
    spread = jnp.mean(center * center, axis=-1, keepdims=True)
    return center * lax.rsqrt(spread + NORM_EPS) * gain_vec


def rope_tables(position, width_dh):
    half_dh = width_dh // 2
    freq_row = jnp.power(ROPE_BASE, jnp.arange(half_dh, dtype=jnp.float32) * (-2.0 / width_dh))
    angle_tab = position.astype(jnp.float32)[:, None] * freq_row[None, :]
    return (jnp.cos(angle_tab), jnp.sin(angle_tab))


def rotate(values, cos_tab, sin_tab):
    half_dh = values.shape[-1] // 2
    first_half = values[..., :half_dh]
    second_half = values[..., half_dh:]
    cos_b = cos_tab[:, None, :]
    sin_b = sin_tab[:, None, :]
    return jnp.concatenate(
        [first_half * cos_b - second_half * sin_b, second_half * cos_b + first_half * sin_b],
        axis=-1,
    )


def rotate_back(grad_rot, cos_tab, sin_tab):
    half_dh = grad_rot.shape[-1] // 2
    grad_first = grad_rot[..., :half_dh]
    grad_second = grad_rot[..., half_dh:]
    cos_b = cos_tab[:, None, :]
    sin_b = sin_tab[:, None, :]
    return jnp.concatenate(
        [grad_first * cos_b + grad_second * sin_b, grad_second * cos_b - grad_first * sin_b],
        axis=-1,
    )


def doc_layout(seg_row, keep_row):
    length_s = seg_row.shape[0]
    column = jnp.arange(length_s, dtype=jnp.int32)
    new_doc = jnp.concatenate([jnp.ones((1,), dtype=jnp.bool_), seg_row[1:] != seg_row[:-1]])
    doc_start = lax.cummax(jnp.where(new_doc, column, jnp.zeros_like(column)), axis=0)
    position = column - doc_start
    same_doc = seg_row[:, None] == seg_row[None, :]
    causal = column[None, :] <= column[:, None]
    visible = (keep_row[None, :] == 1) | (column[None, :] == column[:, None])
    return (position, same_doc & causal & visible)


def slot_table(routes, exp_total, capacity):
    flat_ids = routes.reshape(-1)
    pair_count = flat_ids.shape[0]
    top_k = routes.shape[1]
    sort_order = jnp.argsort(flat_ids, stable=True)
    ranked = flat_ids[sort_order]
    first_slot = jnp.searchsorted(ranked, jnp.arange(exp_total, dtype=jnp.int32), side="left")
    slot_rank = jnp.arange(pair_count, dtype=jnp.int32) - first_slot[ranked]
    slot_dest = ranked * capacity + slot_rank
    owner = jnp.zeros((exp_total * capacity,), jnp.int32).at[slot_dest].set(sort_order // top_k)
    filled = jnp.zeros((exp_total * capacity,), jnp.float32).at[slot_dest].set(1.0)
    slot_of = (
        jnp.zeros((pair_count,), jnp.int32).at[sort_order].set(slot_dest).reshape(routes.shape)
    )
    return (owner, filled, slot_of)


def block_scores(q_blk, k_rows, allowed_blk):
    scores = jnp.einsum("qhd,khd->hqk", q_blk, k_rows, preferred_element_type=jnp.float32)
    return jnp.where(allowed_blk[None, :, :], scores, MASK_FILL)


def attend_forward(pieces):
    q_rows, k_rows, v_rows, allowed = pieces
    length_s = q_rows.shape[0]
    block_len = min(512, length_s)
    outs_list = []
    lse_list = []
    for begin_at in range(0, length_s, block_len):
        scores = block_scores(
            q_rows[begin_at : begin_at + block_len],
            k_rows,
            allowed[begin_at : begin_at + block_len],
        )
        row_max = jnp.max(scores, axis=-1, keepdims=True)
        exp_terms = jnp.exp(scores - row_max)
        row_sum = jnp.sum(exp_terms, axis=-1, keepdims=True)
        probs_bf = (exp_terms / row_sum).astype(jnp.bfloat16)
        outs_list.append(
            jnp.einsum("hqk,khd->qhd", probs_bf, v_rows, preferred_element_type=jnp.float32)
        )
        lse_list.append((row_max + jnp.log(row_sum))[..., 0])
    return (jnp.concatenate(outs_list, axis=0), jnp.concatenate(lse_list, axis=1))


def attend_backward(pieces):
    q_rows, k_rows, v_rows, allowed, log_total, grad_rows = pieces
    length_s = q_rows.shape[0]
    block_len = min(512, length_s)
    grad_q_list = []
    grad_k = jnp.zeros(k_rows.shape, jnp.float32)
    grad_v = jnp.zeros(v_rows.shape, jnp.float32)
    for begin_at in range(0, length_s, block_len):
        q_blk = q_rows[begin_at : begin_at + block_len]
        grad_blk = grad_rows[begin_at : begin_at + block_len]
        scores = block_scores(q_blk, k_rows, allowed[begin_at : begin_at + block_len])
        probs_f = jnp.exp(scores - log_total[:, begin_at : begin_at + block_len, None])
        grad_prob = jnp.einsum("qhd,khd->hqk", grad_blk, v_rows, preferred_element_type=jnp.float32)
        grad_score = (
            probs_f * (grad_prob - jnp.sum(probs_f * grad_prob, axis=-1, keepdims=True))
        ).astype(jnp.bfloat16)
        grad_v = grad_v + jnp.einsum(
            "hqk,qhd->khd",
            probs_f.astype(jnp.bfloat16),
            grad_blk,
            preferred_element_type=jnp.float32,
        )
        grad_q_list.append(
            jnp.einsum("hqk,khd->qhd", grad_score, k_rows, preferred_element_type=jnp.float32)
        )
        grad_k = grad_k + jnp.einsum(
            "hqk,qhd->khd", grad_score, q_blk, preferred_element_type=jnp.float32
        )
    return (jnp.concatenate(grad_q_list, axis=0), grad_k, grad_v)


def dot_nt(left, right):
    return lax.dot_general(left, right, (((1,), (1,)), ((), ())), preferred_element_type=jnp.float32)


def dot_nn(left, right):
    return lax.dot_general(left, right, (((1,), (0,)), ((), ())), preferred_element_type=jnp.float32)


def dot_tn(left, right):
    return lax.dot_general(left, right, (((0,), (0,)), ((), ())), preferred_element_type=jnp.float32)


def spin(values, cos_two, sin_two):
    return values * cos_two + pltpu.roll(values, DH // 2, 1) * sin_two


def spin_back(values, cos_two, sin_two):
    return values * cos_two - pltpu.roll(values, DH // 2, 1) * sin_two


def window_mask(step, tile, start_col, keep_before, keep_now):
    row = step * tile + lax.broadcasted_iota(jnp.int32, (tile, 2 * tile), 0)
    col = (step - 1) * tile + lax.broadcasted_iota(jnp.int32, (tile, 2 * tile), 1)
    keep_row = jnp.concatenate([keep_before, keep_now], axis=1)
    return (col >= start_col) & (col <= row) & ((keep_row == 1) | (col == row))


def neighbour(kind, amount):
    mine, place = lax.axis_index("dp"), lax.axis_index("expert")
    chips = lax.axis_size("expert") // 2
    chip, core = place // 2, lax.rem(place, 2)
    if kind == "dp":
        flipped = [mine, mine + 1 - 2 * lax.rem(mine, 2), lax.rem(mine + 2, 4), 3 - mine]
        return (flipped[amount], place)
    if kind == "core":
        return (mine, place + 1 - 2 * core)
    return (mine, 2 * lax.rem(chip + amount + chips, chips) + core)


def own_part(rows):
    return lambda mine, flipped: mine * rows


def fixed(start):
    return lambda mine, flipped: start


def shift_move(src, dst, hop, src_at, dst_at, count):
    return [(src, dst, "chip", hop, src_at, dst_at, count)]


def greet(peers):
    barrier = pltpu.get_barrier_semaphore()
    for peer in peers:
        pl.semaphore_signal(barrier, inc=1, device_id=peer, device_id_type=pl.DeviceIdType.MESH)
    pl.semaphore_wait(barrier, len(peers))


def peers_of(moves):
    peers = []
    for _, _, kind, amount, _, _, _ in moves:
        peers.append(neighbour(kind, amount))
        if kind == "chip":
            peers.append(neighbour(kind, -amount))
    return peers


def copies_of(moves, ins, outs, send_sem, recv_sem):
    mine = lax.axis_index("dp")
    copies = []
    for i, (src, dst, kind, amount, src_at, dst_at, count) in enumerate(moves):
        peer = neighbour(kind, amount)
        copies.append(
            pltpu.make_async_remote_copy(
                src_ref=ins[src].at[pl.ds(pl.multiple_of(src_at(mine, peer[0]), 16), count)],
                dst_ref=outs[dst].at[pl.ds(pl.multiple_of(dst_at(mine, peer[0]), 16), count)],
                send_sem=send_sem.at[i],
                recv_sem=recv_sem.at[i],
                device_id=peer,
                device_id_type=pl.DeviceIdType.MESH,
            )
        )
    return copies


ANYWHERE = pl.BlockSpec(memory_space=pl.ANY)


def tile_rows(index, tile):
    return pl.ds(pl.multiple_of(index * tile, tile), tile)


def flips():
    mine = lax.axis_index("dp")
    return [mine, mine + 1 - 2 * lax.rem(mine, 2), lax.rem(mine + 2, 4), 3 - mine]


def remote(src, dst, sems, index, peer):
    return pltpu.make_async_remote_copy(
        src_ref=src,
        dst_ref=dst,
        send_sem=sems.at[0, index],
        recv_sem=sems.at[1, index],
        device_id=peer,
        device_id_type=pl.DeviceIdType.MESH,
    )


def span(start, count):
    return pl.ds(pl.multiple_of(start, 16), count)


def halving_first(source, near, far, part, cut, sems, at):
    dp = flips()
    low = part - cut
    copies = []
    for slot, owner in enumerate((1, 3)):
        copies.append(
            remote(
                source.at[span(dp[owner] * part, cut)],
                near.at[pl.ds(slot * cut, cut)],
                sems,
                at + slot,
                neighbour("dp", 1),
            )
        )
    for slot, owner in enumerate((2, 3)):
        copies.append(
            remote(
                source.at[span(dp[owner] * part + cut, low)],
                far.at[pl.ds(slot * low, low)],
                sems,
                at + 2 + slot,
                neighbour("dp", 2),
            )
        )
    return copies


def halving_second(send, land, part, cut, sems, at):
    low = part - cut
    return [
        remote(send.at[pl.ds(0, cut)], land.at[pl.ds(0, cut)], sems, at, neighbour("dp", 2)),
        remote(send.at[pl.ds(cut, low)], land.at[pl.ds(cut, low)], sems, at + 1, neighbour("dp", 1)),
    ]


def as_f32(ref, start, count):
    return ref[pl.ds(start, count), :].astype(jnp.float32)


def spread_first(source, target, part, cut, sems, at):
    mine = lax.axis_index("dp")
    return [
        remote(
            source.at[pl.ds(0, cut)],
            target.at[span(mine * part, cut)],
            sems,
            at,
            neighbour("dp", 1),
        ),
        remote(
            source.at[pl.ds(cut, part - cut)],
            target.at[span(mine * part + cut, part - cut)],
            sems,
            at + 1,
            neighbour("dp", 2),
        ),
    ]


def spread_second(source, target, part, cut, sems, at):
    dp = flips()
    low = part - cut
    mine_up, mine_down = span(dp[0] * part, cut), span(dp[0] * part + cut, low)
    got_up, got_down = span(dp[1] * part, cut), span(dp[2] * part + cut, low)
    return [
        remote(source.at[pl.ds(0, cut)], target.at[mine_up], sems, at, neighbour("dp", 2)),
        remote(target.at[got_up], target.at[got_up], sems, at + 1, neighbour("dp", 2)),
        remote(source.at[pl.ds(cut, low)], target.at[mine_down], sems, at + 2, neighbour("dp", 1)),
        remote(target.at[got_down], target.at[got_down], sems, at + 3, neighbour("dp", 1)),
    ]


def load_own(source, own, part, cut, sems):
    dp = flips()
    low = part - cut
    return [
        pltpu.make_async_copy(
            source.at[span(dp[owner] * part + start, count)], own.at[pl.ds(at, count)], sems.at[i]
        )
        for i, (owner, start, count, at) in enumerate(
            [(0, 0, cut, 0), (2, 0, cut, cut), (0, cut, low, 2 * cut), (1, cut, low, 2 * cut + low)]
        )
    ]


class Halving:
    def __init__(self, source, total, buffers, part, cut):
        near, far, send, land, sems = buffers[:5]
        self.source, self.total, self.part, self.cut = source, total, part, cut
        self.near, self.far, self.send, self.land = near, far, send, land
        self.own, self.loads = None, []
        if len(buffers) > 5:
            self.own, load_sems = buffers[5:]
            self.loads = load_own(source, self.own, part, cut, load_sems)
        self.first = halving_first(source, near, far, part, cut, sems, 0)
        self.second = halving_second(send, land, part, cut, sems, 4)

    def start(self):
        for copy in self.first + self.loads:
            copy.start()

    def own_rows(self, which):
        part, cut = self.part, self.cut
        low = part - cut
        if self.own is not None:
            return as_f32(self.own, (0, cut, 2 * cut, 2 * cut + low)[which], (cut, low)[which // 2])
        owner, start = ((0, 0), (2, 0), (0, cut), (1, cut))[which]
        return as_f32(
            self.source, pl.multiple_of(flips()[owner] * part + start, 16), (cut, low)[which // 2]
        )

    def turn(self):
        part, cut = self.part, self.cut
        low = part - cut
        for copy in self.first + self.loads:
            copy.wait()
        up = self.own_rows(1) + as_f32(self.near, cut, cut)
        down = self.own_rows(3) + as_f32(self.far, low, low)
        self.send[:cut, :] = up.astype(jnp.bfloat16)
        self.send[cut:, :] = down.astype(jnp.bfloat16)
        for copy in self.second:
            copy.start()
        self.total[:cut, :] = (self.own_rows(0) + as_f32(self.near, 0, cut)).astype(jnp.bfloat16)
        self.total[cut:, :] = (self.own_rows(2) + as_f32(self.far, 0, low)).astype(jnp.bfloat16)

    def finish(self):
        for copy in self.second:
            copy.wait()
        total = as_f32(self.total, 0, self.part) + as_f32(self.land, 0, self.part)
        self.total[...] = total.astype(jnp.bfloat16)


def halving_buffers(part, cut, model):
    bf16 = lambda rows: pltpu.VMEM((rows, model), jnp.bfloat16)
    return [
        bf16(2 * cut),
        bf16(2 * (part - cut)),
        bf16(part),
        bf16(part),
        pltpu.SemaphoreType.DMA((2, 6)),
        bf16(2 * part),
        pltpu.SemaphoreType.DMA((4,)),
    ]


class Spreading:
    def __init__(self, target, part, cut, sems, mine):
        self.first = spread_first(mine, target, part, cut, sems, 0)
        self.second = spread_second(mine, target, part, cut, sems, 2)

    def start(self):
        for copy in self.first:
            copy.start()

    def turn(self):
        for copy in self.first:
            copy.wait()
        for copy in self.second:
            copy.start()

    def finish(self):
        for copy in self.second:
            copy.wait()


def forward_body(heads, tile, steps, ahead, *refs):
    (
        own_any,
        cot_any,
        x_ref,
        start_ref,
        keep_ref,
        cos_ref,
        sin_ref,
        mask_ref,
        gain_ref,
        wsel_ref,
        wq_any,
        wk_any,
        wval_any,
        wout_any,
        chunk_any,
        near_any,
        cot_far_any,
        sent_far_any,
        hid_ref,
        norm_ref,
        q_ref,
        k_ref,
        v_ref,
        val_ref,
        att_ref,
        sig_ref,
        lse_ref,
        mix_ref,
        sent_all,
        send_sem,
        recv_sem,
        tile_send,
        tile_recv,
        wqk_ref,
        wval_ref,
        wout_ref,
        load_sem,
    ) = refs
    step = pl.program_id(0)
    narrow = heads * DH
    loads = [
        pltpu.make_async_copy(source, target, load_sem.at[i])
        for i, (source, target) in enumerate(
            [
                (wq_any, wqk_ref.at[:, pl.ds(0, narrow)]),
                (wk_any, wqk_ref.at[:, pl.ds(narrow, narrow)]),
                (wval_any, wval_ref),
                (wout_any, wout_ref),
            ]
        )
    ]

    def loaded(which):
        @pl.when(step == 0)
        def _():
            for i in which:
                loads[i].wait()

    @pl.when(step == 0)
    def _():
        for copy in loads:
            copy.start()

    rows = steps * tile
    quarter = own_any.shape[0] // 4
    moves = shift_move(0, 0, -3, own_part(quarter), own_part(quarter), quarter)
    moves = moves + shift_move(0, 1, -2, own_part(quarter), own_part(quarter), ahead)
    moves = moves + [(1, 2, "core", 1, fixed(0), fixed(0), rows)]
    partner = neighbour("core", 1)
    copies = copies_of(moves, [own_any, cot_any], [chunk_any, near_any, cot_far_any], send_sem, recv_sem)

    def tile_copy(index):
        return pltpu.make_async_remote_copy(
            src_ref=sent_all.at[pl.ds(index * tile, tile)],
            dst_ref=sent_far_any.at[pl.ds(index * tile, tile)],
            send_sem=tile_send.at[index],
            recv_sem=tile_recv.at[index],
            device_id=partner,
            device_id_type=pl.DeviceIdType.MESH,
        )


    @pl.when(step == 0)
    def _():
        greet(peers_of(moves))
        for copy in copies:
            copy.start()

    now = tile_rows(step, tile)
    before = tile_rows(jnp.maximum(step - 1, 0), tile)
    x = x_ref[...]
    x_f = x.astype(jnp.float32)
    center = x_f - jnp.mean(x_f, axis=1, keepdims=True)
    spread = jnp.mean(center * center, axis=1, keepdims=True)
    normed = (center * lax.rsqrt(spread + NORM_EPS) * gain_ref[...]).astype(jnp.bfloat16)
    norm_ref[...] = normed
    sig = 1.0 / (1.0 + jnp.exp(-dot_nn(x, wsel_ref[...])))
    sig_ref[...] = sig
    gates = sig * mask_ref[...].astype(jnp.float32)
    cos_two, sin_two = cos_ref[...], sin_ref[...]
    allowed = window_mask(step, tile, start_ref[...], keep_ref[:, before], keep_ref[:, now])
    scale = DH ** (-0.5)
    lanes = lax.broadcasted_iota(jnp.int32, (tile, LANE), 1)
    lse = jnp.zeros((tile, LANE), jnp.float32)
    loaded((0, 1))
    qk = dot_nn(normed, wqk_ref[...])
    loaded((2,))
    for head in range(heads):
        cols = slice(head * DH, (head + 1) * DH)
        value = dot_nn(x, wval_ref[:, head * VEXP * DH : (head + 1) * VEXP * DH])
        val_ref[:, head * VEXP * DH : (head + 1) * VEXP * DH] = value.astype(jnp.bfloat16)
        total = jnp.zeros((tile, DH), jnp.float32)
        for e in range(VEXP):
            at = head * VEXP + e
            total = total + gates[:, at : at + 1] * value[:, e * DH : (e + 1) * DH]
        v_ref[now, cols] = total.astype(jnp.bfloat16)
    for head in range(heads):
        cols = slice(head * DH, (head + 1) * DH)
        q_head = (spin(qk[:, cols], cos_two, sin_two) * scale).astype(jnp.bfloat16)
        k_head = spin(
            qk[:, (heads + head) * DH : (heads + head + 1) * DH], cos_two, sin_two
        ).astype(jnp.bfloat16)
        q_ref[:, cols] = q_head
        k_ref[now, cols] = k_head
        scores = jnp.concatenate(
            [dot_nt(q_head, k_ref[before, cols]), dot_nt(q_head, k_head)], axis=1
        )
        scores = jnp.where(allowed, scores, MASK_FILL)
        row_max = jnp.max(scores, axis=1, keepdims=True)
        terms = jnp.exp(scores - row_max)
        row_sum = jnp.sum(terms, axis=1, keepdims=True)
        probs = (terms * (1.0 / row_sum)).astype(jnp.bfloat16)
        attended = dot_nn(probs[:, :tile], v_ref[before, cols]) + dot_nn(
            probs[:, tile:], v_ref[now, cols]
        )
        att_ref[:, cols] = attended
        lse = jnp.where(lanes == head, row_max + jnp.log(row_sum), lse)
        for e in range(VEXP):
            at = head * VEXP + e
            gate = gates[:, heads * VEXP + at : heads * VEXP + at + 1]
            mix_ref[:, at * DH : (at + 1) * DH] = (gate * attended).astype(jnp.bfloat16)
    lse_ref[...] = lse
    loaded((3,))
    hidden = x_f + dot_nn(mix_ref[...], wout_ref[...])
    hid_ref[...] = hidden
    sent_all[now, :] = hidden.astype(jnp.bfloat16)
    for index in range(steps):

        @pl.when(step == index)
        def _(index=index):
            tile_copy(index).start()

    @pl.when(step == steps - 1)
    def _():
        for copy in copies:
            copy.wait()
        for index in range(steps):
            tile_copy(index).wait()


def whole_block(shape):
    return pl.BlockSpec(shape, lambda step: (0,) * len(shape), pipeline_mode=pl.Buffered(1))


def attention_forward(ahead, own, cot, x, start, keep, cos_two, sin_two, mask, gain, wsel, wq, wk, wval, wout, tile):
    rows, model = x.shape
    heads = wq.shape[1] // DH
    per_tile = lambda width: pl.BlockSpec((tile, width), lambda step: (step, 0))
    full = lambda arr: whole_block(arr.shape)
    narrow, wide = heads * DH, heads * VEXP * DH
    shapes = [
        (model, jnp.float32, False),
        (model, jnp.bfloat16, False),
        (narrow, jnp.bfloat16, False),
        (narrow, jnp.bfloat16, True),
        (narrow, jnp.bfloat16, True),
        (wide, jnp.bfloat16, False),
        (narrow, jnp.float32, False),
        (LANE, jnp.float32, False),
        (LANE, jnp.float32, False),
        (wide, jnp.bfloat16, False),
        (model, jnp.bfloat16, True),
    ]
    return pl.pallas_call(
        functools.partial(forward_body, heads, tile, rows // tile, ahead),
        grid=(rows // tile,),
        in_specs=[
            ANYWHERE,
            ANYWHERE,
            per_tile(model),
            per_tile(1),
            full(keep),
            per_tile(LANE),
            per_tile(LANE),
            per_tile(LANE),
            full(gain),
            full(wsel),
            ANYWHERE,
            ANYWHERE,
            ANYWHERE,
            ANYWHERE,
        ],
        out_specs=[ANYWHERE] * 4
        + [whole_block((rows, width)) if whole else per_tile(width) for width, _, whole in shapes],
        out_shape=[
            jax.ShapeDtypeStruct(own.shape, jnp.bfloat16),
            jax.ShapeDtypeStruct(own.shape, jnp.bfloat16),
            jax.ShapeDtypeStruct((rows, model), jnp.bfloat16),
            jax.ShapeDtypeStruct((rows, model), jnp.bfloat16),
        ]
        + [jax.ShapeDtypeStruct((rows, width), kind) for width, kind, _ in shapes],
        scratch_shapes=[
            pltpu.SemaphoreType.DMA((3,)),
            pltpu.SemaphoreType.DMA((3,)),
            pltpu.SemaphoreType.DMA((rows // tile,)),
            pltpu.SemaphoreType.DMA((rows // tile,)),
            pltpu.VMEM((model, 2 * narrow), jnp.bfloat16),
            pltpu.VMEM(wval.shape, jnp.bfloat16),
            pltpu.VMEM(wout.shape, jnp.bfloat16),
            pltpu.SemaphoreType.DMA((4,)),
        ],
        compiler_params=pltpu.CompilerParams(
            vmem_limit_bytes=VMEM_BYTES, collective_id=1, has_side_effects=True
        ),
        cost_estimate=pl.CostEstimate(
            flops=2 * rows * model * (2 * narrow + 2 * wide), bytes_accessed=40 << 20, transcendentals=0
        ),
    )(own, cot, x, start, keep, cos_two, sin_two, mask, gain, wsel, wq, wk, wval, wout)


def backward_body(heads, tile, steps, moves, halve, part, n_in, n_out, *refs):
    ins, refs = refs[:n_in], refs[n_in:]
    (
        cot_ref,
        grad_own_ref,
        grad_far_ref,
        q_ref,
        k_ref,
        v_ref,
        att_ref,
        lse_ref,
        start_ref,
        keep_ref,
        sig_now_ref,
        mask_now_ref,
        cos_now_ref,
        sin_now_ref,
        sig_old_ref,
        mask_old_ref,
        cos_old_ref,
        sin_old_ref,
        x_ref,
        val_ref,
        gain_ref,
        wsel_ref,
        wout_ref,
        wq_any,
        wk_any,
        wval_any,
        *outs_and_rest,
    ) = refs
    outs, rest = outs_and_rest[:n_out], outs_and_rest[n_out:]
    (
        gin_ref,
        dqk_ref,
        dval_ref,
        dlog_ref,
        ggain_ref,
        dy_ref,
        *totals_and_rest,
    ) = rest
    totals, rest = totals_and_rest[: len(halve)], totals_and_rest[len(halve) :]
    (
        dk_acc,
        dv_acc,
        dq_keep,
        dgate_keep,
        gain_acc,
        dhid_keep,
        wqk_ref,
        wval_ref,
        load_sem,
        send_sem,
        recv_sem,
        *buffers,
    ) = rest
    step = pl.program_id(0)
    half_qk = heads * DH
    loads = [
        pltpu.make_async_copy(source, target, load_sem.at[i])
        for i, (source, target) in enumerate(
            [
                (wq_any, wqk_ref.at[:, pl.ds(0, half_qk)]),
                (wk_any, wqk_ref.at[:, pl.ds(half_qk, half_qk)]),
                (wval_any, wval_ref),
            ]
        )
    ]
    copies = copies_of(moves, ins, outs, send_sem, recv_sem)
    riders = [
        Halving(ins[source], totals[i], buffers[7 * i : 7 * i + 7], part, part // 32 * 16)
        for i, source in enumerate(halve)
    ]

    @pl.when(step == 0)
    def _():
        for copy in loads:
            copy.start()
        greet(peers_of(moves) + [neighbour("dp", 1), neighbour("dp", 2)])
        for copy in copies:
            copy.start()
        for rider in riders:
            rider.start()

    @pl.when(step == 1)
    def _():
        for copy in loads:
            copy.wait()

    @pl.when(step == steps - 1)
    def _():
        for rider in riders:
            rider.turn()

    slot = lax.rem(step, 2)
    old = 1 - slot
    lanes = lax.broadcasted_iota(jnp.int32, (tile, LANE), 1)
    scale = DH ** (-0.5)
    narrow = heads * DH

    @pl.when(step == 0)
    def _():
        gain_acc[...] = jnp.zeros_like(gain_acc)
        dk_acc[...] = jnp.zeros_like(dk_acc)
        dv_acc[...] = jnp.zeros_like(dv_acc)

    @pl.when(step < steps)
    def _():
        now = tile_rows(jnp.minimum(step, steps - 1), tile)
        before = tile_rows(jnp.maximum(step - 1, 0), tile)
        allowed = window_mask(step, tile, start_ref[...], keep_ref[:, before], keep_ref[:, now])
        gates = sig_now_ref[...] * mask_now_ref[...].astype(jnp.float32)
        dhid = cot_ref[...].astype(jnp.float32) + grad_own_ref[...] + grad_far_ref[...].astype(jnp.float32)
        dhid_keep[slot] = dhid
        dy = dhid.astype(jnp.bfloat16)
        dy_ref[...] = dy
        dgate = jnp.zeros((tile, LANE), jnp.float32)
        for head in range(heads):
            cols = slice(head * DH, (head + 1) * DH)
            dmixed = dot_nt(dy, wout_ref[head * VEXP * DH : (head + 1) * VEXP * DH, :])
            attended = att_ref[:, cols]
            dattend = jnp.zeros((tile, DH), jnp.float32)
            for e in range(VEXP):
                at = (heads + head) * VEXP + e
                part = dmixed[:, e * DH : (e + 1) * DH]
                dattend = dattend + gates[:, at : at + 1] * part
                dgate = jnp.where(
                    lanes == at, jnp.sum(part * attended, axis=1, keepdims=True), dgate
                )
            dattend = dattend.astype(jnp.bfloat16)
            q_head = q_ref[:, cols]
            k_old, k_now = k_ref[before, cols], k_ref[now, cols]
            v_old, v_now = v_ref[before, cols], v_ref[now, cols]
            scores = jnp.concatenate([dot_nt(q_head, k_old), dot_nt(q_head, k_now)], axis=1)
            scores = jnp.where(allowed, scores, MASK_FILL)
            probs = jnp.exp(scores - lse_ref[:, head : head + 1])
            dprob = jnp.concatenate([dot_nt(dattend, v_old), dot_nt(dattend, v_now)], axis=1)
            delta = jnp.sum(probs * dprob, axis=1, keepdims=True)
            dscore = (probs * (dprob - delta)).astype(jnp.bfloat16)
            probs = probs.astype(jnp.bfloat16)
            dv_acc[old, :, cols] += dot_tn(probs[:, :tile], dattend)
            dv_acc[slot, :, cols] = dot_tn(probs[:, tile:], dattend)
            dk_acc[old, :, cols] += dot_tn(dscore[:, :tile], q_head)
            dk_acc[slot, :, cols] = dot_tn(dscore[:, tile:], q_head)
            dq = dot_nn(dscore[:, :tile], k_old) + dot_nn(dscore[:, tile:], k_now)
            dq_keep[slot, :, cols] = (
                spin_back(dq, cos_now_ref[...], sin_now_ref[...]) * scale
            ).astype(jnp.bfloat16)
        dgate_keep[slot] = dgate

    @pl.when(step > 0)
    def _():
        sig = sig_old_ref[...]
        mask = mask_old_ref[...].astype(jnp.float32)
        gates = sig * mask
        dgate = dgate_keep[old]
        for head in range(heads):
            cols = slice(head * DH, (head + 1) * DH)
            dqk_ref[:, cols] = dq_keep[old, :, cols]
            dqk_ref[:, narrow + head * DH : narrow + (head + 1) * DH] = spin_back(
                dk_acc[old, :, cols], cos_old_ref[...], sin_old_ref[...]
            ).astype(jnp.bfloat16)
            dvalue = dv_acc[old, :, cols]
            for e in range(VEXP):
                at = head * VEXP + e
                wide = slice(at * DH, (at + 1) * DH)
                val = val_ref[:, wide].astype(jnp.float32)
                dgate = jnp.where(lanes == at, jnp.sum(dvalue * val, axis=1, keepdims=True), dgate)
                dval_ref[:, wide] = (gates[:, at : at + 1] * dvalue).astype(jnp.bfloat16)
        dlog = (dgate * gates * (1.0 - sig)).astype(jnp.bfloat16)
        dlog_ref[...] = dlog
        dnormed = dot_nt(dqk_ref[...], wqk_ref[...])
        x_f = x_ref[...].astype(jnp.float32)
        center = x_f - jnp.mean(x_f, axis=1, keepdims=True)
        inv = lax.rsqrt(jnp.mean(center * center, axis=1, keepdims=True) + NORM_EPS)
        x_hat = center * inv
        gain_acc[...] += jnp.sum(dnormed * x_hat, axis=0, keepdims=True)
        grad = dnormed * gain_ref[...]
        dx = inv * (
            grad
            - jnp.mean(grad, axis=1, keepdims=True)
            - x_hat * jnp.mean(grad * x_hat, axis=1, keepdims=True)
        )
        dx = dx + dhid_keep[old] + dot_nt(dval_ref[...], wval_ref[...]) + dot_nt(dlog, wsel_ref[...])
        gin_ref[...] = dx.astype(jnp.bfloat16)

    @pl.when(step == steps)
    def _():
        gain = gain_acc[...]
        high = gain.astype(jnp.bfloat16).astype(jnp.float32)
        row = lax.broadcasted_iota(jnp.int32, (GAIN_ROWS, gain.shape[1]), 0)
        split = jnp.where(row == 0, high, jnp.where(row == 1, gain - high, 0.0))
        ggain_ref[...] = split.astype(jnp.bfloat16)
        for rider in riders:
            rider.finish()
        for copy in copies:
            copy.wait()


def attention_backward(
    sources, results, moves, halve, part, cot, grad_own, grad_far, q, k, v, att, lse, start, keep, sig, mask,
    cos_two, sin_two, x, val, gain, wsel, wout, wq, wk, wval, tile
):
    rows, model = x.shape
    heads = wq.shape[1] // DH
    steps = rows // tile
    narrow, wide = heads * DH, heads * VEXP * DH
    at_now = lambda width: pl.BlockSpec((tile, width), lambda step: (jnp.minimum(step, steps - 1), 0))
    at_old = lambda width: pl.BlockSpec((tile, width), lambda step: (jnp.maximum(step - 1, 0), 0))
    full = lambda arr: whole_block(arr.shape)
    return pl.pallas_call(
        functools.partial(
            backward_body, heads, tile, steps, moves, halve, part, len(sources), len(results)
        ),
        grid=(steps + 1,),
        in_specs=[ANYWHERE] * len(sources)
        + [
            at_now(model),
            at_now(model),
            at_now(model),
            at_now(narrow),
            full(k),
            full(v),
            at_now(narrow),
            at_now(LANE),
            at_now(1),
            full(keep),
            at_now(LANE),
            at_now(LANE),
            at_now(LANE),
            at_now(LANE),
            at_old(LANE),
            at_old(LANE),
            at_old(LANE),
            at_old(LANE),
            at_old(model),
            at_old(wide),
            full(gain),
            full(wsel),
            full(wout),
            ANYWHERE,
            ANYWHERE,
            ANYWHERE,
        ],
        out_specs=[ANYWHERE] * len(results)
        + [
            at_old(model),
            at_old(2 * narrow),
            at_old(wide),
            at_old(LANE),
            whole_block((GAIN_ROWS, model)),
            at_now(model),
        ]
        + [whole_block((part, model))] * len(halve),
        out_shape=[jax.ShapeDtypeStruct(shape, jnp.bfloat16) for shape in results]
        + [
            jax.ShapeDtypeStruct((rows, model), jnp.bfloat16),
            jax.ShapeDtypeStruct((rows, 2 * narrow), jnp.bfloat16),
            jax.ShapeDtypeStruct((rows, wide), jnp.bfloat16),
            jax.ShapeDtypeStruct((rows, LANE), jnp.bfloat16),
            jax.ShapeDtypeStruct((GAIN_ROWS, model), jnp.bfloat16),
            jax.ShapeDtypeStruct((rows, model), jnp.bfloat16),
        ]
        + [jax.ShapeDtypeStruct((part, model), jnp.bfloat16)] * len(halve),
        scratch_shapes=[
            pltpu.VMEM((2, tile, narrow), jnp.float32),
            pltpu.VMEM((2, tile, narrow), jnp.float32),
            pltpu.VMEM((2, tile, narrow), jnp.bfloat16),
            pltpu.VMEM((2, tile, LANE), jnp.float32),
            pltpu.VMEM((1, model), jnp.float32),
            pltpu.VMEM((2, tile, model), jnp.float32),
            pltpu.VMEM((model, 2 * narrow), jnp.bfloat16),
            pltpu.VMEM(wval.shape, jnp.bfloat16),
            pltpu.SemaphoreType.DMA((3,)),
            pltpu.SemaphoreType.DMA((len(moves),)),
            pltpu.SemaphoreType.DMA((len(moves),)),
        ]
        + halving_buffers(part, part // 32 * 16, model) * len(halve),
        compiler_params=pltpu.CompilerParams(
            vmem_limit_bytes=VMEM_BYTES, collective_id=6, has_side_effects=True
        ),
        cost_estimate=pl.CostEstimate(
            flops=2 * rows * model * (2 * narrow + 2 * wide), bytes_accessed=50 << 20, transcendentals=0
        ),
    )(
        *sources, cot, grad_own, grad_far, q, k, v, att, lse, start, keep, sig, mask, cos_two, sin_two,
        sig, mask, cos_two, sin_two, x, val, gain, wsel, wout, wq, wk, wval,
    )


def tail_body(blocks, chips, part, cut, *refs):
    (
        part_1,
        part_3,
        part_0,
        got_2,
        gain_ref,
        dlog_ref,
        unit_ref,
        dy_any,
        mix_any,
        x_any,
        dval_any,
        norm_any,
        dqk_any,
        hid_any,
        out_own_any,
        out_far_any,
        dense_ref,
        layer_ref,
        whole_any,
        came,
        quarter,
        product,
        pair,
        near,
        far,
        send,
        land,
        sums,
        last,
        link,
        core_sems,
        xy_sems,
        z_sems,
        local_sem,
        dy_ref,
        mix_ref,
        x_ref,
        dval_ref,
        norm_ref,
        dqk_ref,
        hid_ref,
        out_own,
        out_far,
        load_sem,
    ) = refs
    half = mix_ref.shape[1] // 2
    loads = [
        pltpu.make_async_copy(source, target, load_sem.at[i])
        for i, (source, target) in enumerate(
            [
                (dy_any, dy_ref),
                (mix_any.at[:, pl.ds(0, half)], mix_ref.at[:, pl.ds(0, half)]),
                (mix_any.at[:, pl.ds(half, half)], mix_ref.at[:, pl.ds(half, half)]),
                (x_any, x_ref),
                (dval_any, dval_ref),
                (norm_any, norm_ref),
                (dqk_any, dqk_ref),
                (hid_any, hid_ref),
                (out_own_any, out_own),
                (out_far_any, out_far),
            ]
        )
    ]
    for copy in loads:
        copy.start()
    ready = {0: (0, 1), 1: (2,), 2: (3, 4), 4: (5, 6)}
    place = lax.axis_index("expert")
    chip, core = place // 2, lax.rem(place, 2)
    model = x_ref.shape[1]
    piece = model // 4 // chips // 2
    quart = chips * piece
    halfway = quart // 2
    rights = {"out": mix_ref, "val": dval_ref, "log": dlog_ref, "qk": dqk_ref}
    lefts = {"out": dy_ref, "val": x_ref, "log": x_ref, "qk": norm_ref}

    peers = [neighbour("core", 1)] + [neighbour("dp", flip) for flip in (1, 2)]
    for hop in range(1, chips):
        peers.append(neighbour("chip", hop))
    greet(peers)
    passes = [
        remote(source, came.at[i], link, 7 + i, neighbour("chip", hop))
        for i, (source, hop) in enumerate(((part_1, 1), (part_3, 3)))
    ]
    for copy in passes:
        copy.start()

    def width_of(b):
        return sum(hi - lo for _, lo, hi in blocks[b])

    def core_copy(b):
        width = width_of(b)
        return remote(
            product.at[b % 2, :, span((1 - core) * piece, piece), pl.ds(0, width)],
            pair.at[b, :, :, pl.ds(0, width)],
            core_sems,
            b,
            neighbour("core", 1),
        )

    def compute(b):
        if b >= 2:
            core_copy(b - 2).wait_send()
        for i in ready.get(b, ()):
            loads[i].wait()
        at = 0
        for name, lo, hi in blocks[b]:
            total = dot_tn(lefts[name][...], rights[name][:, lo:hi])
            if name == "log":
                total = total + dot_tn(gain_ref[...], unit_ref[...])
            product[b % 2, :, :, at : at + hi - lo] = total.astype(jnp.bfloat16).reshape(
                4 * chips, 2 * piece, hi - lo
            )
            at += hi - lo
        core_copy(b).start()

    def pair_rows(b):
        return pair.at[b].reshape(4 * quart, pair.shape[3])

    def first_copies(b):
        return halving_first(pair_rows(b), near.at[b], far.at[b], quart, halfway, xy_sems.at[b], 0)

    def second_copies(b):
        return halving_second(send.at[b], land.at[b], quart, halfway, xy_sems.at[b], 4)

    def chip_copies(b):
        copies = []
        for hop in range(1, chips):
            target = lax.rem(chip + hop, chips)
            copies.append(
                remote(
                    sums.at[b, span(target * piece, piece)],
                    last.at[b, hop - 1],
                    z_sems.at[b],
                    hop - 1,
                    neighbour("chip", hop),
                )
            )
        return copies

    def stage_1(b):
        core_copy(b).wait_recv()
        kept = product[b % 2, :, span(core * piece, piece), :].astype(jnp.float32)
        pair[b] = (kept + pair[b].astype(jnp.float32)).astype(jnp.bfloat16)
        for copy in first_copies(b):
            copy.start()

    def own_rows(b, owner, start):
        return as_f32(pair_rows(b), pl.multiple_of(flips()[owner] * quart + start, 16), halfway)

    def stage_2(b):
        for copy in first_copies(b):
            copy.wait()
        send[b, :halfway, :] = (own_rows(b, 2, 0) + as_f32(near.at[b], halfway, halfway)).astype(
            jnp.bfloat16
        )
        send[b, halfway:, :] = (own_rows(b, 1, halfway) + as_f32(far.at[b], halfway, halfway)).astype(
            jnp.bfloat16
        )
        for copy in second_copies(b):
            copy.start()

    def stage_3(b):
        for copy in second_copies(b):
            copy.wait()
        up = own_rows(b, 0, 0) + as_f32(near.at[b], 0, halfway) + as_f32(land.at[b], 0, halfway)
        down = own_rows(b, 0, halfway) + as_f32(far.at[b], 0, halfway)
        down = down + as_f32(land.at[b], halfway, halfway)
        sums[b, :halfway, :] = up.astype(jnp.bfloat16)
        sums[b, halfway:, :] = down.astype(jnp.bfloat16)
        for copy in chip_copies(b):
            copy.start()

    def stage_4(b):
        for copy in chip_copies(b):
            copy.wait()
        total = sums[b, span(chip * piece, piece), :].astype(jnp.float32)
        for hop in range(chips - 1):
            total = total + last[b, hop].astype(jnp.float32)
        start = sum(width_of(i) for i in range(b))
        dense_ref[:, start : start + width_of(b)] = total[:, : width_of(b)]

    def spread_1():
        return spread_first(quarter, whole_any, part, cut, link, 1)

    def spread_2():
        return spread_second(quarter, whole_any, part, cut, link, 3)

    mine = lax.axis_index("dp")
    keep = pltpu.make_async_copy(quarter, whole_any.at[span(mine * part, part)], local_sem)
    count = len(blocks)
    compute(0)
    compute(1)
    for b in range(count):
        stage_1(b)
        if b + 2 < count:
            compute(b + 2)
    for copy in passes:
        copy.wait()
    quarter[...] = sum(
        ref[...].astype(jnp.float32) for ref in (part_0, got_2, came.at[0], came.at[1])
    ).astype(jnp.bfloat16)
    keep.start()
    for copy in spread_1():
        copy.start()
    for b in range(count):
        stage_2(b)
    for copy in loads[7:]:
        copy.wait()
    rows = 4 * quart
    for start in range(0, x_ref.shape[0], rows):
        total = hid_ref[start : start + rows, :] + as_f32(out_own, start, rows)
        layer_ref[start : start + rows, :] = (total + as_f32(out_far, start, rows)).astype(jnp.bfloat16)
    for copy in spread_1():
        copy.wait()
    for copy in spread_2():
        copy.start()
    for b in range(count):
        stage_3(b)
    for b in range(count):
        stage_4(b)
    for copy in spread_2():
        copy.wait()
    keep.wait()
    for b in range(max(0, count - 2), count):
        core_copy(b).wait_send()


def tail(hidden, out_own, out_far, part_1, part_3, part_0, got_2, dy, x, normed, gain_rows, mixed, dval, dlog, dqk, unit, shape, chips):
    rows, model = x.shape
    part = shape[0] // 4
    cut = part // 32 * 16
    wide, narrow = mixed.shape[1], dqk.shape[1]
    narrow_one = narrow // 2
    half = wide // 2
    blocks = [
        [("out", 0, half)],
        [("out", half, wide)],
        [("val", 0, half)],
        [("val", half, wide)],
        [("log", 0, LANE), ("qk", 0, narrow)],
    ]
    width = max(half, LANE + narrow)
    total = 2 * wide + LANE + narrow
    count = len(blocks)
    piece = model // 4 // chips // 2
    quart = chips * piece
    bf16 = lambda *shape: pltpu.VMEM(shape, jnp.bfloat16)
    dma = lambda *shape: pltpu.SemaphoreType.DMA(shape)
    vmem = pl.BlockSpec(memory_space=pltpu.VMEM)
    return pl.pallas_call(
        functools.partial(tail_body, blocks, chips, part, cut),
        in_specs=[ANYWHERE] * 2 + [vmem] * 5 + [ANYWHERE] * 9,
        out_specs=[vmem, vmem, ANYWHERE],
        out_shape=[
            jax.ShapeDtypeStruct((piece, total), jnp.float32),
            jax.ShapeDtypeStruct((rows, model), jnp.bfloat16),
            jax.ShapeDtypeStruct(shape, jnp.bfloat16),
        ],
        scratch_shapes=[
            bf16(2, part, model),
            bf16(part, model),
            bf16(2, 4 * chips, 2 * piece, width),
            bf16(count, 4 * chips, piece, width),
            bf16(count, quart, width),
            bf16(count, quart, width),
            bf16(count, quart, width),
            bf16(count, quart, width),
            bf16(count, quart, width),
            bf16(count, chips - 1, piece, width),
            dma(2, 9),
            dma(2, count),
            dma(count, 2, 6),
            dma(count, 2, chips - 1),
            dma(),
            bf16(rows, model),
            bf16(rows, wide),
            bf16(rows, model),
            bf16(rows, wide),
            bf16(rows, model),
            bf16(rows, 2 * narrow_one),
            pltpu.VMEM((rows, model), jnp.float32),
            bf16(rows, model),
            bf16(rows, model),
            dma(10),
        ],
        compiler_params=pltpu.CompilerParams(
            vmem_limit_bytes=VMEM_BYTES, collective_id=7, has_side_effects=True
        ),
        cost_estimate=pl.CostEstimate(
            flops=2 * rows * model * total, bytes_accessed=20 << 20, transcendentals=0
        ),
    )(part_1, part_3, part_0, got_2, gain_rows, dlog, unit, dy, mixed, x, dval, normed, dqk, hidden, out_own, out_far)


def experts_body(exp_local, ff_dim, tile, steps, chips, ahead, *refs):
    (
        own_any,
        third_any,
        second_any,
        x_own,
        x_far,
        c_own,
        c_far,
        mask_ref,
        digit_ref,
        grad_own,
        out_own,
        grad_far,
        out_far,
        grad_1,
        part_0,
        part_3,
        part_2,
        w_all,
        x_ref,
        c_ref,
        grad_acc,
        out_acc,
        act_all,
        dpre_all,
        g_two,
        given,
        near,
        far,
        send,
        land,
        load_sem,
        local_sem,
        chip_sems,
        spread_sems,
        halve_sems,
        tile_sems,
    ) = refs
    wide = exp_local * ff_dim
    back = wide + ROUTER_ROWS
    half = steps // 2
    part = w_all.shape[1] // 4
    cut = part // 32 * 16
    step = pl.program_id(0)
    turn_of, index = lax.div(step, steps), lax.rem(step, steps)
    mine = span(lax.axis_index("dp") * part, part)
    partner = neighbour("core", 1)

    start = lax.axis_index("dp") * part
    rest = span(start + ahead, part - ahead)
    quarter_2 = remote(
        own_any.at[rest], w_all.at[2, rest], chip_sems, 0, neighbour("chip", -2)
    )
    near_rows = remote(own_any, w_all.at[3], chip_sems, 1, neighbour("chip", -1))
    load_own = pltpu.make_async_copy(own_any, w_all.at[0], local_sem.at[0])
    load_third = pltpu.make_async_copy(third_any.at[mine], w_all.at[1, mine], local_sem.at[1])
    load_second = pltpu.make_async_copy(
        second_any.at[span(start, ahead)], w_all.at[2, span(start, ahead)], local_sem.at[2]
    )
    spread_3 = Spreading(w_all.at[1], part, cut, spread_sems.at[0], third_any.at[mine])
    spread_2 = Spreading(w_all.at[2], part, cut, spread_sems.at[1], w_all.at[2, mine])
    halvings = [
        Halving(
            g_two.at[i % 2],
            total,
            (near.at[i % 2], far.at[i % 2], send.at[i % 2], land.at[i % 2], halve_sems.at[i]),
            part,
            cut,
        )
        for i, total in enumerate((part_0, part_3, part_2))
    ]

    def load(at, kind):
        source = ((x_own, x_far), (c_own, c_far))[kind][at // half]
        return pltpu.make_async_copy(
            source.at[pl.ds(at % half * tile, tile)],
            (x_ref, c_ref)[kind].at[pl.ds(at * tile, tile)],
            load_sem.at[kind, at],
        )

    def tile_copy(at, kind):
        rows = pl.ds(at * tile, tile)
        source = (given.at[rows], out_acc.at[pl.ds((half + at) * tile, tile)])[kind]
        return remote(source, (grad_far, out_far)[kind].at[rows], tile_sems.at[kind], at, partner)

    def store(kind):
        rows = pl.ds(0, half * tile)
        source = (grad_acc, out_acc)[kind].at[rows]
        return pltpu.make_async_copy(source, (grad_own, out_own)[kind], local_sem.at[3 + kind])

    store_grad = pltpu.make_async_copy(g_two.at[(chips - 1) % 2], grad_1, local_sem.at[5])

    def when(at):
        return pl.when(step == at)

    @when(0)
    def _():
        load_own.start()
        for at in range(steps):
            for kind in range(2):
                load(at, kind).start()
        load_third.start()
        load_second.start()
        peers = [partner, neighbour("dp", 1), neighbour("dp", 2)]
        greet(peers + [neighbour("chip", hop) for hop in range(1, chips)])
        spread_3.start()
        quarter_2.start()
        load_own.wait()

    @when(steps - 4)
    def _():
        spread_3.turn()

    @when(steps)
    def _():
        load_second.wait()
        quarter_2.wait()
        spread_2.start()
        near_rows.start()
        load_third.wait()
        spread_3.finish()
        halvings[0].start()

    @when(steps + 3)
    def _():
        spread_2.turn()

    @when(steps + 7)
    def _():
        halvings[0].turn()

    @when(2 * steps)
    def _():
        halvings[1].start()
        spread_2.finish()

    @when(2 * steps + 3)
    def _():
        halvings[0].finish()

    @when(2 * steps + 7)
    def _():
        halvings[1].turn()

    @when(3 * steps)
    def _():
        near_rows.wait()
        halvings[2].start()

    @when(3 * steps + 3)
    def _():
        halvings[1].finish()

    @when(3 * steps + 6)
    def _():
        halvings[2].turn()

    for at in range(steps):

        @when(at)
        def _(at=at):
            for kind in range(2):
                load(at, kind).wait()

    final = lax.div(turn_of, chips - 1)
    place = lax.rem(index + half * final, steps)
    rows = tile_rows(place, tile)
    x, c = x_ref[rows, :], c_ref[rows, :]
    sig = 1.0 / (1.0 + jnp.exp(-dot_nt(x, w_all[turn_of, wide:back, :])))
    gate = sig * mask_ref[:, :ROUTER_ROWS].astype(jnp.float32)
    lanes = lax.broadcasted_iota(jnp.int32, (tile, ROUTER_ROWS), 1)
    dgate = jnp.zeros((tile, ROUTER_ROWS), jnp.float32)
    for pair in range(exp_local // 2):
        lo, hi = 2 * pair * ff_dim, 2 * (pair + 1) * ff_dim
        pre_two = dot_nt(x, w_all[turn_of, lo:hi, :])
        raw_two = dot_nt(c, w_all[turn_of, back + lo : back + hi, :])
        for side in range(2):
            e = 2 * pair + side
            pre = pre_two[:, side * ff_dim : (side + 1) * ff_dim]
            raw = raw_two[:, side * ff_dim : (side + 1) * ff_dim]
            square = pre * pre
            bend = jnp.tanh(pre * (GELU_A + GELU_A * GELU_B * square))
            upper = 0.5 * bend + 0.5
            act = (pre * upper).astype(jnp.bfloat16).astype(jnp.float32)
            slope = upper + (0.5 * pre) * (1.0 - bend * bend) * (GELU_A + 3 * GELU_A * GELU_B * square)
            gate_col = gate[:, e : e + 1]
            act_all[rows, e * ff_dim : (e + 1) * ff_dim] = (gate_col * act).astype(jnp.bfloat16)
            dpre_all[rows, e * ff_dim : (e + 1) * ff_dim] = (gate_col * raw * slope).astype(
                jnp.bfloat16
            )
            dgate = jnp.where(lanes == e, jnp.sum(act * raw, axis=1, keepdims=True), dgate)
    dpre_all[rows, wide:back] = (dgate * gate * (1.0 - sig)).astype(jnp.bfloat16)
    out_new = dot_nn(act_all[rows, :], w_all[turn_of, back:, :])
    grad_new = dot_nn(dpre_all[rows, :], w_all[turn_of, :back, :])

    @pl.when(turn_of == 0)
    def _():
        out_acc[rows, :] = out_new.astype(jnp.bfloat16)
        grad_acc[rows, :] = grad_new

    @pl.when(turn_of > 0)
    def _():
        out_acc[rows, :] = (out_acc[rows, :].astype(jnp.float32) + out_new).astype(jnp.bfloat16)
        grad_acc[rows, :] += grad_new

    for at in range(half):

        @when((chips - 1) * steps + at)
        def _(at=at):
            given[at * tile : (at + 1) * tile, :] = grad_acc[
                (half + at) * tile : (half + at + 1) * tile, :
            ].astype(jnp.bfloat16)
            tile_copy(at, 0).start()
            tile_copy(at, 1).start()

    @pl.when(index == steps - 1)
    def _():
        slot = lax.rem(turn_of, 2)
        for lo in range(0, wide, 2 * ff_dim):
            g_two[slot, lo : lo + 2 * ff_dim, :] = dot_tn(
                dpre_all[:, lo : lo + 2 * ff_dim], x_ref[...]
            ).astype(jnp.bfloat16)
            g_two[slot, back + lo : back + lo + 2 * ff_dim, :] = dot_tn(
                act_all[:, lo : lo + 2 * ff_dim], c_ref[...]
            ).astype(jnp.bfloat16)
        extra = dot_tn(dpre_all[:, wide:back], x_ref[...])
        g_two[slot, wide:back, :LANE] = (extra[:, :LANE] + digit_ref[...]).astype(jnp.bfloat16)
        g_two[slot, wide:back, LANE:] = extra[:, LANE:].astype(jnp.bfloat16)

    @when(chips * steps - 1)
    def _():
        store_grad.start()
        store(0).start()
        store(1).start()
        halvings[2].finish()
        for at in range(half):
            tile_copy(at, 0).wait()
            tile_copy(at, 1).wait()
        store_grad.wait()
        store(0).wait()
        store(1).wait()


def experts(own, third, second, tokens, masks, digits, exp_local, ff_dim, ahead, chips, tile):
    rows, model = 2 * tokens[0].shape[0], tokens[0].shape[1]
    steps = rows // tile
    half = steps // 2
    wide = exp_local * ff_dim
    part = own.shape[0] // 4
    cut = part // 32 * 16

    def mask_block(step):
        turn_of, index = lax.div(step, steps), lax.rem(step, steps)
        place = lax.rem(index + half * lax.div(turn_of, chips - 1), steps)
        return (place, lax.rem(chips - turn_of, chips))

    def digit_block(step):
        return (0, lax.rem(chips - lax.div(step, steps), chips))

    bf16 = lambda *shape: pltpu.VMEM(shape, jnp.bfloat16)
    dma = lambda *shape: pltpu.SemaphoreType.DMA(shape)
    full = lambda count, kind: jax.ShapeDtypeStruct((count, model), kind)
    return pl.pallas_call(
        functools.partial(experts_body, exp_local, ff_dim, tile, steps, chips, ahead),
        grid=(chips * steps,),
        in_specs=[ANYWHERE] * 7
        + [pl.BlockSpec((tile, LANE), mask_block), pl.BlockSpec((ROUTER_ROWS, LANE), digit_block)],
        out_specs=[ANYWHERE] * 5 + [whole_block((part, model))] * 3,
        out_shape=[
            full(rows // 2, jnp.float32),
            full(rows // 2, jnp.bfloat16),
            full(rows // 2, jnp.bfloat16),
            full(rows // 2, jnp.bfloat16),
            full(4 * part, jnp.bfloat16),
            full(part, jnp.bfloat16),
            full(part, jnp.bfloat16),
            full(part, jnp.bfloat16),
        ],
        scratch_shapes=[
            bf16(chips, 4 * part, model),
            bf16(rows, model),
            bf16(rows, model),
            pltpu.VMEM((rows, model), jnp.float32),
            bf16(rows, model),
            bf16(rows, wide),
            bf16(rows, wide + ROUTER_ROWS),
            bf16(2, 4 * part, model),
            bf16(rows // 2, model),
            bf16(2, 2 * cut, model),
            bf16(2, 2 * (part - cut), model),
            bf16(2, part, model),
            bf16(2, part, model),
            dma(2, steps),
            dma(6),
            dma(2, 2),
            dma(2, 2, 6),
            dma(chips - 1, 2, 6),
            dma(2, 2, half),
        ],
        compiler_params=pltpu.CompilerParams(
            vmem_limit_bytes=VMEM_BYTES, collective_id=2, has_side_effects=True
        ),
        cost_estimate=pl.CostEstimate(
            flops=12 * chips * rows * model * wide, bytes_accessed=40 << 20, transcendentals=rows * wide
        ),
    )(own, third, second, *tokens, masks, digits)


def core_swap(arr):
    size = lax.axis_size("expert")
    return lax.ppermute(arr, "expert", [(i, i ^ 1) for i in range(size)])


def row_part(arr, index, count):
    return lax.dynamic_slice_in_dim(arr, index * (arr.shape[0] // count), arr.shape[0] // count, 0)


def own_weights(w_router, w_in, w_out):
    exp_local, model_dim, ff_dim = w_in.shape
    router_rows = jnp.zeros((ROUTER_ROWS, model_dim), jnp.bfloat16).at[:exp_local].set(w_router)
    return jnp.concatenate(
        [
            jnp.swapaxes(w_in, 1, 2).reshape(exp_local * ff_dim, model_dim),
            router_rows,
            w_out.reshape(exp_local * ff_dim, model_dim),
        ]
    )


def block_dense(
    layer_input,
    segments,
    keep_mask,
    att_routes,
    moe_routes,
    expert_counts,
    norm_gain,
    w_query,
    w_key,
    w_select,
    w_value,
    w_output,
    w_router,
    w_in,
    w_out,
    cotangent,
):
    rows, model = layer_input.shape
    seqs, seq_len = segments.shape
    exp_local, _, ff_dim = w_in.shape
    heads = w_query.shape[1] // DH
    chips = lax.axis_size("expert") // 2
    wide, narrow, gates = heads * VEXP * DH, heads * DH, 2 * heads * VEXP
    moe_wide = exp_local * ff_dim
    mine = lax.axis_index("expert")
    chip, core = mine // 2, mine % 2

    own = own_weights(w_router, w_in, w_out)
    exp_total = 2 * chips * exp_local
    named = jnp.sum(
        (moe_routes[..., None] == jnp.arange(exp_total, dtype=jnp.int32)).astype(jnp.bfloat16), axis=1
    )
    named = jnp.concatenate([named, core_swap(named)])

    column = jnp.arange(seq_len, dtype=jnp.int32)
    changed = jnp.concatenate(
        [jnp.ones((seqs, 1), jnp.bool_), segments[:, 1:] != segments[:, :-1]], axis=1
    )
    start = lax.cummax(jnp.where(changed, column, 0), axis=1)
    cos_tab, sin_tab = rope_tables((column - start).reshape(-1), DH)
    cos_two = jnp.concatenate([cos_tab, cos_tab], axis=1)
    sin_two = jnp.concatenate([-sin_tab, sin_tab], axis=1)
    start = (start + seq_len * jnp.arange(seqs, dtype=jnp.int32)[:, None]).reshape(rows, 1)
    keep = keep_mask.reshape(1, rows)
    att_mask = jnp.sum(
        (att_routes[..., None] == jnp.arange(VEXP, dtype=jnp.int32)).astype(jnp.bfloat16), axis=2
    ).reshape(rows, gates)
    att_mask = jnp.pad(att_mask, ((0, 0), (0, LANE - gates)))
    gain_row = norm_gain.reshape(1, model)
    wsel = jnp.pad(w_select, ((0, 0), (0, LANE - gates)))

    shape = own.shape
    part = shape[0] // 4
    ahead = 16
    third, second, cot_far, sent_far, hidden, normed, q_rot, k_rot, value_bf, value_all, attended, sig, lse, mixed, sent = (
        attention_forward(
            ahead, own, cotangent, layer_input, start, keep, cos_two, sin_two, att_mask, gain_row, wsel, w_query, w_key,
            w_value, w_output, TILE,
        )
    )

    lane = jnp.arange(chips * LANE, dtype=jnp.int32)
    owner = ((chip + lane // LANE) % chips * 2 + core) * exp_local + lane % LANE
    pick = (lane % LANE < exp_local) & (jnp.arange(exp_total, dtype=jnp.int32)[:, None] == owner)
    masks = jnp.dot(named, pick.astype(jnp.bfloat16), preferred_element_type=jnp.float32)
    counts = jnp.sum(masks, axis=0).astype(jnp.int32)
    masks = masks.astype(jnp.bfloat16)
    place = jnp.arange(ROUTER_ROWS, dtype=jnp.int32)[:, None] - exp_local
    digits = jnp.where(
        (place >= 0) & (place < DIGITS), (counts >> (2 * jnp.clip(place, 0, DIGITS))) & 3, 0
    ).astype(jnp.float32)

    grad_own, out_own, grad_far, out_far, grad_1, part_0, part_3, part_2 = experts(
        own, third, second, (sent, sent_far, cotangent, cot_far), masks, digits, exp_local, ff_dim, ahead, chips, TILE
    )
    got_2, grad_input, dqk, dval, dlog, gain_rows, dy, part_1 = attention_backward(
        [grad_1, part_2],
        [(part, model)],
        shift_move(1, 0, 2, fixed(0), fixed(0), part),
        (0,),
        part,
        cotangent, grad_own, grad_far, q_rot, k_rot, value_bf, attended, lse, start, keep, sig, att_mask, cos_two,
        sin_two, layer_input, value_all, gain_row, wsel, w_output, w_query, w_key, w_value, TILE,
    )
    unit = (
        (jnp.arange(GAIN_ROWS)[:, None] < 2) & (jnp.arange(LANE)[None, :] == gates)
    ).astype(jnp.bfloat16)
    dense, layer_output, summed = tail(
        hidden, out_own, out_far, part_1, part_3, part_0, got_2, dy, layer_input, normed, gain_rows, mixed, dval, dlog, dqk, unit, shape, chips
    )
    out_sum, dense = dense[:, :wide].T, dense[:, wide:]
    grad_w_in = jnp.swapaxes(
        summed[:moe_wide].astype(jnp.float32).reshape(exp_local, ff_dim, model), 1, 2
    )
    extra = summed[moe_wide : moe_wide + ROUTER_ROWS].astype(jnp.float32)
    grad_router = extra[:exp_local]
    parts = extra[exp_local : exp_local + DIGITS, :exp_local].astype(jnp.int32)
    tally = sum(parts[i] << (2 * i) for i in range(DIGITS))
    grad_w_out = (
        summed[moe_wide + ROUTER_ROWS :].astype(jnp.float32).reshape(exp_local, ff_dim, model)
    )
    at_qk = wide + LANE
    return (
        layer_output,
        grad_input,
        dense[:, wide + gates],
        dense[:, at_qk : at_qk + narrow],
        dense[:, at_qk + narrow : at_qk + 2 * narrow],
        dense[:, wide : wide + gates],
        dense[:, :wide],
        out_sum,
        grad_router,
        grad_w_in,
        grad_w_out,
        expert_counts + tally,
    )


def block_dispatched(
    layer_input,
    segments,
    keep_mask,
    att_routes,
    moe_routes,
    expert_counts,
    norm_gain,
    w_query,
    w_key,
    w_select,
    w_value,
    w_output,
    w_router,
    w_in,
    w_out,
    cotangent,
):
    tok_rows, model_dim = layer_input.shape
    seq_count, seq_len = segments.shape
    head_count = w_query.shape[1] // DH
    score_scale = DH ** (-0.5)
    inputs_f = layer_input.astype(jnp.float32)
    normed, norm_pull = jax.vjp(layer_norm, inputs_f, norm_gain)
    normed_bf = normed.astype(jnp.bfloat16)
    query_rows = jnp.dot(normed_bf, w_query, preferred_element_type=jnp.float32).reshape(
        tok_rows, head_count, DH
    )
    key_rows = jnp.dot(normed_bf, w_key, preferred_element_type=jnp.float32).reshape(
        tok_rows, head_count, DH
    )
    logits = jnp.dot(layer_input, w_select, preferred_element_type=jnp.float32)
    named_mask = jnp.sum(
        (att_routes[..., None] == jnp.arange(VEXP, dtype=jnp.int32)).astype(jnp.float32), axis=2
    )
    select_sig = jax.nn.sigmoid(logits).reshape(tok_rows, 2 * head_count, VEXP)
    head_gates = select_sig * named_mask
    value_all = jnp.dot(layer_input, w_value, preferred_element_type=jnp.float32).reshape(
        tok_rows, head_count, VEXP, DH
    )
    value_bf = jnp.sum(head_gates[:, :head_count, :, None] * value_all, axis=2).astype(jnp.bfloat16)
    position, allowed = jax.vmap(doc_layout)(segments, keep_mask)
    cos_tab, sin_tab = rope_tables(position.reshape(-1), DH)
    q_rot = (rotate(query_rows, cos_tab, sin_tab) * score_scale).astype(jnp.bfloat16)
    k_rot = rotate(key_rows, cos_tab, sin_tab).astype(jnp.bfloat16)
    seq_shape = (seq_count, seq_len, head_count, DH)
    attended, log_total = lax.map(
        attend_forward,
        (q_rot.reshape(seq_shape), k_rot.reshape(seq_shape), value_bf.reshape(seq_shape), allowed),
    )
    attended = attended.reshape(tok_rows, head_count, DH)
    mixed_bf = (
        (head_gates[:, head_count:, :, None] * attended[:, :, None, :])
        .astype(jnp.bfloat16)
        .reshape(tok_rows, head_count * VEXP * DH)
    )
    hidden = inputs_f + jnp.dot(mixed_bf, w_output, preferred_element_type=jnp.float32)
    dev_count = lax.axis_size("expert")
    exp_local = w_in.shape[0]
    exp_total = dev_count * exp_local
    top_k = moe_routes.shape[1]
    capacity = 10 * tok_rows * top_k // (7 * exp_total) + 1
    owner, filled, slot_of = slot_table(moe_routes, exp_total, capacity)
    keep_slot = filled[:, None] > 0
    zero_bf = jnp.zeros((), jnp.bfloat16)
    hidden_bf = hidden.astype(jnp.bfloat16)
    send_rows = jnp.where(keep_slot, hidden_bf[owner], zero_bf).reshape(
        dev_count, exp_local * capacity, model_dim
    )
    rows_in = lax.all_to_all(send_rows, "expert", split_axis=0, concat_axis=0, tiled=True)
    histogram = jnp.zeros((exp_total,), jnp.float32).at[moe_routes.reshape(-1)].add(1.0)
    tally = lax.psum_scatter(histogram, "expert", scatter_dimension=0, tiled=True)
    slot_shape = (dev_count, exp_local, capacity, model_dim)
    rows_four = rows_in.reshape(slot_shape)
    pre_act = jnp.einsum("necd,edf->necf", rows_four, w_in, preferred_element_type=jnp.float32)
    gelu_out, gelu_pull = jax.vjp(jax.nn.gelu, pre_act)
    act_bf = gelu_out.astype(jnp.bfloat16)
    router_logit = jnp.einsum(
        "necd,ed->nec", rows_four, w_router, preferred_element_type=jnp.float32
    )
    gate_moe = jax.nn.sigmoid(router_logit)
    expert_out = jnp.einsum("necf,efd->necd", act_bf, w_out, preferred_element_type=jnp.float32)
    reply = (
        (gate_moe[..., None] * expert_out)
        .astype(jnp.bfloat16)
        .reshape(dev_count, exp_local * capacity, model_dim)
    )
    returned = lax.all_to_all(reply, "expert", split_axis=0, concat_axis=0, tiled=True)
    moe_sum = jnp.sum(returned.reshape(-1, model_dim)[slot_of].astype(jnp.float32), axis=1)
    layer_output = (hidden + moe_sum).astype(jnp.bfloat16)
    cot_f = cotangent.astype(jnp.float32)
    send_cot = jnp.where(keep_slot, cotangent[owner], zero_bf).reshape(
        dev_count, exp_local * capacity, model_dim
    )
    cot_in, rows_again = (
        lax.all_to_all(send_cot, "expert", split_axis=0, concat_axis=0, tiled=True),
        lax.all_to_all(send_rows, "expert", split_axis=0, concat_axis=0, tiled=True),
    )
    rows_grad = rows_again.reshape(slot_shape)
    cot_bf = cot_in.reshape(slot_shape)
    raw_back = jnp.einsum("necd,efd->necf", cot_bf, w_out, preferred_element_type=jnp.float32)
    dgate = jnp.sum(act_bf.astype(jnp.float32) * raw_back, axis=-1)
    dlogit = dgate * gate_moe * (1.0 - gate_moe)
    dexpert = (gate_moe[..., None] * cot_bf.astype(jnp.float32)).astype(jnp.bfloat16)
    grad_w_out = jnp.einsum("necf,necd->efd", act_bf, dexpert, preferred_element_type=jnp.float32)
    dact = jnp.einsum("necd,efd->necf", dexpert, w_out, preferred_element_type=jnp.float32)
    dpre_bf = gelu_pull(dact)[0].astype(jnp.bfloat16)
    grad_w_in = jnp.einsum("necd,necf->edf", rows_grad, dpre_bf, preferred_element_type=jnp.float32)
    grad_router = jnp.einsum(
        "nec,necd->ed",
        dlogit,
        rows_grad.astype(jnp.float32),
        preferred_element_type=jnp.float32,
        precision=HIGHEST,
    )
    dsent = jnp.einsum("necf,edf->necd", dpre_bf, w_in, preferred_element_type=jnp.float32)
    dsent = (dsent + dlogit[..., None] * w_router[None, :, None, :].astype(jnp.float32)).astype(
        jnp.bfloat16
    )
    grad_back = lax.all_to_all(
        dsent.reshape(dev_count, exp_local * capacity, model_dim),
        "expert",
        split_axis=0,
        concat_axis=0,
        tiled=True,
    )
    dhidden = cot_f + jnp.sum(grad_back.reshape(-1, model_dim)[slot_of].astype(jnp.float32), axis=1)
    dy_bf = dhidden.astype(jnp.bfloat16)
    grad_output = jnp.einsum("tk,td->kd", mixed_bf, dy_bf, preferred_element_type=jnp.float32)
    dmixed = jnp.einsum("td,kd->tk", dy_bf, w_output, preferred_element_type=jnp.float32).reshape(
        tok_rows, head_count, VEXP, DH
    )
    dgate_out = jnp.sum(dmixed * attended[:, :, None, :], axis=-1)
    dattend = jnp.sum(head_gates[:, head_count:, :, None] * dmixed, axis=2).astype(jnp.bfloat16)
    grad_q, grad_k, grad_v = lax.map(
        attend_backward,
        (
            q_rot.reshape(seq_shape),
            k_rot.reshape(seq_shape),
            value_bf.reshape(seq_shape),
            allowed,
            log_total,
            dattend.reshape(seq_shape),
        ),
    )
    dquery = (
        (rotate_back(grad_q.reshape(tok_rows, head_count, DH), cos_tab, sin_tab) * score_scale)
        .astype(jnp.bfloat16)
        .reshape(tok_rows, head_count * DH)
    )
    dkey = (
        rotate_back(grad_k.reshape(tok_rows, head_count, DH), cos_tab, sin_tab)
        .astype(jnp.bfloat16)
        .reshape(tok_rows, head_count * DH)
    )
    grad_query = jnp.einsum("td,tk->dk", normed_bf, dquery, preferred_element_type=jnp.float32)
    grad_key = jnp.einsum("td,tk->dk", normed_bf, dkey, preferred_element_type=jnp.float32)
    dnormed = jnp.einsum(
        "tk,dk->td", dquery, w_query, preferred_element_type=jnp.float32
    ) + jnp.einsum("tk,dk->td", dkey, w_key, preferred_element_type=jnp.float32)
    dx_norm, grad_gain = norm_pull(dnormed)
    dvalue = grad_v.reshape(tok_rows, head_count, DH)
    dgate_val = jnp.sum(dvalue[:, :, None, :] * value_all, axis=-1)
    dvalue_all = (
        (head_gates[:, :head_count, :, None] * dvalue[:, :, None, :])
        .astype(jnp.bfloat16)
        .reshape(tok_rows, head_count * VEXP * DH)
    )
    grad_value = jnp.einsum(
        "td,tk->dk", layer_input, dvalue_all, preferred_element_type=jnp.float32
    )
    dgates = jnp.concatenate([dgate_val, dgate_out], axis=1)
    dlogits = (
        (dgates * named_mask * select_sig * (1.0 - select_sig))
        .astype(jnp.bfloat16)
        .reshape(tok_rows, 2 * head_count * VEXP)
    )
    grad_select = jnp.einsum("td,tk->dk", layer_input, dlogits, preferred_element_type=jnp.float32)
    grad_input = (
        dhidden
        + dx_norm
        + jnp.einsum("tk,dk->td", dvalue_all, w_value, preferred_element_type=jnp.float32)
    )
    grad_input = (
        grad_input + jnp.einsum("tk,dk->td", dlogits, w_select, preferred_element_type=jnp.float32)
    ).astype(jnp.bfloat16)
    expert_sums = (
        lax.psum(grad_w_in.astype(jnp.bfloat16), "dp").astype(jnp.float32),
        lax.psum(grad_w_out.astype(jnp.bfloat16), "dp").astype(jnp.float32),
        lax.psum(grad_router.astype(jnp.bfloat16), "dp").astype(jnp.float32),
        lax.psum(tally.astype(jnp.bfloat16), "dp").astype(jnp.float32),
    )
    dense_sums = (
        lax.psum_scatter(grad_gain, ("dp", "expert"), scatter_dimension=0, tiled=True),
        lax.psum_scatter(grad_query, ("dp", "expert"), scatter_dimension=0, tiled=True),
        lax.psum_scatter(grad_key, ("dp", "expert"), scatter_dimension=0, tiled=True),
        lax.psum_scatter(grad_select, ("dp", "expert"), scatter_dimension=0, tiled=True),
        lax.psum_scatter(grad_value, ("dp", "expert"), scatter_dimension=0, tiled=True),
        lax.psum_scatter(grad_output, ("dp", "expert"), scatter_dimension=1, tiled=True),
    )
    counts_out = expert_counts + expert_sums[3].astype(jnp.int32)
    return (
        layer_output,
        grad_input,
        dense_sums[0],
        dense_sums[1],
        dense_sums[2],
        dense_sums[3],
        dense_sums[4],
        dense_sums[5],
        expert_sums[2],
        expert_sums[0],
        expert_sums[1],
        counts_out,
    )


def local(*args):
    rows, top_k = args[4].shape
    experts, _, ff_dim = args[13].shape
    exp_total = lax.axis_size("expert") * experts
    capacity = 10 * rows * top_k // (7 * exp_total) + 1
    regular = lax.axis_size("dp") == 4 and lax.axis_size("expert") == 8 and experts % 2 == 0 and ff_dim == LANE
    return (block_dense if regular and 4 * capacity > rows else block_dispatched)(*args)


def solution(mesh):
    placed = (
        P(("dp", "expert"), None),
        P(("dp", "expert"), None),
        P(("dp", "expert"), None),
        P(("dp", "expert"), None, None),
        P(("dp", "expert"), None),
        P("expert"),
        P(),
        P(),
        P(),
        P(),
        P(),
        P(),
        P("expert", None),
        P("expert", None, None),
        P("expert", None, None),
        P(("dp", "expert"), None),
    )
    return jax.shard_map(
        local,
        mesh=mesh,
        in_specs=placed,
        out_specs=(
            P(("dp", "expert"), None),
            P(("dp", "expert"), None),
            P(("dp", "expert")),
            P(("dp", "expert"), None),
            P(("dp", "expert"), None),
            P(("dp", "expert"), None),
            P(("dp", "expert"), None),
            P(None, ("dp", "expert")),
            P("expert", None),
            P("expert", None, None),
            P("expert", None, None),
            P("expert"),
        ),
        check_vma=False,
    )
```
